32 devices in a mesh: seq: 16 (over z, y, x), head: 2 (over core).
Axes of the slice: x: 2, y: 2, z: 4, core: 2. Of those that a mesh axis runs over, the one named last changes fastest.
Arguments:
- tokens: bfloat16 [2, 2048, 768], P(None, 'seq'), may hold values from -6 to 6
- cotangent: bfloat16 [2, 2048, 768], P(None, 'seq'), may hold values from -6 to 6
- masked: int32 [2, 2048], P(None, 'seq'), may hold values from 0 to 1, as said below
- projections: bfloat16 [2, 3, 768, 768], P(None, None, None, 'head'), may hold values from -0.3125 to 0.3125
- projection_bias: bfloat16 [2, 2, 768], P(None, None, 'head'), may hold values from -4 to 4
- conv_taps: bfloat16 [2, 12, 65], P(None, 'head'), may hold values from -1.75 to 1.75
- output_weight: bfloat16 [2, 768, 768], P(None, 'head'), may hold values from -0.4375 to 0.4375
- output_bias: bfloat16 [2, 2, 768], replicated, may hold values from -4 to 4
- norm_gain: bfloat16 [2, 2, 768], replicated, may hold values from 0.5 to 1.5
- norm_shift: bfloat16 [2, 2, 768], replicated, may hold values from -4 to 4
- inner_weight: bfloat16 [2, 768, 3072], P(None, None, 'head'), may hold values from -0.21875 to 0.21875
- inner_bias: bfloat16 [2, 3072], P(None, 'head'), may hold values from -4 to 4
- outer_weight: bfloat16 [2, 3072, 768], P(None, 'head'), may hold values from -0.109375 to 0.109375
Outputs:
- result: float32 [2, 2048, 768], P(None, 'seq')
- grad_tokens: float32 [2, 2048, 768], P(None, 'seq')
- grad_projections: float32 [2, 3, 768, 768], P(None, None, 'seq', 'head')
- grad_projection_bias: float32 [2, 2, 768], P(None, None, 'head')
- grad_conv_taps: float32 [2, 12, 65], P(None, 'head')
- grad_output_weight: float32 [2, 768, 768], P(None, 'head', 'seq')
- grad_output_bias: float32 [2, 2, 768], replicated
- grad_norm_gain: float32 [2, 2, 768], replicated
- grad_norm_shift: float32 [2, 2, 768], replicated
- grad_inner_weight: float32 [2, 768, 3072], P(None, 'seq', 'head')
- grad_inner_bias: float32 [2, 3072], P(None, 'head')
- grad_outer_weight: float32 [2, 3072, 768], P(None, 'head', 'seq')
The draws below stay inside these ranges and needn't reach their ends.
Inputs may be any that keep to these rules, and one draw needn't show every extreme that they name: Each sequence has its own share of masked positions, drawn between 5 and 25 percent.
All inputs are finite; a program needn't handle non-finite values.
Results may differ from the reference program's by a relative error of at most 0.03.
Values may be sent and summed in bfloat16 or wider, within the bound.
A program may use at most 192 MiB of HBM per device.

```python
import jax
import jax.numpy as jnp
from jax import lax

D = 768
HEADS = 12
FF = 3072
LANDMARKS = 64
KERNEL = 65
PINV_ITERS = 6
LAYERS = 2
ITEMS = 2
LEN = 2048
N_HEAD = 2


def draw_tokens(key, part):
    key = jax.random.fold_in(key, 11)
    span_rows = max(1, LEN // (2 * LANDMARKS))
    group_count = LEN // span_rows
    common_key, noise_key = jax.random.split(key)
    common = jax.random.normal(common_key, (ITEMS, group_count, D), jnp.float32)
    noise = jax.random.normal(noise_key, (ITEMS, LEN, D), jnp.float32)
    expanded = jnp.repeat(common, span_rows, axis=1)
    return jnp.clip(0.8 * expanded + 0.6 * noise, -6.0, 6.0).astype(jnp.bfloat16)


def draw_masked(key, part):
    key = jax.random.fold_in(key, 23)
    rate_key, pick_key = jax.random.split(key)
    shares = jax.random.randint(rate_key, (ITEMS, 1), 5, 26)
    picks = jax.random.randint(pick_key, (ITEMS, LEN), 0, 100)
    return (picks < shares).astype(jnp.int32)


def shard_levels(key, extent, shards, smallest, top_value):
    factor_of = 1.0
    for dim, parts in shards:
        heights = jax.random.uniform(jax.random.fold_in(jax.random.fold_in(key, 6), dim), (parts,), jnp.float32, smallest / len(shards), top_value / len(shards))
        factor_of = factor_of * jnp.repeat(jnp.exp(heights), extent[dim] // parts).reshape((-1,) + (1,) * (len(extent) - 1 - dim))
    return factor_of


def bell_draw(own_key, dims, scale, reach, pieces=(), kind=jnp.bfloat16):
    loudness = shard_levels(own_key, dims, pieces, -0.22, 0.18) if pieces else 1.0
    values = jax.random.normal(own_key, dims, jnp.float32) * scale * loudness
    return jnp.minimum(jnp.maximum(values, -reach), reach).astype(kind)


def setup_inputs(seed: int = 0) -> dict:
    key_list = jax.random.split(jax.random.key(seed), 14)
    tokens = draw_tokens(jax.random.fold_in(key_list[13], 71), 0)
    cotangent = bell_draw(key_list[1], (ITEMS, LEN, D), 1.0, 6.0, ((1, 16),))
    masked = draw_masked(jax.random.fold_in(key_list[13], 71), 0)
    projections = bell_draw(key_list[3], (LAYERS, 3, D, D), (D // 2) ** -0.5, 0.3125, ((3, 2),))
    projection_bias = bell_draw(key_list[4], (LAYERS, 2, D), 0.3, 4.0, ((2, 2),))
    conv_taps = bell_draw(key_list[5], (LAYERS, HEADS, KERNEL), (1.0 / KERNEL ** 0.5), 1.75, ((1, 2),))
    output_weight = bell_draw(key_list[6], (LAYERS, D, D), (D // 4) ** -0.5, 0.4375, ((1, 2),))
    output_bias = bell_draw(key_list[7], (LAYERS, 2, D), 0.3, 4.0)
    norm_gain = jnp.clip(1.0 + 0.1 * jax.random.normal(key_list[8], (LAYERS, 2, D), jnp.float32), 0.5, 1.5).astype(jnp.bfloat16)
    norm_shift = bell_draw(key_list[9], (LAYERS, 2, D), 0.3, 4.0)
    inner_weight = bell_draw(key_list[10], (LAYERS, D, FF), D ** -0.5, 0.21875, ((2, 2),))
    inner_bias = bell_draw(key_list[11], (LAYERS, FF), 0.3, 4.0, ((1, 2),))
    outer_weight = bell_draw(key_list[12], (LAYERS, FF, D), FF ** -0.5, 0.109375, ((1, 2),))
    return {"tokens": tokens, "cotangent": cotangent, "masked": masked, "projections": projections, "projection_bias": projection_bias, "conv_taps": conv_taps, "output_weight": output_weight, "output_bias": output_bias, "norm_gain": norm_gain, "norm_shift": norm_shift, "inner_weight": inner_weight, "inner_bias": inner_bias, "outer_weight": outer_weight}


exact_result = lax.Precision.HIGHEST
epsilon = 1e-05

@jax.custom_vjp
def low(v):
    return lax.optimization_barrier(v.astype(jnp.bfloat16)).astype(jnp.float32)

@jax.custom_vjp
def low_back(v):
    return v

def low_keep(v):
    return (low(v), None)

def low_pass(kept, grad):
    return (grad,)

def back_keep(v):
    return (v, None)

def back_low(kept, grad):
    return (low(grad),)
low.defvjp(low_keep, low_pass)
low_back.defvjp(back_keep, back_low)

def layer_norm(values, scaling, offset):
    centre = lax.optimization_barrier(jnp.mean(values, -1, keepdims=True))
    centred = values - centre
    spread = lax.optimization_barrier(jnp.mean(centred * centred, -1, keepdims=True))
    return centred * lax.rsqrt(spread + epsilon) * scaling + offset

def soft_rows(scores):
    highest = lax.optimization_barrier(jnp.max(scores, -1, keepdims=True))
    powers = jnp.exp(scores - highest)
    return powers / lax.optimization_barrier(jnp.sum(powers, -1, keepdims=True))

def pseudo_inverse(weight_matrix):
    size_of = weight_matrix.shape[-1]
    column_top = lax.optimization_barrier(jnp.max(lax.optimization_barrier(jnp.sum(weight_matrix, axis=-2)), axis=-1))[..., None, None]
    approximate_result = jnp.swapaxes(weight_matrix, -1, -2) / column_top
    identity = jnp.eye(size_of, dtype=jnp.float32)
    for repeat in range(PINV_ITERS):
        product = jnp.matmul(weight_matrix, approximate_result, precision=exact_result)
        nested = 7.0 * identity - product
        nested = 15.0 * identity - jnp.matmul(product, nested, precision=exact_result)
        nested = 13.0 * identity - jnp.matmul(product, nested, precision=exact_result)
        approximate_result = 0.25 * jnp.matmul(approximate_result, nested, precision=exact_result)
    return approximate_result

def product_rows(product_input, weight_matrix):
    return jnp.einsum('yrn,nh->yrh', product_input, weight_matrix, precision=exact_result)

def heads_view(joined):
    batch_count, length, channels = joined.shape
    return joined.reshape(batch_count, length, HEADS, channels // HEADS).transpose(0, 2, 1, 3)

def tokens_view(by_head):
    batch_count, head_count, length, head_depth = by_head.shape
    return by_head.transpose(0, 2, 1, 3).reshape(batch_count, length, head_count * head_depth)

def attention_layer(hidden, projection, projection_shift, conv_kernel, output_matrix, output_shift, gain_pair, shift_pair, inner_matrix, inner_shift, outer_matrix):
    batch_count, length, model_width = hidden.shape
    group_width = D // N_HEAD
    group_inner = FF // N_HEAD
    head_depth = D // HEADS
    segment = length // LANDMARKS
    margin = KERNEL // 2
    scale = float(head_depth) ** (-0.25)
    hidden_low = low(hidden)
    query_parts, key_parts, value_parts = ([], [], [])
    for group_index in range(N_HEAD):
        lowest = group_index * group_width
        upper_end = lowest + group_width
        query_parts.append(product_rows(hidden_low, projection[0, :, lowest:upper_end]) + projection_shift[0, lowest:upper_end])
        key_parts.append(product_rows(hidden_low, projection[1, :, lowest:upper_end]))
        value_parts.append(product_rows(hidden_low, projection[2, :, lowest:upper_end]) + projection_shift[1, lowest:upper_end])
    query_heads = heads_view(low_back(jnp.concatenate(query_parts, -1)) * scale)
    key_heads = heads_view(low_back(jnp.concatenate(key_parts, -1)) * scale)
    value_heads = heads_view(low(low_back(jnp.concatenate(value_parts, -1))))
    query_marks = lax.optimization_barrier(jnp.mean(query_heads.reshape(batch_count, HEADS, LANDMARKS, segment, head_depth), axis=3))
    key_marks = lax.optimization_barrier(jnp.mean(key_heads.reshape(batch_count, HEADS, LANDMARKS, segment, head_depth), axis=3))
    mark_weights = soft_rows(jnp.einsum('bhme,bhne->bhmn', query_marks, key_marks, precision=exact_result))
    inverse = pseudo_inverse(mark_weights)
    row_weights = soft_rows(jnp.einsum('bhte,bhme->bhtm', query_heads, key_marks, precision=exact_result))
    key_weights = soft_rows(jnp.einsum('bhme,bhte->bhmt', query_marks, key_heads, precision=exact_result))
    mixed = jnp.einsum('bhmt,bhte->bhme', key_weights, value_heads, precision=exact_result)
    core = jnp.einsum('bhmn,bhne->bhme', inverse, mixed, precision=exact_result)
    attended = jnp.einsum('bhtm,bhme->bhte', row_weights, core, precision=exact_result)
    padded = jnp.pad(value_heads, ((0, 0), (0, 0), (margin, margin), (0, 0)))
    convolved = jnp.zeros_like(value_heads)
    for offset in range(KERNEL):
        convolved = convolved + padded[:, :, offset:offset + length, :] * conv_kernel[:, offset][None, :, None, None]
    context = low(low_back(tokens_view(attended) + tokens_view(convolved)))
    attention_sum = low_back(product_rows(context, output_matrix))
    normed = layer_norm(hidden + attention_sum + output_shift[0], gain_pair[0], shift_pair[0])
    normed_low = low(normed)
    feed_terms = []
    for group_index in range(N_HEAD):
        lowest = group_index * group_inner
        upper_end = lowest + group_inner
        pre_active = low_back(product_rows(normed_low, inner_matrix[:, lowest:upper_end]) + inner_shift[lowest:upper_end])
        active = low(low_back(jax.nn.gelu(pre_active, approximate=False)))
        feed_terms.append(product_rows(active, outer_matrix[lowest:upper_end, :]))
    feed_sum = low_back(sum(feed_terms))
    return layer_norm(normed + feed_sum + output_shift[1], gain_pair[1], shift_pair[1])

def forward_pass(start_rows, weights):
    hidden = start_rows
    for layer_index in range(LAYERS):
        hidden = attention_layer(hidden, *[tensor[layer_index] for tensor in weights])
    return hidden

def reference(tokens, cotangent, masked, projections, projection_bias, conv_taps, output_weight, output_bias, norm_gain, norm_shift, inner_weight, inner_bias, outer_weight):
    weights = tuple((tensor.astype(jnp.float32) for tensor in (projections, projection_bias, conv_taps, output_weight, output_bias, norm_gain, norm_shift, inner_weight, inner_bias, outer_weight)))
    result, pullback = jax.vjp(forward_pass, tokens.astype(jnp.float32), weights)
    weighted = cotangent.astype(jnp.float32) * masked.astype(jnp.float32)[:, :, None]
    grad_tokens, grad_weights = pullback(weighted)
    return (result, grad_tokens, grad_weights[0], grad_weights[1], grad_weights[2], grad_weights[3], grad_weights[4], grad_weights[5], grad_weights[6], grad_weights[7], grad_weights[8], grad_weights[9])
```

```python
from functools import partial

import jax
import jax.numpy as jnp
from jax import lax
from jax.experimental import pallas as pl
from jax.experimental.pallas import tpu as pltpu
from jax.sharding import PartitionSpec as P

LANDMARKS = 64
PINV_ITERS = 6
LAYERS = 2


exact_result = lax.Precision.HIGHEST
epsilon = 1e-05


VMEM_LIMIT = 64 * 1024 * 1024 - 128 * 1024


def extended(block, sides, width):
    for axis, dim in sides:
        count = lax.axis_size(axis)
        forward = [(i, i + 1) for i in range(count - 1)]
        backward = [(target, source) for source, target in forward]
        low = lax.ppermute(
            lax.slice_in_dim(block, block.shape[dim] - width, None, axis=dim), axis, forward
        )
        high = lax.ppermute(lax.slice_in_dim(block, 0, width, axis=dim), axis, backward)
        block = jnp.concatenate([low, block, high], axis=dim)
    return block


def layer_norm(values, scaling, offset):
    centre = jnp.mean(values, -1, keepdims=True)
    centred = values - centre
    spread = jnp.mean(centred * centred, -1, keepdims=True)
    return centred * lax.rsqrt(spread + epsilon) * scaling + offset


def soft_rows(scores):
    highest = jnp.max(scores, -1, keepdims=True)
    powers = jnp.exp(scores - highest)
    return powers / jnp.sum(powers, -1, keepdims=True)


def pseudo_inverse(weight_matrix):
    size_of = weight_matrix.shape[-1]
    column_top = jnp.max(jnp.sum(weight_matrix, axis=-2), axis=-1)[..., None, None]
    approximate_result = jnp.swapaxes(weight_matrix, -1, -2) / column_top
    identity = jnp.eye(size_of, dtype=jnp.float32)
    for repeat in range(PINV_ITERS):
        product = jnp.matmul(weight_matrix, approximate_result, precision=exact_result)
        nested = 7.0 * identity - product
        nested = 15.0 * identity - jnp.matmul(product, nested, precision=exact_result)
        nested = 13.0 * identity - jnp.matmul(product, nested, precision=exact_result)
        approximate_result = 0.25 * jnp.matmul(approximate_result, nested, precision=exact_result)
    return approximate_result


def rounded(values):
    return lax.optimization_barrier(values.astype(jnp.bfloat16)).astype(jnp.float32)


def heads_view(joined, heads_local):
    batch_count, length, channels = joined.shape
    return joined.reshape(batch_count, length, heads_local, channels // heads_local).transpose(
        0, 2, 1, 3
    )


def tokens_view(by_head):
    batch_count, heads_local, length, head_depth = by_head.shape
    return by_head.transpose(0, 2, 1, 3).reshape(batch_count, length, heads_local * head_depth)


def convolve(padded, broad_kernel_taps, length):

    def add_tap(offset, running):
        window = lax.dynamic_slice_in_dim(padded, offset, length, 1).astype(jnp.float32)
        return running + window * lax.dynamic_index_in_dim(broad_kernel_taps, offset, 0, False)

    initial = jnp.zeros((padded.shape[0], length, padded.shape[2]), jnp.float32)
    return lax.fori_loop(0, broad_kernel_taps.shape[0], add_tap, initial)


def tap_sums(padded, upstream, length, kernel):

    def one_tap(offset):
        window = lax.dynamic_slice_in_dim(padded, offset, length, 1).astype(jnp.float32)
        return jnp.sum(window * upstream, axis=(0, 1))

    return lax.map(one_tap, jnp.arange(kernel, dtype=jnp.int32))


def across_heads(summand):
    return lax.psum_scatter(
        summand.astype(jnp.bfloat16), "head", scatter_dimension=0, tiled=True
    ).astype(jnp.float32)


def rows_low(share):
    return lax.all_gather(share, "head", axis=0, tiled=True)


def rows_float(share):
    return lax.all_gather(share.astype(jnp.bfloat16), "head", axis=0, tiled=True).astype(
        share.dtype
    )


def own_rows(whole_rows):
    share = whole_rows.shape[0] // lax.axis_size("head")
    return lax.dynamic_slice_in_dim(whole_rows, lax.axis_index("head") * share, share, 0)


def spread_heads(share, dim_index):
    groups = lax.axis_size("head")
    full_shape = list(share.shape)
    full_shape[dim_index] = full_shape[dim_index] * groups
    empty = jnp.zeros(full_shape, jnp.float32)
    return lax.dynamic_update_slice_in_dim(
        empty, share, lax.axis_index("head") * share.shape[dim_index], dim_index
    )


def own_heads(whole, width, dim_index):
    return lax.dynamic_slice_in_dim(whole, lax.axis_index("head") * width, width, dim_index)


def forward_layer(hidden, weights, selector, segment):
    (
        projection,
        projection_shift,
        conv_kernel,
        output_matrix,
        output_shift,
        gain_pair,
        shift_pair,
        inner_matrix,
        inner_shift,
        outer_matrix,
    ) = weights
    batch_count, length, model_width = hidden.shape
    heads_local = conv_kernel.shape[0]
    kernel = conv_kernel.shape[1]
    margin = kernel // 2
    local_width = projection.shape[2]
    head_depth = local_width // heads_local
    scale = float(head_depth) ** (-0.25)
    hidden_low = hidden.astype(jnp.bfloat16).reshape(batch_count * length, model_width)
    projected = jnp.einsum(
        "nd,kde->kne", hidden_low, projection, preferred_element_type=jnp.float32
    )
    biases = projection_shift.astype(jnp.float32)
    query_rows = ((projected[0] + biases[0]) * scale).reshape(batch_count, length, local_width)
    key_rows = (projected[1] * scale).reshape(batch_count, length, local_width)
    value_low = (
        (projected[2] + biases[1]).astype(jnp.bfloat16).reshape(batch_count, length, local_width)
    )
    query_sums, key_sums = lax.psum(
        (
            jnp.einsum("mt,btc->bmc", selector, query_rows, precision=exact_result),
            jnp.einsum("mt,btc->bmc", selector, key_rows, precision=exact_result),
        ),
        "seq",
    )
    query_marks = heads_view(query_sums / segment, heads_local)
    key_marks = heads_view(key_sums / segment, heads_local)
    query_heads = heads_view(query_rows, heads_local)
    key_heads = heads_view(key_rows, heads_local)
    value_heads = heads_view(value_low.astype(jnp.float32), heads_local)
    mark_weights = soft_rows(
        jnp.einsum("bhme,bhne->bhmn", query_marks, key_marks, precision=exact_result)
    )
    inverse = pseudo_inverse(mark_weights)
    row_weights = soft_rows(
        jnp.einsum("bhte,bhme->bhtm", query_heads, key_marks, precision=exact_result)
    )
    key_scores = jnp.einsum("bhme,bhte->bhmt", query_marks, key_heads, precision=exact_result)
    local_top = jnp.max(key_scores, -1)
    score_top = lax.pmax(local_top, "seq")
    powers = jnp.exp(key_scores - score_top[..., None])
    neighbour_mixture = jnp.einsum("bhmt,bhte->bhme", powers, value_heads, precision=exact_result)
    score_total, mixed_joined = lax.psum(
        (jnp.sum(powers, -1), neighbour_mixture.reshape(batch_count, heads_local, -1)), "seq"
    )
    mixed_sum = mixed_joined.reshape(neighbour_mixture.shape)
    log_total = score_top + jnp.log(score_total)
    mixed = mixed_sum / score_total[..., None]
    core = jnp.einsum("bhmn,bhne->bhme", inverse, mixed, precision=exact_result)
    attended = jnp.einsum("bhtm,bhme->bhte", row_weights, core, precision=exact_result)
    padded_values = extended(value_low, (("seq", 1),), margin)
    broad_kernel_taps = jnp.repeat(conv_kernel.astype(jnp.float32), head_depth, axis=0).T
    context = tokens_view(attended) + convolve(padded_values, broad_kernel_taps, length)
    context_low = context.astype(jnp.bfloat16).reshape(batch_count * length, local_width)
    attention_share = across_heads(
        jnp.dot(context_low, output_matrix, preferred_element_type=jnp.float32)
    )
    shifts = output_shift.astype(jnp.float32)
    gains = gain_pair.astype(jnp.float32)
    offsets = shift_pair.astype(jnp.float32)
    hidden_share = own_rows(hidden.reshape(batch_count * length, model_width))
    total_first = hidden_share + attention_share + shifts[0]
    normed = layer_norm(total_first, gains[0], offsets[0])
    normed_low = rows_low(normed.astype(jnp.bfloat16))
    pre_active = jnp.dot(
        normed_low, inner_matrix, preferred_element_type=jnp.float32
    ) + inner_shift.astype(jnp.float32)
    active_low = jax.nn.gelu(pre_active, approximate=False).astype(jnp.bfloat16)
    feed_share = across_heads(jnp.dot(active_low, outer_matrix, preferred_element_type=jnp.float32))
    total_second = normed + feed_share + shifts[1]
    output = rows_float(layer_norm(total_second, gains[1], offsets[1])).reshape(hidden.shape)
    retained = (
        hidden_low,
        query_heads,
        key_heads,
        value_heads,
        padded_values,
        query_marks,
        key_marks,
        mark_weights,
        inverse,
        row_weights,
        log_total,
        mixed,
        core,
        context_low,
        total_first,
        normed_low,
        pre_active,
        active_low,
        total_second,
        broad_kernel_taps,
    )
    return (output, retained)


def backward_layer(upstream, retained, weights, selector, segment):
    (
        projection,
        projection_shift,
        conv_kernel,
        output_matrix,
        output_shift,
        gain_pair,
        shift_pair,
        inner_matrix,
        inner_shift,
        outer_matrix,
    ) = weights
    (
        hidden_low,
        query_heads,
        key_heads,
        value_heads,
        padded_values,
        query_marks,
        key_marks,
        mark_weights,
        inverse,
        row_weights,
        log_total,
        mixed,
        core,
        context_low,
        total_first,
        normed_low,
        pre_active,
        active_low,
        total_second,
        broad_kernel_taps,
    ) = retained
    batch_count, length, model_width = upstream.shape
    heads_local = conv_kernel.shape[0]
    kernel = conv_kernel.shape[1]
    margin = kernel // 2
    local_width = projection.shape[2]
    head_depth = local_width // heads_local
    scale = float(head_depth) ** (-0.25)
    gains = gain_pair.astype(jnp.float32)
    offsets = shift_pair.astype(jnp.float32)
    upstream_share = own_rows(upstream.reshape(batch_count * length, model_width))
    second_pull = jax.vjp(layer_norm, total_second, gains[1], offsets[1])[1]
    grad_second, gain_second, offset_second = second_pull(upstream_share)
    feed_low = rows_low(grad_second.astype(jnp.bfloat16))
    grad_outer = jnp.einsum("nf,nd->fd", active_low, feed_low, preferred_element_type=jnp.float32)
    grad_active = rounded(
        jnp.einsum("nd,fd->nf", feed_low, outer_matrix, preferred_element_type=jnp.float32)
    )
    gelu_pull = jax.vjp(partial(jax.nn.gelu, approximate=False), pre_active)[1]
    grad_pre_low = gelu_pull(grad_active)[0].astype(jnp.bfloat16)
    grad_inner_shift = jnp.sum(grad_pre_low.astype(jnp.float32), axis=0)
    grad_inner = jnp.einsum(
        "nd,nf->df", normed_low, grad_pre_low, preferred_element_type=jnp.float32
    )
    normed_term = jnp.einsum(
        "nf,df->nd", grad_pre_low, inner_matrix, preferred_element_type=jnp.float32
    )
    grad_normed = grad_second + across_heads(normed_term)
    first_pull = jax.vjp(layer_norm, total_first, gains[0], offsets[0])[1]
    grad_first, gain_first, offset_first = first_pull(grad_normed)
    attend_low = rows_low(grad_first.astype(jnp.bfloat16))
    grad_output = jnp.einsum(
        "nc,nd->cd", context_low, attend_low, preferred_element_type=jnp.float32
    )
    grad_context_low = (
        jnp.einsum("nd,cd->nc", attend_low, output_matrix, preferred_element_type=jnp.float32)
        .astype(jnp.bfloat16)
        .reshape(batch_count, length, local_width)
    )
    grad_context = lax.optimization_barrier(grad_context_low).astype(jnp.float32)
    padded_grads = extended(grad_context_low, (("seq", 1),), margin)
    grad_conv_values = convolve(padded_grads, broad_kernel_taps[::-1], length)
    kernel_sums = tap_sums(padded_values, grad_context, length, kernel)
    grad_kernel = kernel_sums.reshape(kernel, heads_local, head_depth).sum(-1).T
    grad_attended = heads_view(grad_context, heads_local)
    grad_row = jnp.einsum("bhte,bhme->bhtm", grad_attended, core, precision=exact_result)
    grad_core_local = jnp.einsum(
        "bhtm,bhte->bhme", row_weights, grad_attended, precision=exact_result
    )
    grad_row_scores = row_weights * (grad_row - jnp.sum(row_weights * grad_row, -1, keepdims=True))
    grad_query = jnp.einsum("bhtm,bhme->bhte", grad_row_scores, key_marks, precision=exact_result)
    grad_keymark_local = jnp.einsum(
        "bhtm,bhte->bhme", grad_row_scores, query_heads, precision=exact_result
    )
    grad_core_joined, grad_keymark_joined = lax.psum(
        (
            grad_core_local.reshape(batch_count, heads_local, -1),
            grad_keymark_local.reshape(batch_count, heads_local, -1),
        ),
        "seq",
    )
    grad_core = grad_core_joined.reshape(core.shape)
    grad_inverse = jnp.einsum("bhme,bhne->bhmn", grad_core, mixed, precision=exact_result)
    grad_mixed = jnp.einsum("bhnm,bhne->bhme", inverse, grad_core, precision=exact_result)
    grad_marks = jax.vjp(pseudo_inverse, mark_weights)[1](grad_inverse)[0]
    grad_mark_scores = mark_weights * (
        grad_marks - jnp.sum(mark_weights * grad_marks, -1, keepdims=True)
    )
    grad_querymark = jnp.einsum(
        "bhmn,bhne->bhme", grad_mark_scores, key_marks, precision=exact_result
    )
    grad_keymark = grad_keymark_joined.reshape(key_marks.shape) + jnp.einsum(
        "bhmn,bhme->bhne", grad_mark_scores, query_marks, precision=exact_result
    )
    key_scores = jnp.einsum("bhme,bhte->bhmt", query_marks, key_heads, precision=exact_result)
    key_weights = jnp.exp(key_scores - log_total[..., None])
    grad_values = jnp.einsum("bhmt,bhme->bhte", key_weights, grad_mixed, precision=exact_result)
    offset_term = jnp.sum(grad_mixed * mixed, -1)
    grad_key_scores = key_weights * (
        jnp.einsum("bhme,bhte->bhmt", grad_mixed, value_heads, precision=exact_result)
        - offset_term[..., None]
    )
    grad_key = jnp.einsum("bhmt,bhme->bhte", grad_key_scores, query_marks, precision=exact_result)
    grad_querymark_local = jnp.einsum(
        "bhmt,bhte->bhme", grad_key_scores, key_heads, precision=exact_result
    )
    grad_querymark = grad_querymark + lax.psum(
        grad_querymark_local.reshape(batch_count, heads_local, -1), "seq"
    ).reshape(query_marks.shape)
    grad_query = (
        grad_query
        + jnp.einsum("mt,bhme->bhte", selector, grad_querymark, precision=exact_result) / segment
    )
    grad_key = (
        grad_key
        + jnp.einsum("mt,bhme->bhte", selector, grad_keymark, precision=exact_result) / segment
    )
    grad_values = grad_values + heads_view(grad_conv_values, heads_local)
    query_low = (
        (tokens_view(grad_query) * scale)
        .astype(jnp.bfloat16)
        .reshape(batch_count * length, local_width)
    )
    key_low = (
        (tokens_view(grad_key) * scale)
        .astype(jnp.bfloat16)
        .reshape(batch_count * length, local_width)
    )
    value_grad_low = (
        tokens_view(grad_values).astype(jnp.bfloat16).reshape(batch_count * length, local_width)
    )
    stacked = jnp.stack([query_low, key_low, value_grad_low])
    grad_projection = jnp.einsum(
        "nd,kne->kde", hidden_low, stacked, preferred_element_type=jnp.float32
    )
    grad_projection_shift = jnp.stack(
        [
            jnp.sum(query_low.astype(jnp.float32), axis=0),
            jnp.sum(value_grad_low.astype(jnp.float32), axis=0),
        ]
    )
    input_term = jnp.einsum("kne,kde->nd", stacked, projection, preferred_element_type=jnp.float32)
    grad_hidden = rows_float(grad_first + across_heads(input_term)).reshape(upstream.shape)
    gradients = (
        grad_projection,
        grad_projection_shift,
        grad_kernel,
        grad_output,
        jnp.stack([jnp.sum(grad_first, axis=0), jnp.sum(grad_second, axis=0)]),
        jnp.stack([gain_first, gain_second]),
        jnp.stack([offset_first, offset_second]),
        grad_inner,
        grad_inner_shift,
        grad_outer,
    )
    return (grad_hidden, gradients)


def on_device(
    tokens,
    cotangent,
    masked,
    projections,
    projection_bias,
    conv_taps,
    output_weight,
    output_bias,
    norm_gain,
    norm_shift,
    inner_weight,
    inner_bias,
    outer_weight,
):
    length = tokens.shape[1]
    segment = length * lax.axis_size("seq") // LANDMARKS
    position = lax.axis_index("seq") * length + jnp.arange(length, dtype=jnp.int32)
    selector = (
        position[None, :] // segment == jnp.arange(LANDMARKS, dtype=jnp.int32)[:, None]
    ).astype(jnp.float32)
    arrays = (
        projections,
        projection_bias,
        conv_taps,
        output_weight,
        output_bias,
        norm_gain,
        norm_shift,
        inner_weight,
        inner_bias,
        outer_weight,
    )
    hidden = tokens.astype(jnp.float32)
    stored = []
    for layer_number in range(LAYERS):
        weights = tuple((tensor[layer_number] for tensor in arrays))
        hidden, retained = forward_layer(hidden, weights, selector, segment)
        stored.append((weights, retained))
    upstream = cotangent.astype(jnp.float32) * masked.astype(jnp.float32)[:, :, None]
    layer_grads = [None] * LAYERS
    for layer_number in range(LAYERS - 1, -1, -1):
        weights, retained = stored[layer_number]
        upstream, gradients = backward_layer(upstream, retained, weights, selector, segment)
        larger = (
            lax.psum_scatter(gradients[0], "seq", scatter_dimension=1, tiled=True),
            lax.psum_scatter(gradients[3], "seq", scatter_dimension=1, tiled=True),
            lax.psum_scatter(gradients[7], "seq", scatter_dimension=0, tiled=True),
            lax.psum_scatter(gradients[9], "seq", scatter_dimension=1, tiled=True),
        )
        gradients = (
            larger[0],
            gradients[1],
            gradients[2],
            larger[1],
            gradients[4],
            gradients[5],
            gradients[6],
            larger[2],
            gradients[8],
            larger[3],
        )
        layer_grads[layer_number] = gradients
    stacked = tuple(
        (
            jnp.stack([layer_grads[layer_number][member] for layer_number in range(LAYERS)])
            for member in range(10)
        )
    )
    larger = (stacked[0], stacked[3], stacked[7], stacked[9])
    bias_width = stacked[1].shape[2]
    taps_width = stacked[2].shape[1]
    inner_width = stacked[8].shape[1]
    smaller = lax.psum(
        (
            spread_heads(stacked[1], 2),
            spread_heads(stacked[2], 1),
            stacked[4],
            stacked[5],
            stacked[6],
            spread_heads(stacked[8], 1),
        ),
        ("seq", "head"),
    )
    grad_bias_share = own_heads(smaller[0], bias_width, 2)
    grad_taps_share = own_heads(smaller[1], taps_width, 1)
    grad_inner_share = own_heads(smaller[5], inner_width, 1)
    return (
        hidden,
        upstream,
        larger[0],
        grad_bias_share,
        grad_taps_share,
        larger[1],
        smaller[2],
        smaller[3],
        smaller[4],
        larger[2],
        grad_inner_share,
        larger[3],
    )


F32 = jnp.float32
BF16 = jnp.bfloat16
MESH = pl.DeviceIdType.MESH


def nn(a, b):
    return lax.dot_general(a, b, (((1,), (0,)), ((), ())), preferred_element_type=F32)


def nt(a, b):
    return lax.dot_general(a, b, (((1,), (1,)), ((), ())), preferred_element_type=F32)


def tn(a, b):
    return lax.dot_general(a, b, (((0,), (0,)), ((), ())), preferred_element_type=F32)


def halves(x):
    high = x.astype(BF16)
    return high, (x - high.astype(F32)).astype(BF16)


def left3(pair, axis):
    return jnp.concatenate([pair[0], pair[1], pair[0]], axis=axis)


def right3(pair, axis):
    return jnp.concatenate([pair[0], pair[0], pair[1]], axis=axis)


def nn3(a, b):
    return nn(left3(a, 1), right3(b, 0))


def nt3(a, b):
    return nt(left3(a, 1), right3(b, 1))


def tn3(a, b):
    return tn(left3(a, 0), right3(b, 0))


def nn3f(a, b):
    return nn3(halves(a), halves(b))


def nt3f(a, b):
    return nt3(halves(a), halves(b))


def tn3f(a, b):
    return tn3(halves(a), halves(b))


class Fast:
    def __init__(self, mesh_shape, tokens, conv_taps, inner_weight):
        self.n = mesh_shape["seq"]
        self.heads = mesh_shape["head"]
        self.batch, whole, self.width = tokens.shape
        self.length = whole // self.n
        self.layers, all_heads, self.kernel = conv_taps.shape
        self.local_heads = all_heads // self.heads
        self.depth = self.width // all_heads
        self.cols = self.local_heads * self.depth
        self.hidden = inner_weight.shape[2] // self.heads
        self.rows = self.batch * self.length
        self.segment = whole // LANDMARKS
        self.spans = self.length // self.segment
        self.units = self.batch * self.local_heads // 2
        self.bits = self.n.bit_length() - 1

    def fits(self):
        return (
            self.n == 1 << self.bits
            and self.n >= 16
            and self.heads == 2
            and self.length == 128
            and self.batch == 2
            and self.spans * self.batch == 8
            and self.depth == 64
            and self.local_heads % 2 == 0
            and self.width % (16 * self.n) == 0
            and self.width % 256 == 0
            and self.hidden % 512 == 0
            and self.kernel == 65
            and self.layers == 2
            and LANDMARKS == 64
        )


def fused_kernel(
    z,
    tok, ups, vec, taps, wp_hbm, wo_hbm, wi_hbm, wf_hbm,
    result, gtok, gproj, gout, ginner, gouter, gsmall,
    *,
    WP, WO, WI, WF,
    HL, QS, KS, VX, RW, KSC, CTX, T1, T2, NL, GP, ACT, QM, KM, CR, MX, PA, PV, PZ, PC,
    HID, UP, DT, FL, DPRE, GX, DQ, DK, DV, DP, DQM, DKM, DR, SM, TT, TR,
    MS, MB, XM, OB, SB, SR, HS, HR, SMR, SMT,
    G, RV,
    wsem, hsem_s, hsem_r, msem_s, msem_r, xsem_s, xsem_r, csem_s, csem_r, vsem_s, vsem_r,
    gsem_s, gsem_r, qsem_s, qsem_r, ssem_s, ssem_r, tsem_s, tsem_r,
):
    n, B, L, R, D, C, F = z.n, z.batch, z.length, z.rows, z.width, z.cols, z.hidden
    U, NP, S, K = z.units, z.local_heads // 2, z.spans, z.kernel
    CH = D // n
    NB = z.bits
    M = LANDMARKS
    margin = K // 2
    scale = float(z.depth) ** (-0.25)
    me = lax.axis_index("seq")
    core = lax.axis_index("head")
    first_owner = n // 2 - U // 2
    is_owner = jnp.logical_and(me >= first_owner, me < first_owner + U)
    mine = jnp.clip(me - first_owner, 0, U - 1)

    def weight_copies(l):
        return [
            pltpu.make_async_copy(wp_hbm.at[l], WP.at[l], wsem.at[l, 0]),
            pltpu.make_async_copy(wo_hbm.at[l], WO.at[l], wsem.at[l, 1]),
            pltpu.make_async_copy(wi_hbm.at[l], WI.at[l], wsem.at[l, 2]),
            pltpu.make_async_copy(wf_hbm.at[l], WF.at[l], wsem.at[l, 3]),
        ]

    for l in range(z.layers):
        for c in weight_copies(l):
            c.start()
    pltpu.make_async_copy(ups, UP, wsem.at[0, 4]).start()

    barrier = pltpu.get_barrier_semaphore()

    def greet(d, _):
        pl.semaphore_signal(
            barrier, inc=1, device_id={"seq": lax.rem(me + d, n)}, device_id_type=MESH
        )
        return 0

    lax.fori_loop(1, n, greet, 0)
    pl.semaphore_signal(barrier, inc=1, device_id={"head": 1 - core}, device_id_type=MESH)
    pl.semaphore_wait(barrier, n)

    row_id = lax.broadcasted_iota(jnp.int32, (128, 128), 0)
    lane_id = lax.broadcasted_iota(jnp.int32, (128, 128), 1)
    low_lane = lane_id < 64
    low_lane64 = low_lane[0:64]
    same_head = (row_id < 64) == low_lane
    eye = row_id == lane_id
    flip = jnp.where(row_id + lane_id == 127, 1.0, 0.0).astype(BF16)

    def expand(c):
        return jnp.concatenate(
            [jnp.where(low_lane64, c, 0.0), jnp.where(low_lane64, 0.0, c)], axis=0
        )

    def compress(x):
        return jnp.where(low_lane64, x[0:64], x[64:128])

    def to_row(col):
        return jnp.sum(jnp.where(eye, col, 0.0), axis=0, keepdims=True)

    def to_col(row):
        return jnp.sum(jnp.where(eye, row, 0.0), axis=1, keepdims=True)

    def half_sums(x):
        a = jnp.sum(jnp.where(low_lane, x, 0.0), axis=1, keepdims=True)
        b = jnp.sum(jnp.where(low_lane, 0.0, x), axis=1, keepdims=True)
        return jnp.where(low_lane, a, b)

    def half_tops(x):
        a = jnp.max(jnp.where(low_lane, x, -jnp.inf), axis=1, keepdims=True)
        b = jnp.max(jnp.where(low_lane, -jnp.inf, x), axis=1, keepdims=True)
        return jnp.where(low_lane, a, b)

    def unit(u):
        return u // NP, u % NP

    def tile(ref, l, u):
        b, j = unit(u)
        return ref[l, b * L : (b + 1) * L, j * 128 : (j + 1) * 128]

    def pair_tile(ref, l, u):
        b, j = unit(u)
        return tuple(
            ref[l, p, b * L : (b + 1) * L, j * 128 : (j + 1) * 128] for p in range(2)
        )

    def moments(x):
        centre = jnp.mean(x, -1, keepdims=True)
        centred = x - centre
        spread = jnp.mean(centred * centred, -1, keepdims=True)
        inverse = lax.rsqrt(spread + epsilon)
        return centred * inverse, inverse

    def norm_back(x, grad, gain):
        hat, inverse = moments(x)
        g = grad * gain
        a = jnp.mean(g, -1, keepdims=True)
        b = jnp.mean(g * hat, -1, keepdims=True)
        total = inverse * (g - a - hat * b)
        sums = (
            jnp.sum(grad * hat, axis=0, keepdims=True),
            jnp.sum(grad, axis=0, keepdims=True),
            jnp.sum(total, axis=0, keepdims=True),
        )
        return total, sums

    def put_small(start, vector):
        for i in range(vector.shape[1] // 128):
            SM[start + i : start + i + 1, :] = vector[:, i * 128 : (i + 1) * 128]

    def swap(e):
        return pltpu.make_async_remote_copy(
            HS.at[e % 2], HR.at[e % 2], hsem_s.at[e], hsem_r.at[e],
            device_id={"head": 1 - core}, device_id_type=MESH,
        )

    def both(e):
        return HS[e % 2].astype(F32) + HR[e % 2].astype(F32)

    def spread(src, dst, ss, rs, start):
        def step(d, _):
            t = lax.rem(me + d, n)
            c = pltpu.make_async_remote_copy(
                src(t), dst.at[me], ss.at[t], rs.at[me], device_id={"seq": t}, device_id_type=MESH
            )
            c.start()
            return 0

        def finish(d, _):
            t = lax.rem(me + d, n)
            c = pltpu.make_async_remote_copy(
                src(t), dst.at[t], ss.at[t], rs.at[t], device_id={"seq": t}, device_id_type=MESH
            )
            c.wait_recv()
            c.wait_send()
            return 0

        lax.fori_loop(1, n, step if start else finish, 0)

    def to_owner(u, rows, ss, rs):
        c = pltpu.make_async_remote_copy(
            XM.at[u, pl.ds(0, rows)], OB.at[me, pl.ds(0, rows)], ss.at[u], rs.at[me],
            device_id={"seq": first_owner + u}, device_id_type=MESH,
        )

        @pl.when(me != first_owner + u)
        def _():
            c.start()

        @pl.when(me == first_owner + u)
        def _():
            OB[me, 0:rows] = XM[u, 0:rows]

    def to_owner_sent(u, rows, ss, rs):
        @pl.when(me != first_owner + u)
        def _():
            pltpu.make_async_remote_copy(
                XM.at[u, pl.ds(0, rows)], OB.at[me, pl.ds(0, rows)], ss.at[u], rs.at[me],
                device_id={"seq": first_owner + u}, device_id_type=MESH,
            ).wait_send()

    def owner_gets(rows, ss, rs):
        def step(d, _):
            t = lax.rem(me + d, n)
            pltpu.make_async_remote_copy(
                XM.at[0, pl.ds(0, rows)], OB.at[t, pl.ds(0, rows)], ss.at[0], rs.at[t],
                device_id={"seq": t}, device_id_type=MESH,
            ).wait_recv()
            return 0

        lax.fori_loop(1, n, step, 0)

    def from_owner(slots, ss, rs, start):
        def step(d, _):
            t = lax.rem(me + d, n)
            c = pltpu.make_async_remote_copy(
                slots.at[mine], slots.at[mine], ss.at[t], rs.at[mine],
                device_id={"seq": t}, device_id_type=MESH,
            )
            if start:
                c.start()
            else:
                c.wait_send()
            return 0

        lax.fori_loop(1, n, step, 0)

    def owner_came(slots, u, ss, rs):
        @pl.when(me != first_owner + u)
        def _():
            pltpu.make_async_remote_copy(
                slots.at[u], slots.at[u], ss.at[0], rs.at[u],
                device_id={"seq": first_owner + u}, device_id_type=MESH,
            ).wait_recv()

    def edges(buf, ss, rs, act):
        after = pltpu.make_async_remote_copy(
            buf.at[:, pl.ds(L, margin)], buf.at[:, pl.ds(0, margin)], ss.at[0], rs.at[0],
            device_id={"seq": lax.rem(me + 1, n)}, device_id_type=MESH,
        )
        before = pltpu.make_async_remote_copy(
            buf.at[:, pl.ds(margin, margin)], buf.at[:, pl.ds(margin + L, margin)], ss.at[1], rs.at[1],
            device_id={"seq": lax.rem(me + n - 1, n)}, device_id_type=MESH,
        )
        if act == "start":
            @pl.when(me < n - 1)
            def _():
                after.start()

            @pl.when(me > 0)
            def _():
                before.start()
        else:
            @pl.when(me < n - 1)
            def _():
                after.wait_send()
                before.wait_recv()

            @pl.when(me > 0)
            def _():
                before.wait_send()
                after.wait_recv()

    def edge_zeros(buf):
        none = jnp.zeros((B, margin, C), BF16)
        buf[:, 2 * margin + L :, :] = jnp.zeros((B, 256 - L - 2 * margin, C), BF16)

        @pl.when(me == 0)
        def _():
            buf[:, 0:margin, :] = none

        @pl.when(me == n - 1)
        def _():
            buf[:, margin + L : 2 * margin + L, :] = none

    def conv(bands, buf, u):
        b, j = unit(u)
        x = buf[b, :, j * 128 : (j + 1) * 128]
        return jnp.where(low_lane, nn(bands[2 * j], x), nn(bands[2 * j + 1], x))

    own_bits = [lax.rem(me // (1 << k), 2) for k in range(NB)]
    orders = [
        list(range(NB)),
        [1, 0] + list(range(2, NB)),
    ]
    HALF = G.shape[-1] // 2
    FH = F // 2
    items = {
        "outer0": (0, FH, 0), "inner0": (FH, FH, 0),
        "tail0": (2 * FH, HALF - 2 * FH, 0),
        "outer1": (HALF, FH, 1), "inner1": (HALF + FH, FH, 1),
        "tail1": (HALF + 2 * FH, HALF - 2 * FH, 1),
    }
    item_index = {name: i for i, name in enumerate(items)}

    def kept(name, stage):
        order = orders[items[name][2]]
        index = [slice(None)] * NB
        for k in order[:stage]:
            index[NB - 1 - k] = own_bits[k]
        return index

    def ref_at(ref, index, cols):
        full = tuple(pl.ds(0, ref.shape[i]) if isinstance(v, slice) else v for i, v in enumerate(index))
        return ref.at[full + (pl.ds(0, CH), pl.ds(cols[0], cols[1]))]

    def rs_copy(l, name, stage):
        first, count, order_id = items[name]
        k = orders[order_id][stage]
        index = kept(name, stage)
        index[NB - 1 - k] = 1 - own_bits[k]
        src = ref_at(G, index, (first, count))
        buf = RV[stage]
        lead = (min(l, buf.shape[0] - 1),)
        free = NB - 1 - stage
        dst = buf.at[lead + (pl.ds(0, 2),) * free + (pl.ds(0, CH), pl.ds(first, count))]
        peer = me + (1 - 2 * own_bits[k]) * (1 << k)
        i = item_index[name]
        return pltpu.make_async_remote_copy(
            src, dst, gsem_s.at[l, i, stage], gsem_r.at[l, i, stage],
            device_id={"seq": peer}, device_id_type=MESH,
        )

    def rs_start(l, name, stage):
        rs_copy(l, name, stage).start()

    def rs_add(l, name, stage):
        first, count, order_id = items[name]
        rs_copy(l, name, stage).wait()
        index = kept(name, stage + 1)
        buf = RV[stage]
        lead = min(l, buf.shape[0] - 1)
        free = [i for i, v in enumerate(index) if isinstance(v, slice)]
        cols = slice(first, first + count)
        if free:
            for code in range(1 << len(free)):
                spot = [(code >> (len(free) - 1 - i)) & 1 for i in range(len(free))]
                at = list(index)
                for f, v in zip(free, spot):
                    at[f] = v
                at = tuple(at)
                G[at + (slice(None), cols)] = (
                    G[at + (slice(None), cols)].astype(F32)
                    + buf[(lead,) + tuple(spot) + (slice(None), cols)].astype(F32)
                ).astype(BF16)
        else:
            at = tuple(index)
            for piece, (c0, cn, put) in outs_of(name, first, count):
                a = G[at + (slice(None), slice(c0, c0 + cn))].astype(F32)
                put(l, a + buf[lead, :, c0 : c0 + cn].astype(F32))

    def outs_of(name, first, count):
        def at(ref, *lead):
            def put(l, x, c):
                ref[(l,) + lead + (slice(None), c)] = x

            return put

        def bind(put, c):
            return lambda l, x: put(l, x, c)

        if name.startswith("outer"):
            o = 0 if name.endswith("0") else FH
            return [(0, (first, FH, bind(at(gouter), slice(o, o + FH))))]
        if name.startswith("inner"):
            o = 0 if name.endswith("0") else FH
            return [(0, (first, FH, bind(at(ginner), slice(o, o + FH))))]
        if name == "tail0":
            return [
                (0, (first, 128, bind(at(gout), slice(0, 128)))),
                (0, (first + 128, C, bind(at(gproj, 0), slice(0, C)))),
                (0, (first + 128 + C, 256, bind(at(gproj, 2), slice(0, 256)))),
            ]
        return [
            (0, (first, C - 128, bind(at(gout), slice(128, C)))),
            (0, (first + C - 128, C, bind(at(gproj, 1), slice(0, C)))),
            (0, (first + 2 * C - 128, C - 256, bind(at(gproj, 2), slice(256, C)))),
        ]

    def weight_grad(left_t, right, first, count, width):
        def step(i, _):
            o = pl.multiple_of(i * width, width)
            x = nn(left_t, right(o)).astype(BF16)
            o = pl.multiple_of(first + o, 128)
            for c in range(n):
                spot = tuple((c >> (NB - 1 - i)) & 1 for i in range(NB))
                G[spot + (slice(None), pl.ds(o, width))] = x[c * CH : (c + 1) * CH]
            return 0

        lax.fori_loop(0, count // width, step, 0)

    HID[...] = tok[...].astype(F32)
    for l in range(z.layers):
        for h in range(z.local_heads):
            for which, store in ((0, TT), (1, TR)):
                base = jnp.broadcast_to(taps[l, which, h : h + 1, :], (128, 256))
                store[l, h] = pltpu.roll(base, 0, 1, stride=1, stride_axis=0).astype(BF16)

    def forward(l):
        copies = weight_copies(l)
        e = 2 * l
        hl = HID[...].astype(BF16)
        HL[l] = hl
        copies[0].wait()
        bias_q, bias_v = vec[l, 0:1, 0:C], vec[l, 0:1, C : 2 * C]
        q = (nn(hl, WP[l, 0]) + bias_q) * scale
        k = nn(hl, WP[l, 1]) * scale
        QS[l, 0], QS[l, 1] = halves(q)
        KS[l, 0], KS[l, 1] = halves(k)
        for b in range(B):
            for r in range(S):
                at = b * L + r * z.segment
                i = b * S + r
                MS[i : i + 1, :] = jnp.sum(q[at : at + z.segment], axis=0, keepdims=True) * (1.0 / z.segment)
                MS[8 + i : 9 + i, :] = jnp.sum(k[at : at + z.segment], axis=0, keepdims=True) * (1.0 / z.segment)
        spread(lambda t: MS, MB, msem_s.at[l], msem_r.at[l], True)
        MB[me] = MS[...]
        vl = (nn(hl, WP[l, 2]) + bias_v).astype(BF16)
        for b in range(B):
            VX[l, b, margin : margin + L, :] = vl[b * L : (b + 1) * L]
        edge_zeros(VX.at[l])
        edges(VX.at[l], vsem_s.at[l], vsem_r.at[l], "start")
        spread(lambda t: MS, MB, msem_s.at[l], msem_r.at[l], False)
        for u in range(U):
            b, j = unit(u)
            for i in range(n):
                at = slice(i * S, (i + 1) * S)
                QM[l, u, at, :] = MB[i, b * S : (b + 1) * S, j * 128 : (j + 1) * 128]
                KM[l, u, at, :] = MB[i, 8 + b * S : 8 + (b + 1) * S, j * 128 : (j + 1) * 128]
        for u in range(U):
            b, j = unit(u)
            qb = expand(QM[l, u])
            ksc = nt3(halves(qb), pair_tile(KS, l, u))
            KSC[l, u] = ksc
            top = jnp.max(ksc, axis=1, keepdims=True)
            p = jnp.exp(ksc - top)
            total = jnp.sum(p, axis=1, keepdims=True)
            v = VX[l, b, margin : margin + L, j * 128 : (j + 1) * 128]
            ph = halves(p)
            x = nn(jnp.concatenate(ph, axis=1), jnp.concatenate([v, v], axis=0))
            XM[u, 0:64] = compress(x)
            XM[u, 64:65] = to_row(top)
            XM[u, 65:66] = to_row(total)
            to_owner(u, 72, xsem_s.at[l], xsem_r.at[l])
        for u in range(U):
            kb = expand(KM[l, u])
            s = nt3(pair_tile(QS, l, u), halves(kb))
            p = jnp.exp(s - half_tops(s))
            RW[l, u] = p / half_sums(p)

        @pl.when(is_owner)
        def _():
            qb, kb = expand(QM[l, mine]), expand(KM[l, mine])
            s = jnp.where(same_head, nt3f(qb, kb), -jnp.inf)
            p = jnp.exp(s - jnp.max(s, axis=1, keepdims=True))
            a = p / jnp.sum(p, axis=1, keepdims=True)
            PA[l] = a
            ah = halves(a)
            sums = jnp.sum(a, axis=0, keepdims=True)
            tops = jnp.where(
                low_lane[0:1],
                jnp.max(jnp.where(low_lane[0:1], sums, 0.0), axis=1, keepdims=True),
                jnp.max(jnp.where(low_lane[0:1], 0.0, sums), axis=1, keepdims=True),
            )
            unit_matrix = jnp.where(eye, 1.0, 0.0)

            def iterate(i, zk):
                PV[l, i, 0] = zk
                zh = halves(zk)
                pr = nn3(ah, zh)
                PV[l, i, 1] = pr
                prh = halves(pr)
                n2 = 15.0 * unit_matrix - nn3(prh, halves(7.0 * unit_matrix - pr))
                PV[l, i, 2] = n2
                n3 = 13.0 * unit_matrix - nn3(prh, halves(n2))
                PV[l, i, 3] = n3
                return 0.25 * nn3(zh, halves(n3))

            zk = lax.fori_loop(0, PINV_ITERS, iterate, a.T / tops)
            PZ[l] = zk
            owner_gets(72, xsem_s.at[l], xsem_r.at[l])
            tops = OB[0, 64:65]
            for i in range(1, n):
                tops = jnp.maximum(tops, OB[i, 64:65])
            factors = [jnp.exp(OB[i, 64:65] - tops) for i in range(n)]
            total = factors[0] * OB[0, 65:66]
            for i in range(1, n):
                total = total + factors[i] * OB[i, 65:66]
            mixed = jnp.zeros((64, 128), F32)
            for i in range(n):
                col = to_col(factors[i] / total)
                mixed = mixed + jnp.where(low_lane64, col[0:64], col[64:128]) * OB[i, 0:64]
            MX[l] = mixed
            CR[l, mine, 0:64] = compress(nn3f(zk, expand(mixed)))
            CR[l, mine, 64:65] = tops + jnp.log(total)
            from_owner(CR.at[l], csem_s.at[l], csem_r.at[l], True)

        edges(VX.at[l], vsem_s.at[l], vsem_r.at[l], "wait")
        for u in range(U):
            b, j = unit(u)
            DQ[b * L : (b + 1) * L, j * 128 : (j + 1) * 128] = conv(TT.at[l], VX.at[l], u)
        for u in range(U):
            b, j = unit(u)
            to_owner_sent(u, 72, xsem_s.at[l], xsem_r.at[l])
            owner_came(CR.at[l], u, csem_s.at[l], csem_r.at[l])
            at = (slice(b * L, (b + 1) * L), slice(j * 128, (j + 1) * 128))
            context = nn3f(RW[l, u], expand(CR[l, u, 0:64])) + DQ[at]
            CTX[(l,) + at] = context.astype(BF16)

        @pl.when(is_owner)
        def _():
            from_owner(CR.at[l], csem_s.at[l], csem_r.at[l], False)

        copies[1].wait()
        HS[e % 2] = nn(CTX[l], WO[l]).astype(BF16)
        c = swap(e)
        c.start()
        c.wait()
        total1 = HID[...] + both(e) + vec[l, 2:3, 0:D]
        T1[l] = total1
        normed = moments(total1)[0] * vec[l, 4:5, 0:D] + vec[l, 6:7, 0:D]
        HID[...] = normed
        NL[l] = normed.astype(BF16)
        copies[2].wait()

        def grow(i, _):
            o = pl.ds(pl.multiple_of(i * 256, 256), 256)
            pre = nn(NL[l], WI[l, :, o]) + vec[l, 1:2, o]
            below = 0.5 * (1.0 + lax.erf(pre * (0.5**0.5)))
            ACT[l, :, o] = (pre * below).astype(BF16)
            GP[l, :, o] = (below + pre * jnp.exp(-0.5 * pre * pre) * 0.3989422804014327).astype(BF16)
            return 0

        lax.fori_loop(0, F // 256, grow, 0)
        copies[3].wait()

        def shrink(i, _):
            o = pl.ds(pl.multiple_of(i * 256, 256), 256)
            HS[(e + 1) % 2, :, o] = nn(ACT[l], WF[l, :, o]).astype(BF16)
            return 0

        lax.fori_loop(0, D // 256, shrink, 0)
        c = swap(e + 1)
        c.start()
        c.wait()
        total2 = HID[...] + both(e + 1) + vec[l, 3:4, 0:D]
        T2[l] = total2
        HID[...] = moments(total2)[0] * vec[l, 5:6, 0:D] + vec[l, 7:8, 0:D]

    def backward(l, left):
        e = 2 * z.layers + 2 * (z.layers - 1 - l)
        base = 60 * l
        total2, sums = norm_back(T2[l], UP[...], vec[l, 5:6, 0:D])
        put_small(base + 6, sums[0])
        put_small(base + 18, sums[1])
        put_small(base + 30, sums[2])
        DT[...] = total2
        FL[...] = total2.astype(BF16)

        def widen(i, _):
            o = pl.ds(pl.multiple_of(i * 256, 256), 256)
            grad = nt(FL[...], WF[l, o, :]).astype(BF16).astype(F32)
            pre = (GP[l, :, o].astype(F32) * grad).astype(BF16)
            DPRE[:, o] = pre
            s = jnp.sum(pre.astype(F32), axis=0, keepdims=True)
            SM[pl.ds(base + 36 + 2 * i, 1), :] = s[:, 0:128]
            SM[pl.ds(base + 37 + 2 * i, 1), :] = s[:, 128:256]
            return 0

        lax.fori_loop(0, F // 256, widen, 0)

        def narrow(i, _):
            o = pl.ds(pl.multiple_of(i * 256, 256), 256)
            HS[e % 2, :, o] = nt(DPRE[...], WI[l, o, :]).astype(BF16)
            return 0

        lax.fori_loop(0, D // 256, narrow, 0)
        c = swap(e)
        c.start()
        for done in left[:1]:
            done()
        feed_t = FL[...].T
        norm_t = NL[l].T
        for h in range(2):
            name = f"outer{h}"
            weight_grad(feed_t, lambda o: ACT[l, :, pl.ds(h * FH + o, 256)], items[name][0], FH, 256)
            rs_start(l, name, 0)
        for h in range(2):
            name = f"inner{h}"
            weight_grad(norm_t, lambda o: DPRE[:, pl.ds(h * FH + o, 256)], items[name][0], FH, 256)
            rs_start(l, name, 0)
        c.wait()
        grad_normed = DT[...] + both(e)
        total1, sums = norm_back(T1[l], grad_normed, vec[l, 4:5, 0:D])
        put_small(base + 0, sums[0])
        put_small(base + 12, sums[1])
        put_small(base + 24, sums[2])
        DT[...] = total1
        attend = total1.astype(BF16)
        FL[...] = attend
        grads = nt(attend, WO[l]).astype(BF16)
        for b in range(B):
            GX[b, margin : margin + L, :] = grads[b * L : (b + 1) * L]
        edge_zeros(GX)
        edges(GX, vsem_s.at[z.layers + l], vsem_r.at[z.layers + l], "start")

        def g_tile(u):
            b, j = unit(u)
            return GX[b, margin : margin + L, j * 128 : (j + 1) * 128]

        for u in range(U):
            g = g_tile(u)
            x = tn(jnp.concatenate(halves(RW[l, u]), axis=0), jnp.concatenate([g, g], axis=0))
            XM[u, 0:64] = compress(x)
            to_owner(u, 64, xsem_s.at[z.layers + l], xsem_r.at[z.layers + l])
            DQM[u] = jnp.zeros((64, 128), F32)
        for u in range(U):
            b, j = unit(u)
            at = (slice(b * L, (b + 1) * L), slice(j * 128, (j + 1) * 128))
            g = g_tile(u)
            core_pair = halves(expand(CR[l, u, 0:64]))
            d_row = nt(jnp.concatenate([g, g], axis=1), jnp.concatenate(core_pair, axis=1))
            rw = RW[l, u]
            d_rs = halves(rw * (d_row - half_sums(rw * d_row)))
            DQ[at] = nn3(d_rs, halves(expand(KM[l, u])))
            DKM[u] = compress(tn3(d_rs, pair_tile(QS, l, u)))

        for done in left[1:2]:
            done()
        advance(l, ("outer0", "outer1"), 0)

        @pl.when(is_owner)
        def _():
            owner_gets(64, xsem_s.at[z.layers + l], xsem_r.at[z.layers + l])
            d_core = OB[0, 0:64]
            for i in range(1, n):
                d_core = d_core + OB[i, 0:64]
            PC[...] = d_core
            d_mixed = tn3f(PZ[l], expand(d_core))
            DR[mine, 0:64] = compress(d_mixed)
            DR[mine, 64:65] = to_row(jnp.sum(d_mixed * expand(MX[l]), axis=1, keepdims=True))
            from_owner(DR, csem_s.at[z.layers + l], csem_r.at[z.layers + l], True)

        for u in range(U):
            to_owner_sent(u, 64, xsem_s.at[z.layers + l], xsem_r.at[z.layers + l])

        @pl.when(is_owner)
        def _():
            a = PA[l]
            ah = halves(a)
            unit_matrix = jnp.where(eye, 1.0, 0.0)

            def back(i, carry):
                dz, da = carry
                i = PINV_ITERS - 1 - i
                zh, prh = halves(PV[l, i, 0]), halves(PV[l, i, 1])
                n1h = halves(7.0 * unit_matrix - PV[l, i, 1])
                n2h, n3h = halves(PV[l, i, 2]), halves(PV[l, i, 3])
                dzh = halves(dz)
                dn3 = halves(0.25 * tn3(zh, dzh))
                dn2 = halves(-tn3(prh, dn3))
                dpr = tn3(prh, dn2) - nt3(dn3, n2h) - nt3(dn2, n1h)
                dpr = halves(dpr)
                dz = 0.25 * nt3(dzh, n3h) + tn3(ah, dpr)
                return dz, da + nt3(dpr, zh)

            dz, da = lax.fori_loop(
                0, PINV_ITERS, back, (nt3f(expand(PC[...]), expand(MX[l])), jnp.zeros((128, 128), F32))
            )
            low_row = low_lane[0:1]

            def half_row(x, f):
                return jnp.where(
                    low_row,
                    f(jnp.where(low_row, x, 0.0), axis=1, keepdims=True),
                    f(jnp.where(low_row, 0.0, x), axis=1, keepdims=True),
                )

            sums = jnp.sum(a, axis=0, keepdims=True)
            tops = half_row(sums, jnp.max)
            d_tops = -half_row(jnp.sum(dz * PV[l, 0, 0], axis=0, keepdims=True), jnp.sum) / tops
            at_top = jnp.where(sums == tops, 1.0, 0.0)
            da = da + (dz / tops).T + at_top * d_tops / half_row(at_top, jnp.sum)
            d_ms = halves(a * (da - jnp.sum(a * da, axis=1, keepdims=True)))
            DQM[mine] = compress(nn3(d_ms, halves(expand(KM[l, mine]))))
            DKM[mine] = DKM[mine] + compress(tn3(d_ms, halves(expand(QM[l, mine]))))

        advance(l, ("inner0", "inner1"), 0)
        advance(l, ("outer0", "outer1"), 1)
        edges(GX, vsem_s.at[z.layers + l], vsem_r.at[z.layers + l], "wait")
        for u in range(U):
            b, j = unit(u)
            at = (slice(b * L, (b + 1) * L), slice(j * 128, (j + 1) * 128))
            DV[at] = conv(TR.at[l], GX, u)
        for j in range(NP):
            for h in range(2):
                found = jnp.zeros((128, 256), F32)
                for b in range(B):
                    g = nn(flip, g_tile(b * NP + j))
                    g = jnp.where(low_lane, g, 0.0) if h == 0 else jnp.where(low_lane, 0.0, g)
                    found = found + nt(g.astype(BF16), VX[l, b, :, j * 128 : (j + 1) * 128])
                found = pltpu.roll(found, 129, 1, stride=1, stride_axis=0)
                row = base + 54 + 2 * j + h
                SM[row : row + 1, :] = jnp.sum(found[:, 0:128], axis=0, keepdims=True)
        for u in range(U):
            b, j = unit(u)
            at = (slice(b * L, (b + 1) * L), slice(j * 128, (j + 1) * 128))
            owner_came(DR, u, csem_s.at[z.layers + l], csem_r.at[z.layers + l])
            qbh = halves(expand(QM[l, u]))
            dmh = halves(expand(DR[u, 0:64]))
            off = to_col(DR[u, 64:65])
            kw = jnp.exp(KSC[l, u] - to_col(CR[l, u, 64:65]))
            v = VX[l, b, margin : margin + L, j * 128 : (j + 1) * 128]
            DV[at] = DV[at] + tn3(halves(kw), dmh)
            d_kw = nt(jnp.concatenate(dmh, axis=1), jnp.concatenate([v, v], axis=1))
            d_ks = halves(kw * (d_kw - off))
            DK[at] = tn3(d_ks, qbh)
            DQM[u] = DQM[u] + compress(nn3(d_ks, pair_tile(KS, l, u)))

        @pl.when(is_owner)
        def _():
            from_owner(DR, csem_s.at[z.layers + l], csem_r.at[z.layers + l], False)

        advance(l, ("inner0", "inner1"), 1)
        for done in left[2:3]:
            done()
        for u in range(U):
            b, j = unit(u)
            lanes = slice(j * 128, (j + 1) * 128)
            for i in range(n):
                SB[i, b * S : (b + 1) * S, lanes] = DQM[u, i * S : (i + 1) * S]
                SB[i, 8 + b * S : 8 + (b + 1) * S, lanes] = DKM[u, i * S : (i + 1) * S]
        spread(lambda t: SB.at[t], SR, qsem_s.at[l], qsem_r.at[l], True)
        SR[me] = SB[me]
        advance(l, ("outer0", "outer1"), 2)
        for done in left[3:]:
            done()
        spread(lambda t: SB.at[t], SR, qsem_s.at[l], qsem_r.at[l], False)
        marks = SR[0]
        for i in range(1, n):
            marks = marks + SR[i]
        marks = marks * (1.0 / z.segment)
        for b in range(B):
            for r in range(S):
                at = slice(b * L + r * z.segment, b * L + (r + 1) * z.segment)
                i = b * S + r
                DP[at, 0:C] = ((DQ[at] + marks[i : i + 1]) * scale).astype(BF16)
                DP[at, C : 2 * C] = ((DK[at] + marks[8 + i : 9 + i]) * scale).astype(BF16)
        DP[:, 2 * C : 3 * C] = DV[...].astype(BF16)

        def onto(i, _):
            o = pl.ds(pl.multiple_of(i * 256, 256), 256)
            x = nt(DP[:, 0:C], WP[l, 0, o, :]) + nt(DP[:, C : 2 * C], WP[l, 1, o, :])
            HS[(e + 1) % 2, :, o] = (x + nt(DP[:, 2 * C : 3 * C], WP[l, 2, o, :])).astype(BF16)
            return 0

        lax.fori_loop(0, D // 256, onto, 0)
        c = swap(e + 1)
        c.start()
        bias = jnp.sum(DP[...].astype(F32), axis=0, keepdims=True)
        put_small(base + 48, bias[:, 0:C])
        put_small(base + 51, bias[:, 2 * C : 3 * C])
        attend_t = FL[...].T
        hidden_t = HL[l].T
        t0, t1 = items["tail0"][0], items["tail1"][0]
        weight_grad(attend_t, lambda o: CTX[l, :, pl.ds(o, 128)], t0, 128, 128)
        weight_grad(hidden_t, lambda o: DP[:, pl.ds(o, 128)], t0 + 128, C, 128)
        weight_grad(hidden_t, lambda o: DP[:, pl.ds(2 * C + o, 256)], t0 + 128 + C, 256, 256)
        rs_start(l, "tail0", 0)
        weight_grad(attend_t, lambda o: CTX[l, :, pl.ds(128 + o, 256)], t1, C - 128, 256)
        weight_grad(hidden_t, lambda o: DP[:, pl.ds(C + o, 128)], t1 + C - 128, C, 128)
        weight_grad(hidden_t, lambda o: DP[:, pl.ds(2 * C + 256 + o, 128)], t1 + 2 * C - 128, C - 256, 128)
        rs_start(l, "tail1", 0)
        c.wait()
        UP[...] = DT[...] + both(e + 1)
        advance(l, ("inner0", "inner1"), 2)
        advance(l, ("outer0", "outer1"), 3)

    def advance(l, names, stage):
        for name in names:
            rs_add(l, name, stage)
            if stage + 1 < NB:
                rs_start(l, name, stage + 1)

    for l in range(z.layers):
        forward(l)
    result[...] = HID[...]
    pltpu.make_async_copy(ups, UP, wsem.at[0, 4]).wait()
    left = []
    for l in range(z.layers - 1, -1, -1):
        backward(l, left)
        left = [
            partial(advance, l, ("inner0", "inner1"), 3),
        ] + [partial(advance, l, ("tail0", "tail1"), s) for s in range(NB)]
    gtok[...] = UP[...]
    spread(lambda t: SM.at[pl.ds(pl.multiple_of(t * 8, 8), 8)], SMR, ssem_s, ssem_r, True)
    SMR[me] = SM[pl.ds(pl.multiple_of(me * 8, 8), 8), :]
    left[0]()
    left[1]()
    spread(lambda t: SM.at[pl.ds(pl.multiple_of(t * 8, 8), 8)], SMR, ssem_s, ssem_r, False)
    total = SMR[0]
    for i in range(1, n):
        total = total + SMR[i]
    SMT[me] = total
    spread(lambda t: SMT.at[me], SMT, tsem_s, tsem_r, True)
    for done in left[2:]:
        done()
    spread(lambda t: SMT.at[me], SMT, tsem_s, tsem_r, False)
    for i in range(n):
        gsmall[i * 8 : (i + 1) * 8, :] = SMT[i]


def fused(z, tokens, cotangent, masked, projections, projection_bias, conv_taps, output_weight,
          output_bias, norm_gain, norm_shift, inner_weight, inner_bias, outer_weight):
    n, B, L, R, D, C, F = z.n, z.batch, z.length, z.rows, z.width, z.cols, z.hidden
    U, H, NL_, NB, CH = z.units, z.local_heads, z.layers, z.bits, z.width // z.n
    wide = max(F, 2 * C, D)

    def padded(x):
        return jnp.pad(x.astype(F32), [(0, 0)] * (x.ndim - 1) + [(0, wide - x.shape[-1])])

    vec = jnp.concatenate(
        [
            padded(projection_bias.reshape(NL_, 1, 2 * C)),
            padded(inner_bias[:, None]),
            padded(output_bias),
            padded(norm_gain),
            padded(norm_shift),
        ],
        axis=1,
    )
    taps = jnp.stack([conv_taps, conv_taps[:, :, ::-1]], axis=1).astype(F32)
    taps = jnp.pad(taps, ((0, 0), (0, 0), (0, 8 - H), (0, 256 - z.kernel)))
    ups = (cotangent.astype(F32) * masked.astype(F32)[:, :, None]).reshape(R, D)
    V = pltpu.VMEM
    DMA = pltpu.SemaphoreType.DMA
    cols = 2 * F + 4 * C
    scratch = dict(
        WP=V((NL_, 3, D, C), BF16), WO=V((NL_, C, D), BF16), WI=V((NL_, D, F), BF16), WF=V((NL_, F, D), BF16),
        HL=V((NL_, R, D), BF16), QS=V((NL_, 2, R, C), BF16), KS=V((NL_, 2, R, C), BF16),
        VX=V((NL_, B, 256, C), BF16), RW=V((NL_, U, 128, 128), F32), KSC=V((NL_, U, 128, 128), F32),
        CTX=V((NL_, R, C), BF16), T1=V((NL_, R, D), F32), T2=V((NL_, R, D), F32), NL=V((NL_, R, D), BF16),
        GP=V((NL_, R, F), BF16), ACT=V((NL_, R, F), BF16),
        QM=V((NL_, U, 64, 128), F32), KM=V((NL_, U, 64, 128), F32), CR=V((NL_, U, 72, 128), F32),
        MX=V((NL_, 64, 128), F32), PA=V((NL_, 128, 128), F32), PV=V((NL_, PINV_ITERS, 4, 128, 128), F32),
        PZ=V((NL_, 128, 128), F32), PC=V((64, 128), F32),
        HID=V((R, D), F32), UP=V((R, D), F32), DT=V((R, D), F32), FL=V((R, D), BF16), DPRE=V((R, F), BF16),
        GX=V((B, 256, C), BF16), DQ=V((R, C), F32), DK=V((R, C), F32), DV=V((R, C), F32), DP=V((R, 3 * C), BF16),
        DQM=V((U, 64, 128), F32), DKM=V((U, 64, 128), F32), DR=V((U, 72, 128), F32), SM=V((n * 8, 128), F32),
        TT=V((NL_, H, 128, 256), BF16), TR=V((NL_, H, 128, 256), BF16),
        MS=V((16, C), F32), MB=V((n, 16, C), F32), XM=V((U, 72, 128), F32), OB=V((n, 72, 128), F32),
        SB=V((n, 16, C), F32), SR=V((n, 16, C), F32), HS=V((2, R, D), BF16), HR=V((2, R, D), BF16),
        SMR=V((n, 8, 128), F32), SMT=V((n, 8, 128), F32),
        G=V((2,) * NB + (CH, cols), BF16),
        RV=[V((1 if s < 2 else NL_,) + (2,) * (NB - 1 - s) + (CH, cols), BF16) for s in range(NB)],
        wsem=DMA((NL_, 5)),
        hsem_s=DMA((4 * NL_,)), hsem_r=DMA((4 * NL_,)),
        msem_s=DMA((NL_, n)), msem_r=DMA((NL_, n)), xsem_s=DMA((2 * NL_, U)), xsem_r=DMA((2 * NL_, n)),
        csem_s=DMA((2 * NL_, n)), csem_r=DMA((2 * NL_, U)), vsem_s=DMA((2 * NL_, 2)), vsem_r=DMA((2 * NL_, 2)),
        gsem_s=DMA((NL_, 6, NB)), gsem_r=DMA((NL_, 6, NB)), qsem_s=DMA((NL_, n)), qsem_r=DMA((NL_, n)),
        ssem_s=DMA((n,)), ssem_r=DMA((n,)), tsem_s=DMA((n,)), tsem_r=DMA((n,)),
    )
    in_vmem = pl.BlockSpec(memory_space=pltpu.VMEM)
    in_hbm = pl.BlockSpec(memory_space=pl.ANY)
    out = lambda *s: jax.ShapeDtypeStruct(s, F32)
    outs = pl.pallas_call(
        partial(fused_kernel, z),
        out_shape=(
            out(R, D), out(R, D), out(NL_, 3, CH, C), out(NL_, CH, C), out(NL_, CH, F), out(NL_, CH, F),
            out(n * 8, 128),
        ),
        in_specs=[in_vmem, in_hbm, in_vmem, in_vmem] + [in_hbm] * 4,
        out_specs=(in_vmem,) * 7,
        scratch_shapes=scratch,
        compiler_params=pltpu.CompilerParams(
            collective_id=1, has_side_effects=True, vmem_limit_bytes=VMEM_LIMIT
        ),
    )(tokens.reshape(R, D), ups, vec, taps, projections, output_weight, inner_weight, outer_weight)
    result, gtok, gproj, gout, ginner, gouter, small = outs
    small = small[: 60 * NL_].reshape(NL_, 60, 128)

    def pair(at):
        return small[:, at : at + 2 * (D // 128)].reshape(NL_, 2, D)

    k = D // 128
    gain, shift, bias = pair(0), pair(2 * k), pair(4 * k)
    at = 6 * k
    grad_inner_bias = small[:, at : at + F // 128].reshape(NL_, F)
    at += F // 128
    grad_bias = small[:, at : at + 2 * C // 128].reshape(NL_, 2, C)
    at += 2 * C // 128
    grad_taps = small[:, at : at + H, : z.kernel]
    return (
        result.reshape(B, L, D), gtok.reshape(B, L, D), gproj, grad_bias, grad_taps,
        jnp.swapaxes(gout, 1, 2), bias, gain, shift, ginner, grad_inner_bias, jnp.swapaxes(gouter, 1, 2),
    )


def solution(mesh):
    in_specs = (
        P(None, "seq", None),
        P(None, "seq", None),
        P(None, "seq"),
        P(None, None, None, "head"),
        P(None, None, "head"),
        P(None, "head", None),
        P(None, "head", None),
        P(),
        P(),
        P(),
        P(None, None, "head"),
        P(None, "head"),
        P(None, "head", None),
    )
    out_specs = (
        P(None, "seq", None),
        P(None, "seq", None),
        P(None, None, "seq", "head"),
        P(None, None, "head"),
        P(None, "head", None),
        P(None, "head", "seq"),
        P(),
        P(),
        P(),
        P(None, "seq", "head"),
        P(None, "head"),
        P(None, "head", "seq"),
    )

    def whole(*args):
        z = Fast(mesh.shape, args[0], args[5], args[10])
        body = partial(fused, z) if z.fits() else on_device
        return jax.shard_map(
            body, mesh=mesh, in_specs=in_specs, out_specs=out_specs, check_vma=False
        )(*args)

    return whole
```

```python
from functools import partial

import jax
import jax.numpy as jnp
from jax import lax
from jax.experimental import pallas as pl
from jax.experimental.pallas import tpu as pltpu
from jax.sharding import PartitionSpec as P

LANDMARKS = 64
PINV_ITERS = 6
LAYERS = 2


exact_result = lax.Precision.HIGHEST
epsilon = 1e-05


VMEM_LIMIT = 64 * 1024 * 1024 - 128 * 1024


def extended(block, sides, width):
    for axis, dim in sides:
        count = lax.axis_size(axis)
        forward = [(i, i + 1) for i in range(count - 1)]
        backward = [(target, source) for source, target in forward]
        low = lax.ppermute(
            lax.slice_in_dim(block, block.shape[dim] - width, None, axis=dim), axis, forward
        )
        high = lax.ppermute(lax.slice_in_dim(block, 0, width, axis=dim), axis, backward)
        block = jnp.concatenate([low, block, high], axis=dim)
    return block


def layer_norm(values, scaling, offset):
    centre = jnp.mean(values, -1, keepdims=True)
    centred = values - centre
    spread = jnp.mean(centred * centred, -1, keepdims=True)
    return centred * lax.rsqrt(spread + epsilon) * scaling + offset


def soft_rows(scores):
    highest = jnp.max(scores, -1, keepdims=True)
    powers = jnp.exp(scores - highest)
    return powers / jnp.sum(powers, -1, keepdims=True)


def pseudo_inverse(weight_matrix):
    size_of = weight_matrix.shape[-1]
    column_top = jnp.max(jnp.sum(weight_matrix, axis=-2), axis=-1)[..., None, None]
    approximate_result = jnp.swapaxes(weight_matrix, -1, -2) / column_top
    identity = jnp.eye(size_of, dtype=jnp.float32)
    for repeat in range(PINV_ITERS):
        product = jnp.matmul(weight_matrix, approximate_result, precision=exact_result)
        nested = 7.0 * identity - product
        nested = 15.0 * identity - jnp.matmul(product, nested, precision=exact_result)
        nested = 13.0 * identity - jnp.matmul(product, nested, precision=exact_result)
        approximate_result = 0.25 * jnp.matmul(approximate_result, nested, precision=exact_result)
    return approximate_result


def rounded(values):
    return lax.optimization_barrier(values.astype(jnp.bfloat16)).astype(jnp.float32)


def heads_view(joined, heads_local):
    batch_count, length, channels = joined.shape
    return joined.reshape(batch_count, length, heads_local, channels // heads_local).transpose(
        0, 2, 1, 3
    )


def tokens_view(by_head):
    batch_count, heads_local, length, head_depth = by_head.shape
    return by_head.transpose(0, 2, 1, 3).reshape(batch_count, length, heads_local * head_depth)


def convolve(padded, broad_kernel_taps, length):

    def add_tap(offset, running):
        window = lax.dynamic_slice_in_dim(padded, offset, length, 1).astype(jnp.float32)
        return running + window * lax.dynamic_index_in_dim(broad_kernel_taps, offset, 0, False)

    initial = jnp.zeros((padded.shape[0], length, padded.shape[2]), jnp.float32)
    return lax.fori_loop(0, broad_kernel_taps.shape[0], add_tap, initial)


def tap_sums(padded, upstream, length, kernel):

    def one_tap(offset):
        window = lax.dynamic_slice_in_dim(padded, offset, length, 1).astype(jnp.float32)
        return jnp.sum(window * upstream, axis=(0, 1))

    return lax.map(one_tap, jnp.arange(kernel, dtype=jnp.int32))


def across_heads(summand):
    return lax.psum_scatter(
        summand.astype(jnp.bfloat16), "head", scatter_dimension=0, tiled=True
    ).astype(jnp.float32)


def rows_low(share):
    return lax.all_gather(share, "head", axis=0, tiled=True)


def rows_float(share):
    return lax.all_gather(share.astype(jnp.bfloat16), "head", axis=0, tiled=True).astype(
        share.dtype
    )


def own_rows(whole_rows):
    share = whole_rows.shape[0] // lax.axis_size("head")
    return lax.dynamic_slice_in_dim(whole_rows, lax.axis_index("head") * share, share, 0)


def spread_heads(share, dim_index):
    groups = lax.axis_size("head")
    full_shape = list(share.shape)
    full_shape[dim_index] = full_shape[dim_index] * groups
    empty = jnp.zeros(full_shape, jnp.float32)
    return lax.dynamic_update_slice_in_dim(
        empty, share, lax.axis_index("head") * share.shape[dim_index], dim_index
    )


def own_heads(whole, width, dim_index):
    return lax.dynamic_slice_in_dim(whole, lax.axis_index("head") * width, width, dim_index)


def forward_layer(hidden, weights, selector, segment):
    (
        projection,
        projection_shift,
        conv_kernel,
        output_matrix,
        output_shift,
        gain_pair,
        shift_pair,
        inner_matrix,
        inner_shift,
        outer_matrix,
    ) = weights
    batch_count, length, model_width = hidden.shape
    heads_local = conv_kernel.shape[0]
    kernel = conv_kernel.shape[1]
    margin = kernel // 2
    local_width = projection.shape[2]
    head_depth = local_width // heads_local
    scale = float(head_depth) ** (-0.25)
    hidden_low = hidden.astype(jnp.bfloat16).reshape(batch_count * length, model_width)
    projected = jnp.einsum(
        "nd,kde->kne", hidden_low, projection, preferred_element_type=jnp.float32
    )
    biases = projection_shift.astype(jnp.float32)
    query_rows = ((projected[0] + biases[0]) * scale).reshape(batch_count, length, local_width)
    key_rows = (projected[1] * scale).reshape(batch_count, length, local_width)
    value_low = (
        (projected[2] + biases[1]).astype(jnp.bfloat16).reshape(batch_count, length, local_width)
    )
    query_sums, key_sums = lax.psum(
        (
            jnp.einsum("mt,btc->bmc", selector, query_rows, precision=exact_result),
            jnp.einsum("mt,btc->bmc", selector, key_rows, precision=exact_result),
        ),
        "seq",
    )
    query_marks = heads_view(query_sums / segment, heads_local)
    key_marks = heads_view(key_sums / segment, heads_local)
    query_heads = heads_view(query_rows, heads_local)
    key_heads = heads_view(key_rows, heads_local)
    value_heads = heads_view(value_low.astype(jnp.float32), heads_local)
    mark_weights = soft_rows(
        jnp.einsum("bhme,bhne->bhmn", query_marks, key_marks, precision=exact_result)
    )
    inverse = pseudo_inverse(mark_weights)
    row_weights = soft_rows(
        jnp.einsum("bhte,bhme->bhtm", query_heads, key_marks, precision=exact_result)
    )
    key_scores = jnp.einsum("bhme,bhte->bhmt", query_marks, key_heads, precision=exact_result)
    local_top = jnp.max(key_scores, -1)
    score_top = lax.pmax(local_top, "seq")
    powers = jnp.exp(key_scores - score_top[..., None])
    neighbour_mixture = jnp.einsum("bhmt,bhte->bhme", powers, value_heads, precision=exact_result)
    score_total, mixed_joined = lax.psum(
        (jnp.sum(powers, -1), neighbour_mixture.reshape(batch_count, heads_local, -1)), "seq"
    )
    mixed_sum = mixed_joined.reshape(neighbour_mixture.shape)
    log_total = score_top + jnp.log(score_total)
    mixed = mixed_sum / score_total[..., None]
    core = jnp.einsum("bhmn,bhne->bhme", inverse, mixed, precision=exact_result)
    attended = jnp.einsum("bhtm,bhme->bhte", row_weights, core, precision=exact_result)
    padded_values = extended(value_low, (("seq", 1),), margin)
    broad_kernel_taps = jnp.repeat(conv_kernel.astype(jnp.float32), head_depth, axis=0).T
    context = tokens_view(attended) + convolve(padded_values, broad_kernel_taps, length)
    context_low = context.astype(jnp.bfloat16).reshape(batch_count * length, local_width)
    attention_share = across_heads(
        jnp.dot(context_low, output_matrix, preferred_element_type=jnp.float32)
    )
    shifts = output_shift.astype(jnp.float32)
    gains = gain_pair.astype(jnp.float32)
    offsets = shift_pair.astype(jnp.float32)
    hidden_share = own_rows(hidden.reshape(batch_count * length, model_width))
    total_first = hidden_share + attention_share + shifts[0]
    normed = layer_norm(total_first, gains[0], offsets[0])
    normed_low = rows_low(normed.astype(jnp.bfloat16))
    pre_active = jnp.dot(
        normed_low, inner_matrix, preferred_element_type=jnp.float32
    ) + inner_shift.astype(jnp.float32)
    active_low = jax.nn.gelu(pre_active, approximate=False).astype(jnp.bfloat16)
    feed_share = across_heads(jnp.dot(active_low, outer_matrix, preferred_element_type=jnp.float32))
    total_second = normed + feed_share + shifts[1]
    output = rows_float(layer_norm(total_second, gains[1], offsets[1])).reshape(hidden.shape)
    retained = (
        hidden_low,
        query_heads,
        key_heads,
        value_heads,
        padded_values,
        query_marks,
        key_marks,
        mark_weights,
        inverse,
        row_weights,
        log_total,
        mixed,
        core,
        context_low,
        total_first,
        normed_low,
        pre_active,
        active_low,
        total_second,
        broad_kernel_taps,
    )
    return (output, retained)


def backward_layer(upstream, retained, weights, selector, segment):
    (
        projection,
        projection_shift,
        conv_kernel,
        output_matrix,
        output_shift,
        gain_pair,
        shift_pair,
        inner_matrix,
        inner_shift,
        outer_matrix,
    ) = weights
    (
        hidden_low,
        query_heads,
        key_heads,
        value_heads,
        padded_values,
        query_marks,
        key_marks,
        mark_weights,
        inverse,
        row_weights,
        log_total,
        mixed,
        core,
        context_low,
        total_first,
        normed_low,
        pre_active,
        active_low,
        total_second,
        broad_kernel_taps,
    ) = retained
    batch_count, length, model_width = upstream.shape
    heads_local = conv_kernel.shape[0]
    kernel = conv_kernel.shape[1]
    margin = kernel // 2
    local_width = projection.shape[2]
    head_depth = local_width // heads_local
    scale = float(head_depth) ** (-0.25)
    gains = gain_pair.astype(jnp.float32)
    offsets = shift_pair.astype(jnp.float32)
    upstream_share = own_rows(upstream.reshape(batch_count * length, model_width))
    second_pull = jax.vjp(layer_norm, total_second, gains[1], offsets[1])[1]
    grad_second, gain_second, offset_second = second_pull(upstream_share)
    feed_low = rows_low(grad_second.astype(jnp.bfloat16))
    grad_outer = jnp.einsum("nf,nd->fd", active_low, feed_low, preferred_element_type=jnp.float32)
    grad_active = rounded(
        jnp.einsum("nd,fd->nf", feed_low, outer_matrix, preferred_element_type=jnp.float32)
    )
    gelu_pull = jax.vjp(partial(jax.nn.gelu, approximate=False), pre_active)[1]
    grad_pre_low = gelu_pull(grad_active)[0].astype(jnp.bfloat16)
    grad_inner_shift = jnp.sum(grad_pre_low.astype(jnp.float32), axis=0)
    grad_inner = jnp.einsum(
        "nd,nf->df", normed_low, grad_pre_low, preferred_element_type=jnp.float32
    )
    normed_term = jnp.einsum(
        "nf,df->nd", grad_pre_low, inner_matrix, preferred_element_type=jnp.float32
    )
    grad_normed = grad_second + across_heads(normed_term)
    first_pull = jax.vjp(layer_norm, total_first, gains[0], offsets[0])[1]
    grad_first, gain_first, offset_first = first_pull(grad_normed)
    attend_low = rows_low(grad_first.astype(jnp.bfloat16))
    grad_output = jnp.einsum(
        "nc,nd->cd", context_low, attend_low, preferred_element_type=jnp.float32
    )
    grad_context_low = (
        jnp.einsum("nd,cd->nc", attend_low, output_matrix, preferred_element_type=jnp.float32)
        .astype(jnp.bfloat16)
        .reshape(batch_count, length, local_width)
    )
    grad_context = lax.optimization_barrier(grad_context_low).astype(jnp.float32)
    padded_grads = extended(grad_context_low, (("seq", 1),), margin)
    grad_conv_values = convolve(padded_grads, broad_kernel_taps[::-1], length)
    kernel_sums = tap_sums(padded_values, grad_context, length, kernel)
    grad_kernel = kernel_sums.reshape(kernel, heads_local, head_depth).sum(-1).T
    grad_attended = heads_view(grad_context, heads_local)
    grad_row = jnp.einsum("bhte,bhme->bhtm", grad_attended, core, precision=exact_result)
    grad_core_local = jnp.einsum(
        "bhtm,bhte->bhme", row_weights, grad_attended, precision=exact_result
    )
    grad_row_scores = row_weights * (grad_row - jnp.sum(row_weights * grad_row, -1, keepdims=True))
    grad_query = jnp.einsum("bhtm,bhme->bhte", grad_row_scores, key_marks, precision=exact_result)
    grad_keymark_local = jnp.einsum(
        "bhtm,bhte->bhme", grad_row_scores, query_heads, precision=exact_result
    )
    grad_core_joined, grad_keymark_joined = lax.psum(
        (
            grad_core_local.reshape(batch_count, heads_local, -1),
            grad_keymark_local.reshape(batch_count, heads_local, -1),
        ),
        "seq",
    )
    grad_core = grad_core_joined.reshape(core.shape)
    grad_inverse = jnp.einsum("bhme,bhne->bhmn", grad_core, mixed, precision=exact_result)
    grad_mixed = jnp.einsum("bhnm,bhne->bhme", inverse, grad_core, precision=exact_result)
    grad_marks = jax.vjp(pseudo_inverse, mark_weights)[1](grad_inverse)[0]
    grad_mark_scores = mark_weights * (
        grad_marks - jnp.sum(mark_weights * grad_marks, -1, keepdims=True)
    )
    grad_querymark = jnp.einsum(
        "bhmn,bhne->bhme", grad_mark_scores, key_marks, precision=exact_result
    )
    grad_keymark = grad_keymark_joined.reshape(key_marks.shape) + jnp.einsum(
        "bhmn,bhme->bhne", grad_mark_scores, query_marks, precision=exact_result
    )
    key_scores = jnp.einsum("bhme,bhte->bhmt", query_marks, key_heads, precision=exact_result)
    key_weights = jnp.exp(key_scores - log_total[..., None])
    grad_values = jnp.einsum("bhmt,bhme->bhte", key_weights, grad_mixed, precision=exact_result)
    offset_term = jnp.sum(grad_mixed * mixed, -1)
    grad_key_scores = key_weights * (
        jnp.einsum("bhme,bhte->bhmt", grad_mixed, value_heads, precision=exact_result)
        - offset_term[..., None]
    )
    grad_key = jnp.einsum("bhmt,bhme->bhte", grad_key_scores, query_marks, precision=exact_result)
    grad_querymark_local = jnp.einsum(
        "bhmt,bhte->bhme", grad_key_scores, key_heads, precision=exact_result
    )
    grad_querymark = grad_querymark + lax.psum(
        grad_querymark_local.reshape(batch_count, heads_local, -1), "seq"
    ).reshape(query_marks.shape)
    grad_query = (
        grad_query
        + jnp.einsum("mt,bhme->bhte", selector, grad_querymark, precision=exact_result) / segment
    )
    grad_key = (
        grad_key
        + jnp.einsum("mt,bhme->bhte", selector, grad_keymark, precision=exact_result) / segment
    )
    grad_values = grad_values + heads_view(grad_conv_values, heads_local)
    query_low = (
        (tokens_view(grad_query) * scale)
        .astype(jnp.bfloat16)
        .reshape(batch_count * length, local_width)
    )
    key_low = (
        (tokens_view(grad_key) * scale)
        .astype(jnp.bfloat16)
        .reshape(batch_count * length, local_width)
    )
    value_grad_low = (
        tokens_view(grad_values).astype(jnp.bfloat16).reshape(batch_count * length, local_width)
    )
    stacked = jnp.stack([query_low, key_low, value_grad_low])
    grad_projection = jnp.einsum(
        "nd,kne->kde", hidden_low, stacked, preferred_element_type=jnp.float32
    )
    grad_projection_shift = jnp.stack(
        [
            jnp.sum(query_low.astype(jnp.float32), axis=0),
            jnp.sum(value_grad_low.astype(jnp.float32), axis=0),
        ]
    )
    input_term = jnp.einsum("kne,kde->nd", stacked, projection, preferred_element_type=jnp.float32)
    grad_hidden = rows_float(grad_first + across_heads(input_term)).reshape(upstream.shape)
    gradients = (
        grad_projection,
        grad_projection_shift,
        grad_kernel,
        grad_output,
        jnp.stack([jnp.sum(grad_first, axis=0), jnp.sum(grad_second, axis=0)]),
        jnp.stack([gain_first, gain_second]),
        jnp.stack([offset_first, offset_second]),
        grad_inner,
        grad_inner_shift,
        grad_outer,
    )
    return (grad_hidden, gradients)


def on_device(
    tokens,
    cotangent,
    masked,
    projections,
    projection_bias,
    conv_taps,
    output_weight,
    output_bias,
    norm_gain,
    norm_shift,
    inner_weight,
    inner_bias,
    outer_weight,
):
    length = tokens.shape[1]
    segment = length * lax.axis_size("seq") // LANDMARKS
    position = lax.axis_index("seq") * length + jnp.arange(length, dtype=jnp.int32)
    selector = (
        position[None, :] // segment == jnp.arange(LANDMARKS, dtype=jnp.int32)[:, None]
    ).astype(jnp.float32)
    arrays = (
        projections,
        projection_bias,
        conv_taps,
        output_weight,
        output_bias,
        norm_gain,
        norm_shift,
        inner_weight,
        inner_bias,
        outer_weight,
    )
    hidden = tokens.astype(jnp.float32)
    stored = []
    for layer_number in range(LAYERS):
        weights = tuple((tensor[layer_number] for tensor in arrays))
        hidden, retained = forward_layer(hidden, weights, selector, segment)
        stored.append((weights, retained))
    upstream = cotangent.astype(jnp.float32) * masked.astype(jnp.float32)[:, :, None]
    layer_grads = [None] * LAYERS
    for layer_number in range(LAYERS - 1, -1, -1):
        weights, retained = stored[layer_number]
        upstream, gradients = backward_layer(upstream, retained, weights, selector, segment)
        larger = (
            lax.psum_scatter(gradients[0], "seq", scatter_dimension=1, tiled=True),
            lax.psum_scatter(gradients[3], "seq", scatter_dimension=1, tiled=True),
            lax.psum_scatter(gradients[7], "seq", scatter_dimension=0, tiled=True),
            lax.psum_scatter(gradients[9], "seq", scatter_dimension=1, tiled=True),
        )
        gradients = (
            larger[0],
            gradients[1],
            gradients[2],
            larger[1],
            gradients[4],
            gradients[5],
            gradients[6],
            larger[2],
            gradients[8],
            larger[3],
        )
        layer_grads[layer_number] = gradients
    stacked = tuple(
        (
            jnp.stack([layer_grads[layer_number][member] for layer_number in range(LAYERS)])
            for member in range(10)
        )
    )
    larger = (stacked[0], stacked[3], stacked[7], stacked[9])
    bias_width = stacked[1].shape[2]
    taps_width = stacked[2].shape[1]
    inner_width = stacked[8].shape[1]
    smaller = lax.psum(
        (
            spread_heads(stacked[1], 2),
            spread_heads(stacked[2], 1),
            stacked[4],
            stacked[5],
            stacked[6],
            spread_heads(stacked[8], 1),
        ),
        ("seq", "head"),
    )
    grad_bias_share = own_heads(smaller[0], bias_width, 2)
    grad_taps_share = own_heads(smaller[1], taps_width, 1)
    grad_inner_share = own_heads(smaller[5], inner_width, 1)
    return (
        hidden,
        upstream,
        larger[0],
        grad_bias_share,
        grad_taps_share,
        larger[1],
        smaller[2],
        smaller[3],
        smaller[4],
        larger[2],
        grad_inner_share,
        larger[3],
    )


F32 = jnp.float32
BF16 = jnp.bfloat16
MESH = pl.DeviceIdType.MESH


def nn(a, b):
    return lax.dot_general(a, b, (((1,), (0,)), ((), ())), preferred_element_type=F32)


def nt(a, b):
    return lax.dot_general(a, b, (((1,), (1,)), ((), ())), preferred_element_type=F32)


def tn(a, b):
    return lax.dot_general(a, b, (((0,), (0,)), ((), ())), preferred_element_type=F32)


def halves(x):
    high = x.astype(BF16)
    return high, (x - high.astype(F32)).astype(BF16)


def left3(pair, axis):
    return jnp.concatenate([pair[0], pair[1], pair[0]], axis=axis)


def right3(pair, axis):
    return jnp.concatenate([pair[0], pair[0], pair[1]], axis=axis)


def nn3(a, b):
    return nn(left3(a, 1), right3(b, 0))


def nt3(a, b):
    return nt(left3(a, 1), right3(b, 1))


def tn3(a, b):
    return tn(left3(a, 0), right3(b, 0))


def nn3f(a, b):
    return nn3(halves(a), halves(b))


def nt3f(a, b):
    return nt3(halves(a), halves(b))


def tn3f(a, b):
    return tn3(halves(a), halves(b))


class Fast:
    def __init__(self, mesh_shape, tokens, conv_taps, inner_weight):
        self.n = mesh_shape["seq"]
        self.heads = mesh_shape["head"]
        self.batch, whole, self.width = tokens.shape
        self.length = whole // self.n
        self.layers, all_heads, self.kernel = conv_taps.shape
        self.local_heads = all_heads // self.heads
        self.depth = self.width // all_heads
        self.cols = self.local_heads * self.depth
        self.hidden = inner_weight.shape[2] // self.heads
        self.rows = self.batch * self.length
        self.segment = whole // LANDMARKS
        self.spans = self.length // self.segment
        self.units = self.batch * self.local_heads // 2
        self.bits = self.n.bit_length() - 1

    def fits(self):
        return (
            self.n == 1 << self.bits
            and self.n >= 16
            and self.heads == 2
            and self.length == 128
            and self.batch == 2
            and self.spans * self.batch == 8
            and self.depth == 64
            and self.local_heads % 2 == 0
            and self.width % (16 * self.n) == 0
            and self.width % 256 == 0
            and self.hidden % 512 == 0
            and self.kernel == 65
            and self.layers == 2
            and LANDMARKS == 64
        )


def fused_kernel(
    z,
    tok, cot, mask, pbias, taps, obias, ngain, nshift, ibias, wp_hbm, wo_hbm, wi_hbm, wf_hbm,
    result, gtok, gproj, gbias, gtaps, gout, gobias, ggain, gshift, ginner, gibias, gouter,
    *,
    WP, WO, WI, WF,
    QS, KS, VX, RW, KSC, CTX, T1, T2, GP, ACT, QM, KM, CR, MX, PA, PV, PZ, PC, LTH, LTN,
    HID, UP, LOW, DPRE, GX, DQ, DK, DV, DP, DQM, DKM, DR, SM, TB, TT, TR, LTF, LTA,
    LSH, LSN,
    MS, MB, XM, OB, SB, SR, HS, HR, SMR, SMT,
    G, RV,
    wsem, hsem_s, hsem_r, msem_s, msem_r, xsem_s, xsem_r, csem_s, csem_r, vsem_s, vsem_r,
    asem_s, asem_r, gsem_s, gsem_r, qsem_s, qsem_r, ssem_s, ssem_r, tsem_s, tsem_r,
):
    n, B, L, R, D, C, F = z.n, z.batch, z.length, z.rows, z.width, z.cols, z.hidden
    U, NP, S, K = z.units, z.local_heads // 2, z.spans, z.kernel
    CH = D // n
    NB = z.bits
    M = LANDMARKS
    margin = K // 2
    scale = float(z.depth) ** (-0.25)
    me = lax.axis_index("seq")
    core = lax.axis_index("head")
    first_owner = n // 2 - U // 2
    is_owner = jnp.logical_and(me >= first_owner, me < first_owner + U)
    mine = jnp.clip(me - first_owner, 0, U - 1)

    def weight_copies(l):
        return [
            pltpu.make_async_copy(wp_hbm.at[l], WP.at[l], wsem.at[l, 0]),
            pltpu.make_async_copy(wo_hbm.at[l], WO.at[l], wsem.at[l, 1]),
            pltpu.make_async_copy(wi_hbm.at[l], WI.at[l], wsem.at[l, 2]),
            pltpu.make_async_copy(wf_hbm.at[l], WF.at[l], wsem.at[l, 3]),
        ]

    for l in range(z.layers):
        for c in weight_copies(l):
            c.start()

    barrier = pltpu.get_barrier_semaphore()

    def greet(d, _):
        pl.semaphore_signal(
            barrier, inc=1, device_id={"seq": lax.rem(me + d, n)}, device_id_type=MESH
        )
        return 0

    lax.fori_loop(1, n, greet, 0)
    pl.semaphore_signal(barrier, inc=1, device_id={"head": 1 - core}, device_id_type=MESH)
    pl.semaphore_wait(barrier, n)

    row_id = lax.broadcasted_iota(jnp.int32, (128, 128), 0)
    lane_id = lax.broadcasted_iota(jnp.int32, (128, 128), 1)
    low_lane = lane_id < 64
    low_lane64 = low_lane[0:64]
    same_head = (row_id < 64) == low_lane
    eye = row_id == lane_id
    flip = jnp.where(row_id + lane_id == 127, 1.0, 0.0).astype(BF16)

    def expand(c):
        return jnp.concatenate(
            [jnp.where(low_lane64, c, 0.0), jnp.where(low_lane64, 0.0, c)], axis=0
        )

    def expand_low(c):
        return expand(c.astype(F32)).astype(BF16)

    def compress(x):
        return jnp.where(low_lane64, x[0:64], x[64:128])

    def to_row(col):
        return jnp.sum(jnp.where(eye, col, 0.0), axis=0, keepdims=True)

    def to_col(row):
        return jnp.sum(jnp.where(eye, row, 0.0), axis=1, keepdims=True)

    def half_sums(x):
        a = jnp.sum(jnp.where(low_lane, x, 0.0), axis=1, keepdims=True)
        b = jnp.sum(jnp.where(low_lane, 0.0, x), axis=1, keepdims=True)
        return jnp.where(low_lane, a, b)

    def half_tops(x):
        a = jnp.max(jnp.where(low_lane, x, -jnp.inf), axis=1, keepdims=True)
        b = jnp.max(jnp.where(low_lane, -jnp.inf, x), axis=1, keepdims=True)
        return jnp.where(low_lane, a, b)

    def parts3(x):
        a = x.astype(BF16)
        rest = x - a.astype(F32)
        b = rest.astype(BF16)
        c = (rest - b.astype(F32)).astype(BF16)
        return jnp.concatenate([a.astype(F32), b.astype(F32), c.astype(F32)], axis=0)

    def pack(body, rows):
        tail = jnp.concatenate([parts3(r) for r in rows], axis=0)
        fill = jnp.zeros((16 - tail.shape[0], 128), F32)
        return jnp.concatenate([body, tail, fill], axis=0).astype(BF16)

    def packed_row(message, i):
        x = message[64 + 3 * i : 67 + 3 * i].astype(F32)
        return jnp.sum(x, axis=0, keepdims=True)

    def unit(u):
        return u // NP, u % NP

    def tile(ref, l, u):
        b, j = unit(u)
        return ref[l, b * L : (b + 1) * L, j * 128 : (j + 1) * 128]

    def pair_tile(ref, l, u):
        b, j = unit(u)
        return tuple(
            ref[l, p, b * L : (b + 1) * L, j * 128 : (j + 1) * 128] for p in range(2)
        )

    def moments(x):
        centre = jnp.mean(x, -1, keepdims=True)
        centred = x - centre
        spread = jnp.mean(centred * centred, -1, keepdims=True)
        inverse = lax.rsqrt(spread + epsilon)
        return centred * inverse, inverse

    def norm_back(x, grad, gain):
        hat, inverse = moments(x)
        g = grad * gain
        a = jnp.mean(g, -1, keepdims=True)
        b = jnp.mean(g * hat, -1, keepdims=True)
        total = inverse * (g - a - hat * b)
        sums = (
            jnp.sum(grad * hat, axis=0, keepdims=True),
            jnp.sum(grad, axis=0, keepdims=True),
            jnp.sum(total, axis=0, keepdims=True),
        )
        return total, sums

    def put_small(start, vector):
        for i in range(vector.shape[1] // 128):
            SM[start + i : start + i + 1, :] = vector[:, i * 128 : (i + 1) * 128]

    def swap(e):
        return pltpu.make_async_remote_copy(
            HS.at[e % 2], HR.at[e % 2], hsem_s.at[e], hsem_r.at[e],
            device_id={"head": 1 - core}, device_id_type=MESH,
        )

    def both(e):
        return HS[e % 2].astype(F32) + HR[e % 2].astype(F32)

    def spread(src, dst, ss, rs, start):
        def step(d, _):
            t = lax.rem(me + d, n)
            c = pltpu.make_async_remote_copy(
                src(t), dst.at[me], ss.at[t], rs.at[me], device_id={"seq": t}, device_id_type=MESH
            )
            c.start()
            return 0

        def finish(d, _):
            t = lax.rem(me + d, n)
            c = pltpu.make_async_remote_copy(
                src(t), dst.at[t], ss.at[t], rs.at[t], device_id={"seq": t}, device_id_type=MESH
            )
            c.wait_recv()
            c.wait_send()
            return 0

        lax.fori_loop(1, n, step if start else finish, 0)

    def to_owner(u, rows, ss, rs):
        c = pltpu.make_async_remote_copy(
            XM.at[u, pl.ds(0, rows)], OB.at[me, pl.ds(0, rows)], ss.at[u], rs.at[me],
            device_id={"seq": first_owner + u}, device_id_type=MESH,
        )

        @pl.when(me != first_owner + u)
        def _():
            c.start()

        @pl.when(me == first_owner + u)
        def _():
            OB[me, 0:rows] = XM[u, 0:rows]

    def to_owner_sent(u, rows, ss, rs):
        @pl.when(me != first_owner + u)
        def _():
            pltpu.make_async_remote_copy(
                XM.at[u, pl.ds(0, rows)], OB.at[me, pl.ds(0, rows)], ss.at[u], rs.at[me],
                device_id={"seq": first_owner + u}, device_id_type=MESH,
            ).wait_send()

    def owner_gets(rows, ss, rs):
        def step(d, _):
            t = lax.rem(me + d, n)
            pltpu.make_async_remote_copy(
                XM.at[0, pl.ds(0, rows)], OB.at[t, pl.ds(0, rows)], ss.at[0], rs.at[t],
                device_id={"seq": t}, device_id_type=MESH,
            ).wait_recv()
            return 0

        lax.fori_loop(1, n, step, 0)

    def from_owner(slots, ss, rs, start):
        def step(d, _):
            t = lax.rem(me + d, n)
            c = pltpu.make_async_remote_copy(
                slots.at[mine], slots.at[mine], ss.at[t], rs.at[mine],
                device_id={"seq": t}, device_id_type=MESH,
            )
            if start:
                c.start()
            else:
                c.wait_send()
            return 0

        lax.fori_loop(1, n, step, 0)

    def owner_came(slots, u, ss, rs):
        @pl.when(me != first_owner + u)
        def _():
            pltpu.make_async_remote_copy(
                slots.at[u], slots.at[u], ss.at[0], rs.at[u],
                device_id={"seq": first_owner + u}, device_id_type=MESH,
            ).wait_recv()

    def edges(buf, ss, rs, act):
        after = pltpu.make_async_remote_copy(
            buf.at[:, pl.ds(L, margin)], buf.at[:, pl.ds(0, margin)], ss.at[0], rs.at[0],
            device_id={"seq": lax.rem(me + 1, n)}, device_id_type=MESH,
        )
        before = pltpu.make_async_remote_copy(
            buf.at[:, pl.ds(margin, margin)], buf.at[:, pl.ds(margin + L, margin)], ss.at[1], rs.at[1],
            device_id={"seq": lax.rem(me + n - 1, n)}, device_id_type=MESH,
        )
        if act == "start":
            @pl.when(me < n - 1)
            def _():
                after.start()

            @pl.when(me > 0)
            def _():
                before.start()
        else:
            @pl.when(me < n - 1)
            def _():
                after.wait_send()
                before.wait_recv()

            @pl.when(me > 0)
            def _():
                before.wait_send()
                after.wait_recv()

    def edge_zeros(buf):
        none = jnp.zeros((B, margin, C), BF16)
        buf[:, 2 * margin + L :, :] = jnp.zeros((B, 256 - L - 2 * margin, C), BF16)

        @pl.when(me == 0)
        def _():
            buf[:, 0:margin, :] = none

        @pl.when(me == n - 1)
        def _():
            buf[:, margin + L : 2 * margin + L, :] = none

    def conv(bands, buf, u):
        b, j = unit(u)
        x = buf[b, :, j * 128 : (j + 1) * 128]
        return jnp.where(low_lane, nn(bands[2 * j], x), nn(bands[2 * j + 1], x))

    DT, FL, LSF, LSA = HID, LOW, LSH, LSN
    own_bits = [lax.rem(me // (1 << k), 2) for k in range(NB)]
    dims = [[k for k in reversed(range(NB)) if k != g] for g in range(2)]
    FH = F // 2
    HALF = G.shape[-1]
    everything = pl.ds(0, 2)
    items = {"outer": (0, FH), "inner": (FH, FH), "outval": (2 * FH, C), "keyed": (2 * FH + C, C)}
    item_index = {name: i for i, name in enumerate(items)}

    def peer_of(k):
        return me + (1 - 2 * own_bits[k]) * (1 << k)

    def pair_copy(l, i, g, src, dst):
        return pltpu.make_async_remote_copy(
            src, dst, asem_s.at[l, i, g], asem_r.at[l, i, g],
            device_id={"seq": peer_of(g)}, device_id_type=MESH,
        )

    def right_copies(l, i, ref, ranges):
        return [
            pair_copy(l, i, g, ref.at[pl.ds(0, R), pl.ds(c0, cn)], ref.at[pl.ds(R, R), pl.ds(c0, cn)])
            for g, (c0, cn) in enumerate(ranges)
        ]

    def left_copies(l, i, stage, gathered):
        got = []
        for g in range(2):
            at = [everything] * NB
            at[NB - 1 - g] = 1 - own_bits[g]
            src = stage.at[tuple(at) + (pl.ds(0, CH), pl.ds(0, R))]
            dst = gathered.at[(g,) + (everything,) * (NB - 1) + (pl.ds(0, CH), pl.ds(R, R))]
            got.append(pair_copy(l, i, g, src, dst))
        return got

    def left_put(x, stage, gathered):
        stage[...] = x.T.reshape(stage.shape)
        for g in range(2):
            for code in range(n // 2):
                spot = tuple((code >> (NB - 2 - i)) & 1 for i in range(NB - 1))
                at = list(spot)
                at.insert(NB - 1 - g, own_bits[g])
                gathered[(g,) + spot + (slice(None), slice(0, R))] = stage[tuple(at)]

    def start_all(copies):
        for c in copies:
            c.start()

    def wait_all(copies):
        for c in copies:
            c.wait()

    def weight_grad(g, left, right, first, count, width):
        def step(i, _):
            o = pl.multiple_of(i * width, width)
            x = nn(left[g].reshape(D // 2, 2 * R), right(o)).astype(BF16)
            o = pl.multiple_of(first + o, 128)
            for code in range(n // 2):
                spot = tuple((code >> (NB - 2 - i)) & 1 for i in range(NB - 1))
                G[(g,) + spot + (slice(None), pl.ds(o, width))] = x[code * CH : (code + 1) * CH]
            return 0

        lax.fori_loop(0, count // width, step, 0)

    STAGES = NB - 1

    def rs_copy(l, name, g, stage):
        first, count = items[name]
        cols = (pl.ds(0, CH), pl.ds(first, count))
        d = NB - 2 - stage
        index = [everything] * d + [1 - own_bits[dims[g][d]]] + [own_bits[k] for k in dims[g][d + 1 :]]
        i = item_index[name]
        return pltpu.make_async_remote_copy(
            G.at[(g,) + tuple(index) + cols], RV[stage].at[(l, g) + (everything,) * d + cols],
            gsem_s.at[l, i, g, stage], gsem_r.at[l, i, g, stage],
            device_id={"seq": peer_of(dims[g][d])}, device_id_type=MESH,
        )

    def rs_start(l, name, stage):
        for g in range(2):
            rs_copy(l, name, g, stage).start()

    def rs_add(l, name, stage):
        first, count = items[name]
        for g in range(2):
            rs_copy(l, name, g, stage).wait()
            d = NB - 2 - stage
            mine_at = tuple(own_bits[k] for k in dims[g][d:])
            cols = (slice(None), slice(first, first + count))
            if d:
                for code in range(1 << d):
                    spot = tuple((code >> (d - 1 - i)) & 1 for i in range(d))
                    at = (g,) + spot + mine_at + cols
                    G[at] = G[at] + RV[stage][(l, g) + spot + cols]
            else:
                x = G[(g,) + mine_at + cols].astype(F32) + RV[stage][(l, g) + cols].astype(F32)
                write_out(l, name, g, x)

    def write_out(l, name, g, x):
        if name == "outer":
            gouter[l, :, g * FH : (g + 1) * FH] = x
        elif name == "inner":
            ginner[l, :, g * FH : (g + 1) * FH] = x
        elif name == "keyed":
            gproj[l, g] = x
        elif g == 0:
            gout[l, :, 0:128] = x[:, 0:128]
            gproj[l, 2, :, 0 : C - 128] = x[:, 128:C]
        else:
            gout[l, :, 128:C] = x[:, 0 : C - 128]
            gproj[l, 2, :, C - 128 : C] = x[:, C - 128 : C]

    def advance(l, name, stage):
        rs_add(l, name, stage)
        if stage + 1 < STAGES:
            rs_start(l, name, stage + 1)

    out_ranges = ((0, 128), (128, C - 128))
    val_ranges = ((2 * C, C - 128), (3 * C - 128, 128))
    key_ranges = ((0, C), (C, C))
    ffn_ranges = ((0, FH), (FH, FH))

    for b in range(B):
        HID[b * L : (b + 1) * L, :] = tok[b].astype(F32)
    TB[...] = jnp.zeros_like(TB)
    backwards = jnp.where(row_id + lane_id == K - 1, 1.0, 0.0).astype(BF16)
    for l in range(z.layers):
        TB[0, 0 : z.local_heads, 0:K] = taps[l].astype(F32)
        TB[1, :, 0:128] = nn(TB[0, :, 0:128].astype(BF16), backwards)
        for h in range(z.local_heads):
            for which, store in ((0, TT), (1, TR)):
                base = jnp.broadcast_to(TB[which, h : h + 1, :], (128, 256))
                store[l, h] = pltpu.roll(base, 0, 1, stride=1, stride_axis=0).astype(BF16)

    def forward(l):
        copies = weight_copies(l)
        e = 2 * l
        hl = HID[...].astype(BF16)
        LOW[...] = hl
        copies[0].wait()
        both_bias = pbias[l].astype(F32)
        bias_q, bias_v = both_bias[0:1], both_bias[1:2]
        q = (nn(hl, WP[l, 0]) + bias_q) * scale
        k = nn(hl, WP[l, 1]) * scale
        QS[l, 0], QS[l, 1] = halves(q)
        KS[l, 0], KS[l, 1] = halves(k)
        for b in range(B):
            for r in range(S):
                at = b * L + r * z.segment
                i = b * S + r
                MS[i : i + 1, :] = jnp.sum(q[at : at + z.segment], axis=0, keepdims=True) * (1.0 / z.segment)
                MS[8 + i : 9 + i, :] = jnp.sum(k[at : at + z.segment], axis=0, keepdims=True) * (1.0 / z.segment)
        spread(lambda t: MS, MB, msem_s.at[l], msem_r.at[l], True)
        MB[me] = MS[...]
        vl = (nn(hl, WP[l, 2]) + bias_v).astype(BF16)
        for b in range(B):
            VX[l, b, margin : margin + L, :] = vl[b * L : (b + 1) * L]
        edge_zeros(VX.at[l])
        edges(VX.at[l], vsem_s.at[l], vsem_r.at[l], "start")
        left_put(LOW[...], LSH, LTH.at[l])
        spread(lambda t: MS, MB, msem_s.at[l], msem_r.at[l], False)
        for u in range(U):
            b, j = unit(u)
            for i in range(n):
                at = slice(i * S, (i + 1) * S)
                QM[l, u, at, :] = MB[i, b * S : (b + 1) * S, j * 128 : (j + 1) * 128]
                KM[l, u, at, :] = MB[i, 8 + b * S : 8 + (b + 1) * S, j * 128 : (j + 1) * 128]
        for u in range(U):
            b, j = unit(u)
            qb = expand(QM[l, u])
            ksc = nt3(halves(qb), pair_tile(KS, l, u))
            KSC[l, u] = ksc
            top = jnp.max(ksc, axis=1, keepdims=True)
            p = jnp.exp(ksc - top)
            total = jnp.sum(p, axis=1, keepdims=True)
            v = VX[l, b, margin : margin + L, j * 128 : (j + 1) * 128]
            XM[u] = pack(compress(nn(p.astype(BF16), v)), [to_row(top), to_row(total)])
            to_owner(u, 80, xsem_s.at[l], xsem_r.at[l])
        start_all(left_copies(l, 0, LSH, LTH.at[l]))
        for u in range(U):
            kb = expand(KM[l, u])
            s = nt3(pair_tile(QS, l, u), halves(kb))
            p = jnp.exp(s - half_tops(s))
            RW[l, u] = p / half_sums(p)

        @pl.when(is_owner)
        def _():
            qb, kb = expand(QM[l, mine]), expand(KM[l, mine])
            s = jnp.where(same_head, nt3f(qb, kb), -jnp.inf)
            p = jnp.exp(s - jnp.max(s, axis=1, keepdims=True))
            a = p / jnp.sum(p, axis=1, keepdims=True)
            PA[l] = a
            ah = halves(a)
            sums = jnp.sum(a, axis=0, keepdims=True)
            tops = jnp.where(
                low_lane[0:1],
                jnp.max(jnp.where(low_lane[0:1], sums, 0.0), axis=1, keepdims=True),
                jnp.max(jnp.where(low_lane[0:1], 0.0, sums), axis=1, keepdims=True),
            )
            unit_matrix = jnp.where(eye, 1.0, 0.0)

            def iterate(i, zk):
                PV[l, i, 0] = zk
                zh = halves(zk)
                pr = nn3(ah, zh)
                PV[l, i, 1] = pr
                prh = halves(pr)
                n2 = 15.0 * unit_matrix - nn3(prh, halves(7.0 * unit_matrix - pr))
                PV[l, i, 2] = n2
                n3 = 13.0 * unit_matrix - nn3(prh, halves(n2))
                PV[l, i, 3] = n3
                return 0.25 * nn3(zh, halves(n3))

            zk = lax.fori_loop(0, PINV_ITERS, iterate, a.T / tops)
            PZ[l] = zk
            owner_gets(80, xsem_s.at[l], xsem_r.at[l])
            tops = [packed_row(OB.at[i], 0) for i in range(n)]
            top = tops[0]
            for i in range(1, n):
                top = jnp.maximum(top, tops[i])
            factors = [jnp.exp(x - top) for x in tops]
            total = factors[0] * packed_row(OB.at[0], 1)
            for i in range(1, n):
                total = total + factors[i] * packed_row(OB.at[i], 1)
            mixed = jnp.zeros((64, 128), F32)
            for i in range(n):
                col = to_col(factors[i] / total)
                mixed = mixed + jnp.where(low_lane64, col[0:64], col[64:128]) * OB[i, 0:64].astype(F32)
            MX[l] = mixed
            CR[l, mine] = pack(compress(nn3f(zk, expand(mixed))), [top + jnp.log(total)])
            from_owner(CR.at[l], csem_s.at[l], csem_r.at[l], True)

        edges(VX.at[l], vsem_s.at[l], vsem_r.at[l], "wait")
        for u in range(U):
            b, j = unit(u)
            DQ[b * L : (b + 1) * L, j * 128 : (j + 1) * 128] = conv(TT.at[l], VX.at[l], u)
        for u in range(U):
            b, j = unit(u)
            to_owner_sent(u, 80, xsem_s.at[l], xsem_r.at[l])
            owner_came(CR.at[l], u, csem_s.at[l], csem_r.at[l])
            at = (slice(b * L, (b + 1) * L), slice(j * 128, (j + 1) * 128))
            context = nn(RW[l, u].astype(BF16), expand_low(CR[l, u, 0:64])) + DQ[at]
            CTX[(l,) + at] = context.astype(BF16)
        start_all(right_copies(l, 1, CTX.at[l], out_ranges))

        @pl.when(is_owner)
        def _():
            from_owner(CR.at[l], csem_s.at[l], csem_r.at[l], False)

        copies[1].wait()
        wait_all(left_copies(l, 0, LSH, LTH.at[l]))
        HS[e % 2] = nn(CTX[l, 0:R], WO[l]).astype(BF16)
        c = swap(e)
        c.start()
        c.wait()
        total1 = HID[...] + both(e) + obias[l].astype(F32)[0:1]
        T1[l] = total1
        normed = moments(total1)[0] * ngain[l].astype(F32)[0:1] + nshift[l].astype(F32)[0:1]
        HID[...] = normed
        LOW[...] = normed.astype(BF16)
        left_put(LOW[...], LSN, LTN.at[l])
        start_all(left_copies(l, 2, LSN, LTN.at[l]))
        copies[2].wait()

        def grow(i, _):
            o = pl.ds(pl.multiple_of(i * 256, 256), 256)
            pre = nn(LOW[...], WI[l, :, o]) + ibias[l : l + 1, o].astype(F32)
            below = 0.5 * (1.0 + lax.erf(pre * (0.5**0.5)))
            ACT[l, 0:R, o] = (pre * below).astype(BF16)
            GP[l, :, o] = (below + pre * jnp.exp(-0.5 * pre * pre) * 0.3989422804014327).astype(BF16)
            return 0

        lax.fori_loop(0, F // 256, grow, 0)
        start_all(right_copies(l, 3, ACT.at[l], ffn_ranges))
        copies[3].wait()

        def shrink(i, _):
            o = pl.ds(pl.multiple_of(i * 256, 256), 256)
            HS[(e + 1) % 2, :, o] = nn(ACT[l, 0:R], WF[l, :, o]).astype(BF16)
            return 0

        lax.fori_loop(0, D // 256, shrink, 0)
        c = swap(e + 1)
        c.start()
        c.wait()
        total2 = HID[...] + both(e + 1) + obias[l].astype(F32)[1:2]
        T2[l] = total2
        wait_all(right_copies(l, 1, CTX.at[l], out_ranges))
        wait_all(left_copies(l, 2, LSN, LTN.at[l]))
        wait_all(right_copies(l, 3, ACT.at[l], ffn_ranges))
        HID[...] = moments(total2)[0] * ngain[l].astype(F32)[1:2] + nshift[l].astype(F32)[1:2]

    def backward(l, left):
        e = 2 * z.layers + 2 * (z.layers - 1 - l)
        k = z.layers + l
        base = 60 * l
        total2, sums = norm_back(T2[l], UP[...], ngain[l].astype(F32)[1:2])
        put_small(base + 6, sums[0])
        put_small(base + 18, sums[1])
        put_small(base + 30, sums[2])
        DT[...] = total2
        FL[...] = total2.astype(BF16)
        left_put(FL[...], LSF, LTF)
        feed_copies = left_copies(l, 4, LSF, LTF)
        start_all(feed_copies)

        def widen(i, _):
            o = pl.ds(pl.multiple_of(i * 256, 256), 256)
            grad = nt(FL[...], WF[l, o, :]).astype(BF16).astype(F32)
            pre = (GP[l, :, o].astype(F32) * grad).astype(BF16)
            DPRE[0:R, o] = pre
            s = jnp.sum(pre.astype(F32), axis=0, keepdims=True)
            SM[pl.ds(base + 36 + 2 * i, 1), :] = s[:, 0:128]
            SM[pl.ds(base + 37 + 2 * i, 1), :] = s[:, 128:256]
            return 0

        lax.fori_loop(0, F // 256, widen, 0)
        pre_copies = right_copies(l, 5, DPRE, ffn_ranges)
        start_all(pre_copies)

        def narrow(i, _):
            o = pl.ds(pl.multiple_of(i * 256, 256), 256)
            HS[e % 2, :, o] = nt(DPRE[0:R], WI[l, o, :]).astype(BF16)
            return 0

        lax.fori_loop(0, D // 256, narrow, 0)
        c = swap(e)
        c.start()
        c.wait()
        grad_normed = DT[...] + both(e)
        total1, sums = norm_back(T1[l], grad_normed, ngain[l].astype(F32)[0:1])
        put_small(base + 0, sums[0])
        put_small(base + 12, sums[1])
        put_small(base + 24, sums[2])
        DT[...] = total1
        FL[...] = total1.astype(BF16)
        grads = nt(FL[...], WO[l]).astype(BF16)
        for b in range(B):
            GX[b, margin : margin + L, :] = grads[b * L : (b + 1) * L]
        edge_zeros(GX)
        edges(GX, vsem_s.at[k], vsem_r.at[k], "start")

        def g_tile(u):
            b, j = unit(u)
            return GX[b, margin : margin + L, j * 128 : (j + 1) * 128]

        for u in range(U):
            XM[u, 0:64] = compress(tn(RW[l, u].astype(BF16), g_tile(u))).astype(BF16)
            to_owner(u, 64, xsem_s.at[k], xsem_r.at[k])
            DQM[u] = jnp.zeros((64, 128), F32)
        left_put(FL[...], LSA, LTA)
        attend_copies = left_copies(l, 6, LSA, LTA)
        start_all(attend_copies)
        for done in left[:1]:
            done()
        wait_all(feed_copies)
        for g in range(2):
            weight_grad(g, LTF, lambda o: ACT[l, :, pl.ds(g * FH + o, 256)], items["outer"][0], FH, 256)
        rs_start(l, "outer", 0)

        @pl.when(is_owner)
        def _():
            owner_gets(64, xsem_s.at[k], xsem_r.at[k])
            d_core = OB[0, 0:64].astype(F32)
            for i in range(1, n):
                d_core = d_core + OB[i, 0:64].astype(F32)
            PC[...] = d_core
            d_mixed = tn3f(PZ[l], expand(d_core))
            off = jnp.sum(d_mixed * expand(MX[l]), axis=1, keepdims=True)
            DR[mine] = pack(compress(d_mixed), [to_row(off)])
            from_owner(DR, csem_s.at[k], csem_r.at[k], True)

        for u in range(U):
            b, j = unit(u)
            at = (slice(b * L, (b + 1) * L), slice(j * 128, (j + 1) * 128))
            d_row = nt(g_tile(u), expand_low(CR[l, u, 0:64]))
            rw = RW[l, u]
            d_rs = (rw * (d_row - half_sums(rw * d_row))).astype(BF16)
            DQ[at] = nn(d_rs, expand(KM[l, u]).astype(BF16))
            DKM[u] = compress(tn(d_rs, pair_tile(QS, l, u)[0]))
        for u in range(U):
            to_owner_sent(u, 64, xsem_s.at[k], xsem_r.at[k])

        @pl.when(is_owner)
        def _():
            a = PA[l]
            ah = halves(a)
            unit_matrix = jnp.where(eye, 1.0, 0.0)

            def back(i, carry):
                dz, da = carry
                i = PINV_ITERS - 1 - i
                zh, prh = halves(PV[l, i, 0]), halves(PV[l, i, 1])
                n1h = halves(7.0 * unit_matrix - PV[l, i, 1])
                n2h, n3h = halves(PV[l, i, 2]), halves(PV[l, i, 3])
                dzh = halves(dz)
                dn3 = halves(0.25 * tn3(zh, dzh))
                dn2 = halves(-tn3(prh, dn3))
                dpr = tn3(prh, dn2) - nt3(dn3, n2h) - nt3(dn2, n1h)
                dpr = halves(dpr)
                dz = 0.25 * nt3(dzh, n3h) + tn3(ah, dpr)
                return dz, da + nt3(dpr, zh)

            dz, da = lax.fori_loop(
                0, PINV_ITERS, back, (nt3f(expand(PC[...]), expand(MX[l])), jnp.zeros((128, 128), F32))
            )
            low_row = low_lane[0:1]

            def half_row(x, f):
                return jnp.where(
                    low_row,
                    f(jnp.where(low_row, x, 0.0), axis=1, keepdims=True),
                    f(jnp.where(low_row, 0.0, x), axis=1, keepdims=True),
                )

            sums = jnp.sum(a, axis=0, keepdims=True)
            tops = half_row(sums, jnp.max)
            d_tops = -half_row(jnp.sum(dz * PV[l, 0, 0], axis=0, keepdims=True), jnp.sum) / tops
            at_top = jnp.where(sums == tops, 1.0, 0.0)
            da = da + (dz / tops).T + at_top * d_tops / half_row(at_top, jnp.sum)
            d_ms = halves(a * (da - jnp.sum(a * da, axis=1, keepdims=True)))
            DQM[mine] = compress(nn3(d_ms, halves(expand(KM[l, mine]))))
            DKM[mine] = DKM[mine] + compress(tn3(d_ms, halves(expand(QM[l, mine]))))

        for done in left[1:2]:
            done()
        wait_all(pre_copies)
        for g in range(2):
            weight_grad(g, LTN.at[l], lambda o: DPRE[:, pl.ds(g * FH + o, 256)], items["inner"][0], FH, 256)
        rs_start(l, "inner", 0)
        edges(GX, vsem_s.at[k], vsem_r.at[k], "wait")
        for u in range(U):
            b, j = unit(u)
            at = (slice(b * L, (b + 1) * L), slice(j * 128, (j + 1) * 128))
            DV[at] = conv(TR.at[l], GX, u)
        for j in range(NP):
            for h in range(2):
                found = jnp.zeros((128, 256), F32)
                for b in range(B):
                    g = nn(flip, g_tile(b * NP + j))
                    g = jnp.where(low_lane, g, 0.0) if h == 0 else jnp.where(low_lane, 0.0, g)
                    found = found + nt(g.astype(BF16), VX[l, b, :, j * 128 : (j + 1) * 128])
                found = pltpu.roll(found, 129, 1, stride=1, stride_axis=0)
                row = base + 54 + 2 * j + h
                SM[row : row + 1, :] = jnp.sum(found[:, 0:128], axis=0, keepdims=True)
        advance(l, "outer", 0)
        for u in range(U):
            b, j = unit(u)
            at = (slice(b * L, (b + 1) * L), slice(j * 128, (j + 1) * 128))
            owner_came(DR, u, csem_s.at[k], csem_r.at[k])
            dm = expand_low(DR[u, 0:64])
            off = to_col(packed_row(DR.at[u], 0))
            kw = jnp.exp(KSC[l, u] - to_col(packed_row(CR.at[l, u], 0)))
            v = VX[l, b, margin : margin + L, j * 128 : (j + 1) * 128]
            DV[at] = DV[at] + tn(kw.astype(BF16), dm)
            d_ks = (kw * (nt(dm, v) - off)).astype(BF16)
            DK[at] = tn(d_ks, expand(QM[l, u]).astype(BF16))
            DQM[u] = DQM[u] + compress(nn(d_ks, pair_tile(KS, l, u)[0]))

        @pl.when(is_owner)
        def _():
            from_owner(DR, csem_s.at[k], csem_r.at[k], False)

        for u in range(U):
            b, j = unit(u)
            lanes = slice(j * 128, (j + 1) * 128)
            dq, dk = DQM[u].astype(BF16), DKM[u].astype(BF16)
            for i in range(n):
                SB[i, b * S : (b + 1) * S, lanes] = dq[i * S : (i + 1) * S]
                SB[i, 8 + b * S : 8 + (b + 1) * S, lanes] = dk[i * S : (i + 1) * S]
        for done in left[2:]:
            done()
        DP[0:R, 2 * C : 3 * C] = DV[...].astype(BF16)
        value_copies = right_copies(l, 7, DP, val_ranges)
        wait_all(attend_copies)
        out0 = items["outval"][0]
        weight_grad(0, LTA, lambda o: CTX[l, :, pl.ds(o, 128)], out0, 128, 128)
        weight_grad(1, LTA, lambda o: CTX[l, :, pl.ds(128 + o, 256)], out0, C - 128, 256)
        spread(lambda t: SB.at[t], SR, qsem_s.at[l], qsem_r.at[l], True)
        SR[me] = SB[me]
        start_all(value_copies)
        advance(l, "inner", 0)
        wait_all(value_copies)
        weight_grad(0, LTH.at[l], lambda o: DP[:, pl.ds(2 * C + o, 256)], out0 + 128, C - 128, 256)
        weight_grad(1, LTH.at[l], lambda o: DP[:, pl.ds(3 * C - 128 + o, 128)], out0 + C - 128, 128, 128)
        rs_start(l, "outval", 0)
        spread(lambda t: SB.at[t], SR, qsem_s.at[l], qsem_r.at[l], False)
        marks = SR[0].astype(F32)
        for i in range(1, n):
            marks = marks + SR[i].astype(F32)
        marks = marks * (1.0 / z.segment)
        for b in range(B):
            for r in range(S):
                at = slice(b * L + r * z.segment, b * L + (r + 1) * z.segment)
                i = b * S + r
                DP[at, 0:C] = ((DQ[at] + marks[i : i + 1]) * scale).astype(BF16)
                DP[at, C : 2 * C] = ((DK[at] + marks[8 + i : 9 + i]) * scale).astype(BF16)
        key_copies = right_copies(l, 8, DP, key_ranges)
        start_all(key_copies)

        def onto(i, _):
            o = pl.ds(pl.multiple_of(i * 256, 256), 256)
            x = nt(DP[0:R, 0:C], WP[l, 0, o, :]) + nt(DP[0:R, C : 2 * C], WP[l, 1, o, :])
            HS[(e + 1) % 2, :, o] = (x + nt(DP[0:R, 2 * C : 3 * C], WP[l, 2, o, :])).astype(BF16)
            return 0

        lax.fori_loop(0, D // 256, onto, 0)
        c = swap(e + 1)
        c.start()
        bias = jnp.sum(DP[0:R].astype(F32), axis=0, keepdims=True)
        put_small(base + 48, bias[:, 0:C])
        put_small(base + 51, bias[:, 2 * C : 3 * C])
        advance(l, "outer", 1)
        wait_all(key_copies)
        for g in range(2):
            weight_grad(g, LTH.at[l], lambda o: DP[:, pl.ds(g * C + o, 128)], items["keyed"][0], C, 128)
        rs_start(l, "keyed", 0)
        c.wait()
        UP[...] = DT[...] + both(e + 1)

    for l in range(z.layers):
        forward(l)
    for b in range(B):
        result[b] = HID[b * L : (b + 1) * L, :]
        shown = to_col(mask[b : b + 1, :].astype(F32))
        UP[b * L : (b + 1) * L, :] = cot[b].astype(F32) * shown
    left = []
    for l in range(z.layers - 1, -1, -1):
        backward(l, left)

        def rest(l=l):
            advance(l, "inner", 1)
            advance(l, "outval", 0)
            advance(l, "outer", 2)

        def more(l=l):
            advance(l, "inner", 2)
            advance(l, "keyed", 0)
            advance(l, "outval", 1)

        def last(l=l):
            advance(l, "keyed", 1)
            advance(l, "outval", 2)
            advance(l, "keyed", 2)

        left = [rest, more, last]
    for b in range(B):
        gtok[b] = UP[b * L : (b + 1) * L, :]
    spread(lambda t: SM.at[pl.ds(pl.multiple_of(t * 8, 8), 8)], SMR, ssem_s, ssem_r, True)
    SMR[me] = SM[pl.ds(pl.multiple_of(me * 8, 8), 8), :]
    left[0]()
    spread(lambda t: SM.at[pl.ds(pl.multiple_of(t * 8, 8), 8)], SMR, ssem_s, ssem_r, False)
    total = SMR[0]
    for i in range(1, n):
        total = total + SMR[i]
    SMT[me] = total
    spread(lambda t: SMT.at[me], SMT, tsem_s, tsem_r, True)
    left[1]()
    left[2]()
    spread(lambda t: SMT.at[me], SMT, tsem_s, tsem_r, False)

    def small(at):
        return SMT[at // 8, at % 8 : at % 8 + 1, :]

    for l in range(z.layers):
        base = 60 * l
        for i in range(D // 128):
            lanes = slice(i * 128, (i + 1) * 128)
            for side in range(2):
                ggain[l, side : side + 1, lanes] = small(base + 6 * side + i)
                gshift[l, side : side + 1, lanes] = small(base + 12 + 6 * side + i)
                gobias[l, side : side + 1, lanes] = small(base + 24 + 6 * side + i)
        for i in range(F // 128):
            gibias[l : l + 1, i * 128 : (i + 1) * 128] = small(base + 36 + i)
        for i in range(C // 128):
            gbias[l, 0:1, i * 128 : (i + 1) * 128] = small(base + 48 + i)
            gbias[l, 1:2, i * 128 : (i + 1) * 128] = small(base + 51 + i)
        for h in range(z.local_heads):
            gtaps[l, h : h + 1, :] = small(base + 54 + h)[:, 0:K]


def hand_over(count, *refs):
    sems = refs[-1]
    copies = [
        pltpu.make_async_copy(refs[i], refs[count + i], sems.at[i]) for i in range(count)
    ]
    for c in copies:
        c.start()
    for c in copies:
        c.wait()


def fused(z, tokens, cotangent, masked, projections, projection_bias, conv_taps, output_weight,
          output_bias, norm_gain, norm_shift, inner_weight, inner_bias, outer_weight):
    n, B, L, R, D, C, F = z.n, z.batch, z.length, z.rows, z.width, z.cols, z.hidden
    U, H, NL_, NB, CH = z.units, z.local_heads, z.layers, z.bits, z.width // z.n
    V = pltpu.VMEM
    DMA = pltpu.SemaphoreType.DMA
    cols = F + 2 * C
    staged = lambda: V((2,) * NB + (CH, R), BF16)
    gathered = lambda *lead: V(lead + (2,) * NB + (CH, 2 * R), BF16)
    scratch = dict(
        WP=V((NL_, 3, D, C), BF16), WO=V((NL_, C, D), BF16), WI=V((NL_, D, F), BF16), WF=V((NL_, F, D), BF16),
        QS=V((NL_, 2, R, C), BF16), KS=V((NL_, 2, R, C), BF16),
        VX=V((NL_, B, 256, C), BF16), RW=V((NL_, U, 128, 128), F32), KSC=V((NL_, U, 128, 128), F32),
        CTX=V((NL_, 2 * R, C), BF16), T1=V((NL_, R, D), F32), T2=V((NL_, R, D), F32),
        GP=V((NL_, R, F), BF16), ACT=V((NL_, 2 * R, F), BF16),
        QM=V((NL_, U, 64, 128), F32), KM=V((NL_, U, 64, 128), F32), CR=V((NL_, U, 80, 128), BF16),
        MX=V((NL_, 64, 128), F32), PA=V((NL_, 128, 128), F32), PV=V((NL_, PINV_ITERS, 4, 128, 128), F32),
        PZ=V((NL_, 128, 128), F32), PC=V((64, 128), F32), LTH=gathered(NL_), LTN=gathered(NL_),
        HID=V((R, D), F32), UP=V((R, D), F32), LOW=V((R, D), BF16),
        DPRE=V((2 * R, F), BF16), GX=V((B, 256, C), BF16), DQ=V((R, C), F32), DK=V((R, C), F32), DV=V((R, C), F32),
        DP=V((2 * R, 3 * C), BF16), DQM=V((U, 64, 128), F32), DKM=V((U, 64, 128), F32), DR=V((U, 80, 128), BF16),
        SM=V((n * 8, 128), F32), TB=V((2, 8, 256), F32),
        TT=V((NL_, H, 128, 256), BF16), TR=V((NL_, H, 128, 256), BF16), LTF=gathered(), LTA=gathered(),
        LSH=staged(), LSN=staged(),
        MS=V((16, C), F32), MB=V((n, 16, C), F32), XM=V((U, 80, 128), BF16), OB=V((n, 80, 128), BF16),
        SB=V((n, 16, C), BF16), SR=V((n, 16, C), BF16), HS=V((2, R, D), BF16), HR=V((2, R, D), BF16),
        SMR=V((n, 8, 128), F32), SMT=V((n, 8, 128), F32),
        G=V((2,) * NB + (CH, cols), BF16),
        RV=[V((NL_, 2) + (2,) * (NB - 2 - s) + (CH, cols), BF16) for s in range(NB - 1)],
        wsem=DMA((NL_, 4)),
        hsem_s=DMA((4 * NL_,)), hsem_r=DMA((4 * NL_,)),
        msem_s=DMA((NL_, n)), msem_r=DMA((NL_, n)), xsem_s=DMA((2 * NL_, U)), xsem_r=DMA((2 * NL_, n)),
        csem_s=DMA((2 * NL_, n)), csem_r=DMA((2 * NL_, U)), vsem_s=DMA((2 * NL_, 2)), vsem_r=DMA((2 * NL_, 2)),
        asem_s=DMA((NL_, 9, 2)), asem_r=DMA((NL_, 9, 2)),
        gsem_s=DMA((NL_, 4, 2, NB - 1)), gsem_r=DMA((NL_, 4, 2, NB - 1)), qsem_s=DMA((NL_, n)), qsem_r=DMA((NL_, n)),
        ssem_s=DMA((n,)), ssem_r=DMA((n,)), tsem_s=DMA((n,)), tsem_r=DMA((n,)),
    )
    in_vmem = pl.BlockSpec(memory_space=pltpu.VMEM)
    in_hbm = pl.BlockSpec(memory_space=pl.ANY)
    out = lambda *s: jax.ShapeDtypeStruct(s, F32)
    shapes = (
        out(B, L, D), out(B, L, D), out(NL_, 3, CH, C), out(NL_, 2, C), out(NL_, H, z.kernel), out(NL_, CH, C),
        out(NL_, 2, D), out(NL_, 2, D), out(NL_, 2, D), out(NL_, CH, F), out(NL_, F), out(NL_, CH, F),
    )
    outs = pl.pallas_call(
        partial(fused_kernel, z),
        out_shape=shapes,
        in_specs=[in_vmem] * 9 + [in_hbm] * 4,
        out_specs=(in_vmem,) * len(shapes),
        scratch_shapes=scratch,
        compiler_params=pltpu.CompilerParams(
            collective_id=1, has_side_effects=True, vmem_limit_bytes=VMEM_LIMIT
        ),
    )(tokens, cotangent, masked, projection_bias, conv_taps, output_bias, norm_gain, norm_shift, inner_bias,
      projections, output_weight, inner_weight, outer_weight)
    outs = list(
        pl.pallas_call(
            partial(hand_over, len(shapes)),
            out_shape=shapes,
            in_specs=[in_vmem] * len(shapes),
            out_specs=(in_hbm,) * len(shapes),
            scratch_shapes=[DMA((len(shapes),))],
        )(*outs)
    )
    outs[5], outs[11] = jnp.swapaxes(outs[5], 1, 2), jnp.swapaxes(outs[11], 1, 2)
    return tuple(outs)


def solution(mesh):
    in_specs = (
        P(None, "seq", None),
        P(None, "seq", None),
        P(None, "seq"),
        P(None, None, None, "head"),
        P(None, None, "head"),
        P(None, "head", None),
        P(None, "head", None),
        P(),
        P(),
        P(),
        P(None, None, "head"),
        P(None, "head"),
        P(None, "head", None),
    )
    out_specs = (
        P(None, "seq", None),
        P(None, "seq", None),
        P(None, None, "seq", "head"),
        P(None, None, "head"),
        P(None, "head", None),
        P(None, "head", "seq"),
        P(),
        P(),
        P(),
        P(None, "seq", "head"),
        P(None, "head"),
        P(None, "head", "seq"),
    )

    def whole(*args):
        z = Fast(mesh.shape, args[0], args[5], args[10])
        body = partial(fused, z) if z.fits() else on_device
        return jax.shard_map(
            body, mesh=mesh, in_specs=in_specs, out_specs=out_specs, check_vma=False
        )(*args)

    return whole
```

```python
from functools import partial

import jax
import jax.numpy as jnp
from jax import lax
from jax.experimental import pallas as pl
from jax.experimental.pallas import tpu as pltpu
from jax.sharding import PartitionSpec as P

LANDMARKS = 64
PINV_ITERS = 6
LAYERS = 2


exact_result = lax.Precision.HIGHEST
epsilon = 1e-05


VMEM_LIMIT = 64 * 1024 * 1024 - 128 * 1024


def extended(block, sides, width):
    for axis, dim in sides:
        count = lax.axis_size(axis)
        forward = [(i, i + 1) for i in range(count - 1)]
        backward = [(target, source) for source, target in forward]
        low = lax.ppermute(
            lax.slice_in_dim(block, block.shape[dim] - width, None, axis=dim), axis, forward
        )
        high = lax.ppermute(lax.slice_in_dim(block, 0, width, axis=dim), axis, backward)
        block = jnp.concatenate([low, block, high], axis=dim)
    return block


def layer_norm(values, scaling, offset):
    centre = jnp.mean(values, -1, keepdims=True)
    centred = values - centre
    spread = jnp.mean(centred * centred, -1, keepdims=True)
    return centred * lax.rsqrt(spread + epsilon) * scaling + offset


def soft_rows(scores):
    highest = jnp.max(scores, -1, keepdims=True)
    powers = jnp.exp(scores - highest)
    return powers / jnp.sum(powers, -1, keepdims=True)


def pseudo_inverse(weight_matrix):
    size_of = weight_matrix.shape[-1]
    column_top = jnp.max(jnp.sum(weight_matrix, axis=-2), axis=-1)[..., None, None]
    approximate_result = jnp.swapaxes(weight_matrix, -1, -2) / column_top
    identity = jnp.eye(size_of, dtype=jnp.float32)
    for repeat in range(PINV_ITERS):
        product = jnp.matmul(weight_matrix, approximate_result, precision=exact_result)
        nested = 7.0 * identity - product
        nested = 15.0 * identity - jnp.matmul(product, nested, precision=exact_result)
        nested = 13.0 * identity - jnp.matmul(product, nested, precision=exact_result)
        approximate_result = 0.25 * jnp.matmul(approximate_result, nested, precision=exact_result)
    return approximate_result


def rounded(values):
    return lax.optimization_barrier(values.astype(jnp.bfloat16)).astype(jnp.float32)


def heads_view(joined, heads_local):
    batch_count, length, channels = joined.shape
    return joined.reshape(batch_count, length, heads_local, channels // heads_local).transpose(
        0, 2, 1, 3
    )


def tokens_view(by_head):
    batch_count, heads_local, length, head_depth = by_head.shape
    return by_head.transpose(0, 2, 1, 3).reshape(batch_count, length, heads_local * head_depth)


def convolve(padded, broad_kernel_taps, length):

    def add_tap(offset, running):
        window = lax.dynamic_slice_in_dim(padded, offset, length, 1).astype(jnp.float32)
        return running + window * lax.dynamic_index_in_dim(broad_kernel_taps, offset, 0, False)

    initial = jnp.zeros((padded.shape[0], length, padded.shape[2]), jnp.float32)
    return lax.fori_loop(0, broad_kernel_taps.shape[0], add_tap, initial)


def tap_sums(padded, upstream, length, kernel):

    def one_tap(offset):
        window = lax.dynamic_slice_in_dim(padded, offset, length, 1).astype(jnp.float32)
        return jnp.sum(window * upstream, axis=(0, 1))

    return lax.map(one_tap, jnp.arange(kernel, dtype=jnp.int32))


def across_heads(summand):
    return lax.psum_scatter(
        summand.astype(jnp.bfloat16), "head", scatter_dimension=0, tiled=True
    ).astype(jnp.float32)


def rows_low(share):
    return lax.all_gather(share, "head", axis=0, tiled=True)


def rows_float(share):
    return lax.all_gather(share.astype(jnp.bfloat16), "head", axis=0, tiled=True).astype(
        share.dtype
    )


def own_rows(whole_rows):
    share = whole_rows.shape[0] // lax.axis_size("head")
    return lax.dynamic_slice_in_dim(whole_rows, lax.axis_index("head") * share, share, 0)


def spread_heads(share, dim_index):
    groups = lax.axis_size("head")
    full_shape = list(share.shape)
    full_shape[dim_index] = full_shape[dim_index] * groups
    empty = jnp.zeros(full_shape, jnp.float32)
    return lax.dynamic_update_slice_in_dim(
        empty, share, lax.axis_index("head") * share.shape[dim_index], dim_index
    )


def own_heads(whole, width, dim_index):
    return lax.dynamic_slice_in_dim(whole, lax.axis_index("head") * width, width, dim_index)


def forward_layer(hidden, weights, selector, segment):
    (
        projection,
        projection_shift,
        conv_kernel,
        output_matrix,
        output_shift,
        gain_pair,
        shift_pair,
        inner_matrix,
        inner_shift,
        outer_matrix,
    ) = weights
    batch_count, length, model_width = hidden.shape
    heads_local = conv_kernel.shape[0]
    kernel = conv_kernel.shape[1]
    margin = kernel // 2
    local_width = projection.shape[2]
    head_depth = local_width // heads_local
    scale = float(head_depth) ** (-0.25)
    hidden_low = hidden.astype(jnp.bfloat16).reshape(batch_count * length, model_width)
    projected = jnp.einsum(
        "nd,kde->kne", hidden_low, projection, preferred_element_type=jnp.float32
    )
    biases = projection_shift.astype(jnp.float32)
    query_rows = ((projected[0] + biases[0]) * scale).reshape(batch_count, length, local_width)
    key_rows = (projected[1] * scale).reshape(batch_count, length, local_width)
    value_low = (
        (projected[2] + biases[1]).astype(jnp.bfloat16).reshape(batch_count, length, local_width)
    )
    query_sums, key_sums = lax.psum(
        (
            jnp.einsum("mt,btc->bmc", selector, query_rows, precision=exact_result),
            jnp.einsum("mt,btc->bmc", selector, key_rows, precision=exact_result),
        ),
        "seq",
    )
    query_marks = heads_view(query_sums / segment, heads_local)
    key_marks = heads_view(key_sums / segment, heads_local)
    query_heads = heads_view(query_rows, heads_local)
    key_heads = heads_view(key_rows, heads_local)
    value_heads = heads_view(value_low.astype(jnp.float32), heads_local)
    mark_weights = soft_rows(
        jnp.einsum("bhme,bhne->bhmn", query_marks, key_marks, precision=exact_result)
    )
    inverse = pseudo_inverse(mark_weights)
    row_weights = soft_rows(
        jnp.einsum("bhte,bhme->bhtm", query_heads, key_marks, precision=exact_result)
    )
    key_scores = jnp.einsum("bhme,bhte->bhmt", query_marks, key_heads, precision=exact_result)
    local_top = jnp.max(key_scores, -1)
    score_top = lax.pmax(local_top, "seq")
    powers = jnp.exp(key_scores - score_top[..., None])
    neighbour_mixture = jnp.einsum("bhmt,bhte->bhme", powers, value_heads, precision=exact_result)
    score_total, mixed_joined = lax.psum(
        (jnp.sum(powers, -1), neighbour_mixture.reshape(batch_count, heads_local, -1)), "seq"
    )
    mixed_sum = mixed_joined.reshape(neighbour_mixture.shape)
    log_total = score_top + jnp.log(score_total)
    mixed = mixed_sum / score_total[..., None]
    core = jnp.einsum("bhmn,bhne->bhme", inverse, mixed, precision=exact_result)
    attended = jnp.einsum("bhtm,bhme->bhte", row_weights, core, precision=exact_result)
    padded_values = extended(value_low, (("seq", 1),), margin)
    broad_kernel_taps = jnp.repeat(conv_kernel.astype(jnp.float32), head_depth, axis=0).T
    context = tokens_view(attended) + convolve(padded_values, broad_kernel_taps, length)
    context_low = context.astype(jnp.bfloat16).reshape(batch_count * length, local_width)
    attention_share = across_heads(
        jnp.dot(context_low, output_matrix, preferred_element_type=jnp.float32)
    )
    shifts = output_shift.astype(jnp.float32)
    gains = gain_pair.astype(jnp.float32)
    offsets = shift_pair.astype(jnp.float32)
    hidden_share = own_rows(hidden.reshape(batch_count * length, model_width))
    total_first = hidden_share + attention_share + shifts[0]
    normed = layer_norm(total_first, gains[0], offsets[0])
    normed_low = rows_low(normed.astype(jnp.bfloat16))
    pre_active = jnp.dot(
        normed_low, inner_matrix, preferred_element_type=jnp.float32
    ) + inner_shift.astype(jnp.float32)
    active_low = jax.nn.gelu(pre_active, approximate=False).astype(jnp.bfloat16)
    feed_share = across_heads(jnp.dot(active_low, outer_matrix, preferred_element_type=jnp.float32))
    total_second = normed + feed_share + shifts[1]
    output = rows_float(layer_norm(total_second, gains[1], offsets[1])).reshape(hidden.shape)
    retained = (
        hidden_low,
        query_heads,
        key_heads,
        value_heads,
        padded_values,
        query_marks,
        key_marks,
        mark_weights,
        inverse,
        row_weights,
        log_total,
        mixed,
        core,
        context_low,
        total_first,
        normed_low,
        pre_active,
        active_low,
        total_second,
        broad_kernel_taps,
    )
    return (output, retained)


def backward_layer(upstream, retained, weights, selector, segment):
    (
        projection,
        projection_shift,
        conv_kernel,
        output_matrix,
        output_shift,
        gain_pair,
        shift_pair,
        inner_matrix,
        inner_shift,
        outer_matrix,
    ) = weights
    (
        hidden_low,
        query_heads,
        key_heads,
        value_heads,
        padded_values,
        query_marks,
        key_marks,
        mark_weights,
        inverse,
        row_weights,
        log_total,
        mixed,
        core,
        context_low,
        total_first,
        normed_low,
        pre_active,
        active_low,
        total_second,
        broad_kernel_taps,
    ) = retained
    batch_count, length, model_width = upstream.shape
    heads_local = conv_kernel.shape[0]
    kernel = conv_kernel.shape[1]
    margin = kernel // 2
    local_width = projection.shape[2]
    head_depth = local_width // heads_local
    scale = float(head_depth) ** (-0.25)
    gains = gain_pair.astype(jnp.float32)
    offsets = shift_pair.astype(jnp.float32)
    upstream_share = own_rows(upstream.reshape(batch_count * length, model_width))
    second_pull = jax.vjp(layer_norm, total_second, gains[1], offsets[1])[1]
    grad_second, gain_second, offset_second = second_pull(upstream_share)
    feed_low = rows_low(grad_second.astype(jnp.bfloat16))
    grad_outer = jnp.einsum("nf,nd->fd", active_low, feed_low, preferred_element_type=jnp.float32)
    grad_active = rounded(
        jnp.einsum("nd,fd->nf", feed_low, outer_matrix, preferred_element_type=jnp.float32)
    )
    gelu_pull = jax.vjp(partial(jax.nn.gelu, approximate=False), pre_active)[1]
    grad_pre_low = gelu_pull(grad_active)[0].astype(jnp.bfloat16)
    grad_inner_shift = jnp.sum(grad_pre_low.astype(jnp.float32), axis=0)
    grad_inner = jnp.einsum(
        "nd,nf->df", normed_low, grad_pre_low, preferred_element_type=jnp.float32
    )
    normed_term = jnp.einsum(
        "nf,df->nd", grad_pre_low, inner_matrix, preferred_element_type=jnp.float32
    )
    grad_normed = grad_second + across_heads(normed_term)
    first_pull = jax.vjp(layer_norm, total_first, gains[0], offsets[0])[1]
    grad_first, gain_first, offset_first = first_pull(grad_normed)
    attend_low = rows_low(grad_first.astype(jnp.bfloat16))
    grad_output = jnp.einsum(
        "nc,nd->cd", context_low, attend_low, preferred_element_type=jnp.float32
    )
    grad_context_low = (
        jnp.einsum("nd,cd->nc", attend_low, output_matrix, preferred_element_type=jnp.float32)
        .astype(jnp.bfloat16)
        .reshape(batch_count, length, local_width)
    )
    grad_context = lax.optimization_barrier(grad_context_low).astype(jnp.float32)
    padded_grads = extended(grad_context_low, (("seq", 1),), margin)
    grad_conv_values = convolve(padded_grads, broad_kernel_taps[::-1], length)
    kernel_sums = tap_sums(padded_values, grad_context, length, kernel)
    grad_kernel = kernel_sums.reshape(kernel, heads_local, head_depth).sum(-1).T
    grad_attended = heads_view(grad_context, heads_local)
    grad_row = jnp.einsum("bhte,bhme->bhtm", grad_attended, core, precision=exact_result)
    grad_core_local = jnp.einsum(
        "bhtm,bhte->bhme", row_weights, grad_attended, precision=exact_result
    )
    grad_row_scores = row_weights * (grad_row - jnp.sum(row_weights * grad_row, -1, keepdims=True))
    grad_query = jnp.einsum("bhtm,bhme->bhte", grad_row_scores, key_marks, precision=exact_result)
    grad_keymark_local = jnp.einsum(
        "bhtm,bhte->bhme", grad_row_scores, query_heads, precision=exact_result
    )
    grad_core_joined, grad_keymark_joined = lax.psum(
        (
            grad_core_local.reshape(batch_count, heads_local, -1),
            grad_keymark_local.reshape(batch_count, heads_local, -1),
        ),
        "seq",
    )
    grad_core = grad_core_joined.reshape(core.shape)
    grad_inverse = jnp.einsum("bhme,bhne->bhmn", grad_core, mixed, precision=exact_result)
    grad_mixed = jnp.einsum("bhnm,bhne->bhme", inverse, grad_core, precision=exact_result)
    grad_marks = jax.vjp(pseudo_inverse, mark_weights)[1](grad_inverse)[0]
    grad_mark_scores = mark_weights * (
        grad_marks - jnp.sum(mark_weights * grad_marks, -1, keepdims=True)
    )
    grad_querymark = jnp.einsum(
        "bhmn,bhne->bhme", grad_mark_scores, key_marks, precision=exact_result
    )
    grad_keymark = grad_keymark_joined.reshape(key_marks.shape) + jnp.einsum(
        "bhmn,bhme->bhne", grad_mark_scores, query_marks, precision=exact_result
    )
    key_scores = jnp.einsum("bhme,bhte->bhmt", query_marks, key_heads, precision=exact_result)
    key_weights = jnp.exp(key_scores - log_total[..., None])
    grad_values = jnp.einsum("bhmt,bhme->bhte", key_weights, grad_mixed, precision=exact_result)
    offset_term = jnp.sum(grad_mixed * mixed, -1)
    grad_key_scores = key_weights * (
        jnp.einsum("bhme,bhte->bhmt", grad_mixed, value_heads, precision=exact_result)
        - offset_term[..., None]
    )
    grad_key = jnp.einsum("bhmt,bhme->bhte", grad_key_scores, query_marks, precision=exact_result)
    grad_querymark_local = jnp.einsum(
        "bhmt,bhte->bhme", grad_key_scores, key_heads, precision=exact_result
    )
    grad_querymark = grad_querymark + lax.psum(
        grad_querymark_local.reshape(batch_count, heads_local, -1), "seq"
    ).reshape(query_marks.shape)
    grad_query = (
        grad_query
        + jnp.einsum("mt,bhme->bhte", selector, grad_querymark, precision=exact_result) / segment
    )
    grad_key = (
        grad_key
        + jnp.einsum("mt,bhme->bhte", selector, grad_keymark, precision=exact_result) / segment
    )
    grad_values = grad_values + heads_view(grad_conv_values, heads_local)
    query_low = (
        (tokens_view(grad_query) * scale)
        .astype(jnp.bfloat16)
        .reshape(batch_count * length, local_width)
    )
    key_low = (
        (tokens_view(grad_key) * scale)
        .astype(jnp.bfloat16)
        .reshape(batch_count * length, local_width)
    )
    value_grad_low = (
        tokens_view(grad_values).astype(jnp.bfloat16).reshape(batch_count * length, local_width)
    )
    stacked = jnp.stack([query_low, key_low, value_grad_low])
    grad_projection = jnp.einsum(
        "nd,kne->kde", hidden_low, stacked, preferred_element_type=jnp.float32
    )
    grad_projection_shift = jnp.stack(
        [
            jnp.sum(query_low.astype(jnp.float32), axis=0),
            jnp.sum(value_grad_low.astype(jnp.float32), axis=0),
        ]
    )
    input_term = jnp.einsum("kne,kde->nd", stacked, projection, preferred_element_type=jnp.float32)
    grad_hidden = rows_float(grad_first + across_heads(input_term)).reshape(upstream.shape)
    gradients = (
        grad_projection,
        grad_projection_shift,
        grad_kernel,
        grad_output,
        jnp.stack([jnp.sum(grad_first, axis=0), jnp.sum(grad_second, axis=0)]),
        jnp.stack([gain_first, gain_second]),
        jnp.stack([offset_first, offset_second]),
        grad_inner,
        grad_inner_shift,
        grad_outer,
    )
    return (grad_hidden, gradients)


def on_device(
    tokens,
    cotangent,
    masked,
    projections,
    projection_bias,
    conv_taps,
    output_weight,
    output_bias,
    norm_gain,
    norm_shift,
    inner_weight,
    inner_bias,
    outer_weight,
):
    length = tokens.shape[1]
    segment = length * lax.axis_size("seq") // LANDMARKS
    position = lax.axis_index("seq") * length + jnp.arange(length, dtype=jnp.int32)
    selector = (
        position[None, :] // segment == jnp.arange(LANDMARKS, dtype=jnp.int32)[:, None]
    ).astype(jnp.float32)
    arrays = (
        projections,
        projection_bias,
        conv_taps,
        output_weight,
        output_bias,
        norm_gain,
        norm_shift,
        inner_weight,
        inner_bias,
        outer_weight,
    )
    hidden = tokens.astype(jnp.float32)
    stored = []
    for layer_number in range(LAYERS):
        weights = tuple((tensor[layer_number] for tensor in arrays))
        hidden, retained = forward_layer(hidden, weights, selector, segment)
        stored.append((weights, retained))
    upstream = cotangent.astype(jnp.float32) * masked.astype(jnp.float32)[:, :, None]
    layer_grads = [None] * LAYERS
    for layer_number in range(LAYERS - 1, -1, -1):
        weights, retained = stored[layer_number]
        upstream, gradients = backward_layer(upstream, retained, weights, selector, segment)
        larger = (
            lax.psum_scatter(gradients[0], "seq", scatter_dimension=1, tiled=True),
            lax.psum_scatter(gradients[3], "seq", scatter_dimension=1, tiled=True),
            lax.psum_scatter(gradients[7], "seq", scatter_dimension=0, tiled=True),
            lax.psum_scatter(gradients[9], "seq", scatter_dimension=1, tiled=True),
        )
        gradients = (
            larger[0],
            gradients[1],
            gradients[2],
            larger[1],
            gradients[4],
            gradients[5],
            gradients[6],
            larger[2],
            gradients[8],
            larger[3],
        )
        layer_grads[layer_number] = gradients
    stacked = tuple(
        (
            jnp.stack([layer_grads[layer_number][member] for layer_number in range(LAYERS)])
            for member in range(10)
        )
    )
    larger = (stacked[0], stacked[3], stacked[7], stacked[9])
    bias_width = stacked[1].shape[2]
    taps_width = stacked[2].shape[1]
    inner_width = stacked[8].shape[1]
    smaller = lax.psum(
        (
            spread_heads(stacked[1], 2),
            spread_heads(stacked[2], 1),
            stacked[4],
            stacked[5],
            stacked[6],
            spread_heads(stacked[8], 1),
        ),
        ("seq", "head"),
    )
    grad_bias_share = own_heads(smaller[0], bias_width, 2)
    grad_taps_share = own_heads(smaller[1], taps_width, 1)
    grad_inner_share = own_heads(smaller[5], inner_width, 1)
    return (
        hidden,
        upstream,
        larger[0],
        grad_bias_share,
        grad_taps_share,
        larger[1],
        smaller[2],
        smaller[3],
        smaller[4],
        larger[2],
        grad_inner_share,
        larger[3],
    )


F32 = jnp.float32
BF16 = jnp.bfloat16
MESH = pl.DeviceIdType.MESH


def nn(a, b):
    return lax.dot_general(a, b, (((1,), (0,)), ((), ())), preferred_element_type=F32)


def nt(a, b):
    return lax.dot_general(a, b, (((1,), (1,)), ((), ())), preferred_element_type=F32)


def tn(a, b):
    return lax.dot_general(a, b, (((0,), (0,)), ((), ())), preferred_element_type=F32)


def halves(x):
    high = x.astype(BF16)
    return high, (x - high.astype(F32)).astype(BF16)


def left3(pair, axis):
    return jnp.concatenate([pair[0], pair[1], pair[0]], axis=axis)


def right3(pair, axis):
    return jnp.concatenate([pair[0], pair[0], pair[1]], axis=axis)


def nn3(a, b):
    return nn(left3(a, 1), right3(b, 0))


def nt3(a, b):
    return nt(left3(a, 1), right3(b, 1))


def tn3(a, b):
    return tn(left3(a, 0), right3(b, 0))


def nn3f(a, b):
    return nn3(halves(a), halves(b))


def nt3f(a, b):
    return nt3(halves(a), halves(b))


def tn3f(a, b):
    return tn3(halves(a), halves(b))


class Fast:
    def __init__(self, mesh_shape, tokens, conv_taps, inner_weight):
        self.n = mesh_shape["seq"]
        self.heads = mesh_shape["head"]
        self.batch, whole, self.width = tokens.shape
        self.length = whole // self.n
        self.layers, all_heads, self.kernel = conv_taps.shape
        self.local_heads = all_heads // self.heads
        self.depth = self.width // all_heads
        self.cols = self.local_heads * self.depth
        self.hidden = inner_weight.shape[2] // self.heads
        self.rows = self.batch * self.length
        self.segment = whole // LANDMARKS
        self.spans = self.length // self.segment
        self.units = self.batch * self.local_heads // 2
        self.bits = self.n.bit_length() - 1

    def fits(self):
        return (
            self.n == 1 << self.bits
            and self.n >= 16
            and self.heads == 2
            and self.length == 128
            and self.batch == 2
            and self.spans * self.batch == 8
            and self.depth == 64
            and self.local_heads % 2 == 0
            and self.width % (16 * self.n) == 0
            and self.width % 256 == 0
            and self.hidden % 512 == 0
            and self.kernel == 65
            and self.layers == 2
            and LANDMARKS == 64
        )


def fused_kernel(
    z,
    tok, cot, mask, pbias, taps, obias, ngain, nshift, ibias, wp_hbm, wo_hbm, wi_hbm, wf_hbm,
    result, gtok, gproj, gbias, gtaps, gout, gobias, ggain, gshift, ginner, gibias, gouter,
    *,
    WP, WO, WI, WF,
    QS, KS, VX, RW, CTX, T1, T2, GP, ACT, QM, KM, CR, MX, PA, PV, PZ, PC, LTH, LTN,
    HID, UP, LOW, PN, PF, DPRE, GX, DQ, DK, DV, DP, DQM, DKM, DR, SM, TB, TT, TR, LTF, LTA,
    LSH, OP, OO, OI, OU, OS, OT,
    MS, MB, MD, MO, XM, OB, SB, SR, HS, HR, SMR, SMT,
    G, RV,
    wsem, hsem_s, hsem_r, msem_s, msem_r, dsem_s, dsem_r, xsem_s, xsem_r, csem_s, csem_r, vsem_s, vsem_r,
    osem, asem_s, asem_r, bsem_s, bsem_r, gsem_s, gsem_r, qsem_s, qsem_r, ssem_s, ssem_r, tsem_s, tsem_r,
):
    n, B, L, R, D, C, F = z.n, z.batch, z.length, z.rows, z.width, z.cols, z.hidden
    U, NP, S, K = z.units, z.local_heads // 2, z.spans, z.kernel
    CH = D // n
    NB = z.bits
    M = LANDMARKS
    margin = K // 2
    scale = float(z.depth) ** (-0.25)
    me = lax.axis_index("seq")
    core = lax.axis_index("head")
    first_owner = n // 2 - U // 2
    is_owner = jnp.logical_and(me >= first_owner, me < first_owner + U)
    mine = jnp.clip(me - first_owner, 0, U - 1)

    def weight_copies(l):
        return [
            pltpu.make_async_copy(wp_hbm.at[l], WP.at[l], wsem.at[l, 0]),
            pltpu.make_async_copy(wo_hbm.at[l], WO.at[l], wsem.at[l, 1]),
            pltpu.make_async_copy(wi_hbm.at[l], WI.at[l], wsem.at[l, 2]),
            pltpu.make_async_copy(wf_hbm.at[l], WF.at[l], wsem.at[l, 3]),
        ]

    weight_copies(0)[0].start()

    barrier = pltpu.get_barrier_semaphore()

    def greet(d, _):
        pl.semaphore_signal(
            barrier, inc=1, device_id={"seq": lax.rem(me + d, n)}, device_id_type=MESH
        )
        return 0

    lax.fori_loop(1, n, greet, 0)
    pl.semaphore_signal(barrier, inc=1, device_id={"head": 1 - core}, device_id_type=MESH)

    row_id = lax.broadcasted_iota(jnp.int32, (128, 128), 0)
    lane_id = lax.broadcasted_iota(jnp.int32, (128, 128), 1)
    low_lane = lane_id < 64
    low_lane64 = low_lane[0:64]
    same_head = (row_id < 64) == low_lane
    eye = row_id == lane_id
    flip = jnp.where(row_id + lane_id == 127, 1.0, 0.0).astype(BF16)

    def expand(c):
        return jnp.concatenate(
            [jnp.where(low_lane64, c, 0.0), jnp.where(low_lane64, 0.0, c)], axis=0
        )

    def expand_low(c):
        return expand(c.astype(F32)).astype(BF16)

    def compress(x):
        return jnp.where(low_lane64, x[0:64], x[64:128])

    def to_row(col):
        return jnp.sum(jnp.where(eye, col, 0.0), axis=0, keepdims=True)

    def to_col(row):
        return jnp.sum(jnp.where(eye, row, 0.0), axis=1, keepdims=True)

    def half_sums(x):
        a = jnp.sum(jnp.where(low_lane, x, 0.0), axis=1, keepdims=True)
        b = jnp.sum(jnp.where(low_lane, 0.0, x), axis=1, keepdims=True)
        return jnp.where(low_lane, a, b)

    def half_tops(x):
        a = jnp.max(jnp.where(low_lane, x, -jnp.inf), axis=1, keepdims=True)
        b = jnp.max(jnp.where(low_lane, -jnp.inf, x), axis=1, keepdims=True)
        return jnp.where(low_lane, a, b)

    def parts3(x):
        a = x.astype(BF16)
        rest = x - a.astype(F32)
        b = rest.astype(BF16)
        c = (rest - b.astype(F32)).astype(BF16)
        return jnp.concatenate([a.astype(F32), b.astype(F32), c.astype(F32)], axis=0)

    def pack(body, rows):
        tail = jnp.concatenate([parts3(r) for r in rows], axis=0)
        fill = jnp.zeros((16 - tail.shape[0], 128), F32)
        return jnp.concatenate([body, tail, fill], axis=0).astype(BF16)

    def packed_row(message, i):
        x = message[64 + 3 * i : 67 + 3 * i].astype(F32)
        return jnp.sum(x, axis=0, keepdims=True)

    def unit(u):
        return u // NP, u % NP

    def tile(ref, l, u):
        b, j = unit(u)
        return ref[l, b * L : (b + 1) * L, j * 128 : (j + 1) * 128]

    def moments(x):
        centre = jnp.mean(x, -1, keepdims=True)
        centred = x - centre
        spread = jnp.mean(centred * centred, -1, keepdims=True)
        inverse = lax.rsqrt(spread + epsilon)
        return centred * inverse, inverse

    def norm_back(x, grad, gain):
        hat, inverse = moments(x)
        g = grad * gain
        a = jnp.mean(g, -1, keepdims=True)
        b = jnp.mean(g * hat, -1, keepdims=True)
        total = inverse * (g - a - hat * b)
        sums = (
            jnp.sum(grad * hat, axis=0, keepdims=True),
            jnp.sum(grad, axis=0, keepdims=True),
            jnp.sum(total, axis=0, keepdims=True),
        )
        return total, sums

    def put_small(start, vector):
        for i in range(vector.shape[1] // 128):
            SM[start + i : start + i + 1, :] = vector[:, i * 128 : (i + 1) * 128]

    def swap(e):
        return pltpu.make_async_remote_copy(
            HS.at[e % 2], HR.at[e % 2], hsem_s.at[e], hsem_r.at[e],
            device_id={"head": 1 - core}, device_id_type=MESH,
        )

    def both(e):
        return HS[e % 2].astype(F32) + HR[e % 2].astype(F32)

    def spread(src, dst, ss, rs, start):
        def step(d, _):
            t = lax.rem(me + d, n)
            c = pltpu.make_async_remote_copy(
                src(t), dst.at[me], ss.at[t], rs.at[me], device_id={"seq": t}, device_id_type=MESH
            )
            c.start()
            return 0

        def finish(d, _):
            t = lax.rem(me + d, n)
            c = pltpu.make_async_remote_copy(
                src(t), dst.at[t], ss.at[t], rs.at[t], device_id={"seq": t}, device_id_type=MESH
            )
            c.wait_recv()
            c.wait_send()
            return 0

        lax.fori_loop(1, n, step if start else finish, 0)

    def to_owner_copy(u, src, dst, ss, rs):
        return pltpu.make_async_remote_copy(
            src, dst.at[me], ss.at[u], rs.at[me], device_id={"seq": first_owner + u}, device_id_type=MESH
        )

    def to_owner(u, src, dst, ss, rs):
        @pl.when(me != first_owner + u)
        def _():
            to_owner_copy(u, src, dst, ss, rs).start()

        @pl.when(me == first_owner + u)
        def _():
            dst[me] = src[...]

    def to_owner_sent(u, src, dst, ss, rs):
        @pl.when(me != first_owner + u)
        def _():
            to_owner_copy(u, src, dst, ss, rs).wait_send()

    def owner_gets(src, dst, ss, rs):
        def step(d, _):
            t = lax.rem(me + d, n)
            pltpu.make_async_remote_copy(
                src, dst.at[t], ss.at[0], rs.at[t], device_id={"seq": t}, device_id_type=MESH
            ).wait_recv()
            return 0

        lax.fori_loop(1, n, step, 0)

    def from_owner(slots, ss, rs, start):
        def step(d, _):
            t = lax.rem(me + d, n)
            c = pltpu.make_async_remote_copy(
                slots.at[mine], slots.at[mine], ss.at[t], rs.at[mine],
                device_id={"seq": t}, device_id_type=MESH,
            )
            if start:
                c.start()
            else:
                c.wait_send()
            return 0

        lax.fori_loop(1, n, step, 0)

    def owner_came(slots, u, ss, rs):
        @pl.when(me != first_owner + u)
        def _():
            pltpu.make_async_remote_copy(
                slots.at[u], slots.at[u], ss.at[0], rs.at[u],
                device_id={"seq": first_owner + u}, device_id_type=MESH,
            ).wait_recv()

    def edges(buf, ss, rs, act):
        after = pltpu.make_async_remote_copy(
            buf.at[:, pl.ds(L, margin)], buf.at[:, pl.ds(0, margin)], ss.at[0], rs.at[0],
            device_id={"seq": lax.rem(me + 1, n)}, device_id_type=MESH,
        )
        before = pltpu.make_async_remote_copy(
            buf.at[:, pl.ds(margin, margin)], buf.at[:, pl.ds(margin + L, margin)], ss.at[1], rs.at[1],
            device_id={"seq": lax.rem(me + n - 1, n)}, device_id_type=MESH,
        )
        if act == "start":
            @pl.when(me < n - 1)
            def _():
                after.start()

            @pl.when(me > 0)
            def _():
                before.start()
        else:
            @pl.when(me < n - 1)
            def _():
                after.wait_send()
                before.wait_recv()

            @pl.when(me > 0)
            def _():
                before.wait_send()
                after.wait_recv()

    def edge_zeros(buf):
        none = jnp.zeros((B, margin, C), BF16)
        buf[:, 2 * margin + L :, :] = jnp.zeros((B, 256 - L - 2 * margin, C), BF16)

        @pl.when(me == 0)
        def _():
            buf[:, 0:margin, :] = none

        @pl.when(me == n - 1)
        def _():
            buf[:, margin + L : 2 * margin + L, :] = none

    def conv(bands, buf, u):
        b, j = unit(u)
        x = buf[b, :, j * 128 : (j + 1) * 128]
        return jnp.where(low_lane, nn(bands[2 * j], x), nn(bands[2 * j + 1], x))

    DT, FL = HID, LOW
    own_bits = [lax.rem(me // (1 << k), 2) for k in range(NB)]
    dims = [[k for k in reversed(range(NB)) if k != g] for g in range(2)]
    FH = F // 2
    HALF = G.shape[-1]
    everything = pl.ds(0, 2)
    items = {"outer": (0, FH), "inner": (FH, FH), "outval": (2 * FH, C), "keyed": (2 * FH + C, C)}
    item_index = {name: i for i, name in enumerate(items)}

    def peer_of(k):
        return me + (1 - 2 * own_bits[k]) * (1 << k)

    def pair_copy(l, i, g, src, dst):
        return pltpu.make_async_remote_copy(
            src, dst, asem_s.at[l, i, g], asem_r.at[l, i, g],
            device_id={"seq": peer_of(g)}, device_id_type=MESH,
        )

    def right_copies(l, i, ref, ranges):
        return [
            pair_copy(l, i, g, ref.at[pl.ds(0, R), pl.ds(c0, cn)], ref.at[pl.ds(R, R), pl.ds(c0, cn)])
            for g, (c0, cn) in enumerate(ranges)
        ]

    def left_copies(l, i, stage, gathered):
        got = []
        for g in range(2):
            at = [core] + [everything] * (NB - 1)
            at[NB - 1 - g] = 1 - own_bits[g]
            src = stage.at[tuple(at) + (pl.ds(0, CH), pl.ds(0, R))]
            dst = gathered.at[(g, core) + (everything,) * (NB - 2) + (pl.ds(0, CH), pl.ds(R, R))]
            got.append(pair_copy(l, i, g, src, dst))
        return got

    def core_copy(l, i, g, ref):
        return pltpu.make_async_remote_copy(
            ref, ref, bsem_s.at[l, i, g], bsem_r.at[l, i, g],
            device_id={"head": 1 - core}, device_id_type=MESH,
        )

    def left_hand_on(l, i, gathered):
        return [
            core_copy(l, i, g, gathered.at[(g, core) + (everything,) * (NB - 2) + (pl.ds(0, CH), pl.ds(R, R))])
            for g in range(2)
        ]

    def row_copies(l, i, src, dst):
        at = pl.ds(pl.multiple_of(core * L, L), L)
        return [pair_copy(l, i, g, src.at[at], dst.at[g, at]) for g in range(2)]

    def row_hand_on(l, i, dst):
        at = pl.ds(pl.multiple_of(core * L, L), L)
        return [core_copy(l, i, g, dst.at[g, at]) for g in range(2)]

    def each_half(g, act):
        for code in range(n // 2):
            spot = tuple((code >> (NB - 2 - i)) & 1 for i in range(NB - 1))
            at = list(spot)
            at.insert(NB - 1 - g, own_bits[g])
            act((g,) + spot, tuple(at))

    def left_put(x, stage, gathered):
        stage[...] = x.T.reshape(stage.shape)
        for g in range(2):
            def put(to, at):
                gathered[to + (slice(None), slice(0, R))] = stage[at]

            each_half(g, put)

    def left_put_theirs(rows, stage, gathered):
        for g in range(2):
            stage[...] = rows[g].T.reshape(stage.shape)

            def put(to, at):
                gathered[to + (slice(None), slice(R, 2 * R))] = stage[at]

            each_half(g, put)

    def start_all(copies):
        for c in copies:
            c.start()

    def wait_all(copies):
        for c in copies:
            c.wait()

    def weight_grad(g, left, right, first, count, width):
        def step(i, _):
            o = pl.multiple_of(i * width, width)
            x = nn(left[g].reshape(D // 2, 2 * R), right(o)).astype(BF16)
            o = pl.multiple_of(first + o, 128)
            for code in range(n // 2):
                spot = tuple((code >> (NB - 2 - i)) & 1 for i in range(NB - 1))
                G[(g,) + spot + (slice(None), pl.ds(o, width))] = x[code * CH : (code + 1) * CH]
            return 0

        lax.fori_loop(0, count // width, step, 0)

    STAGES = NB - 1

    def rs_copy(l, name, g, stage):
        first, count = items[name]
        cols = (pl.ds(0, CH), pl.ds(first, count))
        d = NB - 2 - stage
        index = [everything] * d + [1 - own_bits[dims[g][d]]] + [own_bits[k] for k in dims[g][d + 1 :]]
        i = item_index[name]
        return pltpu.make_async_remote_copy(
            G.at[(g,) + tuple(index) + cols], RV[stage].at[(l, g) + (everything,) * d + cols],
            gsem_s.at[l, i, g, stage], gsem_r.at[l, i, g, stage],
            device_id={"seq": peer_of(dims[g][d])}, device_id_type=MESH,
        )

    def rs_start(l, name, stage):
        for g in range(2):
            rs_copy(l, name, g, stage).start()

    def rs_add(l, name, stage):
        first, count = items[name]
        for g in range(2):
            rs_copy(l, name, g, stage).wait()
            d = NB - 2 - stage
            mine_at = tuple(own_bits[k] for k in dims[g][d:])
            cols = (slice(None), slice(first, first + count))
            if d:
                for code in range(1 << d):
                    spot = tuple((code >> (d - 1 - i)) & 1 for i in range(d))
                    at = (g,) + spot + mine_at + cols
                    G[at] = G[at] + RV[stage][(l, g) + spot + cols]
            else:
                x = G[(g,) + mine_at + cols].astype(F32) + RV[stage][(l, g) + cols].astype(F32)
                write_out(l, name, g, x)

    def write_out(l, name, g, x):
        if name == "outer":
            OU[l, :, g * FH : (g + 1) * FH] = x
        elif name == "inner":
            OI[l, :, g * FH : (g + 1) * FH] = x
        elif name == "keyed":
            OP[l, g] = x
        elif g == 0:
            OO[l, :, 0:128] = x[:, 0:128]
            OP[l, 2, :, 0 : C - 128] = x[:, 128:C]
        else:
            OO[l, :, 128:C] = x[:, 0 : C - 128]
            OP[l, 2, :, C - 128 : C] = x[:, C - 128 : C]

    def out_copy(i, src, dst):
        return pltpu.make_async_copy(src, dst, osem.at[i])

    def advance(l, name, stage):
        rs_add(l, name, stage)
        if stage + 1 < STAGES:
            rs_start(l, name, stage + 1)

    out_ranges = ((0, 128), (128, C - 128))
    val_ranges = ((2 * C, C - 128), (3 * C - 128, 128))
    key_ranges = ((0, C), (C, C))
    ffn_ranges = ((0, FH), (FH, FH))

    for b in range(B):
        HID[b * L : (b + 1) * L, :] = tok[b].astype(F32)
    TB[...] = jnp.zeros_like(TB)

    def make_bands(l):
        backwards = jnp.where(row_id + lane_id == K - 1, 1.0, 0.0).astype(BF16)
        TB[0, 0 : z.local_heads, 0:K] = taps[l].astype(F32)
        TB[1, :, 0:128] = nn(TB[0, :, 0:128].astype(BF16), backwards)
        for which, store in ((0, TT), (1, TR)):
            for h in range(z.local_heads):
                base = jnp.broadcast_to(TB[which, h : h + 1, :], (128, 256))
                store[l, h] = pltpu.roll(base, 0, 1, stride=1, stride_axis=0).astype(BF16)

    def regrow(l):
        wait_all(row_hand_on(l, 2, PN))
        left_put_theirs(PN, LSH, LTN.at[l])
        for g in range(2):
            def step(i, _):
                o = pl.ds(pl.multiple_of(g * FH + i * 256, 256), 256)
                act, slope = unit_rows(PN[g], l, o)
                ACT[l, R : 2 * R, o] = act
                GP[l, R : 2 * R, o] = slope
                return 0

            lax.fori_loop(0, FH // 256, step, 0)

    def unit_rows(rows, l, o):
        pre = nn(rows, WI[l, :, o]) + ibias[l : l + 1, o].astype(F32)
        below = 0.5 * (1.0 + lax.erf(pre * (0.5**0.5)))
        slope = below + pre * jnp.exp(-0.5 * pre * pre) * 0.3989422804014327
        return (pre * below).astype(BF16), slope.astype(BF16)

    def forward(l):
        copies = weight_copies(l)
        e = 2 * l
        LOW[...] = HID[...].astype(BF16)
        copies[0].wait()
        if l == 0:
            for c in [weight_copies(0)[i] for i in (1, 2, 3)] + weight_copies(1):
                c.start()
        both_bias = pbias[l].astype(F32)
        bias_q, bias_v = both_bias[0:1], both_bias[1:2]
        q = (nn(LOW[...], WP[l, 0]) + bias_q) * scale
        k = nn(LOW[...], WP[l, 1]) * scale
        QS[l] = q.astype(BF16)
        KS[l] = k.astype(BF16)
        sums = []
        for x in (q, k):
            for b in range(B):
                for r in range(S):
                    at = b * L + r * z.segment
                    sums.append(jnp.sum(x[at : at + z.segment], axis=0, keepdims=True))
        marks = jnp.concatenate(sums, axis=0) * (1.0 / z.segment)
        MS[...] = marks.astype(BF16)
        rest = marks - MS[...].astype(F32)
        middle = rest.astype(BF16).astype(F32)
        rest = rest - middle
        for u in range(U):
            b, j = unit(u)
            parts = [
                x[first + b * S : first + (b + 1) * S, j * 128 : (j + 1) * 128]
                for x in (middle, rest)
                for first in (0, 8)
            ]
            MD[u] = jnp.concatenate(parts, axis=0).astype(BF16)
        if l == 0:
            pl.semaphore_wait(barrier, n)
        spread(lambda t: MS, MB, msem_s.at[l], msem_r.at[l], True)
        for u in range(U):
            to_owner(u, MD.at[u], MO, dsem_s.at[l], dsem_r.at[l])
        MB[me] = MS[...]
        vl = (nn(LOW[...], WP[l, 2]) + bias_v).astype(BF16)
        for b in range(B):
            VX[l, b, margin : margin + L, :] = vl[b * L : (b + 1) * L]
        edge_zeros(VX.at[l])
        edges(VX.at[l], vsem_s.at[l], vsem_r.at[l], "start")
        if l:
            regrow(l - 1)
        left_put(LOW[...], LSH, LTH.at[l])
        make_bands(l)
        edges(VX.at[l], vsem_s.at[l], vsem_r.at[l], "wait")
        for u in range(U):
            b, j = unit(u)
            DQ[b * L : (b + 1) * L, j * 128 : (j + 1) * 128] = conv(TT.at[l], VX.at[l], u)
        spread(lambda t: MS, MB, msem_s.at[l], msem_r.at[l], False)
        hidden_copies = left_copies(l, 0, LSH, LTH.at[l])
        start_all(hidden_copies)
        for u in range(U):
            b, j = unit(u)
            lanes = slice(j * 128, (j + 1) * 128)
            for first, store in ((0, QM), (8, KM)):
                rows = [MB[i, :, lanes].astype(F32)[first + b * S : first + (b + 1) * S] for i in range(n)]
                store[l, u] = jnp.concatenate(rows, axis=0)
        for u in range(U):
            b, j = unit(u)
            ksc = nt(expand(QM[l, u]).astype(BF16), tile(KS, l, u))
            top = jnp.max(ksc, axis=1, keepdims=True)
            p = jnp.exp(ksc - top)
            total = jnp.sum(p, axis=1, keepdims=True)
            v = VX[l, b, margin : margin + L, j * 128 : (j + 1) * 128]
            XM[u] = pack(compress(nn(p.astype(BF16), v)), [to_row(top), to_row(total)])
            to_owner(u, XM.at[u], OB, xsem_s.at[l], xsem_r.at[l])
        for u in range(U):
            s = nt(tile(QS, l, u), expand(KM[l, u]).astype(BF16))
            p = jnp.exp(s - half_tops(s))
            RW[l, u] = p / half_sums(p)

        @pl.when(is_owner)
        def _():
            owner_gets(MD.at[0], MO, dsem_s.at[l], dsem_r.at[l])
            extra = []
            for i in range(n):
                x = MO[i].astype(F32)
                extra.append(x[0:8] + x[8:16])
            qb = expand(QM[l, mine] + jnp.concatenate([x[0:S] for x in extra], axis=0))
            kb = expand(KM[l, mine] + jnp.concatenate([x[S : 2 * S] for x in extra], axis=0))
            s = jnp.where(same_head, nt3f(qb, kb), -jnp.inf)
            p = jnp.exp(s - jnp.max(s, axis=1, keepdims=True))
            a = p / jnp.sum(p, axis=1, keepdims=True)
            PA[l] = a
            ah = halves(a)
            sums = jnp.sum(a, axis=0, keepdims=True)
            tops = jnp.where(
                low_lane[0:1],
                jnp.max(jnp.where(low_lane[0:1], sums, 0.0), axis=1, keepdims=True),
                jnp.max(jnp.where(low_lane[0:1], 0.0, sums), axis=1, keepdims=True),
            )
            unit_matrix = jnp.where(eye, 1.0, 0.0)

            def iterate(i, zk):
                PV[l, i, 0] = zk
                zh = halves(zk)
                pr = nn3(ah, zh)
                PV[l, i, 1] = pr
                prh = halves(pr)
                n2 = 15.0 * unit_matrix - nn3(prh, halves(7.0 * unit_matrix - pr))
                PV[l, i, 2] = n2
                n3 = 13.0 * unit_matrix - nn3(prh, halves(n2))
                PV[l, i, 3] = n3
                return 0.25 * nn3(zh, halves(n3))

            zk = lax.fori_loop(0, PINV_ITERS, iterate, a.T / tops)
            PZ[l] = zk
            owner_gets(XM.at[0], OB, xsem_s.at[l], xsem_r.at[l])
            tops = [packed_row(OB.at[i], 0) for i in range(n)]
            top = tops[0]
            for i in range(1, n):
                top = jnp.maximum(top, tops[i])
            factors = [jnp.exp(x - top) for x in tops]
            total = factors[0] * packed_row(OB.at[0], 1)
            for i in range(1, n):
                total = total + factors[i] * packed_row(OB.at[i], 1)
            mixed = jnp.zeros((64, 128), F32)
            for i in range(n):
                col = to_col(factors[i] / total)
                mixed = mixed + jnp.where(low_lane64, col[0:64], col[64:128]) * OB[i, 0:64].astype(F32)
            MX[l] = mixed
            CR[l, mine] = pack(compress(nn3f(zk, expand(mixed))), [top + jnp.log(total)])
            from_owner(CR.at[l], csem_s.at[l], csem_r.at[l], True)

        wait_all(hidden_copies)
        start_all(left_hand_on(l, 0, LTH.at[l]))
        for u in range(U):
            b, j = unit(u)
            to_owner_sent(u, XM.at[u], OB, xsem_s.at[l], xsem_r.at[l])
            to_owner_sent(u, MD.at[u], MO, dsem_s.at[l], dsem_r.at[l])
            owner_came(CR.at[l], u, csem_s.at[l], csem_r.at[l])
            at = (slice(b * L, (b + 1) * L), slice(j * 128, (j + 1) * 128))
            context = nn(RW[l, u].astype(BF16), expand_low(CR[l, u, 0:64])) + DQ[at]
            CTX[(l,) + at] = context.astype(BF16)
        start_all(right_copies(l, 1, CTX.at[l], out_ranges))

        @pl.when(is_owner)
        def _():
            from_owner(CR.at[l], csem_s.at[l], csem_r.at[l], False)

        copies[1].wait()
        HS[e % 2] = nn(CTX[l, 0:R], WO[l]).astype(BF16)
        c = swap(e)
        c.start()
        c.wait()
        total1 = HID[...] + both(e) + obias[l].astype(F32)[0:1]
        T1[l] = total1
        normed = moments(total1)[0] * ngain[l].astype(F32)[0:1] + nshift[l].astype(F32)[0:1]
        HID[...] = normed
        LOW[...] = normed.astype(BF16)
        norm_copies = row_copies(l, 2, LOW, PN)
        start_all(norm_copies)
        copies[2].wait()

        def grow(i, _):
            o = pl.ds(pl.multiple_of(i * 256, 256), 256)
            act, slope = unit_rows(LOW[...], l, o)
            ACT[l, 0:R, o] = act
            GP[l, 0:R, o] = slope
            return 0

        lax.fori_loop(0, F // 256, grow, 0)
        copies[3].wait()

        def shrink(i, _):
            o = pl.ds(pl.multiple_of(i * 256, 256), 256)
            HS[(e + 1) % 2, :, o] = nn(ACT[l, 0:R], WF[l, :, o]).astype(BF16)
            return 0

        lax.fori_loop(0, D // 256, shrink, 0)
        c = swap(e + 1)
        c.start()
        left_put(LOW[...], LSH, LTN.at[l])
        c.wait()
        total2 = HID[...] + both(e + 1) + obias[l].astype(F32)[1:2]
        T2[l] = total2
        HID[...] = moments(total2)[0] * ngain[l].astype(F32)[1:2] + nshift[l].astype(F32)[1:2]
        wait_all(norm_copies)
        start_all(row_hand_on(l, 2, PN))

    def backward(l, left):
        e = 2 * z.layers + 2 * (z.layers - 1 - l)
        k = z.layers + l
        base = 60 * l
        total2, sums = norm_back(T2[l], UP[...], ngain[l].astype(F32)[1:2])
        put_small(base + 6, sums[0])
        put_small(base + 18, sums[1])
        put_small(base + 30, sums[2])
        DT[...] = total2
        FL[...] = total2.astype(BF16)
        feed_copies = row_copies(l, 4, FL, PF)
        start_all(feed_copies)

        def widen(i, _):
            o = pl.ds(pl.multiple_of(i * 256, 256), 256)
            grad = nt(FL[...], WF[l, o, :]).astype(BF16).astype(F32)
            pre = (GP[l, 0:R, o].astype(F32) * grad).astype(BF16)
            DPRE[0:R, o] = pre
            s = jnp.sum(pre.astype(F32), axis=0, keepdims=True)
            SM[pl.ds(base + 36 + 2 * i, 1), :] = s[:, 0:128]
            SM[pl.ds(base + 37 + 2 * i, 1), :] = s[:, 128:256]
            return 0

        lax.fori_loop(0, F // 256, widen, 0)
        def narrow(i, _):
            o = pl.ds(pl.multiple_of(i * 256, 256), 256)
            HS[e % 2, :, o] = nt(DPRE[0:R], WI[l, o, :]).astype(BF16)
            return 0

        lax.fori_loop(0, D // 256, narrow, 0)
        c = swap(e)
        c.start()
        left_put(FL[...], LSH, LTF)
        if l == z.layers - 1:
            regrow(l)
        wait_all(feed_copies)
        start_all(row_hand_on(l, 4, PF))
        c.wait()
        grad_normed = DT[...] + both(e)
        total1, sums = norm_back(T1[l], grad_normed, ngain[l].astype(F32)[0:1])
        put_small(base + 0, sums[0])
        put_small(base + 12, sums[1])
        put_small(base + 24, sums[2])
        DT[...] = total1
        FL[...] = total1.astype(BF16)
        grads = nt(FL[...], WO[l]).astype(BF16)
        for b in range(B):
            GX[b, margin : margin + L, :] = grads[b * L : (b + 1) * L]
        edge_zeros(GX)
        edges(GX, vsem_s.at[k], vsem_r.at[k], "start")

        def g_tile(u):
            b, j = unit(u)
            return GX[b, margin : margin + L, j * 128 : (j + 1) * 128]

        for u in range(U):
            XM[u, 0:64] = compress(tn(RW[l, u].astype(BF16), g_tile(u))).astype(BF16)
            to_owner(u, XM.at[u, pl.ds(0, 64)], OB.at[:, pl.ds(0, 64)], xsem_s.at[k], xsem_r.at[k])
            DQM[u] = jnp.zeros((64, 128), F32)
        wait_all(row_hand_on(l, 4, PF))
        left_put_theirs(PF, LSH, LTF)
        for g in range(2):
            def step(i, _):
                o = pl.ds(pl.multiple_of(g * FH + i * 256, 256), 256)
                grad = nt(PF[g], WF[l, o, :]).astype(BF16).astype(F32)
                DPRE[R : 2 * R, o] = (GP[l, R : 2 * R, o].astype(F32) * grad).astype(BF16)
                return 0

            lax.fori_loop(0, FH // 256, step, 0)
        left_put(FL[...], LSH, LTA)
        attend_copies = left_copies(l, 6, LSH, LTA)
        start_all(attend_copies)
        for done in left[:1]:
            done()
        for g in range(2):
            weight_grad(g, LTF, lambda o: ACT[l, :, pl.ds(g * FH + o, 256)], items["outer"][0], FH, 256)
        rs_start(l, "outer", 0)

        @pl.when(is_owner)
        def _():
            owner_gets(XM.at[0, pl.ds(0, 64)], OB.at[:, pl.ds(0, 64)], xsem_s.at[k], xsem_r.at[k])
            d_core = OB[0, 0:64].astype(F32)
            for i in range(1, n):
                d_core = d_core + OB[i, 0:64].astype(F32)
            PC[...] = d_core
            d_mixed = tn3f(PZ[l], expand(d_core))
            off = jnp.sum(d_mixed * expand(MX[l]), axis=1, keepdims=True)
            DR[mine] = pack(compress(d_mixed), [to_row(off)])
            from_owner(DR, csem_s.at[k], csem_r.at[k], True)

        for u in range(U):
            b, j = unit(u)
            at = (slice(b * L, (b + 1) * L), slice(j * 128, (j + 1) * 128))
            d_row = nt(g_tile(u), expand_low(CR[l, u, 0:64]))
            rw = RW[l, u]
            d_rs = (rw * (d_row - half_sums(rw * d_row))).astype(BF16)
            DQ[at] = nn(d_rs, expand(KM[l, u]).astype(BF16))
            DKM[u] = compress(tn(d_rs, tile(QS, l, u)))
        for u in range(U):
            to_owner_sent(u, XM.at[u, pl.ds(0, 64)], OB.at[:, pl.ds(0, 64)], xsem_s.at[k], xsem_r.at[k])

        @pl.when(is_owner)
        def _():
            a = PA[l]
            ah = halves(a)
            unit_matrix = jnp.where(eye, 1.0, 0.0)

            def back(i, carry):
                dz, da = carry
                i = PINV_ITERS - 1 - i
                zh, prh = halves(PV[l, i, 0]), halves(PV[l, i, 1])
                n1h = halves(7.0 * unit_matrix - PV[l, i, 1])
                n2h, n3h = halves(PV[l, i, 2]), halves(PV[l, i, 3])
                dzh = halves(dz)
                dn3 = halves(0.25 * tn3(zh, dzh))
                dn2 = halves(-tn3(prh, dn3))
                dpr = tn3(prh, dn2) - nt3(dn3, n2h) - nt3(dn2, n1h)
                dpr = halves(dpr)
                dz = 0.25 * nt3(dzh, n3h) + tn3(ah, dpr)
                return dz, da + nt3(dpr, zh)

            dz, da = lax.fori_loop(
                0, PINV_ITERS, back, (nt3f(expand(PC[...]), expand(MX[l])), jnp.zeros((128, 128), F32))
            )
            low_row = low_lane[0:1]

            def half_row(x, f):
                return jnp.where(
                    low_row,
                    f(jnp.where(low_row, x, 0.0), axis=1, keepdims=True),
                    f(jnp.where(low_row, 0.0, x), axis=1, keepdims=True),
                )

            sums = jnp.sum(a, axis=0, keepdims=True)
            tops = half_row(sums, jnp.max)
            d_tops = -half_row(jnp.sum(dz * PV[l, 0, 0], axis=0, keepdims=True), jnp.sum) / tops
            at_top = jnp.where(sums == tops, 1.0, 0.0)
            da = da + (dz / tops).T + at_top * d_tops / half_row(at_top, jnp.sum)
            d_ms = halves(a * (da - jnp.sum(a * da, axis=1, keepdims=True)))
            DQM[mine] = compress(nn3(d_ms, halves(expand(KM[l, mine]))))
            DKM[mine] = DKM[mine] + compress(tn3(d_ms, halves(expand(QM[l, mine]))))

        for done in left[1:2]:
            done()
        wait_all(attend_copies)
        start_all(left_hand_on(l, 6, LTA))
        for g in range(2):
            weight_grad(g, LTN.at[l], lambda o: DPRE[:, pl.ds(g * FH + o, 256)], items["inner"][0], FH, 256)
        rs_start(l, "inner", 0)
        edges(GX, vsem_s.at[k], vsem_r.at[k], "wait")
        for u in range(U):
            b, j = unit(u)
            at = (slice(b * L, (b + 1) * L), slice(j * 128, (j + 1) * 128))
            DV[at] = conv(TR.at[l], GX, u)
        for j in range(NP):
            for h in range(2):
                found = jnp.zeros((128, 256), F32)
                for b in range(B):
                    g = nn(flip, g_tile(b * NP + j))
                    g = jnp.where(low_lane, g, 0.0) if h == 0 else jnp.where(low_lane, 0.0, g)
                    found = found + nt(g.astype(BF16), VX[l, b, :, j * 128 : (j + 1) * 128])
                found = pltpu.roll(found, 129, 1, stride=1, stride_axis=0)
                row = base + 54 + 2 * j + h
                SM[row : row + 1, :] = jnp.sum(found[:, 0:128], axis=0, keepdims=True)
        advance(l, "outer", 0)
        for u in range(U):
            b, j = unit(u)
            at = (slice(b * L, (b + 1) * L), slice(j * 128, (j + 1) * 128))
            owner_came(DR, u, csem_s.at[k], csem_r.at[k])
            dm = expand_low(DR[u, 0:64])
            off = to_col(packed_row(DR.at[u], 0))
            qb = expand(QM[l, u]).astype(BF16)
            kw = jnp.exp(nt(qb, tile(KS, l, u)) - to_col(packed_row(CR.at[l, u], 0)))
            v = VX[l, b, margin : margin + L, j * 128 : (j + 1) * 128]
            DV[at] = DV[at] + tn(kw.astype(BF16), dm)
            d_ks = (kw * (nt(dm, v) - off)).astype(BF16)
            DK[at] = tn(d_ks, qb)
            DQM[u] = DQM[u] + compress(nn(d_ks, tile(KS, l, u)))

        @pl.when(is_owner)
        def _():
            from_owner(DR, csem_s.at[k], csem_r.at[k], False)

        for u in range(U):
            b, j = unit(u)
            lanes = slice(j * 128, (j + 1) * 128)
            dq, dk = DQM[u].astype(BF16), DKM[u].astype(BF16)
            for i in range(n):
                SB[i, b * S : (b + 1) * S, lanes] = dq[i * S : (i + 1) * S]
                SB[i, 8 + b * S : 8 + (b + 1) * S, lanes] = dk[i * S : (i + 1) * S]
        for done in left[2:]:
            done()
        DP[0:R, 2 * C : 3 * C] = DV[...].astype(BF16)
        value_copies = right_copies(l, 7, DP, val_ranges)
        wait_all(left_hand_on(l, 6, LTA))
        wait_all(right_copies(l, 1, CTX.at[l], out_ranges))
        out0 = items["outval"][0]
        weight_grad(0, LTA, lambda o: CTX[l, :, pl.ds(o, 128)], out0, 128, 128)
        weight_grad(1, LTA, lambda o: CTX[l, :, pl.ds(128 + o, 256)], out0, C - 128, 256)
        spread(lambda t: SB.at[t], SR, qsem_s.at[l], qsem_r.at[l], True)
        SR[me] = SB[me]
        start_all(value_copies)
        advance(l, "inner", 0)
        wait_all(value_copies)
        wait_all(left_hand_on(l, 0, LTH.at[l]))
        weight_grad(0, LTH.at[l], lambda o: DP[:, pl.ds(2 * C + o, 256)], out0 + 128, C - 128, 256)
        weight_grad(1, LTH.at[l], lambda o: DP[:, pl.ds(3 * C - 128 + o, 128)], out0 + C - 128, 128, 128)
        rs_start(l, "outval", 0)
        spread(lambda t: SB.at[t], SR, qsem_s.at[l], qsem_r.at[l], False)
        marks = SR[0].astype(F32)
        for i in range(1, n):
            marks = marks + SR[i].astype(F32)
        marks = marks * (1.0 / z.segment)
        for b in range(B):
            for r in range(S):
                at = slice(b * L + r * z.segment, b * L + (r + 1) * z.segment)
                i = b * S + r
                DP[at, 0:C] = ((DQ[at] + marks[i : i + 1]) * scale).astype(BF16)
                DP[at, C : 2 * C] = ((DK[at] + marks[8 + i : 9 + i]) * scale).astype(BF16)
        key_copies = right_copies(l, 8, DP, key_ranges)
        start_all(key_copies)

        def onto(i, _):
            o = pl.ds(pl.multiple_of(i * 256, 256), 256)
            x = nt(DP[0:R, 0:C], WP[l, 0, o, :]) + nt(DP[0:R, C : 2 * C], WP[l, 1, o, :])
            HS[(e + 1) % 2, :, o] = (x + nt(DP[0:R, 2 * C : 3 * C], WP[l, 2, o, :])).astype(BF16)
            return 0

        lax.fori_loop(0, D // 256, onto, 0)
        c = swap(e + 1)
        c.start()
        bias = jnp.sum(DP[0:R].astype(F32), axis=0, keepdims=True)
        put_small(base + 48, bias[:, 0:C])
        put_small(base + 51, bias[:, 2 * C : 3 * C])
        advance(l, "outer", 1)
        wait_all(key_copies)
        for g in range(2):
            weight_grad(g, LTH.at[l], lambda o: DP[:, pl.ds(g * C + o, 128)], items["keyed"][0], C, 128)
        rs_start(l, "keyed", 0)
        c.wait()
        UP[...] = DT[...] + both(e + 1)

    for l in range(z.layers):
        forward(l)
    results = [out_copy(b, HID.at[pl.ds(b * L, L)], result.at[b]) for b in range(B)]
    start_all(results)
    for b in range(B):
        shown = to_col(mask[b : b + 1, :].astype(F32))
        UP[b * L : (b + 1) * L, :] = cot[b].astype(F32) * shown
    wait_all(results)
    left = []
    for l in range(z.layers - 1, -1, -1):
        backward(l, left)

        def rest(l=l):
            advance(l, "inner", 1)
            advance(l, "outval", 0)
            advance(l, "outer", 2)

        def more(l=l):
            advance(l, "inner", 2)
            advance(l, "keyed", 0)
            advance(l, "outval", 1)

        def last(l=l):
            advance(l, "keyed", 1)
            advance(l, "outval", 2)
            advance(l, "keyed", 2)

        left = [rest, more, last]
    tokens_out = [out_copy(B + b, UP.at[pl.ds(b * L, L)], gtok.at[b]) for b in range(B)]
    start_all(tokens_out)
    spread(lambda t: SM.at[pl.ds(pl.multiple_of(t * 8, 8), 8)], SMR, ssem_s, ssem_r, True)
    SMR[me] = SM[pl.ds(pl.multiple_of(me * 8, 8), 8), :]
    left[0]()
    spread(lambda t: SM.at[pl.ds(pl.multiple_of(t * 8, 8), 8)], SMR, ssem_s, ssem_r, False)
    total = SMR[0]
    for i in range(1, n):
        total = total + SMR[i]
    SMT[me] = total
    spread(lambda t: SMT.at[me], SMT, tsem_s, tsem_r, True)
    left[1]()
    ffn_out = [out_copy(2 * B, OU, gouter), out_copy(2 * B + 1, OI, ginner)]
    start_all(ffn_out)
    spread(lambda t: SMT.at[me], SMT, tsem_s, tsem_r, False)

    def little(at):
        return SMT[at // 8, at % 8 : at % 8 + 1, :]

    for l in range(z.layers):
        base = 60 * l
        for i in range(D // 128):
            lanes = slice(i * 128, (i + 1) * 128)
            for side in range(2):
                for what in range(3):
                    OS[what, l, side : side + 1, lanes] = little(base + 12 * what + 6 * side + i)
        for i in range(F // 128):
            OT[l : l + 1, i * 128 : (i + 1) * 128] = little(base + 36 + i)
        for i in range(C // 128):
            gbias[l, 0:1, i * 128 : (i + 1) * 128] = little(base + 48 + i)
            gbias[l, 1:2, i * 128 : (i + 1) * 128] = little(base + 51 + i)
        for h in range(z.local_heads):
            gtaps[l, h : h + 1, :] = little(base + 54 + h)[:, 0:K]
    small_out = [
        out_copy(2 * B + 2 + i, src, dst)
        for i, (src, dst) in enumerate(
            [(OS.at[0], ggain), (OS.at[1], gshift), (OS.at[2], gobias), (OT, gibias)]
        )
    ]
    start_all(small_out)
    left[2]()
    rest_out = [out_copy(2 * B + 6, OP, gproj), out_copy(2 * B + 7, OO, gout)]
    start_all(rest_out)
    wait_all(tokens_out + ffn_out + small_out + rest_out)


def hand_over(count, *refs):
    sems = refs[-1]
    copies = [
        pltpu.make_async_copy(refs[i], refs[count + i], sems.at[i]) for i in range(count)
    ]
    for c in copies:
        c.start()
    for c in copies:
        c.wait()


def fused(z, tokens, cotangent, masked, projections, projection_bias, conv_taps, output_weight,
          output_bias, norm_gain, norm_shift, inner_weight, inner_bias, outer_weight):
    n, B, L, R, D, C, F = z.n, z.batch, z.length, z.rows, z.width, z.cols, z.hidden
    U, H, NL_, NB, CH = z.units, z.local_heads, z.layers, z.bits, z.width // z.n
    V = pltpu.VMEM
    DMA = pltpu.SemaphoreType.DMA
    cols = F + 2 * C
    staged = lambda: V((2,) * NB + (CH, R), BF16)
    gathered = lambda *lead: V(lead + (2,) * NB + (CH, 2 * R), BF16)
    scratch = dict(
        WP=V((NL_, 3, D, C), BF16), WO=V((NL_, C, D), BF16), WI=V((NL_, D, F), BF16), WF=V((NL_, F, D), BF16),
        QS=V((NL_, R, C), BF16), KS=V((NL_, R, C), BF16),
        VX=V((NL_, B, 256, C), BF16), RW=V((NL_, U, 128, 128), F32),
        CTX=V((NL_, 2 * R, C), BF16), T1=V((NL_, R, D), F32), T2=V((NL_, R, D), F32),
        GP=V((NL_, 2 * R, F), BF16), ACT=V((NL_, 2 * R, F), BF16),
        QM=V((NL_, U, 64, 128), F32), KM=V((NL_, U, 64, 128), F32), CR=V((NL_, U, 80, 128), BF16),
        MX=V((NL_, 64, 128), F32), PA=V((NL_, 128, 128), F32), PV=V((NL_, PINV_ITERS, 4, 128, 128), F32),
        PZ=V((NL_, 128, 128), F32), PC=V((64, 128), F32), LTH=gathered(NL_), LTN=gathered(NL_),
        HID=V((R, D), F32), UP=V((R, D), F32), LOW=V((R, D), BF16), PN=V((2, R, D), BF16), PF=V((2, R, D), BF16),
        DPRE=V((2 * R, F), BF16), GX=V((B, 256, C), BF16), DQ=V((R, C), F32), DK=V((R, C), F32), DV=V((R, C), F32),
        DP=V((2 * R, 3 * C), BF16), DQM=V((U, 64, 128), F32), DKM=V((U, 64, 128), F32), DR=V((U, 80, 128), BF16),
        SM=V((n * 8, 128), F32), TB=V((2, 8, 256), F32),
        TT=V((NL_, H, 128, 256), BF16), TR=V((NL_, H, 128, 256), BF16), LTF=gathered(), LTA=gathered(),
        LSH=staged(), OP=V((NL_, 3, CH, C), F32), OO=V((NL_, CH, C), F32), OI=V((NL_, CH, F), F32),
        OU=V((NL_, CH, F), F32), OS=V((3, NL_, 2, D), F32), OT=V((NL_, F), F32),
        MS=V((16, C), BF16), MB=V((n, 16, C), BF16), MD=V((U, 16, 128), BF16), MO=V((n, 16, 128), BF16), XM=V((U, 80, 128), BF16), OB=V((n, 80, 128), BF16),
        SB=V((n, 16, C), BF16), SR=V((n, 16, C), BF16), HS=V((2, R, D), BF16), HR=V((2, R, D), BF16),
        SMR=V((n, 8, 128), F32), SMT=V((n, 8, 128), F32),
        G=V((2,) * NB + (CH, cols), BF16),
        RV=[V((NL_, 2) + (2,) * (NB - 2 - s) + (CH, cols), BF16) for s in range(NB - 1)],
        wsem=DMA((NL_, 4)),
        hsem_s=DMA((4 * NL_,)), hsem_r=DMA((4 * NL_,)),
        msem_s=DMA((NL_, n)), msem_r=DMA((NL_, n)), dsem_s=DMA((NL_, U)), dsem_r=DMA((NL_, n)), xsem_s=DMA((2 * NL_, U)), xsem_r=DMA((2 * NL_, n)),
        csem_s=DMA((2 * NL_, n)), csem_r=DMA((2 * NL_, U)), vsem_s=DMA((2 * NL_, 2)), vsem_r=DMA((2 * NL_, 2)),
        osem=DMA((2 * B + 8,)),
        asem_s=DMA((NL_, 9, 2)), asem_r=DMA((NL_, 9, 2)), bsem_s=DMA((NL_, 9, 2)), bsem_r=DMA((NL_, 9, 2)),
        gsem_s=DMA((NL_, 4, 2, NB - 1)), gsem_r=DMA((NL_, 4, 2, NB - 1)), qsem_s=DMA((NL_, n)), qsem_r=DMA((NL_, n)),
        ssem_s=DMA((n,)), ssem_r=DMA((n,)), tsem_s=DMA((n,)), tsem_r=DMA((n,)),
    )
    in_vmem = pl.BlockSpec(memory_space=pltpu.VMEM)
    in_hbm = pl.BlockSpec(memory_space=pl.ANY)
    out = lambda *s: jax.ShapeDtypeStruct(s, F32)
    shapes = (
        out(B, L, D), out(B, L, D), out(NL_, 3, CH, C), out(NL_, 2, C), out(NL_, H, z.kernel), out(NL_, CH, C),
        out(NL_, 2, D), out(NL_, 2, D), out(NL_, 2, D), out(NL_, CH, F), out(NL_, F), out(NL_, CH, F),
    )
    outs = pl.pallas_call(
        partial(fused_kernel, z),
        out_shape=shapes,
        in_specs=[in_vmem] * 9 + [in_hbm] * 4,
        out_specs=tuple(in_vmem if i in (3, 4) else in_hbm for i in range(len(shapes))),
        scratch_shapes=scratch,
        compiler_params=pltpu.CompilerParams(
            collective_id=1, has_side_effects=True, vmem_limit_bytes=VMEM_LIMIT
        ),
    )(tokens, cotangent, masked, projection_bias, conv_taps, output_bias, norm_gain, norm_shift, inner_bias,
      projections, output_weight, inner_weight, outer_weight)
    outs = list(
        pl.pallas_call(
            partial(hand_over, len(shapes)),
            out_shape=shapes,
            in_specs=[in_vmem] * len(shapes),
            out_specs=(in_hbm,) * len(shapes),
            scratch_shapes=[DMA((len(shapes),))],
        )(*outs)
    )
    for i in (5, 11):
        outs[i] = jnp.swapaxes(outs[i], 1, 2)
    return tuple(outs)


def solution(mesh):
    in_specs = (
        P(None, "seq", None),
        P(None, "seq", None),
        P(None, "seq"),
        P(None, None, None, "head"),
        P(None, None, "head"),
        P(None, "head", None),
        P(None, "head", None),
        P(),
        P(),
        P(),
        P(None, None, "head"),
        P(None, "head"),
        P(None, "head", None),
    )
    out_specs = (
        P(None, "seq", None),
        P(None, "seq", None),
        P(None, None, "seq", "head"),
        P(None, None, "head"),
        P(None, "head", None),
        P(None, "head", "seq"),
        P(),
        P(),
        P(),
        P(None, "seq", "head"),
        P(None, "head"),
        P(None, "head", "seq"),
    )

    def whole(*args):
        z = Fast(mesh.shape, args[0], args[5], args[10])
        body = partial(fused, z) if z.fits() else on_device
        return jax.shard_map(
            body, mesh=mesh, in_specs=in_specs, out_specs=out_specs, check_vma=False
        )(*args)

    return whole
```

```python
from functools import partial

import jax
import jax.numpy as jnp
from jax import lax
from jax.experimental import pallas as pl
from jax.experimental.pallas import tpu as pltpu
from jax.sharding import PartitionSpec as P

LANDMARKS = 64
PINV_ITERS = 6
LAYERS = 2


exact_result = lax.Precision.HIGHEST
epsilon = 1e-05


VMEM_LIMIT = 64 * 1024 * 1024 - 128 * 1024


def extended(block, sides, width):
    for axis, dim in sides:
        count = lax.axis_size(axis)
        forward = [(i, i + 1) for i in range(count - 1)]
        backward = [(target, source) for source, target in forward]
        low = lax.ppermute(
            lax.slice_in_dim(block, block.shape[dim] - width, None, axis=dim), axis, forward
        )
        high = lax.ppermute(lax.slice_in_dim(block, 0, width, axis=dim), axis, backward)
        block = jnp.concatenate([low, block, high], axis=dim)
    return block


def layer_norm(values, scaling, offset):
    centre = jnp.mean(values, -1, keepdims=True)
    centred = values - centre
    spread = jnp.mean(centred * centred, -1, keepdims=True)
    return centred * lax.rsqrt(spread + epsilon) * scaling + offset


def soft_rows(scores):
    highest = jnp.max(scores, -1, keepdims=True)
    powers = jnp.exp(scores - highest)
    return powers / jnp.sum(powers, -1, keepdims=True)


def pseudo_inverse(weight_matrix):
    size_of = weight_matrix.shape[-1]
    column_top = jnp.max(jnp.sum(weight_matrix, axis=-2), axis=-1)[..., None, None]
    approximate_result = jnp.swapaxes(weight_matrix, -1, -2) / column_top
    identity = jnp.eye(size_of, dtype=jnp.float32)
    for repeat in range(PINV_ITERS):
        product = jnp.matmul(weight_matrix, approximate_result, precision=exact_result)
        nested = 7.0 * identity - product
        nested = 15.0 * identity - jnp.matmul(product, nested, precision=exact_result)
        nested = 13.0 * identity - jnp.matmul(product, nested, precision=exact_result)
        approximate_result = 0.25 * jnp.matmul(approximate_result, nested, precision=exact_result)
    return approximate_result


def rounded(values):
    return lax.optimization_barrier(values.astype(jnp.bfloat16)).astype(jnp.float32)


def heads_view(joined, heads_local):
    batch_count, length, channels = joined.shape
    return joined.reshape(batch_count, length, heads_local, channels // heads_local).transpose(
        0, 2, 1, 3
    )


def tokens_view(by_head):
    batch_count, heads_local, length, head_depth = by_head.shape
    return by_head.transpose(0, 2, 1, 3).reshape(batch_count, length, heads_local * head_depth)


def convolve(padded, broad_kernel_taps, length):

    def add_tap(offset, running):
        window = lax.dynamic_slice_in_dim(padded, offset, length, 1).astype(jnp.float32)
        return running + window * lax.dynamic_index_in_dim(broad_kernel_taps, offset, 0, False)

    initial = jnp.zeros((padded.shape[0], length, padded.shape[2]), jnp.float32)
    return lax.fori_loop(0, broad_kernel_taps.shape[0], add_tap, initial)


def tap_sums(padded, upstream, length, kernel):

    def one_tap(offset):
        window = lax.dynamic_slice_in_dim(padded, offset, length, 1).astype(jnp.float32)
        return jnp.sum(window * upstream, axis=(0, 1))

    return lax.map(one_tap, jnp.arange(kernel, dtype=jnp.int32))


def across_heads(summand):
    return lax.psum_scatter(
        summand.astype(jnp.bfloat16), "head", scatter_dimension=0, tiled=True
    ).astype(jnp.float32)


def rows_low(share):
    return lax.all_gather(share, "head", axis=0, tiled=True)


def rows_float(share):
    return lax.all_gather(share.astype(jnp.bfloat16), "head", axis=0, tiled=True).astype(
        share.dtype
    )


def own_rows(whole_rows):
    share = whole_rows.shape[0] // lax.axis_size("head")
    return lax.dynamic_slice_in_dim(whole_rows, lax.axis_index("head") * share, share, 0)


def spread_heads(share, dim_index):
    groups = lax.axis_size("head")
    full_shape = list(share.shape)
    full_shape[dim_index] = full_shape[dim_index] * groups
    empty = jnp.zeros(full_shape, jnp.float32)
    return lax.dynamic_update_slice_in_dim(
        empty, share, lax.axis_index("head") * share.shape[dim_index], dim_index
    )


def own_heads(whole, width, dim_index):
    return lax.dynamic_slice_in_dim(whole, lax.axis_index("head") * width, width, dim_index)


def forward_layer(hidden, weights, selector, segment):
    (
        projection,
        projection_shift,
        conv_kernel,
        output_matrix,
        output_shift,
        gain_pair,
        shift_pair,
        inner_matrix,
        inner_shift,
        outer_matrix,
    ) = weights
    batch_count, length, model_width = hidden.shape
    heads_local = conv_kernel.shape[0]
    kernel = conv_kernel.shape[1]
    margin = kernel // 2
    local_width = projection.shape[2]
    head_depth = local_width // heads_local
    scale = float(head_depth) ** (-0.25)
    hidden_low = hidden.astype(jnp.bfloat16).reshape(batch_count * length, model_width)
    projected = jnp.einsum(
        "nd,kde->kne", hidden_low, projection, preferred_element_type=jnp.float32
    )
    biases = projection_shift.astype(jnp.float32)
    query_rows = ((projected[0] + biases[0]) * scale).reshape(batch_count, length, local_width)
    key_rows = (projected[1] * scale).reshape(batch_count, length, local_width)
    value_low = (
        (projected[2] + biases[1]).astype(jnp.bfloat16).reshape(batch_count, length, local_width)
    )
    query_sums, key_sums = lax.psum(
        (
            jnp.einsum("mt,btc->bmc", selector, query_rows, precision=exact_result),
            jnp.einsum("mt,btc->bmc", selector, key_rows, precision=exact_result),
        ),
        "seq",
    )
    query_marks = heads_view(query_sums / segment, heads_local)
    key_marks = heads_view(key_sums / segment, heads_local)
    query_heads = heads_view(query_rows, heads_local)
    key_heads = heads_view(key_rows, heads_local)
    value_heads = heads_view(value_low.astype(jnp.float32), heads_local)
    mark_weights = soft_rows(
        jnp.einsum("bhme,bhne->bhmn", query_marks, key_marks, precision=exact_result)
    )
    inverse = pseudo_inverse(mark_weights)
    row_weights = soft_rows(
        jnp.einsum("bhte,bhme->bhtm", query_heads, key_marks, precision=exact_result)
    )
    key_scores = jnp.einsum("bhme,bhte->bhmt", query_marks, key_heads, precision=exact_result)
    local_top = jnp.max(key_scores, -1)
    score_top = lax.pmax(local_top, "seq")
    powers = jnp.exp(key_scores - score_top[..., None])
    neighbour_mixture = jnp.einsum("bhmt,bhte->bhme", powers, value_heads, precision=exact_result)
    score_total, mixed_joined = lax.psum(
        (jnp.sum(powers, -1), neighbour_mixture.reshape(batch_count, heads_local, -1)), "seq"
    )
    mixed_sum = mixed_joined.reshape(neighbour_mixture.shape)
    log_total = score_top + jnp.log(score_total)
    mixed = mixed_sum / score_total[..., None]
    core = jnp.einsum("bhmn,bhne->bhme", inverse, mixed, precision=exact_result)
    attended = jnp.einsum("bhtm,bhme->bhte", row_weights, core, precision=exact_result)
    padded_values = extended(value_low, (("seq", 1),), margin)
    broad_kernel_taps = jnp.repeat(conv_kernel.astype(jnp.float32), head_depth, axis=0).T
    context = tokens_view(attended) + convolve(padded_values, broad_kernel_taps, length)
    context_low = context.astype(jnp.bfloat16).reshape(batch_count * length, local_width)
    attention_share = across_heads(
        jnp.dot(context_low, output_matrix, preferred_element_type=jnp.float32)
    )
    shifts = output_shift.astype(jnp.float32)
    gains = gain_pair.astype(jnp.float32)
    offsets = shift_pair.astype(jnp.float32)
    hidden_share = own_rows(hidden.reshape(batch_count * length, model_width))
    total_first = hidden_share + attention_share + shifts[0]
    normed = layer_norm(total_first, gains[0], offsets[0])
    normed_low = rows_low(normed.astype(jnp.bfloat16))
    pre_active = jnp.dot(
        normed_low, inner_matrix, preferred_element_type=jnp.float32
    ) + inner_shift.astype(jnp.float32)
    active_low = jax.nn.gelu(pre_active, approximate=False).astype(jnp.bfloat16)
    feed_share = across_heads(jnp.dot(active_low, outer_matrix, preferred_element_type=jnp.float32))
    total_second = normed + feed_share + shifts[1]
    output = rows_float(layer_norm(total_second, gains[1], offsets[1])).reshape(hidden.shape)
    retained = (
        hidden_low,
        query_heads,
        key_heads,
        value_heads,
        padded_values,
        query_marks,
        key_marks,
        mark_weights,
        inverse,
        row_weights,
        log_total,
        mixed,
        core,
        context_low,
        total_first,
        normed_low,
        pre_active,
        active_low,
        total_second,
        broad_kernel_taps,
    )
    return (output, retained)


def backward_layer(upstream, retained, weights, selector, segment):
    (
        projection,
        projection_shift,
        conv_kernel,
        output_matrix,
        output_shift,
        gain_pair,
        shift_pair,
        inner_matrix,
        inner_shift,
        outer_matrix,
    ) = weights
    (
        hidden_low,
        query_heads,
        key_heads,
        value_heads,
        padded_values,
        query_marks,
        key_marks,
        mark_weights,
        inverse,
        row_weights,
        log_total,
        mixed,
        core,
        context_low,
        total_first,
        normed_low,
        pre_active,
        active_low,
        total_second,
        broad_kernel_taps,
    ) = retained
    batch_count, length, model_width = upstream.shape
    heads_local = conv_kernel.shape[0]
    kernel = conv_kernel.shape[1]
    margin = kernel // 2
    local_width = projection.shape[2]
    head_depth = local_width // heads_local
    scale = float(head_depth) ** (-0.25)
    gains = gain_pair.astype(jnp.float32)
    offsets = shift_pair.astype(jnp.float32)
    upstream_share = own_rows(upstream.reshape(batch_count * length, model_width))
    second_pull = jax.vjp(layer_norm, total_second, gains[1], offsets[1])[1]
    grad_second, gain_second, offset_second = second_pull(upstream_share)
    feed_low = rows_low(grad_second.astype(jnp.bfloat16))
    grad_outer = jnp.einsum("nf,nd->fd", active_low, feed_low, preferred_element_type=jnp.float32)
    grad_active = rounded(
        jnp.einsum("nd,fd->nf", feed_low, outer_matrix, preferred_element_type=jnp.float32)
    )
    gelu_pull = jax.vjp(partial(jax.nn.gelu, approximate=False), pre_active)[1]
    grad_pre_low = gelu_pull(grad_active)[0].astype(jnp.bfloat16)
    grad_inner_shift = jnp.sum(grad_pre_low.astype(jnp.float32), axis=0)
    grad_inner = jnp.einsum(
        "nd,nf->df", normed_low, grad_pre_low, preferred_element_type=jnp.float32
    )
    normed_term = jnp.einsum(
        "nf,df->nd", grad_pre_low, inner_matrix, preferred_element_type=jnp.float32
    )
    grad_normed = grad_second + across_heads(normed_term)
    first_pull = jax.vjp(layer_norm, total_first, gains[0], offsets[0])[1]
    grad_first, gain_first, offset_first = first_pull(grad_normed)
    attend_low = rows_low(grad_first.astype(jnp.bfloat16))
    grad_output = jnp.einsum(
        "nc,nd->cd", context_low, attend_low, preferred_element_type=jnp.float32
    )
    grad_context_low = (
        jnp.einsum("nd,cd->nc", attend_low, output_matrix, preferred_element_type=jnp.float32)
        .astype(jnp.bfloat16)
        .reshape(batch_count, length, local_width)
    )
    grad_context = lax.optimization_barrier(grad_context_low).astype(jnp.float32)
    padded_grads = extended(grad_context_low, (("seq", 1),), margin)
    grad_conv_values = convolve(padded_grads, broad_kernel_taps[::-1], length)
    kernel_sums = tap_sums(padded_values, grad_context, length, kernel)
    grad_kernel = kernel_sums.reshape(kernel, heads_local, head_depth).sum(-1).T
    grad_attended = heads_view(grad_context, heads_local)
    grad_row = jnp.einsum("bhte,bhme->bhtm", grad_attended, core, precision=exact_result)
    grad_core_local = jnp.einsum(
        "bhtm,bhte->bhme", row_weights, grad_attended, precision=exact_result
    )
    grad_row_scores = row_weights * (grad_row - jnp.sum(row_weights * grad_row, -1, keepdims=True))
    grad_query = jnp.einsum("bhtm,bhme->bhte", grad_row_scores, key_marks, precision=exact_result)
    grad_keymark_local = jnp.einsum(
        "bhtm,bhte->bhme", grad_row_scores, query_heads, precision=exact_result
    )
    grad_core_joined, grad_keymark_joined = lax.psum(
        (
            grad_core_local.reshape(batch_count, heads_local, -1),
            grad_keymark_local.reshape(batch_count, heads_local, -1),
        ),
        "seq",
    )
    grad_core = grad_core_joined.reshape(core.shape)
    grad_inverse = jnp.einsum("bhme,bhne->bhmn", grad_core, mixed, precision=exact_result)
    grad_mixed = jnp.einsum("bhnm,bhne->bhme", inverse, grad_core, precision=exact_result)
    grad_marks = jax.vjp(pseudo_inverse, mark_weights)[1](grad_inverse)[0]
    grad_mark_scores = mark_weights * (
        grad_marks - jnp.sum(mark_weights * grad_marks, -1, keepdims=True)
    )
    grad_querymark = jnp.einsum(
        "bhmn,bhne->bhme", grad_mark_scores, key_marks, precision=exact_result
    )
    grad_keymark = grad_keymark_joined.reshape(key_marks.shape) + jnp.einsum(
        "bhmn,bhme->bhne", grad_mark_scores, query_marks, precision=exact_result
    )
    key_scores = jnp.einsum("bhme,bhte->bhmt", query_marks, key_heads, precision=exact_result)
    key_weights = jnp.exp(key_scores - log_total[..., None])
    grad_values = jnp.einsum("bhmt,bhme->bhte", key_weights, grad_mixed, precision=exact_result)
    offset_term = jnp.sum(grad_mixed * mixed, -1)
    grad_key_scores = key_weights * (
        jnp.einsum("bhme,bhte->bhmt", grad_mixed, value_heads, precision=exact_result)
        - offset_term[..., None]
    )
    grad_key = jnp.einsum("bhmt,bhme->bhte", grad_key_scores, query_marks, precision=exact_result)
    grad_querymark_local = jnp.einsum(
        "bhmt,bhte->bhme", grad_key_scores, key_heads, precision=exact_result
    )
    grad_querymark = grad_querymark + lax.psum(
        grad_querymark_local.reshape(batch_count, heads_local, -1), "seq"
    ).reshape(query_marks.shape)
    grad_query = (
        grad_query
        + jnp.einsum("mt,bhme->bhte", selector, grad_querymark, precision=exact_result) / segment
    )
    grad_key = (
        grad_key
        + jnp.einsum("mt,bhme->bhte", selector, grad_keymark, precision=exact_result) / segment
    )
    grad_values = grad_values + heads_view(grad_conv_values, heads_local)
    query_low = (
        (tokens_view(grad_query) * scale)
        .astype(jnp.bfloat16)
        .reshape(batch_count * length, local_width)
    )
    key_low = (
        (tokens_view(grad_key) * scale)
        .astype(jnp.bfloat16)
        .reshape(batch_count * length, local_width)
    )
    value_grad_low = (
        tokens_view(grad_values).astype(jnp.bfloat16).reshape(batch_count * length, local_width)
    )
    stacked = jnp.stack([query_low, key_low, value_grad_low])
    grad_projection = jnp.einsum(
        "nd,kne->kde", hidden_low, stacked, preferred_element_type=jnp.float32
    )
    grad_projection_shift = jnp.stack(
        [
            jnp.sum(query_low.astype(jnp.float32), axis=0),
            jnp.sum(value_grad_low.astype(jnp.float32), axis=0),
        ]
    )
    input_term = jnp.einsum("kne,kde->nd", stacked, projection, preferred_element_type=jnp.float32)
    grad_hidden = rows_float(grad_first + across_heads(input_term)).reshape(upstream.shape)
    gradients = (
        grad_projection,
        grad_projection_shift,
        grad_kernel,
        grad_output,
        jnp.stack([jnp.sum(grad_first, axis=0), jnp.sum(grad_second, axis=0)]),
        jnp.stack([gain_first, gain_second]),
        jnp.stack([offset_first, offset_second]),
        grad_inner,
        grad_inner_shift,
        grad_outer,
    )
    return (grad_hidden, gradients)


def on_device(
    tokens,
    cotangent,
    masked,
    projections,
    projection_bias,
    conv_taps,
    output_weight,
    output_bias,
    norm_gain,
    norm_shift,
    inner_weight,
    inner_bias,
    outer_weight,
):
    length = tokens.shape[1]
    segment = length * lax.axis_size("seq") // LANDMARKS
    position = lax.axis_index("seq") * length + jnp.arange(length, dtype=jnp.int32)
    selector = (
        position[None, :] // segment == jnp.arange(LANDMARKS, dtype=jnp.int32)[:, None]
    ).astype(jnp.float32)
    arrays = (
        projections,
        projection_bias,
        conv_taps,
        output_weight,
        output_bias,
        norm_gain,
        norm_shift,
        inner_weight,
        inner_bias,
        outer_weight,
    )
    hidden = tokens.astype(jnp.float32)
    stored = []
    for layer_number in range(LAYERS):
        weights = tuple((tensor[layer_number] for tensor in arrays))
        hidden, retained = forward_layer(hidden, weights, selector, segment)
        stored.append((weights, retained))
    upstream = cotangent.astype(jnp.float32) * masked.astype(jnp.float32)[:, :, None]
    layer_grads = [None] * LAYERS
    for layer_number in range(LAYERS - 1, -1, -1):
        weights, retained = stored[layer_number]
        upstream, gradients = backward_layer(upstream, retained, weights, selector, segment)
        larger = (
            lax.psum_scatter(gradients[0], "seq", scatter_dimension=1, tiled=True),
            lax.psum_scatter(gradients[3], "seq", scatter_dimension=1, tiled=True),
            lax.psum_scatter(gradients[7], "seq", scatter_dimension=0, tiled=True),
            lax.psum_scatter(gradients[9], "seq", scatter_dimension=1, tiled=True),
        )
        gradients = (
            larger[0],
            gradients[1],
            gradients[2],
            larger[1],
            gradients[4],
            gradients[5],
            gradients[6],
            larger[2],
            gradients[8],
            larger[3],
        )
        layer_grads[layer_number] = gradients
    stacked = tuple(
        (
            jnp.stack([layer_grads[layer_number][member] for layer_number in range(LAYERS)])
            for member in range(10)
        )
    )
    larger = (stacked[0], stacked[3], stacked[7], stacked[9])
    bias_width = stacked[1].shape[2]
    taps_width = stacked[2].shape[1]
    inner_width = stacked[8].shape[1]
    smaller = lax.psum(
        (
            spread_heads(stacked[1], 2),
            spread_heads(stacked[2], 1),
            stacked[4],
            stacked[5],
            stacked[6],
            spread_heads(stacked[8], 1),
        ),
        ("seq", "head"),
    )
    grad_bias_share = own_heads(smaller[0], bias_width, 2)
    grad_taps_share = own_heads(smaller[1], taps_width, 1)
    grad_inner_share = own_heads(smaller[5], inner_width, 1)
    return (
        hidden,
        upstream,
        larger[0],
        grad_bias_share,
        grad_taps_share,
        larger[1],
        smaller[2],
        smaller[3],
        smaller[4],
        larger[2],
        grad_inner_share,
        larger[3],
    )


F32 = jnp.float32
BF16 = jnp.bfloat16
MESH = pl.DeviceIdType.MESH


def nn(a, b):
    return lax.dot_general(a, b, (((1,), (0,)), ((), ())), preferred_element_type=F32)


def nt(a, b):
    return lax.dot_general(a, b, (((1,), (1,)), ((), ())), preferred_element_type=F32)


def tn(a, b):
    return lax.dot_general(a, b, (((0,), (0,)), ((), ())), preferred_element_type=F32)


def halves(x):
    high = x.astype(BF16)
    return high, (x - high.astype(F32)).astype(BF16)


def left3(pair, axis):
    return jnp.concatenate([pair[0], pair[1], pair[0]], axis=axis)


def right3(pair, axis):
    return jnp.concatenate([pair[0], pair[0], pair[1]], axis=axis)


def nn3(a, b):
    return nn(left3(a, 1), right3(b, 0))


def nt3(a, b):
    return nt(left3(a, 1), right3(b, 1))


def tn3(a, b):
    return tn(left3(a, 0), right3(b, 0))


def nn3f(a, b):
    return nn3(halves(a), halves(b))


def nt3f(a, b):
    return nt3(halves(a), halves(b))


def tn3f(a, b):
    return tn3(halves(a), halves(b))


class Fast:
    def __init__(self, mesh_shape, tokens, conv_taps, inner_weight):
        self.n = mesh_shape["seq"]
        self.heads = mesh_shape["head"]
        self.batch, whole, self.width = tokens.shape
        self.length = whole // self.n
        self.layers, all_heads, self.kernel = conv_taps.shape
        self.local_heads = all_heads // self.heads
        self.depth = self.width // all_heads
        self.cols = self.local_heads * self.depth
        self.hidden = inner_weight.shape[2] // self.heads
        self.rows = self.batch * self.length
        self.segment = whole // LANDMARKS
        self.spans = self.length // self.segment
        self.units = self.batch * self.local_heads // 2
        self.bits = self.n.bit_length() - 1

    def fits(self):
        return (
            self.n == 1 << self.bits
            and self.n >= 16
            and self.heads == 2
            and self.length == 128
            and self.batch == 2
            and self.spans * self.batch == 8
            and self.depth == 64
            and self.local_heads % 2 == 0
            and self.width % (16 * self.n) == 0
            and self.width % 256 == 0
            and self.hidden % 512 == 0
            and self.kernel == 65
            and self.layers == 2
            and LANDMARKS == 64
        )


def fused_kernel(
    z,
    tok, cot, mask, pbias, taps, obias, ngain, nshift, ibias, wp_hbm, wo_hbm, wi_hbm, wf_hbm,
    result, gtok, gproj, gbias, gtaps, gout, gobias, ggain, gshift, ginner, gibias, gouter,
    *,
    WP, WO, WI, WF,
    QS, KS, VX, RW, CTX, T1, T2, GP, ACT, QM, KM, CR, MX, PA, PV, PZ, PC, LTH, LTN,
    HID, UP, LOW, PN, PF, DPRE, GX, DQ, DK, DV, DP, DQM, DKM, DR, SM, TB, TT, TR, LTF, LTA,
    LSH, OP, OO, OI, OU, OS, OT,
    MS, MB, MD, MO, XM, OB, SB, SR, HS, HR, SMR, SMT,
    G, RV,
    wsem, hsem_s, hsem_r, msem_s, msem_r, dsem_s, dsem_r, xsem_s, xsem_r, csem_s, csem_r, vsem_s, vsem_r,
    osem, asem_s, asem_r, bsem_s, bsem_r, gsem_s, gsem_r, qsem_s, qsem_r, ssem_s, ssem_r, tsem_s, tsem_r,
):
    n, B, L, R, D, C, F = z.n, z.batch, z.length, z.rows, z.width, z.cols, z.hidden
    U, NP, S, K = z.units, z.local_heads // 2, z.spans, z.kernel
    CH = D // n
    NB = z.bits
    M = LANDMARKS
    margin = K // 2
    scale = float(z.depth) ** (-0.25)
    me = lax.axis_index("seq")
    core = lax.axis_index("head")
    first_owner = n // 2 - U // 2
    is_owner = jnp.logical_and(me >= first_owner, me < first_owner + U)
    mine = jnp.clip(me - first_owner, 0, U - 1)

    def weight_copies(l):
        return [
            pltpu.make_async_copy(wp_hbm.at[l], WP.at[l], wsem.at[l, 0]),
            pltpu.make_async_copy(wo_hbm.at[l], WO.at[l], wsem.at[l, 1]),
            pltpu.make_async_copy(wi_hbm.at[l], WI.at[l], wsem.at[l, 2]),
            pltpu.make_async_copy(wf_hbm.at[l], WF.at[l], wsem.at[l, 3]),
        ]

    weight_copies(0)[0].start()

    barrier = pltpu.get_barrier_semaphore()

    def greet(d, _):
        pl.semaphore_signal(
            barrier, inc=1, device_id={"seq": lax.rem(me + d, n)}, device_id_type=MESH
        )
        return 0

    lax.fori_loop(1, n, greet, 0)
    pl.semaphore_signal(barrier, inc=1, device_id={"head": 1 - core}, device_id_type=MESH)

    row_id = lax.broadcasted_iota(jnp.int32, (128, 128), 0)
    lane_id = lax.broadcasted_iota(jnp.int32, (128, 128), 1)
    low_lane = lane_id < 64
    low_lane64 = low_lane[0:64]
    same_head = (row_id < 64) == low_lane
    eye = row_id == lane_id
    flip = jnp.where(row_id + lane_id == 127, 1.0, 0.0).astype(BF16)

    def expand(c):
        return jnp.concatenate(
            [jnp.where(low_lane64, c, 0.0), jnp.where(low_lane64, 0.0, c)], axis=0
        )

    def expand_low(c):
        return expand(c.astype(F32)).astype(BF16)

    def compress(x):
        return jnp.where(low_lane64, x[0:64], x[64:128])

    def to_row(col):
        return jnp.sum(jnp.where(eye, col, 0.0), axis=0, keepdims=True)

    def to_col(row):
        return jnp.sum(jnp.where(eye, row, 0.0), axis=1, keepdims=True)

    def half_sums(x):
        a = jnp.sum(jnp.where(low_lane, x, 0.0), axis=1, keepdims=True)
        b = jnp.sum(jnp.where(low_lane, 0.0, x), axis=1, keepdims=True)
        return jnp.where(low_lane, a, b)

    def half_tops(x):
        a = jnp.max(jnp.where(low_lane, x, -jnp.inf), axis=1, keepdims=True)
        b = jnp.max(jnp.where(low_lane, -jnp.inf, x), axis=1, keepdims=True)
        return jnp.where(low_lane, a, b)

    def parts3(x):
        a = x.astype(BF16)
        rest = x - a.astype(F32)
        b = rest.astype(BF16)
        c = (rest - b.astype(F32)).astype(BF16)
        return jnp.concatenate([a.astype(F32), b.astype(F32), c.astype(F32)], axis=0)

    def pack(body, rows):
        tail = jnp.concatenate([parts3(r) for r in rows], axis=0)
        fill = jnp.zeros((16 - tail.shape[0], 128), F32)
        return jnp.concatenate([body, tail, fill], axis=0).astype(BF16)

    def packed_row(message, i):
        x = message[64 + 3 * i : 67 + 3 * i].astype(F32)
        return jnp.sum(x, axis=0, keepdims=True)

    def unit(u):
        return u // NP, u % NP

    def tile(ref, l, u):
        b, j = unit(u)
        return ref[l, b * L : (b + 1) * L, j * 128 : (j + 1) * 128]

    def moments(x):
        centre = jnp.mean(x, -1, keepdims=True)
        centred = x - centre
        spread = jnp.mean(centred * centred, -1, keepdims=True)
        inverse = lax.rsqrt(spread + epsilon)
        return centred * inverse, inverse

    def norm_back(x, grad, gain):
        hat, inverse = moments(x)
        g = grad * gain
        a = jnp.mean(g, -1, keepdims=True)
        b = jnp.mean(g * hat, -1, keepdims=True)
        total = inverse * (g - a - hat * b)
        sums = (
            jnp.sum(grad * hat, axis=0, keepdims=True),
            jnp.sum(grad, axis=0, keepdims=True),
            jnp.sum(total, axis=0, keepdims=True),
        )
        return total, sums

    def put_small(start, vector):
        for i in range(vector.shape[1] // 128):
            SM[start + i : start + i + 1, :] = vector[:, i * 128 : (i + 1) * 128]

    PARTS = D // 256

    def swap_part(e, i):
        at = (e % 2, pl.ds(0, R), pl.ds(i * 256, 256))
        return pltpu.make_async_remote_copy(
            HS.at[at], HR.at[at], hsem_s.at[e, i], hsem_r.at[e, i],
            device_id={"head": 1 - core}, device_id_type=MESH,
        )

    def swap_start(e, part):
        for i in range(PARTS):
            o = slice(i * 256, (i + 1) * 256)
            HS[e % 2, :, o] = part(o).astype(BF16)
            swap_part(e, i).start()

    def swap_wait(e):
        for i in range(PARTS):
            swap_part(e, i).wait()

    def both(e):
        return HS[e % 2].astype(F32) + HR[e % 2].astype(F32)

    own_bits = [lax.rem(me // (1 << k), 2) for k in range(NB)]

    def peer_across(d):
        return me + sum((1 - 2 * own_bits[k]) * (1 << k) for k in range(NB) if d >> k & 1)

    others = range(n - 1, 0, -1)

    def spread(src, dst, ss, rs, start):
        def copy(d, to):
            return pltpu.make_async_remote_copy(
                src(peer_across(d)), dst.at[to], ss.at[d], rs.at[d],
                device_id={"seq": peer_across(d)}, device_id_type=MESH,
            )

        if start:
            for d in others:
                copy(d, me).start()
        else:
            for d in others:
                copy(d, peer_across(d)).wait_recv()
            for d in others:
                copy(d, peer_across(d)).wait_send()

    def to_owner_copy(u, src, dst, ss, rs):
        return pltpu.make_async_remote_copy(
            src, dst.at[me], ss.at[u], rs.at[me], device_id={"seq": first_owner + u}, device_id_type=MESH
        )

    def to_owner(u, src, dst, ss, rs):
        @pl.when(me != first_owner + u)
        def _():
            to_owner_copy(u, src, dst, ss, rs).start()

        @pl.when(me == first_owner + u)
        def _():
            dst[me] = src[...]

    def to_owner_sent(u, src, dst, ss, rs):
        @pl.when(me != first_owner + u)
        def _():
            to_owner_copy(u, src, dst, ss, rs).wait_send()

    def owner_gets(src, dst, ss, rs):
        def step(d, _):
            t = lax.rem(me + d, n)
            pltpu.make_async_remote_copy(
                src, dst.at[t], ss.at[0], rs.at[t], device_id={"seq": t}, device_id_type=MESH
            ).wait_recv()
            return 0

        lax.fori_loop(1, n, step, 0)

    def from_owner(slots, ss, rs, start):
        for d in others:
            c = pltpu.make_async_remote_copy(
                slots.at[mine], slots.at[mine], ss.at[d], rs.at[mine],
                device_id={"seq": peer_across(d)}, device_id_type=MESH,
            )
            if start:
                c.start()
            else:
                c.wait_send()

    def owner_came(slots, u, ss, rs):
        @pl.when(me != first_owner + u)
        def _():
            pltpu.make_async_remote_copy(
                slots.at[u], slots.at[u], ss.at[0], rs.at[u],
                device_id={"seq": first_owner + u}, device_id_type=MESH,
            ).wait_recv()

    def edges(buf, ss, rs, act):
        after = pltpu.make_async_remote_copy(
            buf.at[:, pl.ds(L, margin)], buf.at[:, pl.ds(0, margin)], ss.at[0], rs.at[0],
            device_id={"seq": lax.rem(me + 1, n)}, device_id_type=MESH,
        )
        before = pltpu.make_async_remote_copy(
            buf.at[:, pl.ds(margin, margin)], buf.at[:, pl.ds(margin + L, margin)], ss.at[1], rs.at[1],
            device_id={"seq": lax.rem(me + n - 1, n)}, device_id_type=MESH,
        )
        if act == "start":
            @pl.when(me < n - 1)
            def _():
                after.start()

            @pl.when(me > 0)
            def _():
                before.start()
        else:
            @pl.when(me < n - 1)
            def _():
                after.wait_send()
                before.wait_recv()

            @pl.when(me > 0)
            def _():
                before.wait_send()
                after.wait_recv()

    def edge_zeros(buf):
        none = jnp.zeros((B, margin, C), BF16)
        buf[:, 2 * margin + L :, :] = jnp.zeros((B, 256 - L - 2 * margin, C), BF16)

        @pl.when(me == 0)
        def _():
            buf[:, 0:margin, :] = none

        @pl.when(me == n - 1)
        def _():
            buf[:, margin + L : 2 * margin + L, :] = none

    def conv(bands, buf, u):
        b, j = unit(u)
        x = buf[b, :, j * 128 : (j + 1) * 128]
        return jnp.where(low_lane, nn(bands[2 * j], x), nn(bands[2 * j + 1], x))

    DT, FL = HID, LOW
    dims = [[k for k in reversed(range(NB)) if k != g] for g in range(2)]
    FH = F // 2
    HALF = G.shape[-1]
    everything = pl.ds(0, 2)
    items = {"outer": (0, FH), "inner": (FH, FH), "outval": (2 * FH, C), "keyed": (2 * FH + C, C)}
    item_index = {name: i for i, name in enumerate(items)}

    def peer_of(k):
        return me + (1 - 2 * own_bits[k]) * (1 << k)

    def pair_copy(l, i, g, src, dst):
        return pltpu.make_async_remote_copy(
            src, dst, asem_s.at[l, i, g], asem_r.at[l, i, g],
            device_id={"seq": peer_of(g)}, device_id_type=MESH,
        )

    def right_copies(l, i, ref, ranges):
        return [
            pair_copy(l, i, g, ref.at[pl.ds(0, R), pl.ds(c0, cn)], ref.at[pl.ds(R, R), pl.ds(c0, cn)])
            for g, (c0, cn) in enumerate(ranges)
        ]

    def left_copies(l, i, stage, gathered):
        got = []
        for g in range(2):
            at = [core] + [everything] * (NB - 1)
            at[NB - 1 - g] = 1 - own_bits[g]
            src = stage.at[tuple(at) + (pl.ds(0, CH), pl.ds(0, R))]
            dst = gathered.at[(g, core) + (everything,) * (NB - 2) + (pl.ds(0, CH), pl.ds(R, R))]
            got.append(pair_copy(l, i, g, src, dst))
        return got

    def core_copy(l, i, g, ref):
        return pltpu.make_async_remote_copy(
            ref, ref, bsem_s.at[l, i, g], bsem_r.at[l, i, g],
            device_id={"head": 1 - core}, device_id_type=MESH,
        )

    def left_hand_on(l, i, gathered):
        return [
            core_copy(l, i, g, gathered.at[(g, core) + (everything,) * (NB - 2) + (pl.ds(0, CH), pl.ds(R, R))])
            for g in range(2)
        ]

    def row_copies(l, i, src, dst):
        at = pl.ds(pl.multiple_of(core * L, L), L)
        return [pair_copy(l, i, g, src.at[at], dst.at[g, at]) for g in range(2)]

    def row_hand_on(l, i, dst):
        at = pl.ds(pl.multiple_of(core * L, L), L)
        return [core_copy(l, i, g, dst.at[g, at]) for g in range(2)]

    def each_half(g, act):
        for code in range(n // 2):
            spot = tuple((code >> (NB - 2 - i)) & 1 for i in range(NB - 1))
            at = list(spot)
            at.insert(NB - 1 - g, own_bits[g])
            act((g,) + spot, tuple(at))

    def left_put(x, stage, gathered):
        stage[...] = x.T.reshape(stage.shape)
        for g in range(2):
            def put(to, at):
                gathered[to + (slice(None), slice(0, R))] = stage[at]

            each_half(g, put)

    def left_put_theirs(rows, stage, gathered):
        for g in range(2):
            stage[...] = rows[g].T.reshape(stage.shape)

            def put(to, at):
                gathered[to + (slice(None), slice(R, 2 * R))] = stage[at]

            each_half(g, put)

    def start_all(copies):
        for c in copies:
            c.start()

    def wait_all(copies):
        for c in copies:
            c.wait()

    def weight_grad(g, left, right, first, count, width):
        def step(i, _):
            o = pl.multiple_of(i * width, width)
            x = nn(left[g].reshape(D // 2, 2 * R), right(o)).astype(BF16)
            o = pl.multiple_of(first + o, 128)
            for code in range(n // 2):
                spot = tuple((code >> (NB - 2 - i)) & 1 for i in range(NB - 1))
                G[(g,) + spot + (slice(None), pl.ds(o, width))] = x[code * CH : (code + 1) * CH]
            return 0

        lax.fori_loop(0, count // width, step, 0)

    STAGES = NB - 1

    def rs_copy(l, name, g, stage):
        first, count = items[name]
        cols = (pl.ds(0, CH), pl.ds(first, count))
        d = NB - 2 - stage
        index = [everything] * d + [1 - own_bits[dims[g][d]]] + [own_bits[k] for k in dims[g][d + 1 :]]
        i = item_index[name]
        return pltpu.make_async_remote_copy(
            G.at[(g,) + tuple(index) + cols], RV[stage].at[(l, g) + (everything,) * d + cols],
            gsem_s.at[l, i, g, stage], gsem_r.at[l, i, g, stage],
            device_id={"seq": peer_of(dims[g][d])}, device_id_type=MESH,
        )

    def rs_start(l, name, stage):
        for g in range(2):
            rs_copy(l, name, g, stage).start()

    def rs_add(l, name, stage):
        first, count = items[name]
        for g in range(2):
            rs_copy(l, name, g, stage).wait()
            d = NB - 2 - stage
            mine_at = tuple(own_bits[k] for k in dims[g][d:])
            cols = (slice(None), slice(first, first + count))
            if d:
                for code in range(1 << d):
                    spot = tuple((code >> (d - 1 - i)) & 1 for i in range(d))
                    at = (g,) + spot + mine_at + cols
                    G[at] = G[at] + RV[stage][(l, g) + spot + cols]
            else:
                x = G[(g,) + mine_at + cols].astype(F32) + RV[stage][(l, g) + cols].astype(F32)
                write_out(l, name, g, x)

    def write_out(l, name, g, x):
        if name == "outer":
            OU[l, :, g * FH : (g + 1) * FH] = x
        elif name == "inner":
            OI[l, :, g * FH : (g + 1) * FH] = x
        elif name == "keyed":
            OP[l, g] = x
        elif g == 0:
            OO[l, :, 0:128] = x[:, 0:128]
            OP[l, 2, :, 0 : C - 128] = x[:, 128:C]
        else:
            OO[l, :, 128:C] = x[:, 0 : C - 128]
            OP[l, 2, :, C - 128 : C] = x[:, C - 128 : C]

    def out_copy(i, src, dst):
        return pltpu.make_async_copy(src, dst, osem.at[i])

    def advance(l, name, stage):
        rs_add(l, name, stage)
        if stage + 1 < STAGES:
            rs_start(l, name, stage + 1)

    out_ranges = ((0, 128), (128, C - 128))
    val_ranges = ((2 * C, C - 128), (3 * C - 128, 128))
    key_ranges = ((0, C), (C, C))
    ffn_ranges = ((0, FH), (FH, FH))

    for b in range(B):
        HID[b * L : (b + 1) * L, :] = tok[b].astype(F32)
    TB[...] = jnp.zeros_like(TB)

    def make_bands(l):
        backwards = jnp.where(row_id + lane_id == K - 1, 1.0, 0.0).astype(BF16)
        for h in range(z.local_heads):
            TB[0, h : h + 1, 0:K] = taps[h].astype(F32)[l : l + 1]
        TB[1, :, 0:128] = nn(TB[0, :, 0:128].astype(BF16), backwards)
        for which, store in ((0, TT), (1, TR)):
            for h in range(z.local_heads):
                base = jnp.broadcast_to(TB[which, h : h + 1, :], (128, 256))
                store[l, h] = pltpu.roll(base, 0, 1, stride=1, stride_axis=0).astype(BF16)

    def regrow(l):
        wait_all(row_hand_on(l, 2, PN))
        left_put_theirs(PN, LSH, LTN.at[l])
        for g in range(2):
            def step(i, _):
                o = pl.ds(pl.multiple_of(g * FH + i * 256, 256), 256)
                act, slope = unit_rows(PN[g], l, o)
                ACT[l, R : 2 * R, o] = act
                GP[l, R : 2 * R, o] = slope
                return 0

            lax.fori_loop(0, FH // 256, step, 0)

    def unit_rows(rows, l, o):
        pre = nn(rows, WI[l, :, o]) + ibias[l : l + 1, o].astype(F32)
        below = 0.5 * (1.0 + lax.erf(pre * (0.5**0.5)))
        slope = below + pre * jnp.exp(-0.5 * pre * pre) * 0.3989422804014327
        return (pre * below).astype(BF16), slope.astype(BF16)

    def forward(l):
        copies = weight_copies(l)
        e = 2 * l
        LOW[...] = HID[...].astype(BF16)
        copies[0].wait()
        if l == 0:
            for c in [weight_copies(0)[i] for i in (1, 2, 3)] + weight_copies(1):
                c.start()
        both_bias = pbias[l].astype(F32)
        bias_q, bias_v = both_bias[0:1], both_bias[1:2]
        q = (nn(LOW[...], WP[l, 0]) + bias_q) * scale
        k = nn(LOW[...], WP[l, 1]) * scale
        QS[l] = q.astype(BF16)
        KS[l] = k.astype(BF16)
        sums = []
        for x in (q, k):
            for b in range(B):
                for r in range(S):
                    at = b * L + r * z.segment
                    sums.append(jnp.sum(x[at : at + z.segment], axis=0, keepdims=True))
        marks = jnp.concatenate(sums, axis=0) * (1.0 / z.segment)
        MS[...] = marks.astype(BF16)
        rest = marks - MS[...].astype(F32)
        middle = rest.astype(BF16).astype(F32)
        rest = rest - middle
        for u in range(U):
            b, j = unit(u)
            parts = [
                x[first + b * S : first + (b + 1) * S, j * 128 : (j + 1) * 128]
                for x in (middle, rest)
                for first in (0, 8)
            ]
            MD[u] = jnp.concatenate(parts, axis=0).astype(BF16)
        if l == 0:
            pl.semaphore_wait(barrier, n)
        spread(lambda t: MS, MB, msem_s.at[l], msem_r.at[l], True)
        for u in range(U):
            to_owner(u, MD.at[u], MO, dsem_s.at[l], dsem_r.at[l])
        MB[me] = MS[...]
        vl = (nn(LOW[...], WP[l, 2]) + bias_v).astype(BF16)
        for b in range(B):
            VX[l, b, margin : margin + L, :] = vl[b * L : (b + 1) * L]
        edge_zeros(VX.at[l])
        edges(VX.at[l], vsem_s.at[l], vsem_r.at[l], "start")
        if l:
            regrow(l - 1)
        left_put(LOW[...], LSH, LTH.at[l])
        make_bands(l)
        edges(VX.at[l], vsem_s.at[l], vsem_r.at[l], "wait")
        for u in range(U):
            b, j = unit(u)
            DQ[b * L : (b + 1) * L, j * 128 : (j + 1) * 128] = conv(TT.at[l], VX.at[l], u)
        spread(lambda t: MS, MB, msem_s.at[l], msem_r.at[l], False)
        hidden_copies = left_copies(l, 0, LSH, LTH.at[l])
        start_all(hidden_copies)
        for u in range(U):
            b, j = unit(u)
            lanes = slice(j * 128, (j + 1) * 128)
            for first, store in ((0, QM), (8, KM)):
                rows = [MB[i, :, lanes].astype(F32)[first + b * S : first + (b + 1) * S] for i in range(n)]
                store[l, u] = jnp.concatenate(rows, axis=0)
        for u in range(U):
            b, j = unit(u)
            ksc = nt(expand(QM[l, u]).astype(BF16), tile(KS, l, u))
            top = jnp.max(ksc, axis=1, keepdims=True)
            p = jnp.exp(ksc - top)
            total = jnp.sum(p, axis=1, keepdims=True)
            v = VX[l, b, margin : margin + L, j * 128 : (j + 1) * 128]
            XM[u] = pack(compress(nn(p.astype(BF16), v)), [to_row(top), to_row(total)])
            to_owner(u, XM.at[u], OB, xsem_s.at[l], xsem_r.at[l])
        @pl.when(is_owner)
        def _():
            owner_gets(MD.at[0], MO, dsem_s.at[l], dsem_r.at[l])
            extra = []
            for i in range(n):
                x = MO[i].astype(F32)
                extra.append(x[0:8] + x[8:16])
            qb = expand(QM[l, mine] + jnp.concatenate([x[0:S] for x in extra], axis=0))
            kb = expand(KM[l, mine] + jnp.concatenate([x[S : 2 * S] for x in extra], axis=0))
            s = lax.dot_general(
                qb, kb, (((1,), (1,)), ((), ())), precision=exact_result, preferred_element_type=F32
            )
            s = jnp.where(same_head, s, -jnp.inf)
            p = jnp.exp(s - jnp.max(s, axis=1, keepdims=True))
            a = p / jnp.sum(p, axis=1, keepdims=True)
            PA[l] = a
            ah = halves(a)
            at = a.T
            sums = jnp.sum(a, axis=0, keepdims=True)
            tops = jnp.where(
                low_lane[0:1],
                jnp.max(jnp.where(low_lane[0:1], sums, 0.0), axis=1, keepdims=True),
                jnp.max(jnp.where(low_lane[0:1], 0.0, sums), axis=1, keepdims=True),
            )
            unit_matrix = jnp.where(eye, 1.0, 0.0)

            def iterate(i, zk):
                PV[l, i, 0] = zk
                PV[l, i, 4] = zk.T
                zh = halves(zk)
                pr = nn3(ah, zh)
                PV[l, i, 1] = pr
                prh = halves(pr)
                n2 = 15.0 * unit_matrix - nn3(prh, halves(7.0 * unit_matrix - pr))
                PV[l, i, 2] = n2
                n3 = 13.0 * unit_matrix - nn3(prh, halves(n2))
                PV[l, i, 3] = n3
                return 0.25 * nn3(zh, halves(n3))

            zk = lax.fori_loop(0, PINV_ITERS, iterate, at / tops)
            PZ[l] = zk.T
            owner_gets(XM.at[0], OB, xsem_s.at[l], xsem_r.at[l])
            stats = [OB[i, 64:80].astype(F32) for i in range(n)]
            tops = jnp.concatenate([jnp.sum(x[0:3], axis=0, keepdims=True) for x in stats], axis=0)
            totals = jnp.concatenate([jnp.sum(x[3:6], axis=0, keepdims=True) for x in stats], axis=0)
            top = jnp.max(tops, axis=0, keepdims=True)
            factors = jnp.exp(tops - top)
            total = jnp.sum(factors * totals, axis=0, keepdims=True)
            shares = halves(factors / total)
            device = lax.broadcasted_iota(jnp.int32, (n, n * 128), 0)
            place = lax.broadcasted_iota(jnp.int32, (n, n * 128), 1) // 128
            pick = jnp.where(device == place, 1.0, 0.0).astype(BF16)
            columns = tn(shares[0], pick) + tn(shares[1], pick)
            mixed = jnp.zeros((64, 128), F32)
            for i in range(n):
                share = compress(columns[:, i * 128 : (i + 1) * 128])
                mixed = mixed + share * OB[i, 0:64].astype(F32)
            MX[l] = mixed
            CR[l, mine] = pack(compress(nn3f(zk, expand(mixed))), [top + jnp.log(total)])
            from_owner(CR.at[l], csem_s.at[l], csem_r.at[l], True)

        for u in range(U):
            s = nt(tile(QS, l, u), expand(KM[l, u]).astype(BF16))
            p = jnp.exp(s - half_tops(s))
            RW[l, u] = p / half_sums(p)

        wait_all(hidden_copies)
        start_all(left_hand_on(l, 0, LTH.at[l]))
        for u in range(U):
            b, j = unit(u)
            to_owner_sent(u, XM.at[u], OB, xsem_s.at[l], xsem_r.at[l])
            to_owner_sent(u, MD.at[u], MO, dsem_s.at[l], dsem_r.at[l])
            owner_came(CR.at[l], u, csem_s.at[l], csem_r.at[l])
            at = (slice(b * L, (b + 1) * L), slice(j * 128, (j + 1) * 128))
            context = nn(RW[l, u].astype(BF16), expand_low(CR[l, u, 0:64])) + DQ[at]
            CTX[(l,) + at] = context.astype(BF16)
        start_all(right_copies(l, 1, CTX.at[l], out_ranges))

        @pl.when(is_owner)
        def _():
            from_owner(CR.at[l], csem_s.at[l], csem_r.at[l], False)

        copies[1].wait()
        swap_start(e, lambda o: nn(CTX[l, 0:R], WO[l, :, o]))
        swap_wait(e)
        total1 = HID[...] + both(e) + obias[l].astype(F32)[0:1]
        T1[l] = total1
        normed = moments(total1)[0] * ngain[l].astype(F32)[0:1] + nshift[l].astype(F32)[0:1]
        HID[...] = normed
        LOW[...] = normed.astype(BF16)
        norm_copies = row_copies(l, 2, LOW, PN)
        start_all(norm_copies)
        copies[2].wait()

        def grow(i, _):
            o = pl.ds(pl.multiple_of(i * 256, 256), 256)
            act, slope = unit_rows(LOW[...], l, o)
            ACT[l, 0:R, o] = act
            GP[l, 0:R, o] = slope
            return 0

        lax.fori_loop(0, F // 256, grow, 0)
        copies[3].wait()

        swap_start(e + 1, lambda o: nn(ACT[l, 0:R], WF[l, :, o]))
        left_put(LOW[...], LSH, LTN.at[l])
        swap_wait(e + 1)
        total2 = HID[...] + both(e + 1) + obias[l].astype(F32)[1:2]
        T2[l] = total2
        HID[...] = moments(total2)[0] * ngain[l].astype(F32)[1:2] + nshift[l].astype(F32)[1:2]
        wait_all(norm_copies)
        start_all(row_hand_on(l, 2, PN))

    def backward(l, slots):
        def slot(name):
            for step in slots.get(name, ()):
                advance(z.layers - 1, *step)

        e = 2 * z.layers + 2 * (z.layers - 1 - l)
        k = z.layers + l
        base = 60 * l
        total2, sums = norm_back(T2[l], UP[...], ngain[l].astype(F32)[1:2])
        put_small(base + 6, sums[0])
        put_small(base + 18, sums[1])
        put_small(base + 30, sums[2])
        DT[...] = total2
        FL[...] = total2.astype(BF16)
        feed_copies = row_copies(l, 4, FL, PF)
        start_all(feed_copies)
        slot("fed")

        def widen(i, _):
            o = pl.ds(pl.multiple_of(i * 256, 256), 256)
            grad = nt(FL[...], WF[l, o, :]).astype(BF16).astype(F32)
            pre = (GP[l, 0:R, o].astype(F32) * grad).astype(BF16)
            DPRE[0:R, o] = pre
            s = jnp.sum(pre.astype(F32), axis=0, keepdims=True)
            SM[pl.ds(base + 36 + 2 * i, 1), :] = s[:, 0:128]
            SM[pl.ds(base + 37 + 2 * i, 1), :] = s[:, 128:256]
            return 0

        lax.fori_loop(0, F // 256, widen, 0)
        slot("widened")
        swap_start(e, lambda o: nt(DPRE[0:R], WI[l, o, :]))
        slot("narrowed")
        left_put(FL[...], LSH, LTF)
        if l == z.layers - 1:
            regrow(l)
        wait_all(feed_copies)
        start_all(row_hand_on(l, 4, PF))
        swap_wait(e)
        grad_normed = DT[...] + both(e)
        total1, sums = norm_back(T1[l], grad_normed, ngain[l].astype(F32)[0:1])
        put_small(base + 0, sums[0])
        put_small(base + 12, sums[1])
        put_small(base + 24, sums[2])
        DT[...] = total1
        FL[...] = total1.astype(BF16)
        grads = nt(FL[...], WO[l]).astype(BF16)
        for b in range(B):
            GX[b, margin : margin + L, :] = grads[b * L : (b + 1) * L]
        edge_zeros(GX)
        edges(GX, vsem_s.at[k], vsem_r.at[k], "start")

        def g_tile(u):
            b, j = unit(u)
            return GX[b, margin : margin + L, j * 128 : (j + 1) * 128]

        for u in range(U):
            XM[u, 0:64] = compress(tn(RW[l, u].astype(BF16), g_tile(u))).astype(BF16)
            to_owner(u, XM.at[u, pl.ds(0, 64)], OB.at[:, pl.ds(0, 64)], xsem_s.at[k], xsem_r.at[k])
            DQM[u] = jnp.zeros((64, 128), F32)
        slot("asked")
        wait_all(row_hand_on(l, 4, PF))
        left_put_theirs(PF, LSH, LTF)
        for g in range(2):
            def step(i, _):
                o = pl.ds(pl.multiple_of(g * FH + i * 256, 256), 256)
                grad = nt(PF[g], WF[l, o, :]).astype(BF16).astype(F32)
                DPRE[R : 2 * R, o] = (GP[l, R : 2 * R, o].astype(F32) * grad).astype(BF16)
                return 0

            lax.fori_loop(0, FH // 256, step, 0)
        left_put(FL[...], LSH, LTA)
        attend_copies = left_copies(l, 6, LSH, LTA)
        start_all(attend_copies)
        slot("regrown")
        for g in range(2):
            weight_grad(g, LTF, lambda o: ACT[l, :, pl.ds(g * FH + o, FH)], items["outer"][0], FH, FH)
        rs_start(l, "outer", 0)
        slot("outer")

        @pl.when(is_owner)
        def _():
            owner_gets(XM.at[0, pl.ds(0, 64)], OB.at[:, pl.ds(0, 64)], xsem_s.at[k], xsem_r.at[k])
            d_core = OB[0, 0:64].astype(F32)
            for i in range(1, n):
                d_core = d_core + OB[i, 0:64].astype(F32)
            PC[...] = d_core
            d_mixed = nn3f(PZ[l], expand(d_core))
            off = jnp.sum(d_mixed * expand(MX[l]), axis=1, keepdims=True)
            DR[mine] = pack(compress(d_mixed), [to_row(off)])
            from_owner(DR, csem_s.at[k], csem_r.at[k], True)

        for u in range(U):
            b, j = unit(u)
            at = (slice(b * L, (b + 1) * L), slice(j * 128, (j + 1) * 128))
            d_row = nt(g_tile(u), expand_low(CR[l, u, 0:64]))
            rw = RW[l, u]
            d_rs = (rw * (d_row - half_sums(rw * d_row))).astype(BF16)
            DQ[at] = nn(d_rs, expand(KM[l, u]).astype(BF16))
            DKM[u] = compress(tn(d_rs, tile(QS, l, u)))
        for u in range(U):
            to_owner_sent(u, XM.at[u, pl.ds(0, 64)], OB.at[:, pl.ds(0, 64)], xsem_s.at[k], xsem_r.at[k])

        @pl.when(is_owner)
        def _():
            a = PA[l]
            ath = halves(a.T)
            unit_matrix = jnp.where(eye, 1.0, 0.0)

            def back(i, carry):
                dz, da = carry
                i = PINV_ITERS - 1 - i
                zh, zth, prh = halves(PV[l, i, 0]), halves(PV[l, i, 4]), halves(PV[l, i, 1])
                n1h = halves(7.0 * unit_matrix - PV[l, i, 1])
                n2h, n3h = halves(PV[l, i, 2]), halves(PV[l, i, 3])
                dzh = halves(dz)
                dn3 = halves(0.25 * nn3(zth, dzh))
                dn2 = halves(-nn3(prh, dn3))
                dpr = nn3(prh, dn2) - nt3(dn3, n2h) - nt3(dn2, n1h)
                dpr = halves(dpr)
                dz = 0.25 * nt3(dzh, n3h) + nn3(ath, dpr)
                return dz, da + nt3(dpr, zh)

            dz, da = lax.fori_loop(
                0, PINV_ITERS, back, (nt3f(expand(PC[...]), expand(MX[l])), jnp.zeros((128, 128), F32))
            )
            low_row = low_lane[0:1]

            def half_row(x, f):
                return jnp.where(
                    low_row,
                    f(jnp.where(low_row, x, 0.0), axis=1, keepdims=True),
                    f(jnp.where(low_row, 0.0, x), axis=1, keepdims=True),
                )

            sums = jnp.sum(a, axis=0, keepdims=True)
            tops = half_row(sums, jnp.max)
            d_tops = -half_row(jnp.sum(dz * PV[l, 0, 0], axis=0, keepdims=True), jnp.sum) / tops
            at_top = jnp.where(sums == tops, 1.0, 0.0)
            da = da + (dz / tops).T + at_top * d_tops / half_row(at_top, jnp.sum)
            d_ms = halves(a * (da - jnp.sum(a * da, axis=1, keepdims=True)))
            DQM[mine] = compress(nn3(d_ms, halves(expand(KM[l, mine]))))
            DKM[mine] = DKM[mine] + compress(tn3(d_ms, halves(expand(QM[l, mine]))))

        slot("pinv")
        wait_all(attend_copies)
        start_all(left_hand_on(l, 6, LTA))
        for g in range(2):
            weight_grad(g, LTN.at[l], lambda o: DPRE[:, pl.ds(g * FH + o, FH)], items["inner"][0], FH, FH)
        rs_start(l, "inner", 0)
        edges(GX, vsem_s.at[k], vsem_r.at[k], "wait")
        for u in range(U):
            b, j = unit(u)
            at = (slice(b * L, (b + 1) * L), slice(j * 128, (j + 1) * 128))
            DV[at] = conv(TR.at[l], GX, u)
        for j in range(NP):
            for h in range(2):
                found = jnp.zeros((128, 256), F32)
                for b in range(B):
                    g = nn(flip, g_tile(b * NP + j))
                    g = jnp.where(low_lane, g, 0.0) if h == 0 else jnp.where(low_lane, 0.0, g)
                    found = found + nt(g.astype(BF16), VX[l, b, :, j * 128 : (j + 1) * 128])
                found = pltpu.roll(found, 129, 1, stride=1, stride_axis=0)
                row = base + 54 + 2 * j + h
                SM[row : row + 1, :] = jnp.sum(found[:, 0:128], axis=0, keepdims=True)
        advance(l, "outer", 0)
        for u in range(U):
            b, j = unit(u)
            at = (slice(b * L, (b + 1) * L), slice(j * 128, (j + 1) * 128))
            owner_came(DR, u, csem_s.at[k], csem_r.at[k])
            dm = expand_low(DR[u, 0:64])
            off = to_col(packed_row(DR.at[u], 0))
            qb = expand(QM[l, u]).astype(BF16)
            kw = jnp.exp(nt(qb, tile(KS, l, u)) - to_col(packed_row(CR.at[l, u], 0)))
            v = VX[l, b, margin : margin + L, j * 128 : (j + 1) * 128]
            DV[at] = DV[at] + tn(kw.astype(BF16), dm)
            d_ks = (kw * (nt(dm, v) - off)).astype(BF16)
            DK[at] = tn(d_ks, qb)
            DQM[u] = DQM[u] + compress(nn(d_ks, tile(KS, l, u)))

        @pl.when(is_owner)
        def _():
            from_owner(DR, csem_s.at[k], csem_r.at[k], False)

        for u in range(U):
            b, j = unit(u)
            lanes = slice(j * 128, (j + 1) * 128)
            dq, dk = DQM[u].astype(BF16), DKM[u].astype(BF16)
            for i in range(n):
                SB[i, b * S : (b + 1) * S, lanes] = dq[i * S : (i + 1) * S]
                SB[i, 8 + b * S : 8 + (b + 1) * S, lanes] = dk[i * S : (i + 1) * S]
        DP[0:R, 2 * C : 3 * C] = DV[...].astype(BF16)
        value_copies = right_copies(l, 7, DP, val_ranges)
        wait_all(left_hand_on(l, 6, LTA))
        wait_all(right_copies(l, 1, CTX.at[l], out_ranges))
        out0 = items["outval"][0]
        weight_grad(0, LTA, lambda o: CTX[l, :, pl.ds(o, 128)], out0, 128, 128)
        weight_grad(1, LTA, lambda o: CTX[l, :, pl.ds(128 + o, 256)], out0, C - 128, 256)
        spread(lambda t: SB.at[t], SR, qsem_s.at[l], qsem_r.at[l], True)
        SR[me] = SB[me]
        start_all(value_copies)
        advance(l, "inner", 0)
        wait_all(value_copies)
        wait_all(left_hand_on(l, 0, LTH.at[l]))
        weight_grad(0, LTH.at[l], lambda o: DP[:, pl.ds(2 * C + o, 256)], out0 + 128, C - 128, 256)
        weight_grad(1, LTH.at[l], lambda o: DP[:, pl.ds(3 * C - 128 + o, 128)], out0 + C - 128, 128, 128)
        rs_start(l, "outval", 0)
        spread(lambda t: SB.at[t], SR, qsem_s.at[l], qsem_r.at[l], False)
        marks = SR[0].astype(F32)
        for i in range(1, n):
            marks = marks + SR[i].astype(F32)
        marks = marks * (1.0 / z.segment)
        for b in range(B):
            for r in range(S):
                at = slice(b * L + r * z.segment, b * L + (r + 1) * z.segment)
                i = b * S + r
                DP[at, 0:C] = ((DQ[at] + marks[i : i + 1]) * scale).astype(BF16)
                DP[at, C : 2 * C] = ((DK[at] + marks[8 + i : 9 + i]) * scale).astype(BF16)
        key_copies = right_copies(l, 8, DP, key_ranges)
        start_all(key_copies)

        def onto(o):
            x = nt(DP[0:R, 0:C], WP[l, 0, o, :]) + nt(DP[0:R, C : 2 * C], WP[l, 1, o, :])
            return x + nt(DP[0:R, 2 * C : 3 * C], WP[l, 2, o, :])

        swap_start(e + 1, onto)
        bias = jnp.sum(DP[0:R].astype(F32), axis=0, keepdims=True)
        put_small(base + 48, bias[:, 0:C])
        put_small(base + 51, bias[:, 2 * C : 3 * C])
        advance(l, "outer", 1)
        wait_all(key_copies)
        for g in range(2):
            weight_grad(g, LTH.at[l], lambda o: DP[:, pl.ds(g * C + o, 128)], items["keyed"][0], C, 128)
        rs_start(l, "keyed", 0)
        swap_wait(e + 1)
        UP[...] = DT[...] + both(e + 1)

    for l in range(z.layers):
        forward(l)
    results = [out_copy(b, HID.at[pl.ds(b * L, L)], result.at[b]) for b in range(B)]
    start_all(results)
    for b in range(B):
        shown = to_col(mask[b : b + 1, :].astype(F32))
        UP[b * L : (b + 1) * L, :] = cot[b].astype(F32) * shown
    wait_all(results)
    backward(1, {})
    backward(
        0,
        {
            "fed": [("outer", 2)],
            "widened": [("inner", 1), ("outval", 0)],
            "narrowed": [("keyed", 0)],
            "asked": [("outval", 1), ("inner", 2)],
            "regrown": [("keyed", 1)],
            "outer": [("outval", 2)],
            "pinv": [("keyed", 2)],
        },
    )

    def finish(*steps):
        for step in steps:
            advance(0, *step)

    tokens_out = [out_copy(B + b, UP.at[pl.ds(b * L, L)], gtok.at[b]) for b in range(B)]
    start_all(tokens_out)
    spread(lambda t: SM.at[pl.ds(pl.multiple_of(t * 8, 8), 8)], SMR, ssem_s, ssem_r, True)
    SMR[me] = SM[pl.ds(pl.multiple_of(me * 8, 8), 8), :]
    finish(("inner", 1), ("outval", 0), ("outer", 2))
    spread(lambda t: SM.at[pl.ds(pl.multiple_of(t * 8, 8), 8)], SMR, ssem_s, ssem_r, False)
    total = SMR[0]
    for i in range(1, n):
        total = total + SMR[i]
    SMT[me] = total
    spread(lambda t: SMT.at[me], SMT, tsem_s, tsem_r, True)
    finish(("inner", 2), ("keyed", 0), ("outval", 1))
    ffn_out = [out_copy(2 * B, OU, gouter), out_copy(2 * B + 1, OI, ginner)]
    start_all(ffn_out)
    spread(lambda t: SMT.at[me], SMT, tsem_s, tsem_r, False)

    def little(at):
        return SMT[at // 8, at % 8 : at % 8 + 1, :]

    for l in range(z.layers):
        base = 60 * l
        for i in range(D // 128):
            lanes = slice(i * 128, (i + 1) * 128)
            for side in range(2):
                for what in range(3):
                    OS[what, l, side : side + 1, lanes] = little(base + 12 * what + 6 * side + i)
        for i in range(F // 128):
            OT[l : l + 1, i * 128 : (i + 1) * 128] = little(base + 36 + i)
        for i in range(C // 128):
            gbias[l, 0:1, i * 128 : (i + 1) * 128] = little(base + 48 + i)
            gbias[l, 1:2, i * 128 : (i + 1) * 128] = little(base + 51 + i)
        for h in range(z.local_heads):
            gtaps[h, l : l + 1, :] = little(base + 54 + h)[:, 0:K]
    small_out = [
        out_copy(2 * B + 2 + i, src, dst)
        for i, (src, dst) in enumerate(
            [(OS.at[0], ggain), (OS.at[1], gshift), (OS.at[2], gobias), (OT, gibias)]
        )
    ]
    start_all(small_out)
    finish(("keyed", 1), ("outval", 2), ("keyed", 2))
    rest_out = [out_copy(2 * B + 6, OP, gproj), out_copy(2 * B + 7, OO, gout)]
    start_all(rest_out)
    wait_all(tokens_out + ffn_out + small_out + rest_out)


def hand_over(count, *refs):
    sems = refs[-1]
    copies = [
        pltpu.make_async_copy(refs[i], refs[count + i], sems.at[i]) for i in range(count)
    ]
    for c in copies:
        c.start()
    for c in copies:
        c.wait()


def fused(z, tokens, cotangent, masked, projections, projection_bias, conv_taps, output_weight,
          output_bias, norm_gain, norm_shift, inner_weight, inner_bias, outer_weight):
    n, B, L, R, D, C, F = z.n, z.batch, z.length, z.rows, z.width, z.cols, z.hidden
    U, H, NL_, NB, CH = z.units, z.local_heads, z.layers, z.bits, z.width // z.n
    V = pltpu.VMEM
    DMA = pltpu.SemaphoreType.DMA
    cols = F + 2 * C
    staged = lambda: V((2,) * NB + (CH, R), BF16)
    gathered = lambda *lead: V(lead + (2,) * NB + (CH, 2 * R), BF16)
    scratch = dict(
        WP=V((NL_, 3, D, C), BF16), WO=V((NL_, C, D), BF16), WI=V((NL_, D, F), BF16), WF=V((NL_, F, D), BF16),
        QS=V((NL_, R, C), BF16), KS=V((NL_, R, C), BF16),
        VX=V((NL_, B, 256, C), BF16), RW=V((NL_, U, 128, 128), F32),
        CTX=V((NL_, 2 * R, C), BF16), T1=V((NL_, R, D), F32), T2=V((NL_, R, D), F32),
        GP=V((NL_, 2 * R, F), BF16), ACT=V((NL_, 2 * R, F), BF16),
        QM=V((NL_, U, 64, 128), F32), KM=V((NL_, U, 64, 128), F32), CR=V((NL_, U, 80, 128), BF16),
        MX=V((NL_, 64, 128), F32), PA=V((NL_, 128, 128), F32), PV=V((NL_, PINV_ITERS, 5, 128, 128), F32),
        PZ=V((NL_, 128, 128), F32), PC=V((64, 128), F32), LTH=gathered(NL_), LTN=gathered(NL_),
        HID=V((R, D), F32), UP=V((R, D), F32), LOW=V((R, D), BF16), PN=V((2, R, D), BF16), PF=V((2, R, D), BF16),
        DPRE=V((2 * R, F), BF16), GX=V((B, 256, C), BF16), DQ=V((R, C), F32), DK=V((R, C), F32), DV=V((R, C), F32),
        DP=V((2 * R, 3 * C), BF16), DQM=V((U, 64, 128), F32), DKM=V((U, 64, 128), F32), DR=V((U, 80, 128), BF16),
        SM=V((n * 8, 128), F32), TB=V((2, 8, 256), F32),
        TT=V((NL_, H, 128, 256), BF16), TR=V((NL_, H, 128, 256), BF16), LTF=gathered(), LTA=gathered(),
        LSH=staged(), OP=V((NL_, 3, CH, C), F32), OO=V((NL_, CH, C), F32), OI=V((NL_, CH, F), F32),
        OU=V((NL_, CH, F), F32), OS=V((3, NL_, 2, D), F32), OT=V((NL_, F), F32),
        MS=V((16, C), BF16), MB=V((n, 16, C), BF16), MD=V((U, 16, 128), BF16), MO=V((n, 16, 128), BF16), XM=V((U, 80, 128), BF16), OB=V((n, 80, 128), BF16),
        SB=V((n, 16, C), BF16), SR=V((n, 16, C), BF16), HS=V((2, R, D), BF16), HR=V((2, R, D), BF16),
        SMR=V((n, 8, 128), F32), SMT=V((n, 8, 128), F32),
        G=V((2,) * NB + (CH, cols), BF16),
        RV=[V((NL_, 2) + (2,) * (NB - 2 - s) + (CH, cols), BF16) for s in range(NB - 1)],
        wsem=DMA((NL_, 4)),
        hsem_s=DMA((4 * NL_, D // 256)), hsem_r=DMA((4 * NL_, D // 256)),
        msem_s=DMA((NL_, n)), msem_r=DMA((NL_, n)), dsem_s=DMA((NL_, U)), dsem_r=DMA((NL_, n)), xsem_s=DMA((2 * NL_, U)), xsem_r=DMA((2 * NL_, n)),
        csem_s=DMA((2 * NL_, n)), csem_r=DMA((2 * NL_, U)), vsem_s=DMA((2 * NL_, 2)), vsem_r=DMA((2 * NL_, 2)),
        osem=DMA((2 * B + 8,)),
        asem_s=DMA((NL_, 9, 2)), asem_r=DMA((NL_, 9, 2)), bsem_s=DMA((NL_, 9, 2)), bsem_r=DMA((NL_, 9, 2)),
        gsem_s=DMA((NL_, 4, 2, NB - 1)), gsem_r=DMA((NL_, 4, 2, NB - 1)), qsem_s=DMA((NL_, n)), qsem_r=DMA((NL_, n)),
        ssem_s=DMA((n,)), ssem_r=DMA((n,)), tsem_s=DMA((n,)), tsem_r=DMA((n,)),
    )
    in_vmem = pl.BlockSpec(memory_space=pltpu.VMEM)
    in_hbm = pl.BlockSpec(memory_space=pl.ANY)
    out = lambda *s: jax.ShapeDtypeStruct(s, F32)
    shapes = (
        out(B, L, D), out(B, L, D), out(NL_, 3, CH, C), out(NL_, 2, C), out(H, NL_, z.kernel), out(NL_, CH, C),
        out(NL_, 2, D), out(NL_, 2, D), out(NL_, 2, D), out(NL_, CH, F), out(NL_, F), out(NL_, CH, F),
    )
    outs = pl.pallas_call(
        partial(fused_kernel, z),
        out_shape=shapes,
        in_specs=[in_vmem] * 9 + [in_hbm] * 4,
        out_specs=tuple(in_vmem if i in (3, 4) else in_hbm for i in range(len(shapes))),
        scratch_shapes=scratch,
        compiler_params=pltpu.CompilerParams(
            collective_id=1, has_side_effects=True, vmem_limit_bytes=VMEM_LIMIT
        ),
    )(tokens, cotangent, masked, projection_bias, jnp.swapaxes(conv_taps, 0, 1), output_bias, norm_gain, norm_shift, inner_bias,
      projections, output_weight, inner_weight, outer_weight)
    outs = list(
        pl.pallas_call(
            partial(hand_over, len(shapes)),
            out_shape=shapes,
            in_specs=[in_vmem] * len(shapes),
            out_specs=(in_hbm,) * len(shapes),
            scratch_shapes=[DMA((len(shapes),))],
        )(*outs)
    )
    outs[4] = jnp.swapaxes(outs[4], 0, 1)
    for i in (5, 11):
        outs[i] = jnp.swapaxes(outs[i], 1, 2)
    return tuple(outs)


def solution(mesh):
    in_specs = (
        P(None, "seq", None),
        P(None, "seq", None),
        P(None, "seq"),
        P(None, None, None, "head"),
        P(None, None, "head"),
        P(None, "head", None),
        P(None, "head", None),
        P(),
        P(),
        P(),
        P(None, None, "head"),
        P(None, "head"),
        P(None, "head", None),
    )
    out_specs = (
        P(None, "seq", None),
        P(None, "seq", None),
        P(None, None, "seq", "head"),
        P(None, None, "head"),
        P(None, "head", None),
        P(None, "head", "seq"),
        P(),
        P(),
        P(),
        P(None, "seq", "head"),
        P(None, "head"),
        P(None, "head", "seq"),
    )

    def whole(*args):
        z = Fast(mesh.shape, args[0], args[5], args[10])
        body = partial(fused, z) if z.fits() else on_device
        return jax.shard_map(
            body, mesh=mesh, in_specs=in_specs, out_specs=out_specs, check_vma=False
        )(*args)

    return whole
```

```python
from functools import partial

import jax
import jax.numpy as jnp
from jax import lax
from jax.experimental import pallas as pl
from jax.experimental.pallas import tpu as pltpu
from jax.sharding import PartitionSpec as P

LANDMARKS = 64
PINV_ITERS = 6
LAYERS = 2


exact_result = lax.Precision.HIGHEST
epsilon = 1e-05


VMEM_LIMIT = 64 * 1024 * 1024 - 128 * 1024


def extended(block, sides, width):
    for axis, dim in sides:
        count = lax.axis_size(axis)
        forward = [(i, i + 1) for i in range(count - 1)]
        backward = [(target, source) for source, target in forward]
        low = lax.ppermute(
            lax.slice_in_dim(block, block.shape[dim] - width, None, axis=dim), axis, forward
        )
        high = lax.ppermute(lax.slice_in_dim(block, 0, width, axis=dim), axis, backward)
        block = jnp.concatenate([low, block, high], axis=dim)
    return block


def layer_norm(values, scaling, offset):
    centre = jnp.mean(values, -1, keepdims=True)
    centred = values - centre
    spread = jnp.mean(centred * centred, -1, keepdims=True)
    return centred * lax.rsqrt(spread + epsilon) * scaling + offset


def soft_rows(scores):
    highest = jnp.max(scores, -1, keepdims=True)
    powers = jnp.exp(scores - highest)
    return powers / jnp.sum(powers, -1, keepdims=True)


def pseudo_inverse(weight_matrix):
    size_of = weight_matrix.shape[-1]
    column_top = jnp.max(jnp.sum(weight_matrix, axis=-2), axis=-1)[..., None, None]
    approximate_result = jnp.swapaxes(weight_matrix, -1, -2) / column_top
    identity = jnp.eye(size_of, dtype=jnp.float32)
    for repeat in range(PINV_ITERS):
        product = jnp.matmul(weight_matrix, approximate_result, precision=exact_result)
        nested = 7.0 * identity - product
        nested = 15.0 * identity - jnp.matmul(product, nested, precision=exact_result)
        nested = 13.0 * identity - jnp.matmul(product, nested, precision=exact_result)
        approximate_result = 0.25 * jnp.matmul(approximate_result, nested, precision=exact_result)
    return approximate_result


def rounded(values):
    return lax.optimization_barrier(values.astype(jnp.bfloat16)).astype(jnp.float32)


def heads_view(joined, heads_local):
    batch_count, length, channels = joined.shape
    return joined.reshape(batch_count, length, heads_local, channels // heads_local).transpose(
        0, 2, 1, 3
    )


def tokens_view(by_head):
    batch_count, heads_local, length, head_depth = by_head.shape
    return by_head.transpose(0, 2, 1, 3).reshape(batch_count, length, heads_local * head_depth)


def convolve(padded, broad_kernel_taps, length):

    def add_tap(offset, running):
        window = lax.dynamic_slice_in_dim(padded, offset, length, 1).astype(jnp.float32)
        return running + window * lax.dynamic_index_in_dim(broad_kernel_taps, offset, 0, False)

    initial = jnp.zeros((padded.shape[0], length, padded.shape[2]), jnp.float32)
    return lax.fori_loop(0, broad_kernel_taps.shape[0], add_tap, initial)


def tap_sums(padded, upstream, length, kernel):

    def one_tap(offset):
        window = lax.dynamic_slice_in_dim(padded, offset, length, 1).astype(jnp.float32)
        return jnp.sum(window * upstream, axis=(0, 1))

    return lax.map(one_tap, jnp.arange(kernel, dtype=jnp.int32))


def across_heads(summand):
    return lax.psum_scatter(
        summand.astype(jnp.bfloat16), "head", scatter_dimension=0, tiled=True
    ).astype(jnp.float32)


def rows_low(share):
    return lax.all_gather(share, "head", axis=0, tiled=True)


def rows_float(share):
    return lax.all_gather(share.astype(jnp.bfloat16), "head", axis=0, tiled=True).astype(
        share.dtype
    )


def own_rows(whole_rows):
    share = whole_rows.shape[0] // lax.axis_size("head")
    return lax.dynamic_slice_in_dim(whole_rows, lax.axis_index("head") * share, share, 0)


def spread_heads(share, dim_index):
    groups = lax.axis_size("head")
    full_shape = list(share.shape)
    full_shape[dim_index] = full_shape[dim_index] * groups
    empty = jnp.zeros(full_shape, jnp.float32)
    return lax.dynamic_update_slice_in_dim(
        empty, share, lax.axis_index("head") * share.shape[dim_index], dim_index
    )


def own_heads(whole, width, dim_index):
    return lax.dynamic_slice_in_dim(whole, lax.axis_index("head") * width, width, dim_index)


def forward_layer(hidden, weights, selector, segment):
    (
        projection,
        projection_shift,
        conv_kernel,
        output_matrix,
        output_shift,
        gain_pair,
        shift_pair,
        inner_matrix,
        inner_shift,
        outer_matrix,
    ) = weights
    batch_count, length, model_width = hidden.shape
    heads_local = conv_kernel.shape[0]
    kernel = conv_kernel.shape[1]
    margin = kernel // 2
    local_width = projection.shape[2]
    head_depth = local_width // heads_local
    scale = float(head_depth) ** (-0.25)
    hidden_low = hidden.astype(jnp.bfloat16).reshape(batch_count * length, model_width)
    projected = jnp.einsum(
        "nd,kde->kne", hidden_low, projection, preferred_element_type=jnp.float32
    )
    biases = projection_shift.astype(jnp.float32)
    query_rows = ((projected[0] + biases[0]) * scale).reshape(batch_count, length, local_width)
    key_rows = (projected[1] * scale).reshape(batch_count, length, local_width)
    value_low = (
        (projected[2] + biases[1]).astype(jnp.bfloat16).reshape(batch_count, length, local_width)
    )
    query_sums, key_sums = lax.psum(
        (
            jnp.einsum("mt,btc->bmc", selector, query_rows, precision=exact_result),
            jnp.einsum("mt,btc->bmc", selector, key_rows, precision=exact_result),
        ),
        "seq",
    )
    query_marks = heads_view(query_sums / segment, heads_local)
    key_marks = heads_view(key_sums / segment, heads_local)
    query_heads = heads_view(query_rows, heads_local)
    key_heads = heads_view(key_rows, heads_local)
    value_heads = heads_view(value_low.astype(jnp.float32), heads_local)
    mark_weights = soft_rows(
        jnp.einsum("bhme,bhne->bhmn", query_marks, key_marks, precision=exact_result)
    )
    inverse = pseudo_inverse(mark_weights)
    row_weights = soft_rows(
        jnp.einsum("bhte,bhme->bhtm", query_heads, key_marks, precision=exact_result)
    )
    key_scores = jnp.einsum("bhme,bhte->bhmt", query_marks, key_heads, precision=exact_result)
    local_top = jnp.max(key_scores, -1)
    score_top = lax.pmax(local_top, "seq")
    powers = jnp.exp(key_scores - score_top[..., None])
    neighbour_mixture = jnp.einsum("bhmt,bhte->bhme", powers, value_heads, precision=exact_result)
    score_total, mixed_joined = lax.psum(
        (jnp.sum(powers, -1), neighbour_mixture.reshape(batch_count, heads_local, -1)), "seq"
    )
    mixed_sum = mixed_joined.reshape(neighbour_mixture.shape)
    log_total = score_top + jnp.log(score_total)
    mixed = mixed_sum / score_total[..., None]
    core = jnp.einsum("bhmn,bhne->bhme", inverse, mixed, precision=exact_result)
    attended = jnp.einsum("bhtm,bhme->bhte", row_weights, core, precision=exact_result)
    padded_values = extended(value_low, (("seq", 1),), margin)
    broad_kernel_taps = jnp.repeat(conv_kernel.astype(jnp.float32), head_depth, axis=0).T
    context = tokens_view(attended) + convolve(padded_values, broad_kernel_taps, length)
    context_low = context.astype(jnp.bfloat16).reshape(batch_count * length, local_width)
    attention_share = across_heads(
        jnp.dot(context_low, output_matrix, preferred_element_type=jnp.float32)
    )
    shifts = output_shift.astype(jnp.float32)
    gains = gain_pair.astype(jnp.float32)
    offsets = shift_pair.astype(jnp.float32)
    hidden_share = own_rows(hidden.reshape(batch_count * length, model_width))
    total_first = hidden_share + attention_share + shifts[0]
    normed = layer_norm(total_first, gains[0], offsets[0])
    normed_low = rows_low(normed.astype(jnp.bfloat16))
    pre_active = jnp.dot(
        normed_low, inner_matrix, preferred_element_type=jnp.float32
    ) + inner_shift.astype(jnp.float32)
    active_low = jax.nn.gelu(pre_active, approximate=False).astype(jnp.bfloat16)
    feed_share = across_heads(jnp.dot(active_low, outer_matrix, preferred_element_type=jnp.float32))
    total_second = normed + feed_share + shifts[1]
    output = rows_float(layer_norm(total_second, gains[1], offsets[1])).reshape(hidden.shape)
    retained = (
        hidden_low,
        query_heads,
        key_heads,
        value_heads,
        padded_values,
        query_marks,
        key_marks,
        mark_weights,
        inverse,
        row_weights,
        log_total,
        mixed,
        core,
        context_low,
        total_first,
        normed_low,
        pre_active,
        active_low,
        total_second,
        broad_kernel_taps,
    )
    return (output, retained)


def backward_layer(upstream, retained, weights, selector, segment):
    (
        projection,
        projection_shift,
        conv_kernel,
        output_matrix,
        output_shift,
        gain_pair,
        shift_pair,
        inner_matrix,
        inner_shift,
        outer_matrix,
    ) = weights
    (
        hidden_low,
        query_heads,
        key_heads,
        value_heads,
        padded_values,
        query_marks,
        key_marks,
        mark_weights,
        inverse,
        row_weights,
        log_total,
        mixed,
        core,
        context_low,
        total_first,
        normed_low,
        pre_active,
        active_low,
        total_second,
        broad_kernel_taps,
    ) = retained
    batch_count, length, model_width = upstream.shape
    heads_local = conv_kernel.shape[0]
    kernel = conv_kernel.shape[1]
    margin = kernel // 2
    local_width = projection.shape[2]
    head_depth = local_width // heads_local
    scale = float(head_depth) ** (-0.25)
    gains = gain_pair.astype(jnp.float32)
    offsets = shift_pair.astype(jnp.float32)
    upstream_share = own_rows(upstream.reshape(batch_count * length, model_width))
    second_pull = jax.vjp(layer_norm, total_second, gains[1], offsets[1])[1]
    grad_second, gain_second, offset_second = second_pull(upstream_share)
    feed_low = rows_low(grad_second.astype(jnp.bfloat16))
    grad_outer = jnp.einsum("nf,nd->fd", active_low, feed_low, preferred_element_type=jnp.float32)
    grad_active = rounded(
        jnp.einsum("nd,fd->nf", feed_low, outer_matrix, preferred_element_type=jnp.float32)
    )
    gelu_pull = jax.vjp(partial(jax.nn.gelu, approximate=False), pre_active)[1]
    grad_pre_low = gelu_pull(grad_active)[0].astype(jnp.bfloat16)
    grad_inner_shift = jnp.sum(grad_pre_low.astype(jnp.float32), axis=0)
    grad_inner = jnp.einsum(
        "nd,nf->df", normed_low, grad_pre_low, preferred_element_type=jnp.float32
    )
    normed_term = jnp.einsum(
        "nf,df->nd", grad_pre_low, inner_matrix, preferred_element_type=jnp.float32
    )
    grad_normed = grad_second + across_heads(normed_term)
    first_pull = jax.vjp(layer_norm, total_first, gains[0], offsets[0])[1]
    grad_first, gain_first, offset_first = first_pull(grad_normed)
    attend_low = rows_low(grad_first.astype(jnp.bfloat16))
    grad_output = jnp.einsum(
        "nc,nd->cd", context_low, attend_low, preferred_element_type=jnp.float32
    )
    grad_context_low = (
        jnp.einsum("nd,cd->nc", attend_low, output_matrix, preferred_element_type=jnp.float32)
        .astype(jnp.bfloat16)
        .reshape(batch_count, length, local_width)
    )
    grad_context = lax.optimization_barrier(grad_context_low).astype(jnp.float32)
    padded_grads = extended(grad_context_low, (("seq", 1),), margin)
    grad_conv_values = convolve(padded_grads, broad_kernel_taps[::-1], length)
    kernel_sums = tap_sums(padded_values, grad_context, length, kernel)
    grad_kernel = kernel_sums.reshape(kernel, heads_local, head_depth).sum(-1).T
    grad_attended = heads_view(grad_context, heads_local)
    grad_row = jnp.einsum("bhte,bhme->bhtm", grad_attended, core, precision=exact_result)
    grad_core_local = jnp.einsum(
        "bhtm,bhte->bhme", row_weights, grad_attended, precision=exact_result
    )
    grad_row_scores = row_weights * (grad_row - jnp.sum(row_weights * grad_row, -1, keepdims=True))
    grad_query = jnp.einsum("bhtm,bhme->bhte", grad_row_scores, key_marks, precision=exact_result)
    grad_keymark_local = jnp.einsum(
        "bhtm,bhte->bhme", grad_row_scores, query_heads, precision=exact_result
    )
    grad_core_joined, grad_keymark_joined = lax.psum(
        (
            grad_core_local.reshape(batch_count, heads_local, -1),
            grad_keymark_local.reshape(batch_count, heads_local, -1),
        ),
        "seq",
    )
    grad_core = grad_core_joined.reshape(core.shape)
    grad_inverse = jnp.einsum("bhme,bhne->bhmn", grad_core, mixed, precision=exact_result)
    grad_mixed = jnp.einsum("bhnm,bhne->bhme", inverse, grad_core, precision=exact_result)
    grad_marks = jax.vjp(pseudo_inverse, mark_weights)[1](grad_inverse)[0]
    grad_mark_scores = mark_weights * (
        grad_marks - jnp.sum(mark_weights * grad_marks, -1, keepdims=True)
    )
    grad_querymark = jnp.einsum(
        "bhmn,bhne->bhme", grad_mark_scores, key_marks, precision=exact_result
    )
    grad_keymark = grad_keymark_joined.reshape(key_marks.shape) + jnp.einsum(
        "bhmn,bhme->bhne", grad_mark_scores, query_marks, precision=exact_result
    )
    key_scores = jnp.einsum("bhme,bhte->bhmt", query_marks, key_heads, precision=exact_result)
    key_weights = jnp.exp(key_scores - log_total[..., None])
    grad_values = jnp.einsum("bhmt,bhme->bhte", key_weights, grad_mixed, precision=exact_result)
    offset_term = jnp.sum(grad_mixed * mixed, -1)
    grad_key_scores = key_weights * (
        jnp.einsum("bhme,bhte->bhmt", grad_mixed, value_heads, precision=exact_result)
        - offset_term[..., None]
    )
    grad_key = jnp.einsum("bhmt,bhme->bhte", grad_key_scores, query_marks, precision=exact_result)
    grad_querymark_local = jnp.einsum(
        "bhmt,bhte->bhme", grad_key_scores, key_heads, precision=exact_result
    )
    grad_querymark = grad_querymark + lax.psum(
        grad_querymark_local.reshape(batch_count, heads_local, -1), "seq"
    ).reshape(query_marks.shape)
    grad_query = (
        grad_query
        + jnp.einsum("mt,bhme->bhte", selector, grad_querymark, precision=exact_result) / segment
    )
    grad_key = (
        grad_key
        + jnp.einsum("mt,bhme->bhte", selector, grad_keymark, precision=exact_result) / segment
    )
    grad_values = grad_values + heads_view(grad_conv_values, heads_local)
    query_low = (
        (tokens_view(grad_query) * scale)
        .astype(jnp.bfloat16)
        .reshape(batch_count * length, local_width)
    )
    key_low = (
        (tokens_view(grad_key) * scale)
        .astype(jnp.bfloat16)
        .reshape(batch_count * length, local_width)
    )
    value_grad_low = (
        tokens_view(grad_values).astype(jnp.bfloat16).reshape(batch_count * length, local_width)
    )
    stacked = jnp.stack([query_low, key_low, value_grad_low])
    grad_projection = jnp.einsum(
        "nd,kne->kde", hidden_low, stacked, preferred_element_type=jnp.float32
    )
    grad_projection_shift = jnp.stack(
        [
            jnp.sum(query_low.astype(jnp.float32), axis=0),
            jnp.sum(value_grad_low.astype(jnp.float32), axis=0),
        ]
    )
    input_term = jnp.einsum("kne,kde->nd", stacked, projection, preferred_element_type=jnp.float32)
    grad_hidden = rows_float(grad_first + across_heads(input_term)).reshape(upstream.shape)
    gradients = (
        grad_projection,
        grad_projection_shift,
        grad_kernel,
        grad_output,
        jnp.stack([jnp.sum(grad_first, axis=0), jnp.sum(grad_second, axis=0)]),
        jnp.stack([gain_first, gain_second]),
        jnp.stack([offset_first, offset_second]),
        grad_inner,
        grad_inner_shift,
        grad_outer,
    )
    return (grad_hidden, gradients)


def on_device(
    tokens,
    cotangent,
    masked,
    projections,
    projection_bias,
    conv_taps,
    output_weight,
    output_bias,
    norm_gain,
    norm_shift,
    inner_weight,
    inner_bias,
    outer_weight,
):
    length = tokens.shape[1]
    segment = length * lax.axis_size("seq") // LANDMARKS
    position = lax.axis_index("seq") * length + jnp.arange(length, dtype=jnp.int32)
    selector = (
        position[None, :] // segment == jnp.arange(LANDMARKS, dtype=jnp.int32)[:, None]
    ).astype(jnp.float32)
    arrays = (
        projections,
        projection_bias,
        conv_taps,
        output_weight,
        output_bias,
        norm_gain,
        norm_shift,
        inner_weight,
        inner_bias,
        outer_weight,
    )
    hidden = tokens.astype(jnp.float32)
    stored = []
    for layer_number in range(LAYERS):
        weights = tuple((tensor[layer_number] for tensor in arrays))
        hidden, retained = forward_layer(hidden, weights, selector, segment)
        stored.append((weights, retained))
    upstream = cotangent.astype(jnp.float32) * masked.astype(jnp.float32)[:, :, None]
    layer_grads = [None] * LAYERS
    for layer_number in range(LAYERS - 1, -1, -1):
        weights, retained = stored[layer_number]
        upstream, gradients = backward_layer(upstream, retained, weights, selector, segment)
        larger = (
            lax.psum_scatter(gradients[0], "seq", scatter_dimension=1, tiled=True),
            lax.psum_scatter(gradients[3], "seq", scatter_dimension=1, tiled=True),
            lax.psum_scatter(gradients[7], "seq", scatter_dimension=0, tiled=True),
            lax.psum_scatter(gradients[9], "seq", scatter_dimension=1, tiled=True),
        )
        gradients = (
            larger[0],
            gradients[1],
            gradients[2],
            larger[1],
            gradients[4],
            gradients[5],
            gradients[6],
            larger[2],
            gradients[8],
            larger[3],
        )
        layer_grads[layer_number] = gradients
    stacked = tuple(
        (
            jnp.stack([layer_grads[layer_number][member] for layer_number in range(LAYERS)])
            for member in range(10)
        )
    )
    larger = (stacked[0], stacked[3], stacked[7], stacked[9])
    bias_width = stacked[1].shape[2]
    taps_width = stacked[2].shape[1]
    inner_width = stacked[8].shape[1]
    smaller = lax.psum(
        (
            spread_heads(stacked[1], 2),
            spread_heads(stacked[2], 1),
            stacked[4],
            stacked[5],
            stacked[6],
            spread_heads(stacked[8], 1),
        ),
        ("seq", "head"),
    )
    grad_bias_share = own_heads(smaller[0], bias_width, 2)
    grad_taps_share = own_heads(smaller[1], taps_width, 1)
    grad_inner_share = own_heads(smaller[5], inner_width, 1)
    return (
        hidden,
        upstream,
        larger[0],
        grad_bias_share,
        grad_taps_share,
        larger[1],
        smaller[2],
        smaller[3],
        smaller[4],
        larger[2],
        grad_inner_share,
        larger[3],
    )


F32 = jnp.float32
BF16 = jnp.bfloat16
MESH = pl.DeviceIdType.MESH


def nn(a, b):
    return lax.dot_general(a, b, (((1,), (0,)), ((), ())), preferred_element_type=F32)


def nt(a, b):
    return lax.dot_general(a, b, (((1,), (1,)), ((), ())), preferred_element_type=F32)


def tn(a, b):
    return lax.dot_general(a, b, (((0,), (0,)), ((), ())), preferred_element_type=F32)


def halves(x):
    high = x.astype(BF16)
    return high, (x - high.astype(F32)).astype(BF16)


def left3(pair, axis):
    return jnp.concatenate([pair[0], pair[1], pair[0]], axis=axis)


def right3(pair, axis):
    return jnp.concatenate([pair[0], pair[0], pair[1]], axis=axis)


def nn3(a, b):
    return nn(left3(a, 1), right3(b, 0))


def nt3(a, b):
    return nt(left3(a, 1), right3(b, 1))


def tn3(a, b):
    return tn(left3(a, 0), right3(b, 0))


def nn3f(a, b):
    return nn3(halves(a), halves(b))


def nt3f(a, b):
    return nt3(halves(a), halves(b))


def tn3f(a, b):
    return tn3(halves(a), halves(b))


class Fast:
    def __init__(self, mesh_shape, tokens, conv_taps, inner_weight):
        self.n = mesh_shape["seq"]
        self.heads = mesh_shape["head"]
        self.batch, whole, self.width = tokens.shape
        self.length = whole // self.n
        self.layers, all_heads, self.kernel = conv_taps.shape
        self.local_heads = all_heads // self.heads
        self.depth = self.width // all_heads
        self.cols = self.local_heads * self.depth
        self.hidden = inner_weight.shape[2] // self.heads
        self.rows = self.batch * self.length
        self.segment = whole // LANDMARKS
        self.spans = self.length // self.segment
        self.units = self.batch * self.local_heads // 2
        self.bits = self.n.bit_length() - 1

    def fits(self):
        return (
            self.n == 1 << self.bits
            and self.n >= 16
            and self.heads == 2
            and self.length == 128
            and self.batch == 2
            and self.spans * self.batch == 8
            and self.depth == 64
            and self.local_heads % 2 == 0
            and self.width % (16 * self.n) == 0
            and self.width % 256 == 0
            and self.hidden % 512 == 0
            and self.kernel == 65
            and self.layers == 2
            and LANDMARKS == 64
        )


def fused_kernel(
    z,
    tok_hbm, cot_hbm, mask_hbm, pbias_hbm, taps_hbm, obias_hbm, ngain_hbm, nshift_hbm, ibias_hbm,
    wp_hbm, wo_hbm, wi_hbm, wf_hbm,
    result, gtok, gproj, gbias, gtaps, gout, gobias, ggain, gshift, ginner, gibias, gouter,
    *,
    tok, cot, mask, pbias, taps, obias, ngain, nshift, ibias, WP, WO, WI, WF,
    QS, KS, VX, RW, CTX, T1, T2, GP, ACT, QM, KM, CR, MX, PA, PV, PZ, PC, LTH, LTN,
    HID, UP, LOW, PN, PF, DPRE, GXS, DQ, DK, DV, DP, DQM, DKM, DR, SM, TB, TT, TR, LTF, LTA,
    LSH, OP, OO, OI, OU, OS, OT, OB1, OT1,
    MS, MB, MD, MO, XM, OB, SB, SR, HS, HR, SMR, SMT,
    G, RV,
    isem, wsem, hsem_s, hsem_r, msem_s, msem_r, dsem_s, dsem_r, xsem_s, xsem_r, csem_s, csem_r, vsem_s, vsem_r,
    osem, asem_s, asem_r, bsem_s, bsem_r, gsem_s, gsem_r, qsem_s, qsem_r, ssem_s, ssem_r, tsem_s, tsem_r,
):
    n, B, L, R, D, C, F = z.n, z.batch, z.length, z.rows, z.width, z.cols, z.hidden
    U, NP, S, K = z.units, z.local_heads // 2, z.spans, z.kernel
    CH = D // n
    NB = z.bits
    M = LANDMARKS
    margin = K // 2
    scale = float(z.depth) ** (-0.25)
    me = lax.axis_index("seq")
    core = lax.axis_index("head")
    first_owner = n // 2 - U // 2
    is_owner = jnp.logical_and(me >= first_owner, me < first_owner + U)
    mine = jnp.clip(me - first_owner, 0, U - 1)

    def weight_copies(l):
        return [
            pltpu.make_async_copy(wp_hbm.at[l], WP.at[l], wsem.at[l, 0]),
            pltpu.make_async_copy(wo_hbm.at[l], WO.at[l], wsem.at[l, 1]),
            pltpu.make_async_copy(wi_hbm.at[l], WI.at[l], wsem.at[l, 2]),
            pltpu.make_async_copy(wf_hbm.at[l], WF.at[l], wsem.at[l, 3]),
        ]

    arguments = [
        pltpu.make_async_copy(src, dst, isem.at[i])
        for i, (src, dst) in enumerate(
            [
                (tok_hbm, tok), (pbias_hbm, pbias), (taps_hbm, taps), (obias_hbm, obias), (ngain_hbm, ngain),
                (nshift_hbm, nshift), (ibias_hbm, ibias), (cot_hbm, cot), (mask_hbm, mask),
            ]
        )
    ]
    arguments[0].start()
    weight_copies(0)[0].start()
    for c in arguments[1:]:
        c.start()

    barrier = pltpu.get_barrier_semaphore()

    def greet(d, _):
        pl.semaphore_signal(
            barrier, inc=1, device_id={"seq": lax.rem(me + d, n)}, device_id_type=MESH
        )
        return 0

    lax.fori_loop(1, n, greet, 0)
    pl.semaphore_signal(barrier, inc=1, device_id={"head": 1 - core}, device_id_type=MESH)

    row_id = lax.broadcasted_iota(jnp.int32, (128, 128), 0)
    lane_id = lax.broadcasted_iota(jnp.int32, (128, 128), 1)
    low_lane = lane_id < 64
    low_lane64 = low_lane[0:64]
    same_head = (row_id < 64) == low_lane
    eye = row_id == lane_id
    flip = jnp.where(row_id + lane_id == 127, 1.0, 0.0).astype(BF16)

    def expand(c):
        return jnp.concatenate(
            [jnp.where(low_lane64, c, 0.0), jnp.where(low_lane64, 0.0, c)], axis=0
        )

    def expand_low(c):
        return expand(c.astype(F32)).astype(BF16)

    def compress(x):
        return jnp.where(low_lane64, x[0:64], x[64:128])

    def to_row(col):
        return jnp.sum(jnp.where(eye, col, 0.0), axis=0, keepdims=True)

    def to_col(row):
        return jnp.sum(jnp.where(eye, row, 0.0), axis=1, keepdims=True)

    def half_sums(x):
        a = jnp.sum(jnp.where(low_lane, x, 0.0), axis=1, keepdims=True)
        b = jnp.sum(jnp.where(low_lane, 0.0, x), axis=1, keepdims=True)
        return jnp.where(low_lane, a, b)

    def half_tops(x):
        a = jnp.max(jnp.where(low_lane, x, -jnp.inf), axis=1, keepdims=True)
        b = jnp.max(jnp.where(low_lane, -jnp.inf, x), axis=1, keepdims=True)
        return jnp.where(low_lane, a, b)

    def parts3(x):
        a = x.astype(BF16)
        rest = x - a.astype(F32)
        b = rest.astype(BF16)
        c = (rest - b.astype(F32)).astype(BF16)
        return jnp.concatenate([a.astype(F32), b.astype(F32), c.astype(F32)], axis=0)

    def pack(body, rows):
        tail = jnp.concatenate([parts3(r) for r in rows], axis=0)
        fill = jnp.zeros((16 - tail.shape[0], 128), F32)
        return jnp.concatenate([body, tail, fill], axis=0).astype(BF16)

    def packed_row(message, i):
        x = message[64 + 3 * i : 67 + 3 * i].astype(F32)
        return jnp.sum(x, axis=0, keepdims=True)

    def unit(u):
        return u // NP, u % NP

    def tile(ref, l, u):
        b, j = unit(u)
        return ref[l, b * L : (b + 1) * L, j * 128 : (j + 1) * 128]

    def moments(x):
        centre = jnp.mean(x, -1, keepdims=True)
        centred = x - centre
        spread = jnp.mean(centred * centred, -1, keepdims=True)
        inverse = lax.rsqrt(spread + epsilon)
        return centred * inverse, inverse

    def norm_back(x, grad, gain):
        hat, inverse = moments(x)
        g = grad * gain
        a = jnp.mean(g, -1, keepdims=True)
        b = jnp.mean(g * hat, -1, keepdims=True)
        total = inverse * (g - a - hat * b)
        sums = (
            jnp.sum(grad * hat, axis=0, keepdims=True),
            jnp.sum(grad, axis=0, keepdims=True),
            jnp.sum(total, axis=0, keepdims=True),
        )
        return total, sums

    def put_small(start, vector):
        for i in range(vector.shape[1] // 128):
            SM[start + i : start + i + 1, :] = vector[:, i * 128 : (i + 1) * 128]

    PARTS = D // 256

    def swap_part(e, i):
        at = (e % 2, pl.ds(0, R), pl.ds(i * 256, 256))
        return pltpu.make_async_remote_copy(
            HS.at[at], HR.at[at], hsem_s.at[e, i], hsem_r.at[e, i],
            device_id={"head": 1 - core}, device_id_type=MESH,
        )

    def swap_start(e, part):
        for i in range(PARTS):
            o = slice(i * 256, (i + 1) * 256)
            HS[e % 2, :, o] = part(o).astype(BF16)
            swap_part(e, i).start()

    def swap_wait(e):
        for i in range(PARTS):
            swap_part(e, i).wait()

    def both(e):
        return HS[e % 2].astype(F32) + HR[e % 2].astype(F32)

    own_bits = [lax.rem(me // (1 << k), 2) for k in range(NB)]

    def peer_across(d):
        return me + sum((1 - 2 * own_bits[k]) * (1 << k) for k in range(NB) if d >> k & 1)

    others = range(n - 1, 0, -1)

    def spread(src, dst, ss, rs, start):
        def copy(d, to):
            return pltpu.make_async_remote_copy(
                src(peer_across(d)), dst.at[to], ss.at[d], rs.at[d],
                device_id={"seq": peer_across(d)}, device_id_type=MESH,
            )

        if start:
            for d in others:
                copy(d, me).start()
        else:
            for d in others:
                copy(d, peer_across(d)).wait_recv()
            for d in others:
                copy(d, peer_across(d)).wait_send()

    def to_owner_copy(u, src, dst, ss, rs):
        return pltpu.make_async_remote_copy(
            src, dst.at[me], ss.at[u], rs.at[me], device_id={"seq": first_owner + u}, device_id_type=MESH
        )

    def to_owner(u, src, dst, ss, rs):
        @pl.when(me != first_owner + u)
        def _():
            to_owner_copy(u, src, dst, ss, rs).start()

        @pl.when(me == first_owner + u)
        def _():
            dst[me] = src[...]

    def to_owner_sent(u, src, dst, ss, rs):
        @pl.when(me != first_owner + u)
        def _():
            to_owner_copy(u, src, dst, ss, rs).wait_send()

    def owner_gets(src, dst, ss, rs):
        def step(d, _):
            t = lax.rem(me + d, n)
            pltpu.make_async_remote_copy(
                src, dst.at[t], ss.at[0], rs.at[t], device_id={"seq": t}, device_id_type=MESH
            ).wait_recv()
            return 0

        lax.fori_loop(1, n, step, 0)

    def from_owner(slots, ss, rs, start):
        for d in others:
            c = pltpu.make_async_remote_copy(
                slots.at[mine], slots.at[mine], ss.at[d], rs.at[mine],
                device_id={"seq": peer_across(d)}, device_id_type=MESH,
            )
            if start:
                c.start()
            else:
                c.wait_send()

    def owner_came(slots, u, ss, rs):
        @pl.when(me != first_owner + u)
        def _():
            pltpu.make_async_remote_copy(
                slots.at[u], slots.at[u], ss.at[0], rs.at[u],
                device_id={"seq": first_owner + u}, device_id_type=MESH,
            ).wait_recv()

    def edges(buf, ss, rs, act):
        after = pltpu.make_async_remote_copy(
            buf.at[:, pl.ds(L, margin)], buf.at[:, pl.ds(0, margin)], ss.at[0], rs.at[0],
            device_id={"seq": lax.rem(me + 1, n)}, device_id_type=MESH,
        )
        before = pltpu.make_async_remote_copy(
            buf.at[:, pl.ds(margin, margin)], buf.at[:, pl.ds(margin + L, margin)], ss.at[1], rs.at[1],
            device_id={"seq": lax.rem(me + n - 1, n)}, device_id_type=MESH,
        )
        if act == "start":
            @pl.when(me < n - 1)
            def _():
                after.start()

            @pl.when(me > 0)
            def _():
                before.start()
        else:
            @pl.when(me < n - 1)
            def _():
                after.wait_send()
                before.wait_recv()

            @pl.when(me > 0)
            def _():
                before.wait_send()
                after.wait_recv()

    def edge_zeros(buf):
        none = jnp.zeros((B, margin, C), BF16)
        buf[:, 2 * margin + L :, :] = jnp.zeros((B, 256 - L - 2 * margin, C), BF16)

        @pl.when(me == 0)
        def _():
            buf[:, 0:margin, :] = none

        @pl.when(me == n - 1)
        def _():
            buf[:, margin + L : 2 * margin + L, :] = none

    def conv(bands, buf, u):
        b, j = unit(u)
        x = buf[b, :, j * 128 : (j + 1) * 128]
        return jnp.where(low_lane, nn(bands[2 * j], x), nn(bands[2 * j + 1], x))

    DT, FL = HID, LOW
    dims = [[k for k in reversed(range(NB)) if k != g] for g in range(2)]
    FH = F // 2
    HALF = G.shape[-1]
    everything = pl.ds(0, 2)
    items = {"outer": (0, FH), "inner": (FH, FH), "outval": (2 * FH, C), "keyed": (2 * FH + C, C)}
    item_index = {name: i for i, name in enumerate(items)}

    def peer_of(k):
        return me + (1 - 2 * own_bits[k]) * (1 << k)

    def pair_copy(l, i, g, src, dst):
        return pltpu.make_async_remote_copy(
            src, dst, asem_s.at[l, i, g], asem_r.at[l, i, g],
            device_id={"seq": peer_of(g)}, device_id_type=MESH,
        )

    def right_copies(l, i, ref, ranges):
        return [
            pair_copy(l, i, g, ref.at[pl.ds(0, R), pl.ds(c0, cn)], ref.at[pl.ds(R, R), pl.ds(c0, cn)])
            for g, (c0, cn) in enumerate(ranges)
        ]

    def left_copies(l, i, stage, gathered):
        got = []
        for g in range(2):
            at = [core] + [everything] * (NB - 1)
            at[NB - 1 - g] = 1 - own_bits[g]
            src = stage.at[tuple(at) + (pl.ds(0, CH), pl.ds(0, R))]
            dst = gathered.at[(g, core) + (everything,) * (NB - 2) + (pl.ds(0, CH), pl.ds(R, R))]
            got.append(pair_copy(l, i, g, src, dst))
        return got

    def core_copy(l, i, g, ref):
        return pltpu.make_async_remote_copy(
            ref, ref, bsem_s.at[l, i, g], bsem_r.at[l, i, g],
            device_id={"head": 1 - core}, device_id_type=MESH,
        )

    def left_hand_on(l, i, gathered):
        return [
            core_copy(l, i, g, gathered.at[(g, core) + (everything,) * (NB - 2) + (pl.ds(0, CH), pl.ds(R, R))])
            for g in range(2)
        ]

    def row_copies(l, i, src, dst):
        at = pl.ds(pl.multiple_of(core * L, L), L)
        return [pair_copy(l, i, g, src.at[at], dst.at[g, at]) for g in range(2)]

    def row_hand_on(l, i, dst):
        at = pl.ds(pl.multiple_of(core * L, L), L)
        return [core_copy(l, i, g, dst.at[g, at]) for g in range(2)]

    def each_half(g, act):
        for code in range(n // 2):
            spot = tuple((code >> (NB - 2 - i)) & 1 for i in range(NB - 1))
            at = list(spot)
            at.insert(NB - 1 - g, own_bits[g])
            act((g,) + spot, tuple(at))

    def left_put(x, stage, gathered):
        stage[...] = x.T.reshape(stage.shape)
        for g in range(2):
            def put(to, at):
                gathered[to + (slice(None), slice(0, R))] = stage[at]

            each_half(g, put)

    def left_put_theirs(rows, stage, gathered):
        for g in range(2):
            stage[...] = rows[g].T.reshape(stage.shape)

            def put(to, at):
                gathered[to + (slice(None), slice(R, 2 * R))] = stage[at]

            each_half(g, put)

    def start_all(copies):
        for c in copies:
            c.start()

    def wait_all(copies):
        for c in copies:
            c.wait()

    def weight_grad(g, left, right, first, count, width):
        def step(i, _):
            o = pl.multiple_of(i * width, width)
            x = nn(left[g].reshape(D // 2, 2 * R), right(o)).astype(BF16)
            o = pl.multiple_of(first + o, 128)
            for code in range(n // 2):
                spot = tuple((code >> (NB - 2 - i)) & 1 for i in range(NB - 1))
                G[(g,) + spot + (slice(None), pl.ds(o, width))] = x[code * CH : (code + 1) * CH]
            return 0

        lax.fori_loop(0, count // width, step, 0)

    STAGES = NB - 1

    def rs_copy(l, name, g, stage):
        first, count = items[name]
        cols = (pl.ds(0, CH), pl.ds(first, count))
        d = NB - 2 - stage
        index = [everything] * d + [1 - own_bits[dims[g][d]]] + [own_bits[k] for k in dims[g][d + 1 :]]
        i = item_index[name]
        return pltpu.make_async_remote_copy(
            G.at[(g,) + tuple(index) + cols], RV[stage].at[(l, g) + (everything,) * d + cols],
            gsem_s.at[l, i, g, stage], gsem_r.at[l, i, g, stage],
            device_id={"seq": peer_of(dims[g][d])}, device_id_type=MESH,
        )

    def rs_start(l, name, stage):
        for g in range(2):
            rs_copy(l, name, g, stage).start()

    def rs_add(l, name, stage):
        first, count = items[name]
        for g in range(2):
            rs_copy(l, name, g, stage).wait()
            d = NB - 2 - stage
            mine_at = tuple(own_bits[k] for k in dims[g][d:])
            cols = (slice(None), slice(first, first + count))
            if d:
                for code in range(1 << d):
                    spot = tuple((code >> (d - 1 - i)) & 1 for i in range(d))
                    at = (g,) + spot + mine_at + cols
                    G[at] = G[at] + RV[stage][(l, g) + spot + cols]
            else:
                x = G[(g,) + mine_at + cols].astype(F32) + RV[stage][(l, g) + cols].astype(F32)
                write_out(l, name, g, x)

    def write_out(l, name, g, x):
        if name == "outer":
            OU[l, :, g * FH : (g + 1) * FH] = x
        elif name == "inner":
            OI[l, :, g * FH : (g + 1) * FH] = x
        elif name == "keyed":
            OP[l, g] = x
        elif g == 0:
            OO[l, :, 0:128] = x[:, 0:128]
            OP[l, 2, :, 0 : C - 128] = x[:, 128:C]
        else:
            OO[l, :, 128:C] = x[:, 0 : C - 128]
            OP[l, 2, :, C - 128 : C] = x[:, C - 128 : C]

    def out_copy(i, src, dst):
        return pltpu.make_async_copy(src, dst, osem.at[i])

    def advance(l, name, stage):
        rs_add(l, name, stage)
        if stage + 1 < STAGES:
            rs_start(l, name, stage + 1)

    out_ranges = ((0, 128), (128, C - 128))
    val_ranges = ((2 * C, C - 128), (3 * C - 128, 128))
    key_ranges = ((0, C), (C, C))
    ffn_ranges = ((0, FH), (FH, FH))

    arguments[0].wait()
    for b in range(B):
        HID[b * L : (b + 1) * L, :] = tok[b].astype(F32)
    TB[...] = jnp.zeros_like(TB)

    def make_bands(l):
        backwards = jnp.where(row_id + lane_id == K - 1, 1.0, 0.0).astype(BF16)
        for h in range(z.local_heads):
            TB[0, h : h + 1, 0:K] = taps[h].astype(F32)[l : l + 1]
        TB[1, :, 0:128] = nn(TB[0, :, 0:128].astype(BF16), backwards)
        for which, store in ((0, TT), (1, TR)):
            for h in range(z.local_heads):
                base = jnp.broadcast_to(TB[which, h : h + 1, :], (128, 256))
                store[l, h] = pltpu.roll(base, 0, 1, stride=1, stride_axis=0).astype(BF16)

    def regrow(l):
        wait_all(row_hand_on(l, 2, PN))
        left_put_theirs(PN, LSH, LTN.at[l])
        for g in range(2):
            def step(i, _):
                o = pl.ds(pl.multiple_of(g * FH + i * 256, 256), 256)
                act, slope = unit_rows(PN[g], l, o)
                ACT[l, R : 2 * R, o] = act
                GP[l, R : 2 * R, o] = slope
                return 0

            lax.fori_loop(0, FH // 256, step, 0)

    def unit_rows(rows, l, o):
        pre = nn(rows, WI[l, :, o]) + ibias[l : l + 1, o].astype(F32)
        below = 0.5 * (1.0 + lax.erf(pre * (0.5**0.5)))
        slope = below + pre * jnp.exp(-0.5 * pre * pre) * 0.3989422804014327
        return (pre * below).astype(BF16), slope.astype(BF16)

    def forward(l):
        copies = weight_copies(l)
        e = 2 * l
        LOW[...] = HID[...].astype(BF16)
        copies[0].wait()
        if l == 0:
            for c in [weight_copies(0)[i] for i in (1, 2, 3)] + weight_copies(1):
                c.start()
            for c in arguments[1:]:
                c.wait()
        both_bias = pbias[l].astype(F32)
        bias_q, bias_v = both_bias[0:1], both_bias[1:2]
        q = (nn(LOW[...], WP[l, 0]) + bias_q) * scale
        k = nn(LOW[...], WP[l, 1]) * scale
        QS[l] = q.astype(BF16)
        KS[l] = k.astype(BF16)
        sums = []
        for x in (q, k):
            for b in range(B):
                for r in range(S):
                    at = b * L + r * z.segment
                    sums.append(jnp.sum(x[at : at + z.segment], axis=0, keepdims=True))
        marks = jnp.concatenate(sums, axis=0) * (1.0 / z.segment)
        MS[...] = marks.astype(BF16)
        rest = marks - MS[...].astype(F32)
        middle = rest.astype(BF16).astype(F32)
        rest = rest - middle
        for u in range(U):
            b, j = unit(u)
            parts = [
                x[first + b * S : first + (b + 1) * S, j * 128 : (j + 1) * 128]
                for x in (middle, rest)
                for first in (0, 8)
            ]
            MD[u] = jnp.concatenate(parts, axis=0).astype(BF16)
        if l == 0:
            pl.semaphore_wait(barrier, n)
        spread(lambda t: MS, MB, msem_s.at[l], msem_r.at[l], True)
        for u in range(U):
            to_owner(u, MD.at[u], MO, dsem_s.at[l], dsem_r.at[l])
        MB[me] = MS[...]
        vl = (nn(LOW[...], WP[l, 2]) + bias_v).astype(BF16)
        for b in range(B):
            VX[l, b, margin : margin + L, :] = vl[b * L : (b + 1) * L]
        edge_zeros(VX.at[l])
        edges(VX.at[l], vsem_s.at[l], vsem_r.at[l], "start")
        if l:
            regrow(l - 1)
        left_put(LOW[...], LSH, LTH.at[l])
        make_bands(l)
        edges(VX.at[l], vsem_s.at[l], vsem_r.at[l], "wait")
        for u in range(U):
            b, j = unit(u)
            DQ[b * L : (b + 1) * L, j * 128 : (j + 1) * 128] = conv(TT.at[l], VX.at[l], u)
        spread(lambda t: MS, MB, msem_s.at[l], msem_r.at[l], False)
        hidden_copies = left_copies(l, 0, LSH, LTH.at[l])
        start_all(hidden_copies)
        for u in range(U):
            b, j = unit(u)
            lanes = slice(j * 128, (j + 1) * 128)
            for first, store in ((0, QM), (8, KM)):
                rows = [MB[i, :, lanes].astype(F32)[first + b * S : first + (b + 1) * S] for i in range(n)]
                store[l, u] = jnp.concatenate(rows, axis=0)
        for u in range(U):
            b, j = unit(u)
            ksc = nt(expand(QM[l, u]).astype(BF16), tile(KS, l, u))
            top = jnp.max(ksc, axis=1, keepdims=True)
            p = jnp.exp(ksc - top)
            total = jnp.sum(p, axis=1, keepdims=True)
            v = VX[l, b, margin : margin + L, j * 128 : (j + 1) * 128]
            XM[u] = pack(compress(nn(p.astype(BF16), v)), [to_row(top), to_row(total)])
            to_owner(u, XM.at[u], OB, xsem_s.at[l], xsem_r.at[l])
        @pl.when(is_owner)
        def _():
            owner_gets(MD.at[0], MO, dsem_s.at[l], dsem_r.at[l])
            extra = []
            for i in range(n):
                x = MO[i].astype(F32)
                extra.append(x[0:8] + x[8:16])
            qb = expand(QM[l, mine] + jnp.concatenate([x[0:S] for x in extra], axis=0))
            kb = expand(KM[l, mine] + jnp.concatenate([x[S : 2 * S] for x in extra], axis=0))
            s = lax.dot_general(
                qb, kb, (((1,), (1,)), ((), ())), precision=exact_result, preferred_element_type=F32
            )
            s = jnp.where(same_head, s, -jnp.inf)
            p = jnp.exp(s - jnp.max(s, axis=1, keepdims=True))
            a = p / jnp.sum(p, axis=1, keepdims=True)
            PA[l] = a
            ah = halves(a)
            at = a.T
            sums = jnp.sum(a, axis=0, keepdims=True)
            tops = jnp.where(
                low_lane[0:1],
                jnp.max(jnp.where(low_lane[0:1], sums, 0.0), axis=1, keepdims=True),
                jnp.max(jnp.where(low_lane[0:1], 0.0, sums), axis=1, keepdims=True),
            )
            unit_matrix = jnp.where(eye, 1.0, 0.0)

            def iterate(i, zk):
                PV[l, i, 0] = zk
                PV[l, i, 4] = zk.T
                zh = halves(zk)
                pr = nn3(ah, zh)
                PV[l, i, 1] = pr
                prh = halves(pr)
                n2 = 15.0 * unit_matrix - nn3(prh, halves(7.0 * unit_matrix - pr))
                PV[l, i, 2] = n2
                n3 = 13.0 * unit_matrix - nn3(prh, halves(n2))
                PV[l, i, 3] = n3
                return 0.25 * nn3(zh, halves(n3))

            zk = lax.fori_loop(0, PINV_ITERS, iterate, at / tops)
            PZ[l] = zk.T
            owner_gets(XM.at[0], OB, xsem_s.at[l], xsem_r.at[l])
            stats = [OB[i, 64:80].astype(F32) for i in range(n)]
            tops = jnp.concatenate([jnp.sum(x[0:3], axis=0, keepdims=True) for x in stats], axis=0)
            totals = jnp.concatenate([jnp.sum(x[3:6], axis=0, keepdims=True) for x in stats], axis=0)
            top = jnp.max(tops, axis=0, keepdims=True)
            factors = jnp.exp(tops - top)
            total = jnp.sum(factors * totals, axis=0, keepdims=True)
            shares = halves(factors / total)
            device = lax.broadcasted_iota(jnp.int32, (n, n * 128), 0)
            place = lax.broadcasted_iota(jnp.int32, (n, n * 128), 1) // 128
            pick = jnp.where(device == place, 1.0, 0.0).astype(BF16)
            columns = tn(shares[0], pick) + tn(shares[1], pick)
            mixed = jnp.zeros((64, 128), F32)
            for i in range(n):
                share = compress(columns[:, i * 128 : (i + 1) * 128])
                mixed = mixed + share * OB[i, 0:64].astype(F32)
            MX[l] = mixed
            CR[l, mine] = pack(compress(nn3f(zk, expand(mixed))), [top + jnp.log(total)])
            from_owner(CR.at[l], csem_s.at[l], csem_r.at[l], True)

        for u in range(U):
            s = nt(tile(QS, l, u), expand(KM[l, u]).astype(BF16))
            p = jnp.exp(s - half_tops(s))
            RW[l, u] = p / half_sums(p)

        wait_all(hidden_copies)
        start_all(left_hand_on(l, 0, LTH.at[l]))
        for u in range(U):
            b, j = unit(u)
            to_owner_sent(u, XM.at[u], OB, xsem_s.at[l], xsem_r.at[l])
            to_owner_sent(u, MD.at[u], MO, dsem_s.at[l], dsem_r.at[l])
            owner_came(CR.at[l], u, csem_s.at[l], csem_r.at[l])
            at = (slice(b * L, (b + 1) * L), slice(j * 128, (j + 1) * 128))
            context = nn(RW[l, u].astype(BF16), expand_low(CR[l, u, 0:64])) + DQ[at]
            CTX[(l,) + at] = context.astype(BF16)
        start_all(right_copies(l, 1, CTX.at[l], out_ranges))

        @pl.when(is_owner)
        def _():
            from_owner(CR.at[l], csem_s.at[l], csem_r.at[l], False)

        copies[1].wait()
        swap_start(e, lambda o: nn(CTX[l, 0:R], WO[l, :, o]))
        swap_wait(e)
        total1 = HID[...] + both(e) + obias[l].astype(F32)[0:1]
        T1[l] = total1
        normed = moments(total1)[0] * ngain[l].astype(F32)[0:1] + nshift[l].astype(F32)[0:1]
        HID[...] = normed
        LOW[...] = normed.astype(BF16)
        norm_copies = row_copies(l, 2, LOW, PN)
        start_all(norm_copies)
        copies[2].wait()

        def grow(i, _):
            o = pl.ds(pl.multiple_of(i * 256, 256), 256)
            act, slope = unit_rows(LOW[...], l, o)
            ACT[l, 0:R, o] = act
            GP[l, 0:R, o] = slope
            return 0

        lax.fori_loop(0, F // 256, grow, 0)
        copies[3].wait()

        swap_start(e + 1, lambda o: nn(ACT[l, 0:R], WF[l, :, o]))
        left_put(LOW[...], LSH, LTN.at[l])
        swap_wait(e + 1)
        total2 = HID[...] + both(e + 1) + obias[l].astype(F32)[1:2]
        T2[l] = total2
        HID[...] = moments(total2)[0] * ngain[l].astype(F32)[1:2] + nshift[l].astype(F32)[1:2]
        wait_all(norm_copies)
        start_all(row_hand_on(l, 2, PN))

    def backward(l, slots):
        GX = GXS.at[l]

        def slot(name):
            for step in slots.get(name, ()):
                advance(z.layers - 1, *step)

        e = 2 * z.layers + 2 * (z.layers - 1 - l)
        k = z.layers + l
        base = 60 * l
        total2, sums = norm_back(T2[l], UP[...], ngain[l].astype(F32)[1:2])
        put_small(base + 6, sums[0])
        put_small(base + 18, sums[1])
        put_small(base + 30, sums[2])
        DT[...] = total2
        FL[...] = total2.astype(BF16)
        feed_copies = row_copies(l, 4, FL, PF)
        start_all(feed_copies)
        slot("fed")

        def widen(i, _):
            o = pl.ds(pl.multiple_of(i * 256, 256), 256)
            grad = nt(FL[...], WF[l, o, :]).astype(BF16).astype(F32)
            pre = (GP[l, 0:R, o].astype(F32) * grad).astype(BF16)
            DPRE[0:R, o] = pre
            s = jnp.sum(pre.astype(F32), axis=0, keepdims=True)
            SM[pl.ds(base + 36 + 2 * i, 1), :] = s[:, 0:128]
            SM[pl.ds(base + 37 + 2 * i, 1), :] = s[:, 128:256]
            return 0

        lax.fori_loop(0, F // 256, widen, 0)
        slot("widened")
        swap_start(e, lambda o: nt(DPRE[0:R], WI[l, o, :]))
        slot("narrowed")
        left_put(FL[...], LSH, LTF)
        if l == z.layers - 1:
            regrow(l)
        wait_all(feed_copies)
        start_all(row_hand_on(l, 4, PF))
        swap_wait(e)
        grad_normed = DT[...] + both(e)
        total1, sums = norm_back(T1[l], grad_normed, ngain[l].astype(F32)[0:1])
        put_small(base + 0, sums[0])
        put_small(base + 12, sums[1])
        put_small(base + 24, sums[2])
        DT[...] = total1
        FL[...] = total1.astype(BF16)
        grads = nt(FL[...], WO[l]).astype(BF16)
        for b in range(B):
            GX[b, margin : margin + L, :] = grads[b * L : (b + 1) * L]
        edge_zeros(GX)
        edges(GX, vsem_s.at[k], vsem_r.at[k], "start")

        def g_tile(u):
            b, j = unit(u)
            return GX[b, margin : margin + L, j * 128 : (j + 1) * 128]

        for u in range(U):
            XM[u, 0:64] = compress(tn(RW[l, u].astype(BF16), g_tile(u))).astype(BF16)
            to_owner(u, XM.at[u, pl.ds(0, 64)], OB.at[:, pl.ds(0, 64)], xsem_s.at[k], xsem_r.at[k])
            DQM[u] = jnp.zeros((64, 128), F32)
        slot("asked")
        wait_all(row_hand_on(l, 4, PF))
        left_put_theirs(PF, LSH, LTF)
        for g in range(2):
            def step(i, _):
                o = pl.ds(pl.multiple_of(g * FH + i * 256, 256), 256)
                grad = nt(PF[g], WF[l, o, :]).astype(BF16).astype(F32)
                DPRE[R : 2 * R, o] = (GP[l, R : 2 * R, o].astype(F32) * grad).astype(BF16)
                return 0

            lax.fori_loop(0, FH // 256, step, 0)
        left_put(FL[...], LSH, LTA)
        attend_copies = left_copies(l, 6, LSH, LTA)
        start_all(attend_copies)
        slot("regrown")
        for g in range(2):
            weight_grad(g, LTF, lambda o: ACT[l, :, pl.ds(g * FH + o, FH)], items["outer"][0], FH, FH)
        rs_start(l, "outer", 0)
        slot("outer")

        @pl.when(is_owner)
        def _():
            owner_gets(XM.at[0, pl.ds(0, 64)], OB.at[:, pl.ds(0, 64)], xsem_s.at[k], xsem_r.at[k])
            d_core = OB[0, 0:64].astype(F32)
            for i in range(1, n):
                d_core = d_core + OB[i, 0:64].astype(F32)
            PC[...] = d_core
            d_mixed = nn3f(PZ[l], expand(d_core))
            off = jnp.sum(d_mixed * expand(MX[l]), axis=1, keepdims=True)
            DR[mine] = pack(compress(d_mixed), [to_row(off)])
            from_owner(DR, csem_s.at[k], csem_r.at[k], True)

        for u in range(U):
            b, j = unit(u)
            at = (slice(b * L, (b + 1) * L), slice(j * 128, (j + 1) * 128))
            d_row = nt(g_tile(u), expand_low(CR[l, u, 0:64]))
            rw = RW[l, u]
            d_rs = (rw * (d_row - half_sums(rw * d_row))).astype(BF16)
            DQ[at] = nn(d_rs, expand(KM[l, u]).astype(BF16))
            DKM[u] = compress(tn(d_rs, tile(QS, l, u)))
        for u in range(U):
            to_owner_sent(u, XM.at[u, pl.ds(0, 64)], OB.at[:, pl.ds(0, 64)], xsem_s.at[k], xsem_r.at[k])

        @pl.when(is_owner)
        def _():
            a = PA[l]
            ath = halves(a.T)
            unit_matrix = jnp.where(eye, 1.0, 0.0)

            def back(i, carry):
                dz, da = carry
                i = PINV_ITERS - 1 - i
                zh, zth, prh = halves(PV[l, i, 0]), halves(PV[l, i, 4]), halves(PV[l, i, 1])
                n1h = halves(7.0 * unit_matrix - PV[l, i, 1])
                n2h, n3h = halves(PV[l, i, 2]), halves(PV[l, i, 3])
                dzh = halves(dz)
                dn3 = halves(0.25 * nn3(zth, dzh))
                dn2 = halves(-nn3(prh, dn3))
                dpr = nn3(prh, dn2) - nt3(dn3, n2h) - nt3(dn2, n1h)
                dpr = halves(dpr)
                dz = 0.25 * nt3(dzh, n3h) + nn3(ath, dpr)
                return dz, da + nt3(dpr, zh)

            dz, da = lax.fori_loop(
                0, PINV_ITERS, back, (nt3f(expand(PC[...]), expand(MX[l])), jnp.zeros((128, 128), F32))
            )
            low_row = low_lane[0:1]

            def half_row(x, f):
                return jnp.where(
                    low_row,
                    f(jnp.where(low_row, x, 0.0), axis=1, keepdims=True),
                    f(jnp.where(low_row, 0.0, x), axis=1, keepdims=True),
                )

            sums = jnp.sum(a, axis=0, keepdims=True)
            tops = half_row(sums, jnp.max)
            d_tops = -half_row(jnp.sum(dz * PV[l, 0, 0], axis=0, keepdims=True), jnp.sum) / tops
            at_top = jnp.where(sums == tops, 1.0, 0.0)
            da = da + (dz / tops).T + at_top * d_tops / half_row(at_top, jnp.sum)
            d_ms = halves(a * (da - jnp.sum(a * da, axis=1, keepdims=True)))
            DQM[mine] = compress(nn3(d_ms, halves(expand(KM[l, mine]))))
            DKM[mine] = DKM[mine] + compress(tn3(d_ms, halves(expand(QM[l, mine]))))

        slot("pinv")
        wait_all(attend_copies)
        start_all(left_hand_on(l, 6, LTA))
        for g in range(2):
            weight_grad(g, LTN.at[l], lambda o: DPRE[:, pl.ds(g * FH + o, FH)], items["inner"][0], FH, FH)
        rs_start(l, "inner", 0)
        advance(l, "outer", 0)
        for u in range(U):
            b, j = unit(u)
            at = (slice(b * L, (b + 1) * L), slice(j * 128, (j + 1) * 128))
            owner_came(DR, u, csem_s.at[k], csem_r.at[k])
            dm = expand_low(DR[u, 0:64])
            off = to_col(packed_row(DR.at[u], 0))
            qb = expand(QM[l, u]).astype(BF16)
            kw = jnp.exp(nt(qb, tile(KS, l, u)) - to_col(packed_row(CR.at[l, u], 0)))
            v = VX[l, b, margin : margin + L, j * 128 : (j + 1) * 128]
            DV[at] = tn(kw.astype(BF16), dm)
            d_ks = (kw * (nt(dm, v) - off)).astype(BF16)
            DK[at] = tn(d_ks, qb)
            DQM[u] = DQM[u] + compress(nn(d_ks, tile(KS, l, u)))

        @pl.when(is_owner)
        def _():
            from_owner(DR, csem_s.at[k], csem_r.at[k], False)

        for u in range(U):
            b, j = unit(u)
            lanes = slice(j * 128, (j + 1) * 128)
            dq, dk = DQM[u].astype(BF16), DKM[u].astype(BF16)
            for i in range(n):
                SB[i, b * S : (b + 1) * S, lanes] = dq[i * S : (i + 1) * S]
                SB[i, 8 + b * S : 8 + (b + 1) * S, lanes] = dk[i * S : (i + 1) * S]
        spread(lambda t: SB.at[t], SR, qsem_s.at[l], qsem_r.at[l], True)
        SR[me] = SB[me]
        edges(GX, vsem_s.at[k], vsem_r.at[k], "wait")
        for u in range(U):
            b, j = unit(u)
            at = (slice(b * L, (b + 1) * L), slice(j * 128, (j + 1) * 128))
            DP[b * L : (b + 1) * L, 2 * C + j * 128 : 2 * C + (j + 1) * 128] = (
                DV[at] + conv(TR.at[l], GX, u)
            ).astype(BF16)
        value_copies = right_copies(l, 7, DP, val_ranges)
        start_all(value_copies)
        for j in range(NP):
            for h in range(2):
                found = jnp.zeros((128, 256), F32)
                for b in range(B):
                    g = nn(flip, g_tile(b * NP + j))
                    g = jnp.where(low_lane, g, 0.0) if h == 0 else jnp.where(low_lane, 0.0, g)
                    found = found + nt(g.astype(BF16), VX[l, b, :, j * 128 : (j + 1) * 128])
                found = pltpu.roll(found, 129, 1, stride=1, stride_axis=0)
                row = base + 54 + 2 * j + h
                SM[row : row + 1, :] = jnp.sum(found[:, 0:128], axis=0, keepdims=True)
        wait_all(left_hand_on(l, 6, LTA))
        wait_all(right_copies(l, 1, CTX.at[l], out_ranges))
        out0 = items["outval"][0]
        weight_grad(0, LTA, lambda o: CTX[l, :, pl.ds(o, 128)], out0, 128, 128)
        weight_grad(1, LTA, lambda o: CTX[l, :, pl.ds(128 + o, 256)], out0, C - 128, 256)
        advance(l, "inner", 0)
        wait_all(value_copies)
        wait_all(left_hand_on(l, 0, LTH.at[l]))
        weight_grad(0, LTH.at[l], lambda o: DP[:, pl.ds(2 * C + o, 256)], out0 + 128, C - 128, 256)
        weight_grad(1, LTH.at[l], lambda o: DP[:, pl.ds(3 * C - 128 + o, 128)], out0 + C - 128, 128, 128)
        rs_start(l, "outval", 0)
        spread(lambda t: SB.at[t], SR, qsem_s.at[l], qsem_r.at[l], False)
        marks = SR[0].astype(F32)
        for i in range(1, n):
            marks = marks + SR[i].astype(F32)
        marks = marks * (1.0 / z.segment)
        for b in range(B):
            for r in range(S):
                at = slice(b * L + r * z.segment, b * L + (r + 1) * z.segment)
                i = b * S + r
                DP[at, 0:C] = ((DQ[at] + marks[i : i + 1]) * scale).astype(BF16)
                DP[at, C : 2 * C] = ((DK[at] + marks[8 + i : 9 + i]) * scale).astype(BF16)
        key_copies = right_copies(l, 8, DP, key_ranges)
        start_all(key_copies)

        def onto(o):
            x = nt(DP[0:R, 0:C], WP[l, 0, o, :]) + nt(DP[0:R, C : 2 * C], WP[l, 1, o, :])
            return x + nt(DP[0:R, 2 * C : 3 * C], WP[l, 2, o, :])

        swap_start(e + 1, onto)
        bias = jnp.sum(DP[0:R].astype(F32), axis=0, keepdims=True)
        put_small(base + 48, bias[:, 0:C])
        put_small(base + 51, bias[:, 2 * C : 3 * C])
        if l == 0:
            spread(lambda t: SM.at[pl.ds(pl.multiple_of(t * 8, 8), 8)], SMR, ssem_s, ssem_r, True)
            SMR[me] = SM[pl.ds(pl.multiple_of(me * 8, 8), 8), :]
        advance(l, "outer", 1)
        wait_all(key_copies)
        for g in range(2):
            weight_grad(g, LTH.at[l], lambda o: DP[:, pl.ds(g * C + o, 128)], items["keyed"][0], C, 128)
        rs_start(l, "keyed", 0)
        swap_wait(e + 1)
        UP[...] = DT[...] + both(e + 1)

    for l in range(z.layers):
        forward(l)
    results = [out_copy(b, HID.at[pl.ds(b * L, L)], result.at[b]) for b in range(B)]
    start_all(results)
    for b in range(B):
        shown = to_col(mask[b : b + 1, :].astype(F32))
        UP[b * L : (b + 1) * L, :] = cot[b].astype(F32) * shown
    wait_all(results)
    backward(1, {})
    backward(
        0,
        {
            "fed": [("outer", 2)],
            "widened": [("inner", 1), ("outval", 0)],
            "narrowed": [("keyed", 0)],
            "asked": [("outval", 1), ("inner", 2)],
            "regrown": [("keyed", 1)],
            "outer": [("outval", 2)],
            "pinv": [("keyed", 2)],
        },
    )

    def finish(*steps):
        for step in steps:
            advance(0, *step)

    tokens_out = [out_copy(B + b, UP.at[pl.ds(b * L, L)], gtok.at[b]) for b in range(B)]
    start_all(tokens_out)
    spread(lambda t: SM.at[pl.ds(pl.multiple_of(t * 8, 8), 8)], SMR, ssem_s, ssem_r, False)
    total = SMR[0]
    for i in range(1, n):
        total = total + SMR[i]
    SMT[me] = total
    spread(lambda t: SMT.at[me], SMT, tsem_s, tsem_r, True)
    finish(("inner", 1), ("outval", 0), ("outer", 2))
    finish(("keyed", 0), ("inner", 2), ("outval", 1))
    ffn_out = [out_copy(2 * B, OU, gouter), out_copy(2 * B + 1, OI, ginner)]
    start_all(ffn_out)
    spread(lambda t: SMT.at[me], SMT, tsem_s, tsem_r, False)

    def little(at):
        return SMT[at // 8, at % 8 : at % 8 + 1, :]

    for l in range(z.layers):
        base = 60 * l
        for i in range(D // 128):
            lanes = slice(i * 128, (i + 1) * 128)
            for side in range(2):
                for what in range(3):
                    OS[what, l, side : side + 1, lanes] = little(base + 12 * what + 6 * side + i)
        for i in range(F // 128):
            OT[l : l + 1, i * 128 : (i + 1) * 128] = little(base + 36 + i)
        for i in range(C // 128):
            OB1[l, 0:1, i * 128 : (i + 1) * 128] = little(base + 48 + i)
            OB1[l, 1:2, i * 128 : (i + 1) * 128] = little(base + 51 + i)
        for h in range(z.local_heads):
            OT1[l, h : h + 1, :] = little(base + 54 + h)[:, 0:K]
    small_out = [
        out_copy(2 * B + 2 + i, src, dst)
        for i, (src, dst) in enumerate(
            [(OS.at[0], ggain), (OS.at[1], gshift), (OS.at[2], gobias), (OT, gibias), (OB1, gbias), (OT1, gtaps)]
        )
    ]
    start_all(small_out)
    finish(("keyed", 1), ("outval", 2), ("keyed", 2))
    rest_out = [out_copy(2 * B + 8, OP, gproj), out_copy(2 * B + 9, OO, gout)]
    start_all(rest_out)
    wait_all(tokens_out + ffn_out + small_out + rest_out)


def hand_over(count, *refs):
    sems = refs[-1]
    copies = [
        pltpu.make_async_copy(refs[i], refs[count + i], sems.at[i]) for i in range(count)
    ]
    for c in copies:
        c.start()
    for c in copies:
        c.wait()


def fused(z, tokens, cotangent, masked, projections, projection_bias, conv_taps, output_weight,
          output_bias, norm_gain, norm_shift, inner_weight, inner_bias, outer_weight):
    n, B, L, R, D, C, F = z.n, z.batch, z.length, z.rows, z.width, z.cols, z.hidden
    U, H, NL_, NB, CH = z.units, z.local_heads, z.layers, z.bits, z.width // z.n
    V = pltpu.VMEM
    DMA = pltpu.SemaphoreType.DMA
    cols = F + 2 * C
    staged = lambda: V((2,) * NB + (CH, R), BF16)
    gathered = lambda *lead: V(lead + (2,) * NB + (CH, 2 * R), BF16)
    scratch = dict(
        WP=V((NL_, 3, D, C), BF16), WO=V((NL_, C, D), BF16), WI=V((NL_, D, F), BF16), WF=V((NL_, F, D), BF16),
        QS=V((NL_, R, C), BF16), KS=V((NL_, R, C), BF16),
        VX=V((NL_, B, 256, C), BF16), RW=V((NL_, U, 128, 128), F32),
        CTX=V((NL_, 2 * R, C), BF16), T1=V((NL_, R, D), F32), T2=V((NL_, R, D), F32),
        GP=V((NL_, 2 * R, F), BF16), ACT=V((NL_, 2 * R, F), BF16),
        QM=V((NL_, U, 64, 128), F32), KM=V((NL_, U, 64, 128), F32), CR=V((NL_, U, 80, 128), BF16),
        MX=V((NL_, 64, 128), F32), PA=V((NL_, 128, 128), F32), PV=V((NL_, PINV_ITERS, 5, 128, 128), F32),
        PZ=V((NL_, 128, 128), F32), PC=V((64, 128), F32), LTH=gathered(NL_), LTN=gathered(NL_),
        HID=V((R, D), F32), UP=V((R, D), F32), LOW=V((R, D), BF16), PN=V((2, R, D), BF16), PF=V((2, R, D), BF16),
        DPRE=V((2 * R, F), BF16), GXS=V((NL_, B, 256, C), BF16), DQ=V((R, C), F32), DK=V((R, C), F32), DV=V((R, C), F32),
        DP=V((2 * R, 3 * C), BF16), DQM=V((U, 64, 128), F32), DKM=V((U, 64, 128), F32), DR=V((U, 80, 128), BF16),
        SM=V((n * 8, 128), F32), TB=V((2, 8, 256), F32),
        TT=V((NL_, H, 128, 256), BF16), TR=V((NL_, H, 128, 256), BF16), LTF=gathered(), LTA=gathered(),
        LSH=staged(), OP=V((NL_, 3, CH, C), F32), OO=V((NL_, CH, C), F32), OI=V((NL_, CH, F), F32),
        OU=V((NL_, CH, F), F32), OS=V((3, NL_, 2, D), F32), OT=V((NL_, F), F32),
        OB1=V((NL_, 2, C), F32), OT1=V((NL_, H, z.kernel), F32),
        tok=V((B, L, D), BF16), cot=V((B, L, D), BF16), mask=V((B, L), jnp.int32), pbias=V((NL_, 2, C), BF16),
        taps=V((H, NL_, z.kernel), BF16), obias=V((NL_, 2, D), BF16), ngain=V((NL_, 2, D), BF16),
        nshift=V((NL_, 2, D), BF16), ibias=V((NL_, F), BF16),
        MS=V((16, C), BF16), MB=V((n, 16, C), BF16), MD=V((U, 16, 128), BF16), MO=V((n, 16, 128), BF16), XM=V((U, 80, 128), BF16), OB=V((n, 80, 128), BF16),
        SB=V((n, 16, C), BF16), SR=V((n, 16, C), BF16), HS=V((2, R, D), BF16), HR=V((2, R, D), BF16),
        SMR=V((n, 8, 128), F32), SMT=V((n, 8, 128), F32),
        G=V((2,) * NB + (CH, cols), BF16),
        RV=[V((NL_, 2) + (2,) * (NB - 2 - s) + (CH, cols), BF16) for s in range(NB - 1)],
        wsem=DMA((NL_, 4)),
        hsem_s=DMA((4 * NL_, D // 256)), hsem_r=DMA((4 * NL_, D // 256)),
        msem_s=DMA((NL_, n)), msem_r=DMA((NL_, n)), dsem_s=DMA((NL_, U)), dsem_r=DMA((NL_, n)), xsem_s=DMA((2 * NL_, U)), xsem_r=DMA((2 * NL_, n)),
        csem_s=DMA((2 * NL_, n)), csem_r=DMA((2 * NL_, U)), vsem_s=DMA((2 * NL_, 2)), vsem_r=DMA((2 * NL_, 2)),
        osem=DMA((2 * B + 10,)), isem=DMA((9,)),
        asem_s=DMA((NL_, 9, 2)), asem_r=DMA((NL_, 9, 2)), bsem_s=DMA((NL_, 9, 2)), bsem_r=DMA((NL_, 9, 2)),
        gsem_s=DMA((NL_, 4, 2, NB - 1)), gsem_r=DMA((NL_, 4, 2, NB - 1)), qsem_s=DMA((NL_, n)), qsem_r=DMA((NL_, n)),
        ssem_s=DMA((n,)), ssem_r=DMA((n,)), tsem_s=DMA((n,)), tsem_r=DMA((n,)),
    )
    in_vmem = pl.BlockSpec(memory_space=pltpu.VMEM)
    in_hbm = pl.BlockSpec(memory_space=pl.ANY)
    out = lambda *s: jax.ShapeDtypeStruct(s, F32)
    shapes = (
        out(B, L, D), out(B, L, D), out(NL_, 3, CH, C), out(NL_, 2, C), out(NL_, H, z.kernel), out(NL_, CH, C),
        out(NL_, 2, D), out(NL_, 2, D), out(NL_, 2, D), out(NL_, CH, F), out(NL_, F), out(NL_, CH, F),
    )
    outs = pl.pallas_call(
        partial(fused_kernel, z),
        out_shape=shapes,
        in_specs=[in_hbm] * 13,
        out_specs=(in_hbm,) * len(shapes),
        scratch_shapes=scratch,
        compiler_params=pltpu.CompilerParams(
            collective_id=1, has_side_effects=True, vmem_limit_bytes=VMEM_LIMIT
        ),
    )(tokens, cotangent, masked, projection_bias, jnp.swapaxes(conv_taps, 0, 1), output_bias, norm_gain, norm_shift, inner_bias,
      projections, output_weight, inner_weight, outer_weight)
    outs = list(
        pl.pallas_call(
            partial(hand_over, len(shapes)),
            out_shape=shapes,
            in_specs=[in_vmem] * len(shapes),
            out_specs=(in_hbm,) * len(shapes),
            scratch_shapes=[DMA((len(shapes),))],
        )(*outs)
    )
    for i in (5, 11):
        outs[i] = jnp.swapaxes(outs[i], 1, 2)
    return tuple(outs)


def solution(mesh):
    in_specs = (
        P(None, "seq", None),
        P(None, "seq", None),
        P(None, "seq"),
        P(None, None, None, "head"),
        P(None, None, "head"),
        P(None, "head", None),
        P(None, "head", None),
        P(),
        P(),
        P(),
        P(None, None, "head"),
        P(None, "head"),
        P(None, "head", None),
    )
    out_specs = (
        P(None, "seq", None),
        P(None, "seq", None),
        P(None, None, "seq", "head"),
        P(None, None, "head"),
        P(None, "head", None),
        P(None, "head", "seq"),
        P(),
        P(),
        P(),
        P(None, "seq", "head"),
        P(None, "head"),
        P(None, "head", "seq"),
    )

    def whole(*args):
        z = Fast(mesh.shape, args[0], args[5], args[10])
        body = partial(fused, z) if z.fits() else on_device
        return jax.shard_map(
            body, mesh=mesh, in_specs=in_specs, out_specs=out_specs, check_vma=False
        )(*args)

    return whole
```

```python
from functools import partial

import jax
import jax.numpy as jnp
from jax import lax
from jax.experimental import pallas as pl
from jax.experimental.pallas import tpu as pltpu
from jax.sharding import PartitionSpec as P

LANDMARKS = 64
PINV_ITERS = 6
LAYERS = 2


exact_result = lax.Precision.HIGHEST
epsilon = 1e-05


VMEM_LIMIT = 64 * 1024 * 1024 - 128 * 1024


def extended(block, sides, width):
    for axis, dim in sides:
        count = lax.axis_size(axis)
        forward = [(i, i + 1) for i in range(count - 1)]
        backward = [(target, source) for source, target in forward]
        low = lax.ppermute(
            lax.slice_in_dim(block, block.shape[dim] - width, None, axis=dim), axis, forward
        )
        high = lax.ppermute(lax.slice_in_dim(block, 0, width, axis=dim), axis, backward)
        block = jnp.concatenate([low, block, high], axis=dim)
    return block


def layer_norm(values, scaling, offset):
    centre = jnp.mean(values, -1, keepdims=True)
    centred = values - centre
    spread = jnp.mean(centred * centred, -1, keepdims=True)
    return centred * lax.rsqrt(spread + epsilon) * scaling + offset


def soft_rows(scores):
    highest = jnp.max(scores, -1, keepdims=True)
    powers = jnp.exp(scores - highest)
    return powers / jnp.sum(powers, -1, keepdims=True)


def pseudo_inverse(weight_matrix):
    size_of = weight_matrix.shape[-1]
    column_top = jnp.max(jnp.sum(weight_matrix, axis=-2), axis=-1)[..., None, None]
    approximate_result = jnp.swapaxes(weight_matrix, -1, -2) / column_top
    identity = jnp.eye(size_of, dtype=jnp.float32)
    for repeat in range(PINV_ITERS):
        product = jnp.matmul(weight_matrix, approximate_result, precision=exact_result)
        nested = 7.0 * identity - product
        nested = 15.0 * identity - jnp.matmul(product, nested, precision=exact_result)
        nested = 13.0 * identity - jnp.matmul(product, nested, precision=exact_result)
        approximate_result = 0.25 * jnp.matmul(approximate_result, nested, precision=exact_result)
    return approximate_result


def rounded(values):
    return lax.optimization_barrier(values.astype(jnp.bfloat16)).astype(jnp.float32)


def heads_view(joined, heads_local):
    batch_count, length, channels = joined.shape
    return joined.reshape(batch_count, length, heads_local, channels // heads_local).transpose(
        0, 2, 1, 3
    )


def tokens_view(by_head):
    batch_count, heads_local, length, head_depth = by_head.shape
    return by_head.transpose(0, 2, 1, 3).reshape(batch_count, length, heads_local * head_depth)


def convolve(padded, broad_kernel_taps, length):

    def add_tap(offset, running):
        window = lax.dynamic_slice_in_dim(padded, offset, length, 1).astype(jnp.float32)
        return running + window * lax.dynamic_index_in_dim(broad_kernel_taps, offset, 0, False)

    initial = jnp.zeros((padded.shape[0], length, padded.shape[2]), jnp.float32)
    return lax.fori_loop(0, broad_kernel_taps.shape[0], add_tap, initial)


def tap_sums(padded, upstream, length, kernel):

    def one_tap(offset):
        window = lax.dynamic_slice_in_dim(padded, offset, length, 1).astype(jnp.float32)
        return jnp.sum(window * upstream, axis=(0, 1))

    return lax.map(one_tap, jnp.arange(kernel, dtype=jnp.int32))


def across_heads(summand):
    return lax.psum_scatter(
        summand.astype(jnp.bfloat16), "head", scatter_dimension=0, tiled=True
    ).astype(jnp.float32)


def rows_low(share):
    return lax.all_gather(share, "head", axis=0, tiled=True)


def rows_float(share):
    return lax.all_gather(share.astype(jnp.bfloat16), "head", axis=0, tiled=True).astype(
        share.dtype
    )


def own_rows(whole_rows):
    share = whole_rows.shape[0] // lax.axis_size("head")
    return lax.dynamic_slice_in_dim(whole_rows, lax.axis_index("head") * share, share, 0)


def spread_heads(share, dim_index):
    groups = lax.axis_size("head")
    full_shape = list(share.shape)
    full_shape[dim_index] = full_shape[dim_index] * groups
    empty = jnp.zeros(full_shape, jnp.float32)
    return lax.dynamic_update_slice_in_dim(
        empty, share, lax.axis_index("head") * share.shape[dim_index], dim_index
    )


def own_heads(whole, width, dim_index):
    return lax.dynamic_slice_in_dim(whole, lax.axis_index("head") * width, width, dim_index)


def forward_layer(hidden, weights, selector, segment):
    (
        projection,
        projection_shift,
        conv_kernel,
        output_matrix,
        output_shift,
        gain_pair,
        shift_pair,
        inner_matrix,
        inner_shift,
        outer_matrix,
    ) = weights
    batch_count, length, model_width = hidden.shape
    heads_local = conv_kernel.shape[0]
    kernel = conv_kernel.shape[1]
    margin = kernel // 2
    local_width = projection.shape[2]
    head_depth = local_width // heads_local
    scale = float(head_depth) ** (-0.25)
    hidden_low = hidden.astype(jnp.bfloat16).reshape(batch_count * length, model_width)
    projected = jnp.einsum(
        "nd,kde->kne", hidden_low, projection, preferred_element_type=jnp.float32
    )
    biases = projection_shift.astype(jnp.float32)
    query_rows = ((projected[0] + biases[0]) * scale).reshape(batch_count, length, local_width)
    key_rows = (projected[1] * scale).reshape(batch_count, length, local_width)
    value_low = (
        (projected[2] + biases[1]).astype(jnp.bfloat16).reshape(batch_count, length, local_width)
    )
    query_sums, key_sums = lax.psum(
        (
            jnp.einsum("mt,btc->bmc", selector, query_rows, precision=exact_result),
            jnp.einsum("mt,btc->bmc", selector, key_rows, precision=exact_result),
        ),
        "seq",
    )
    query_marks = heads_view(query_sums / segment, heads_local)
    key_marks = heads_view(key_sums / segment, heads_local)
    query_heads = heads_view(query_rows, heads_local)
    key_heads = heads_view(key_rows, heads_local)
    value_heads = heads_view(value_low.astype(jnp.float32), heads_local)
    mark_weights = soft_rows(
        jnp.einsum("bhme,bhne->bhmn", query_marks, key_marks, precision=exact_result)
    )
    inverse = pseudo_inverse(mark_weights)
    row_weights = soft_rows(
        jnp.einsum("bhte,bhme->bhtm", query_heads, key_marks, precision=exact_result)
    )
    key_scores = jnp.einsum("bhme,bhte->bhmt", query_marks, key_heads, precision=exact_result)
    local_top = jnp.max(key_scores, -1)
    score_top = lax.pmax(local_top, "seq")
    powers = jnp.exp(key_scores - score_top[..., None])
    neighbour_mixture = jnp.einsum("bhmt,bhte->bhme", powers, value_heads, precision=exact_result)
    score_total, mixed_joined = lax.psum(
        (jnp.sum(powers, -1), neighbour_mixture.reshape(batch_count, heads_local, -1)), "seq"
    )
    mixed_sum = mixed_joined.reshape(neighbour_mixture.shape)
    log_total = score_top + jnp.log(score_total)
    mixed = mixed_sum / score_total[..., None]
    core = jnp.einsum("bhmn,bhne->bhme", inverse, mixed, precision=exact_result)
    attended = jnp.einsum("bhtm,bhme->bhte", row_weights, core, precision=exact_result)
    padded_values = extended(value_low, (("seq", 1),), margin)
    broad_kernel_taps = jnp.repeat(conv_kernel.astype(jnp.float32), head_depth, axis=0).T
    context = tokens_view(attended) + convolve(padded_values, broad_kernel_taps, length)
    context_low = context.astype(jnp.bfloat16).reshape(batch_count * length, local_width)
    attention_share = across_heads(
        jnp.dot(context_low, output_matrix, preferred_element_type=jnp.float32)
    )
    shifts = output_shift.astype(jnp.float32)
    gains = gain_pair.astype(jnp.float32)
    offsets = shift_pair.astype(jnp.float32)
    hidden_share = own_rows(hidden.reshape(batch_count * length, model_width))
    total_first = hidden_share + attention_share + shifts[0]
    normed = layer_norm(total_first, gains[0], offsets[0])
    normed_low = rows_low(normed.astype(jnp.bfloat16))
    pre_active = jnp.dot(
        normed_low, inner_matrix, preferred_element_type=jnp.float32
    ) + inner_shift.astype(jnp.float32)
    active_low = jax.nn.gelu(pre_active, approximate=False).astype(jnp.bfloat16)
    feed_share = across_heads(jnp.dot(active_low, outer_matrix, preferred_element_type=jnp.float32))
    total_second = normed + feed_share + shifts[1]
    output = rows_float(layer_norm(total_second, gains[1], offsets[1])).reshape(hidden.shape)
    retained = (
        hidden_low,
        query_heads,
        key_heads,
        value_heads,
        padded_values,
        query_marks,
        key_marks,
        mark_weights,
        inverse,
        row_weights,
        log_total,
        mixed,
        core,
        context_low,
        total_first,
        normed_low,
        pre_active,
        active_low,
        total_second,
        broad_kernel_taps,
    )
    return (output, retained)


def backward_layer(upstream, retained, weights, selector, segment):
    (
        projection,
        projection_shift,
        conv_kernel,
        output_matrix,
        output_shift,
        gain_pair,
        shift_pair,
        inner_matrix,
        inner_shift,
        outer_matrix,
    ) = weights
    (
        hidden_low,
        query_heads,
        key_heads,
        value_heads,
        padded_values,
        query_marks,
        key_marks,
        mark_weights,
        inverse,
        row_weights,
        log_total,
        mixed,
        core,
        context_low,
        total_first,
        normed_low,
        pre_active,
        active_low,
        total_second,
        broad_kernel_taps,
    ) = retained
    batch_count, length, model_width = upstream.shape
    heads_local = conv_kernel.shape[0]
    kernel = conv_kernel.shape[1]
    margin = kernel // 2
    local_width = projection.shape[2]
    head_depth = local_width // heads_local
    scale = float(head_depth) ** (-0.25)
    gains = gain_pair.astype(jnp.float32)
    offsets = shift_pair.astype(jnp.float32)
    upstream_share = own_rows(upstream.reshape(batch_count * length, model_width))
    second_pull = jax.vjp(layer_norm, total_second, gains[1], offsets[1])[1]
    grad_second, gain_second, offset_second = second_pull(upstream_share)
    feed_low = rows_low(grad_second.astype(jnp.bfloat16))
    grad_outer = jnp.einsum("nf,nd->fd", active_low, feed_low, preferred_element_type=jnp.float32)
    grad_active = rounded(
        jnp.einsum("nd,fd->nf", feed_low, outer_matrix, preferred_element_type=jnp.float32)
    )
    gelu_pull = jax.vjp(partial(jax.nn.gelu, approximate=False), pre_active)[1]
    grad_pre_low = gelu_pull(grad_active)[0].astype(jnp.bfloat16)
    grad_inner_shift = jnp.sum(grad_pre_low.astype(jnp.float32), axis=0)
    grad_inner = jnp.einsum(
        "nd,nf->df", normed_low, grad_pre_low, preferred_element_type=jnp.float32
    )
    normed_term = jnp.einsum(
        "nf,df->nd", grad_pre_low, inner_matrix, preferred_element_type=jnp.float32
    )
    grad_normed = grad_second + across_heads(normed_term)
    first_pull = jax.vjp(layer_norm, total_first, gains[0], offsets[0])[1]
    grad_first, gain_first, offset_first = first_pull(grad_normed)
    attend_low = rows_low(grad_first.astype(jnp.bfloat16))
    grad_output = jnp.einsum(
        "nc,nd->cd", context_low, attend_low, preferred_element_type=jnp.float32
    )
    grad_context_low = (
        jnp.einsum("nd,cd->nc", attend_low, output_matrix, preferred_element_type=jnp.float32)
        .astype(jnp.bfloat16)
        .reshape(batch_count, length, local_width)
    )
    grad_context = lax.optimization_barrier(grad_context_low).astype(jnp.float32)
    padded_grads = extended(grad_context_low, (("seq", 1),), margin)
    grad_conv_values = convolve(padded_grads, broad_kernel_taps[::-1], length)
    kernel_sums = tap_sums(padded_values, grad_context, length, kernel)
    grad_kernel = kernel_sums.reshape(kernel, heads_local, head_depth).sum(-1).T
    grad_attended = heads_view(grad_context, heads_local)
    grad_row = jnp.einsum("bhte,bhme->bhtm", grad_attended, core, precision=exact_result)
    grad_core_local = jnp.einsum(
        "bhtm,bhte->bhme", row_weights, grad_attended, precision=exact_result
    )
    grad_row_scores = row_weights * (grad_row - jnp.sum(row_weights * grad_row, -1, keepdims=True))
    grad_query = jnp.einsum("bhtm,bhme->bhte", grad_row_scores, key_marks, precision=exact_result)
    grad_keymark_local = jnp.einsum(
        "bhtm,bhte->bhme", grad_row_scores, query_heads, precision=exact_result
    )
    grad_core_joined, grad_keymark_joined = lax.psum(
        (
            grad_core_local.reshape(batch_count, heads_local, -1),
            grad_keymark_local.reshape(batch_count, heads_local, -1),
        ),
        "seq",
    )
    grad_core = grad_core_joined.reshape(core.shape)
    grad_inverse = jnp.einsum("bhme,bhne->bhmn", grad_core, mixed, precision=exact_result)
    grad_mixed = jnp.einsum("bhnm,bhne->bhme", inverse, grad_core, precision=exact_result)
    grad_marks = jax.vjp(pseudo_inverse, mark_weights)[1](grad_inverse)[0]
    grad_mark_scores = mark_weights * (
        grad_marks - jnp.sum(mark_weights * grad_marks, -1, keepdims=True)
    )
    grad_querymark = jnp.einsum(
        "bhmn,bhne->bhme", grad_mark_scores, key_marks, precision=exact_result
    )
    grad_keymark = grad_keymark_joined.reshape(key_marks.shape) + jnp.einsum(
        "bhmn,bhme->bhne", grad_mark_scores, query_marks, precision=exact_result
    )
    key_scores = jnp.einsum("bhme,bhte->bhmt", query_marks, key_heads, precision=exact_result)
    key_weights = jnp.exp(key_scores - log_total[..., None])
    grad_values = jnp.einsum("bhmt,bhme->bhte", key_weights, grad_mixed, precision=exact_result)
    offset_term = jnp.sum(grad_mixed * mixed, -1)
    grad_key_scores = key_weights * (
        jnp.einsum("bhme,bhte->bhmt", grad_mixed, value_heads, precision=exact_result)
        - offset_term[..., None]
    )
    grad_key = jnp.einsum("bhmt,bhme->bhte", grad_key_scores, query_marks, precision=exact_result)
    grad_querymark_local = jnp.einsum(
        "bhmt,bhte->bhme", grad_key_scores, key_heads, precision=exact_result
    )
    grad_querymark = grad_querymark + lax.psum(
        grad_querymark_local.reshape(batch_count, heads_local, -1), "seq"
    ).reshape(query_marks.shape)
    grad_query = (
        grad_query
        + jnp.einsum("mt,bhme->bhte", selector, grad_querymark, precision=exact_result) / segment
    )
    grad_key = (
        grad_key
        + jnp.einsum("mt,bhme->bhte", selector, grad_keymark, precision=exact_result) / segment
    )
    grad_values = grad_values + heads_view(grad_conv_values, heads_local)
    query_low = (
        (tokens_view(grad_query) * scale)
        .astype(jnp.bfloat16)
        .reshape(batch_count * length, local_width)
    )
    key_low = (
        (tokens_view(grad_key) * scale)
        .astype(jnp.bfloat16)
        .reshape(batch_count * length, local_width)
    )
    value_grad_low = (
        tokens_view(grad_values).astype(jnp.bfloat16).reshape(batch_count * length, local_width)
    )
    stacked = jnp.stack([query_low, key_low, value_grad_low])
    grad_projection = jnp.einsum(
        "nd,kne->kde", hidden_low, stacked, preferred_element_type=jnp.float32
    )
    grad_projection_shift = jnp.stack(
        [
            jnp.sum(query_low.astype(jnp.float32), axis=0),
            jnp.sum(value_grad_low.astype(jnp.float32), axis=0),
        ]
    )
    input_term = jnp.einsum("kne,kde->nd", stacked, projection, preferred_element_type=jnp.float32)
    grad_hidden = rows_float(grad_first + across_heads(input_term)).reshape(upstream.shape)
    gradients = (
        grad_projection,
        grad_projection_shift,
        grad_kernel,
        grad_output,
        jnp.stack([jnp.sum(grad_first, axis=0), jnp.sum(grad_second, axis=0)]),
        jnp.stack([gain_first, gain_second]),
        jnp.stack([offset_first, offset_second]),
        grad_inner,
        grad_inner_shift,
        grad_outer,
    )
    return (grad_hidden, gradients)


def on_device(
    tokens,
    cotangent,
    masked,
    projections,
    projection_bias,
    conv_taps,
    output_weight,
    output_bias,
    norm_gain,
    norm_shift,
    inner_weight,
    inner_bias,
    outer_weight,
):
    length = tokens.shape[1]
    segment = length * lax.axis_size("seq") // LANDMARKS
    position = lax.axis_index("seq") * length + jnp.arange(length, dtype=jnp.int32)
    selector = (
        position[None, :] // segment == jnp.arange(LANDMARKS, dtype=jnp.int32)[:, None]
    ).astype(jnp.float32)
    arrays = (
        projections,
        projection_bias,
        conv_taps,
        output_weight,
        output_bias,
        norm_gain,
        norm_shift,
        inner_weight,
        inner_bias,
        outer_weight,
    )
    hidden = tokens.astype(jnp.float32)
    stored = []
    for layer_number in range(LAYERS):
        weights = tuple((tensor[layer_number] for tensor in arrays))
        hidden, retained = forward_layer(hidden, weights, selector, segment)
        stored.append((weights, retained))
    upstream = cotangent.astype(jnp.float32) * masked.astype(jnp.float32)[:, :, None]
    layer_grads = [None] * LAYERS
    for layer_number in range(LAYERS - 1, -1, -1):
        weights, retained = stored[layer_number]
        upstream, gradients = backward_layer(upstream, retained, weights, selector, segment)
        larger = (
            lax.psum_scatter(gradients[0], "seq", scatter_dimension=1, tiled=True),
            lax.psum_scatter(gradients[3], "seq", scatter_dimension=1, tiled=True),
            lax.psum_scatter(gradients[7], "seq", scatter_dimension=0, tiled=True),
            lax.psum_scatter(gradients[9], "seq", scatter_dimension=1, tiled=True),
        )
        gradients = (
            larger[0],
            gradients[1],
            gradients[2],
            larger[1],
            gradients[4],
            gradients[5],
            gradients[6],
            larger[2],
            gradients[8],
            larger[3],
        )
        layer_grads[layer_number] = gradients
    stacked = tuple(
        (
            jnp.stack([layer_grads[layer_number][member] for layer_number in range(LAYERS)])
            for member in range(10)
        )
    )
    larger = (stacked[0], stacked[3], stacked[7], stacked[9])
    bias_width = stacked[1].shape[2]
    taps_width = stacked[2].shape[1]
    inner_width = stacked[8].shape[1]
    smaller = lax.psum(
        (
            spread_heads(stacked[1], 2),
            spread_heads(stacked[2], 1),
            stacked[4],
            stacked[5],
            stacked[6],
            spread_heads(stacked[8], 1),
        ),
        ("seq", "head"),
    )
    grad_bias_share = own_heads(smaller[0], bias_width, 2)
    grad_taps_share = own_heads(smaller[1], taps_width, 1)
    grad_inner_share = own_heads(smaller[5], inner_width, 1)
    return (
        hidden,
        upstream,
        larger[0],
        grad_bias_share,
        grad_taps_share,
        larger[1],
        smaller[2],
        smaller[3],
        smaller[4],
        larger[2],
        grad_inner_share,
        larger[3],
    )


F32 = jnp.float32
BF16 = jnp.bfloat16
MESH = pl.DeviceIdType.MESH


def nn(a, b):
    return lax.dot_general(a, b, (((1,), (0,)), ((), ())), preferred_element_type=F32)


def nt(a, b):
    return lax.dot_general(a, b, (((1,), (1,)), ((), ())), preferred_element_type=F32)


def tn(a, b):
    return lax.dot_general(a, b, (((0,), (0,)), ((), ())), preferred_element_type=F32)


def halves(x):
    high = x.astype(BF16)
    return high, (x - high.astype(F32)).astype(BF16)


def left3(pair, axis):
    return jnp.concatenate([pair[0], pair[1], pair[0]], axis=axis)


def right3(pair, axis):
    return jnp.concatenate([pair[0], pair[0], pair[1]], axis=axis)


def nn3(a, b):
    return nn(left3(a, 1), right3(b, 0))


def nt3(a, b):
    return nt(left3(a, 1), right3(b, 1))


def tn3(a, b):
    return tn(left3(a, 0), right3(b, 0))


def nn3f(a, b):
    return nn3(halves(a), halves(b))


def nt3f(a, b):
    return nt3(halves(a), halves(b))


def tn3f(a, b):
    return tn3(halves(a), halves(b))


class Fast:
    def __init__(self, mesh_shape, tokens, conv_taps, inner_weight):
        self.n = mesh_shape["seq"]
        self.heads = mesh_shape["head"]
        self.batch, whole, self.width = tokens.shape
        self.length = whole // self.n
        self.layers, all_heads, self.kernel = conv_taps.shape
        self.local_heads = all_heads // self.heads
        self.depth = self.width // all_heads
        self.cols = self.local_heads * self.depth
        self.hidden = inner_weight.shape[2] // self.heads
        self.rows = self.batch * self.length
        self.segment = whole // LANDMARKS
        self.spans = self.length // self.segment
        self.units = self.batch * self.local_heads // 2
        self.bits = self.n.bit_length() - 1

    def fits(self):
        return (
            self.n == 1 << self.bits
            and self.n >= 16
            and self.heads == 2
            and self.length == 128
            and self.batch == 2
            and self.spans * self.batch == 8
            and self.depth == 64
            and self.local_heads % 2 == 0
            and self.width % (16 * self.n) == 0
            and self.width % 256 == 0
            and self.hidden % 512 == 0
            and self.kernel == 65
            and self.layers == 2
            and LANDMARKS == 64
        )


def fused_kernel(
    z,
    tok_hbm, cot_hbm, mask_hbm, pbias_hbm, taps_hbm, obias_hbm, ngain_hbm, nshift_hbm, ibias_hbm,
    wp_hbm, wo_hbm, wi_hbm, wf_hbm,
    result, gtok, gproj, gbias, gtaps, gout, gobias, ggain, gshift, ginner, gibias, gouter,
    *,
    tok, cot, mask, pbias, taps, obias, ngain, nshift, ibias, WP, WO, WI, WF,
    QS, KS, VX, RW, CTX, T1, T2, GP, ACT, QM, KM, CR, MX, PA, PV, PZ, PC, LTH, LTN,
    HID, UP, LOW, PN, PF, DPRE, GXS, DQ, DK, DV, DP, DQM, DKM, DR, SM, TB, TT, TR, LTF, LTA,
    LSH, OP, OO, OI, OU, OS, OT, OB1, OT1,
    MS, MB, MD, MO, XM, OB, SB, SR, HS, HR, SMR, SMT,
    G, RV,
    isem, wsem, hsem_s, hsem_r, msem_s, msem_r, dsem_s, dsem_r, xsem_s, xsem_r, csem_s, csem_r, vsem_s, vsem_r,
    osem, asem_s, asem_r, bsem_s, bsem_r, gsem_s, gsem_r, qsem_s, qsem_r, ssem_s, ssem_r, tsem_s, tsem_r,
):
    n, B, L, R, D, C, F = z.n, z.batch, z.length, z.rows, z.width, z.cols, z.hidden
    U, NP, S, K = z.units, z.local_heads // 2, z.spans, z.kernel
    CH = D // n
    NB = z.bits
    M = LANDMARKS
    margin = K // 2
    scale = float(z.depth) ** (-0.25)
    me = lax.axis_index("seq")
    core = lax.axis_index("head")
    first_owner = n // 2 - U // 2
    is_owner = jnp.logical_and(me >= first_owner, me < first_owner + U)
    mine = jnp.clip(me - first_owner, 0, U - 1)

    def weight_copies(l):
        return [
            pltpu.make_async_copy(wp_hbm.at[l], WP.at[l], wsem.at[l, 0]),
            pltpu.make_async_copy(wo_hbm.at[l], WO.at[l], wsem.at[l, 1]),
            pltpu.make_async_copy(wi_hbm.at[l], WI.at[l], wsem.at[l, 2]),
            pltpu.make_async_copy(wf_hbm.at[l], WF.at[l], wsem.at[l, 3]),
        ]

    arguments = [
        pltpu.make_async_copy(src, dst, isem.at[i])
        for i, (src, dst) in enumerate(
            [
                (tok_hbm, tok), (pbias_hbm, pbias), (taps_hbm, taps), (obias_hbm, obias), (ngain_hbm, ngain),
                (nshift_hbm, nshift), (ibias_hbm, ibias), (cot_hbm, cot), (mask_hbm, mask),
            ]
        )
    ]
    arguments[0].start()
    weight_copies(0)[0].start()
    for c in arguments[1:]:
        c.start()

    barrier = pltpu.get_barrier_semaphore()

    def greet(d, _):
        pl.semaphore_signal(
            barrier, inc=1, device_id={"seq": lax.rem(me + d, n)}, device_id_type=MESH
        )
        return 0

    lax.fori_loop(1, n, greet, 0)
    pl.semaphore_signal(barrier, inc=1, device_id={"head": 1 - core}, device_id_type=MESH)

    row_id = lax.broadcasted_iota(jnp.int32, (128, 128), 0)
    lane_id = lax.broadcasted_iota(jnp.int32, (128, 128), 1)
    low_lane = lane_id < 64
    low_lane64 = low_lane[0:64]
    same_head = (row_id < 64) == low_lane
    eye = row_id == lane_id
    flip = jnp.where(row_id + lane_id == 127, 1.0, 0.0).astype(BF16)

    def expand(c):
        return jnp.concatenate(
            [jnp.where(low_lane64, c, 0.0), jnp.where(low_lane64, 0.0, c)], axis=0
        )

    def expand_low(c):
        return expand(c.astype(F32)).astype(BF16)

    def compress(x):
        return jnp.where(low_lane64, x[0:64], x[64:128])

    def to_row(col):
        return jnp.sum(jnp.where(eye, col, 0.0), axis=0, keepdims=True)

    def to_col(row):
        return jnp.sum(jnp.where(eye, row, 0.0), axis=1, keepdims=True)

    def half_sums(x):
        a = jnp.sum(jnp.where(low_lane, x, 0.0), axis=1, keepdims=True)
        b = jnp.sum(jnp.where(low_lane, 0.0, x), axis=1, keepdims=True)
        return jnp.where(low_lane, a, b)

    def half_tops(x):
        a = jnp.max(jnp.where(low_lane, x, -jnp.inf), axis=1, keepdims=True)
        b = jnp.max(jnp.where(low_lane, -jnp.inf, x), axis=1, keepdims=True)
        return jnp.where(low_lane, a, b)

    def parts3(x):
        a = x.astype(BF16)
        rest = x - a.astype(F32)
        b = rest.astype(BF16)
        c = (rest - b.astype(F32)).astype(BF16)
        return jnp.concatenate([a.astype(F32), b.astype(F32), c.astype(F32)], axis=0)

    def pack(body, rows):
        tail = jnp.concatenate([parts3(r) for r in rows], axis=0)
        fill = jnp.zeros((16 - tail.shape[0], 128), F32)
        return jnp.concatenate([body, tail, fill], axis=0).astype(BF16)

    def packed_row(message, i):
        x = message[64 + 3 * i : 67 + 3 * i].astype(F32)
        return jnp.sum(x, axis=0, keepdims=True)

    def unit(u):
        return u // NP, u % NP

    def tile(ref, l, u):
        b, j = unit(u)
        return ref[l, b * L : (b + 1) * L, j * 128 : (j + 1) * 128]

    def moments(x):
        centre = jnp.mean(x, -1, keepdims=True)
        centred = x - centre
        spread = jnp.mean(centred * centred, -1, keepdims=True)
        inverse = lax.rsqrt(spread + epsilon)
        return centred * inverse, inverse

    def norm_back(x, grad, gain):
        hat, inverse = moments(x)
        g = grad * gain
        a = jnp.mean(g, -1, keepdims=True)
        b = jnp.mean(g * hat, -1, keepdims=True)
        total = inverse * (g - a - hat * b)
        sums = (
            jnp.sum(grad * hat, axis=0, keepdims=True),
            jnp.sum(grad, axis=0, keepdims=True),
            jnp.sum(total, axis=0, keepdims=True),
        )
        return total, sums

    def put_small(start, vector):
        for i in range(vector.shape[1] // 128):
            SM[start + i : start + i + 1, :] = vector[:, i * 128 : (i + 1) * 128]

    PARTS = D // 256

    def swap_part(e, i):
        at = (e % 2, pl.ds(0, R), pl.ds(i * 256, 256))
        return pltpu.make_async_remote_copy(
            HS.at[at], HR.at[at], hsem_s.at[e, i], hsem_r.at[e, i],
            device_id={"head": 1 - core}, device_id_type=MESH,
        )

    def swap_start(e, part):
        for i in range(PARTS):
            o = slice(i * 256, (i + 1) * 256)
            HS[e % 2, :, o] = part(o).astype(BF16)
            swap_part(e, i).start()

    def swap_wait(e):
        for i in range(PARTS):
            swap_part(e, i).wait()

    def both(e):
        return HS[e % 2].astype(F32) + HR[e % 2].astype(F32)

    own_bits = [lax.rem(me // (1 << k), 2) for k in range(NB)]

    def peer_across(d):
        return me + sum((1 - 2 * own_bits[k]) * (1 << k) for k in range(NB) if d >> k & 1)

    others = range(n - 1, 0, -1)

    def spread(src, dst, ss, rs, start):
        def copy(d, to):
            return pltpu.make_async_remote_copy(
                src(peer_across(d)), dst.at[to], ss.at[d], rs.at[d],
                device_id={"seq": peer_across(d)}, device_id_type=MESH,
            )

        if start:
            for d in others:
                copy(d, me).start()
        else:
            for d in others:
                copy(d, peer_across(d)).wait_recv()
            for d in others:
                copy(d, peer_across(d)).wait_send()

    def to_owner_copy(u, src, dst, ss, rs):
        return pltpu.make_async_remote_copy(
            src, dst.at[me], ss.at[u], rs.at[me], device_id={"seq": first_owner + u}, device_id_type=MESH
        )

    def to_owner(u, src, dst, ss, rs):
        @pl.when(me != first_owner + u)
        def _():
            to_owner_copy(u, src, dst, ss, rs).start()

        @pl.when(me == first_owner + u)
        def _():
            dst[me] = src[...]

    def to_owner_sent(u, src, dst, ss, rs):
        @pl.when(me != first_owner + u)
        def _():
            to_owner_copy(u, src, dst, ss, rs).wait_send()

    def owner_gets(src, dst, ss, rs):
        def step(d, _):
            t = lax.rem(me + d, n)
            pltpu.make_async_remote_copy(
                src, dst.at[t], ss.at[0], rs.at[t], device_id={"seq": t}, device_id_type=MESH
            ).wait_recv()
            return 0

        lax.fori_loop(1, n, step, 0)

    def from_owner(slots, ss, rs, start):
        for d in others:
            c = pltpu.make_async_remote_copy(
                slots.at[mine], slots.at[mine], ss.at[d], rs.at[mine],
                device_id={"seq": peer_across(d)}, device_id_type=MESH,
            )
            if start:
                c.start()
            else:
                c.wait_send()

    def owner_came(slots, u, ss, rs):
        @pl.when(me != first_owner + u)
        def _():
            pltpu.make_async_remote_copy(
                slots.at[u], slots.at[u], ss.at[0], rs.at[u],
                device_id={"seq": first_owner + u}, device_id_type=MESH,
            ).wait_recv()

    def edges(buf, ss, rs, act):
        after = pltpu.make_async_remote_copy(
            buf.at[:, pl.ds(L, margin)], buf.at[:, pl.ds(0, margin)], ss.at[0], rs.at[0],
            device_id={"seq": lax.rem(me + 1, n)}, device_id_type=MESH,
        )
        before = pltpu.make_async_remote_copy(
            buf.at[:, pl.ds(margin, margin)], buf.at[:, pl.ds(margin + L, margin)], ss.at[1], rs.at[1],
            device_id={"seq": lax.rem(me + n - 1, n)}, device_id_type=MESH,
        )
        if act == "start":
            @pl.when(me < n - 1)
            def _():
                after.start()

            @pl.when(me > 0)
            def _():
                before.start()
        else:
            @pl.when(me < n - 1)
            def _():
                after.wait_send()
                before.wait_recv()

            @pl.when(me > 0)
            def _():
                before.wait_send()
                after.wait_recv()

    def edge_zeros(buf):
        none = jnp.zeros((B, margin, C), BF16)
        buf[:, 2 * margin + L :, :] = jnp.zeros((B, 256 - L - 2 * margin, C), BF16)

        @pl.when(me == 0)
        def _():
            buf[:, 0:margin, :] = none

        @pl.when(me == n - 1)
        def _():
            buf[:, margin + L : 2 * margin + L, :] = none

    def conv(bands, buf, u):
        b, j = unit(u)
        x = buf[b, :, j * 128 : (j + 1) * 128]
        return jnp.where(low_lane, nn(bands[2 * j], x), nn(bands[2 * j + 1], x))

    DT, FL = HID, LOW
    dims = [[k for k in reversed(range(NB)) if k != g] for g in range(2)]
    FH = F // 2
    HALF = G.shape[-1]
    everything = pl.ds(0, 2)
    items = {"outer": (0, FH), "inner": (FH, FH), "outval": (2 * FH, C), "keyed": (2 * FH + C, C)}
    item_index = {name: i for i, name in enumerate(items)}

    def peer_of(k):
        return me + (1 - 2 * own_bits[k]) * (1 << k)

    def pair_copy(l, i, g, src, dst):
        return pltpu.make_async_remote_copy(
            src, dst, asem_s.at[l, i, g], asem_r.at[l, i, g],
            device_id={"seq": peer_of(g)}, device_id_type=MESH,
        )

    def right_copies(l, i, ref, ranges):
        return [
            pair_copy(l, i, g, ref.at[pl.ds(0, R), pl.ds(c0, cn)], ref.at[pl.ds(R, R), pl.ds(c0, cn)])
            for g, (c0, cn) in enumerate(ranges)
        ]

    def left_copies(l, i, stage, gathered):
        got = []
        for g in range(2):
            at = [core] + [everything] * (NB - 1)
            at[NB - 1 - g] = 1 - own_bits[g]
            src = stage.at[tuple(at) + (pl.ds(0, CH), pl.ds(0, R))]
            dst = gathered.at[(g, core) + (everything,) * (NB - 2) + (pl.ds(0, CH), pl.ds(R, R))]
            got.append(pair_copy(l, i, g, src, dst))
        return got

    def core_copy(l, i, g, ref):
        return pltpu.make_async_remote_copy(
            ref, ref, bsem_s.at[l, i, g], bsem_r.at[l, i, g],
            device_id={"head": 1 - core}, device_id_type=MESH,
        )

    def left_hand_on(l, i, gathered):
        return [
            core_copy(l, i, g, gathered.at[(g, core) + (everything,) * (NB - 2) + (pl.ds(0, CH), pl.ds(R, R))])
            for g in range(2)
        ]

    def row_copies(l, i, src, dst):
        at = pl.ds(pl.multiple_of(core * L, L), L)
        return [pair_copy(l, i, g, src.at[at], dst.at[g, at]) for g in range(2)]

    def row_hand_on(l, i, dst):
        at = pl.ds(pl.multiple_of(core * L, L), L)
        return [core_copy(l, i, g, dst.at[g, at]) for g in range(2)]

    def each_half(g, act):
        for code in range(n // 2):
            spot = tuple((code >> (NB - 2 - i)) & 1 for i in range(NB - 1))
            at = list(spot)
            at.insert(NB - 1 - g, own_bits[g])
            act((g,) + spot, tuple(at))

    def left_put(x, stage, gathered):
        stage[...] = x.T.reshape(stage.shape)
        for g in range(2):
            def put(to, at):
                gathered[to + (slice(None), slice(0, R))] = stage[at]

            each_half(g, put)

    def left_put_theirs(rows, stage, gathered):
        for g in range(2):
            stage[...] = rows[g].T.reshape(stage.shape)

            def put(to, at):
                gathered[to + (slice(None), slice(R, 2 * R))] = stage[at]

            each_half(g, put)

    def start_all(copies):
        for c in copies:
            c.start()

    def wait_all(copies):
        for c in copies:
            c.wait()

    def weight_grad(g, left, right, first, count, width):
        def step(i, _):
            o = pl.multiple_of(i * width, width)
            x = nn(left[g].reshape(D // 2, 2 * R), right(o)).astype(BF16)
            o = pl.multiple_of(first + o, 128)
            for code in range(n // 2):
                spot = tuple((code >> (NB - 2 - i)) & 1 for i in range(NB - 1))
                G[(g,) + spot + (slice(None), pl.ds(o, width))] = x[code * CH : (code + 1) * CH]
            return 0

        lax.fori_loop(0, count // width, step, 0)

    STAGES = NB - 1

    def rs_copy(l, name, g, stage):
        first, count = items[name]
        cols = (pl.ds(0, CH), pl.ds(first, count))
        d = NB - 2 - stage
        index = [everything] * d + [1 - own_bits[dims[g][d]]] + [own_bits[k] for k in dims[g][d + 1 :]]
        i = item_index[name]
        return pltpu.make_async_remote_copy(
            G.at[(g,) + tuple(index) + cols], RV[stage].at[(l, g) + (everything,) * d + cols],
            gsem_s.at[l, i, g, stage], gsem_r.at[l, i, g, stage],
            device_id={"seq": peer_of(dims[g][d])}, device_id_type=MESH,
        )

    def rs_start(l, name, stage):
        for g in range(2):
            rs_copy(l, name, g, stage).start()

    def rs_add(l, name, stage):
        first, count = items[name]
        for g in range(2):
            rs_copy(l, name, g, stage).wait()
            d = NB - 2 - stage
            mine_at = tuple(own_bits[k] for k in dims[g][d:])
            cols = (slice(None), slice(first, first + count))
            if d:
                for code in range(1 << d):
                    spot = tuple((code >> (d - 1 - i)) & 1 for i in range(d))
                    at = (g,) + spot + mine_at + cols
                    G[at] = G[at] + RV[stage][(l, g) + spot + cols]
            else:
                x = G[(g,) + mine_at + cols].astype(F32) + RV[stage][(l, g) + cols].astype(F32)
                write_out(l, name, g, x)

    def write_out(l, name, g, x):
        if name == "outer":
            OU[l, :, g * FH : (g + 1) * FH] = x
        elif name == "inner":
            OI[l, :, g * FH : (g + 1) * FH] = x
        elif name == "keyed":
            OP[l, g] = x
        elif g == 0:
            OO[l, :, 0:128] = x[:, 0:128]
            OP[l, 2, :, 0 : C - 128] = x[:, 128:C]
        else:
            OO[l, :, 128:C] = x[:, 0 : C - 128]
            OP[l, 2, :, C - 128 : C] = x[:, C - 128 : C]

    def out_copy(i, src, dst):
        return pltpu.make_async_copy(src, dst, osem.at[i])

    def advance(l, name, stage):
        rs_add(l, name, stage)
        if stage + 1 < STAGES:
            rs_start(l, name, stage + 1)

    out_ranges = ((0, 128), (128, C - 128))
    val_ranges = ((2 * C, C - 128), (3 * C - 128, 128))
    key_ranges = ((0, C), (C, C))
    ffn_ranges = ((0, FH), (FH, FH))

    arguments[0].wait()
    for b in range(B):
        HID[b * L : (b + 1) * L, :] = tok[b].astype(F32)
    TB[...] = jnp.zeros_like(TB)

    def make_bands(l):
        backwards = jnp.where(row_id + lane_id == K - 1, 1.0, 0.0).astype(BF16)
        TB[0, 0 : z.local_heads, 0:K] = taps[l].astype(F32)
        TB[1, :, 0:128] = nn(TB[0, :, 0:128].astype(BF16), backwards)
        for which, store in ((0, TT), (1, TR)):
            for h in range(z.local_heads):
                base = jnp.broadcast_to(TB[which, h : h + 1, :], (128, 256))
                store[l, h] = pltpu.roll(base, 0, 1, stride=1, stride_axis=0).astype(BF16)

    def regrow(l):
        wait_all(row_hand_on(l, 2, PN))
        left_put_theirs(PN, LSH, LTN.at[l])
        for g in range(2):
            def step(i, _):
                o = pl.ds(pl.multiple_of(g * FH + i * 256, 256), 256)
                act, slope = unit_rows(PN[g], l, o)
                ACT[l, R : 2 * R, o] = act
                GP[l, R : 2 * R, o] = slope
                return 0

            lax.fori_loop(0, FH // 256, step, 0)

    def unit_rows(rows, l, o):
        pre = nn(rows, WI[l, :, o]) + ibias[l : l + 1, o].astype(F32)
        below = 0.5 * (1.0 + lax.erf(pre * (0.5**0.5)))
        slope = below + pre * jnp.exp(-0.5 * pre * pre) * 0.3989422804014327
        return (pre * below).astype(BF16), slope.astype(BF16)

    def forward(l):
        copies = weight_copies(l)
        e = 2 * l
        LOW[...] = HID[...].astype(BF16)
        copies[0].wait()
        if l == 0:
            for c in [weight_copies(0)[i] for i in (1, 2, 3)] + weight_copies(1):
                c.start()
            for c in arguments[1:]:
                c.wait()
        both_bias = pbias[l].astype(F32)
        bias_q, bias_v = both_bias[0:1], both_bias[1:2]
        q = (nn(LOW[...], WP[l, 0]) + bias_q) * scale
        k = nn(LOW[...], WP[l, 1]) * scale
        QS[l] = q.astype(BF16)
        KS[l] = k.astype(BF16)
        sums = []
        for x in (q, k):
            for b in range(B):
                for r in range(S):
                    at = b * L + r * z.segment
                    sums.append(jnp.sum(x[at : at + z.segment], axis=0, keepdims=True))
        marks = jnp.concatenate(sums, axis=0) * (1.0 / z.segment)
        MS[...] = marks.astype(BF16)
        rest = marks - MS[...].astype(F32)
        middle = rest.astype(BF16).astype(F32)
        rest = rest - middle
        for u in range(U):
            b, j = unit(u)
            parts = [
                x[first + b * S : first + (b + 1) * S, j * 128 : (j + 1) * 128]
                for x in (middle, rest)
                for first in (0, 8)
            ]
            MD[u] = jnp.concatenate(parts, axis=0).astype(BF16)
        if l == 0:
            pl.semaphore_wait(barrier, n)
        spread(lambda t: MS, MB, msem_s.at[l], msem_r.at[l], True)
        for u in range(U):
            to_owner(u, MD.at[u], MO, dsem_s.at[l], dsem_r.at[l])
        MB[me] = MS[...]
        vl = (nn(LOW[...], WP[l, 2]) + bias_v).astype(BF16)
        for b in range(B):
            VX[l, b, margin : margin + L, :] = vl[b * L : (b + 1) * L]
        edge_zeros(VX.at[l])
        edges(VX.at[l], vsem_s.at[l], vsem_r.at[l], "start")
        if l:
            regrow(l - 1)
        left_put(LOW[...], LSH, LTH.at[l])
        make_bands(l)
        edges(VX.at[l], vsem_s.at[l], vsem_r.at[l], "wait")
        for u in range(U):
            b, j = unit(u)
            DQ[b * L : (b + 1) * L, j * 128 : (j + 1) * 128] = conv(TT.at[l], VX.at[l], u)
        spread(lambda t: MS, MB, msem_s.at[l], msem_r.at[l], False)
        hidden_copies = left_copies(l, 0, LSH, LTH.at[l])
        start_all(hidden_copies)
        for u in range(U):
            b, j = unit(u)
            lanes = slice(j * 128, (j + 1) * 128)
            for first, store in ((0, QM), (8, KM)):
                rows = [MB[i, :, lanes].astype(F32)[first + b * S : first + (b + 1) * S] for i in range(n)]
                store[l, u] = jnp.concatenate(rows, axis=0)
        for u in range(U):
            b, j = unit(u)
            ksc = nt(expand(QM[l, u]).astype(BF16), tile(KS, l, u))
            top = jnp.max(ksc, axis=1, keepdims=True)
            p = jnp.exp(ksc - top)
            total = jnp.sum(p, axis=1, keepdims=True)
            v = VX[l, b, margin : margin + L, j * 128 : (j + 1) * 128]
            XM[u] = pack(compress(nn(p.astype(BF16), v)), [to_row(top), to_row(total)])
            to_owner(u, XM.at[u], OB, xsem_s.at[l], xsem_r.at[l])
        @pl.when(is_owner)
        def _():
            owner_gets(MD.at[0], MO, dsem_s.at[l], dsem_r.at[l])
            extra = []
            for i in range(n):
                x = MO[i].astype(F32)
                extra.append(x[0:8] + x[8:16])
            qb = expand(QM[l, mine] + jnp.concatenate([x[0:S] for x in extra], axis=0))
            kb = expand(KM[l, mine] + jnp.concatenate([x[S : 2 * S] for x in extra], axis=0))
            s = lax.dot_general(
                qb, kb, (((1,), (1,)), ((), ())), precision=exact_result, preferred_element_type=F32
            )
            s = jnp.where(same_head, s, -jnp.inf)
            p = jnp.exp(s - jnp.max(s, axis=1, keepdims=True))
            a = p / jnp.sum(p, axis=1, keepdims=True)
            PA[l] = a
            ah = halves(a)
            at = a.T
            sums = jnp.sum(a, axis=0, keepdims=True)
            tops = jnp.where(
                low_lane[0:1],
                jnp.max(jnp.where(low_lane[0:1], sums, 0.0), axis=1, keepdims=True),
                jnp.max(jnp.where(low_lane[0:1], 0.0, sums), axis=1, keepdims=True),
            )
            unit_matrix = jnp.where(eye, 1.0, 0.0)

            def iterate(i, zk):
                PV[l, i, 0] = zk
                PV[l, i, 4] = zk.T
                zh = halves(zk)
                pr = nn3(ah, zh)
                PV[l, i, 1] = pr
                prh = halves(pr)
                n2 = 15.0 * unit_matrix - nn3(prh, halves(7.0 * unit_matrix - pr))
                PV[l, i, 2] = n2
                n3 = 13.0 * unit_matrix - nn3(prh, halves(n2))
                PV[l, i, 3] = n3
                return 0.25 * nn3(zh, halves(n3))

            zk = lax.fori_loop(0, PINV_ITERS, iterate, at / tops)
            PZ[l] = zk.T
            owner_gets(XM.at[0], OB, xsem_s.at[l], xsem_r.at[l])
            stats = [OB[i, 64:80].astype(F32) for i in range(n)]
            tops = jnp.concatenate([jnp.sum(x[0:3], axis=0, keepdims=True) for x in stats], axis=0)
            totals = jnp.concatenate([jnp.sum(x[3:6], axis=0, keepdims=True) for x in stats], axis=0)
            top = jnp.max(tops, axis=0, keepdims=True)
            factors = jnp.exp(tops - top)
            total = jnp.sum(factors * totals, axis=0, keepdims=True)
            shares = halves(factors / total)
            device = lax.broadcasted_iota(jnp.int32, (n, n * 128), 0)
            place = lax.broadcasted_iota(jnp.int32, (n, n * 128), 1) // 128
            pick = jnp.where(device == place, 1.0, 0.0).astype(BF16)
            columns = tn(shares[0], pick) + tn(shares[1], pick)
            mixed = jnp.zeros((64, 128), F32)
            for i in range(n):
                share = compress(columns[:, i * 128 : (i + 1) * 128])
                mixed = mixed + share * OB[i, 0:64].astype(F32)
            MX[l] = mixed
            CR[l, mine] = pack(compress(nn3f(zk, expand(mixed))), [top + jnp.log(total)])
            from_owner(CR.at[l], csem_s.at[l], csem_r.at[l], True)

        for u in range(U):
            s = nt(tile(QS, l, u), expand(KM[l, u]).astype(BF16))
            p = jnp.exp(s - half_tops(s))
            RW[l, u] = p / half_sums(p)

        wait_all(hidden_copies)
        start_all(left_hand_on(l, 0, LTH.at[l]))
        for u in range(U):
            b, j = unit(u)
            to_owner_sent(u, XM.at[u], OB, xsem_s.at[l], xsem_r.at[l])
            to_owner_sent(u, MD.at[u], MO, dsem_s.at[l], dsem_r.at[l])
            owner_came(CR.at[l], u, csem_s.at[l], csem_r.at[l])
            at = (slice(b * L, (b + 1) * L), slice(j * 128, (j + 1) * 128))
            context = nn(RW[l, u].astype(BF16), expand_low(CR[l, u, 0:64])) + DQ[at]
            CTX[(l,) + at] = context.astype(BF16)
        start_all(right_copies(l, 1, CTX.at[l], out_ranges))

        @pl.when(is_owner)
        def _():
            from_owner(CR.at[l], csem_s.at[l], csem_r.at[l], False)

        copies[1].wait()
        swap_start(e, lambda o: nn(CTX[l, 0:R], WO[l, :, o]))
        swap_wait(e)
        total1 = HID[...] + both(e) + obias[l].astype(F32)[0:1]
        T1[l] = total1
        normed = moments(total1)[0] * ngain[l].astype(F32)[0:1] + nshift[l].astype(F32)[0:1]
        HID[...] = normed
        LOW[...] = normed.astype(BF16)
        norm_copies = row_copies(l, 2, LOW, PN)
        start_all(norm_copies)
        copies[2].wait()

        def grow(i, _):
            o = pl.ds(pl.multiple_of(i * 256, 256), 256)
            act, slope = unit_rows(LOW[...], l, o)
            ACT[l, 0:R, o] = act
            GP[l, 0:R, o] = slope
            return 0

        lax.fori_loop(0, F // 256, grow, 0)
        copies[3].wait()

        swap_start(e + 1, lambda o: nn(ACT[l, 0:R], WF[l, :, o]))
        left_put(LOW[...], LSH, LTN.at[l])
        swap_wait(e + 1)
        total2 = HID[...] + both(e + 1) + obias[l].astype(F32)[1:2]
        T2[l] = total2
        HID[...] = moments(total2)[0] * ngain[l].astype(F32)[1:2] + nshift[l].astype(F32)[1:2]
        wait_all(norm_copies)
        start_all(row_hand_on(l, 2, PN))

    def backward(l, slots):
        GX = GXS.at[l]

        def slot(name):
            for step in slots.get(name, ()):
                advance(z.layers - 1, *step)

        e = 2 * z.layers + 2 * (z.layers - 1 - l)
        k = z.layers + l
        base = 60 * l
        total2, sums = norm_back(T2[l], UP[...], ngain[l].astype(F32)[1:2])
        put_small(base + 6, sums[0])
        put_small(base + 18, sums[1])
        put_small(base + 30, sums[2])
        DT[...] = total2
        FL[...] = total2.astype(BF16)
        feed_copies = row_copies(l, 4, FL, PF)
        start_all(feed_copies)
        slot("fed")

        def widen(i, _):
            o = pl.ds(pl.multiple_of(i * 256, 256), 256)
            grad = nt(FL[...], WF[l, o, :]).astype(BF16).astype(F32)
            pre = (GP[l, 0:R, o].astype(F32) * grad).astype(BF16)
            DPRE[0:R, o] = pre
            s = jnp.sum(pre.astype(F32), axis=0, keepdims=True)
            SM[pl.ds(base + 36 + 2 * i, 1), :] = s[:, 0:128]
            SM[pl.ds(base + 37 + 2 * i, 1), :] = s[:, 128:256]
            return 0

        lax.fori_loop(0, F // 256, widen, 0)
        slot("widened")
        swap_start(e, lambda o: nt(DPRE[0:R], WI[l, o, :]))
        slot("narrowed")
        left_put(FL[...], LSH, LTF)
        if l == z.layers - 1:
            regrow(l)
        wait_all(feed_copies)
        start_all(row_hand_on(l, 4, PF))
        swap_wait(e)
        grad_normed = DT[...] + both(e)
        total1, sums = norm_back(T1[l], grad_normed, ngain[l].astype(F32)[0:1])
        put_small(base + 0, sums[0])
        put_small(base + 12, sums[1])
        put_small(base + 24, sums[2])
        DT[...] = total1
        FL[...] = total1.astype(BF16)
        grads = nt(FL[...], WO[l]).astype(BF16)
        for b in range(B):
            GX[b, margin : margin + L, :] = grads[b * L : (b + 1) * L]
        edge_zeros(GX)
        edges(GX, vsem_s.at[k], vsem_r.at[k], "start")

        def g_tile(u):
            b, j = unit(u)
            return GX[b, margin : margin + L, j * 128 : (j + 1) * 128]

        for u in range(U):
            XM[u, 0:64] = compress(tn(RW[l, u].astype(BF16), g_tile(u))).astype(BF16)
            to_owner(u, XM.at[u, pl.ds(0, 64)], OB.at[:, pl.ds(0, 64)], xsem_s.at[k], xsem_r.at[k])
            DQM[u] = jnp.zeros((64, 128), F32)
        slot("asked")
        wait_all(row_hand_on(l, 4, PF))
        left_put_theirs(PF, LSH, LTF)
        for g in range(2):
            def step(i, _):
                o = pl.ds(pl.multiple_of(g * FH + i * 256, 256), 256)
                grad = nt(PF[g], WF[l, o, :]).astype(BF16).astype(F32)
                DPRE[R : 2 * R, o] = (GP[l, R : 2 * R, o].astype(F32) * grad).astype(BF16)
                return 0

            lax.fori_loop(0, FH // 256, step, 0)
        left_put(FL[...], LSH, LTA)
        attend_copies = left_copies(l, 6, LSH, LTA)
        start_all(attend_copies)
        slot("regrown")
        for g in range(2):
            weight_grad(g, LTF, lambda o: ACT[l, :, pl.ds(g * FH + o, FH)], items["outer"][0], FH, FH)
        rs_start(l, "outer", 0)
        slot("outer")

        @pl.when(is_owner)
        def _():
            owner_gets(XM.at[0, pl.ds(0, 64)], OB.at[:, pl.ds(0, 64)], xsem_s.at[k], xsem_r.at[k])
            d_core = OB[0, 0:64].astype(F32)
            for i in range(1, n):
                d_core = d_core + OB[i, 0:64].astype(F32)
            PC[...] = d_core
            d_mixed = nn3f(PZ[l], expand(d_core))
            off = jnp.sum(d_mixed * expand(MX[l]), axis=1, keepdims=True)
            DR[mine] = pack(compress(d_mixed), [to_row(off)])
            from_owner(DR, csem_s.at[k], csem_r.at[k], True)

        for u in range(U):
            b, j = unit(u)
            at = (slice(b * L, (b + 1) * L), slice(j * 128, (j + 1) * 128))
            d_row = nt(g_tile(u), expand_low(CR[l, u, 0:64]))
            rw = RW[l, u]
            d_rs = (rw * (d_row - half_sums(rw * d_row))).astype(BF16)
            DQ[at] = nn(d_rs, expand(KM[l, u]).astype(BF16))
            DKM[u] = compress(tn(d_rs, tile(QS, l, u)))
        for u in range(U):
            to_owner_sent(u, XM.at[u, pl.ds(0, 64)], OB.at[:, pl.ds(0, 64)], xsem_s.at[k], xsem_r.at[k])

        @pl.when(is_owner)
        def _():
            a = PA[l]
            ath = halves(a.T)
            unit_matrix = jnp.where(eye, 1.0, 0.0)

            def back(i, carry):
                dz, da = carry
                i = PINV_ITERS - 1 - i
                zh, zth, prh = halves(PV[l, i, 0]), halves(PV[l, i, 4]), halves(PV[l, i, 1])
                n1h = halves(7.0 * unit_matrix - PV[l, i, 1])
                n2h, n3h = halves(PV[l, i, 2]), halves(PV[l, i, 3])
                dzh = halves(dz)
                dn3 = halves(0.25 * nn3(zth, dzh))
                dn2 = halves(-nn3(prh, dn3))
                dpr = nn3(prh, dn2) - nt3(dn3, n2h) - nt3(dn2, n1h)
                dpr = halves(dpr)
                dz = 0.25 * nt3(dzh, n3h) + nn3(ath, dpr)
                return dz, da + nt3(dpr, zh)

            dz, da = lax.fori_loop(
                0, PINV_ITERS, back, (nt3f(expand(PC[...]), expand(MX[l])), jnp.zeros((128, 128), F32))
            )
            low_row = low_lane[0:1]

            def half_row(x, f):
                return jnp.where(
                    low_row,
                    f(jnp.where(low_row, x, 0.0), axis=1, keepdims=True),
                    f(jnp.where(low_row, 0.0, x), axis=1, keepdims=True),
                )

            sums = jnp.sum(a, axis=0, keepdims=True)
            tops = half_row(sums, jnp.max)
            d_tops = -half_row(jnp.sum(dz * PV[l, 0, 0], axis=0, keepdims=True), jnp.sum) / tops
            at_top = jnp.where(sums == tops, 1.0, 0.0)
            da = da + (dz / tops).T + at_top * d_tops / half_row(at_top, jnp.sum)
            d_ms = halves(a * (da - jnp.sum(a * da, axis=1, keepdims=True)))
            DQM[mine] = compress(nn3(d_ms, halves(expand(KM[l, mine]))))
            DKM[mine] = DKM[mine] + compress(tn3(d_ms, halves(expand(QM[l, mine]))))

        slot("pinv")
        wait_all(attend_copies)
        start_all(left_hand_on(l, 6, LTA))
        for g in range(2):
            weight_grad(g, LTN.at[l], lambda o: DPRE[:, pl.ds(g * FH + o, FH)], items["inner"][0], FH, FH)
        rs_start(l, "inner", 0)
        advance(l, "outer", 0)
        for u in range(U):
            b, j = unit(u)
            at = (slice(b * L, (b + 1) * L), slice(j * 128, (j + 1) * 128))
            owner_came(DR, u, csem_s.at[k], csem_r.at[k])
            dm = expand_low(DR[u, 0:64])
            off = to_col(packed_row(DR.at[u], 0))
            qb = expand(QM[l, u]).astype(BF16)
            kw = jnp.exp(nt(qb, tile(KS, l, u)) - to_col(packed_row(CR.at[l, u], 0)))
            v = VX[l, b, margin : margin + L, j * 128 : (j + 1) * 128]
            DV[at] = tn(kw.astype(BF16), dm)
            d_ks = (kw * (nt(dm, v) - off)).astype(BF16)
            DK[at] = tn(d_ks, qb)
            DQM[u] = DQM[u] + compress(nn(d_ks, tile(KS, l, u)))

        @pl.when(is_owner)
        def _():
            from_owner(DR, csem_s.at[k], csem_r.at[k], False)

        for u in range(U):
            b, j = unit(u)
            lanes = slice(j * 128, (j + 1) * 128)
            dq, dk = DQM[u].astype(BF16), DKM[u].astype(BF16)
            for i in range(n):
                SB[i, b * S : (b + 1) * S, lanes] = dq[i * S : (i + 1) * S]
                SB[i, 8 + b * S : 8 + (b + 1) * S, lanes] = dk[i * S : (i + 1) * S]
        spread(lambda t: SB.at[t], SR, qsem_s.at[l], qsem_r.at[l], True)
        SR[me] = SB[me]
        edges(GX, vsem_s.at[k], vsem_r.at[k], "wait")
        for u in range(U):
            b, j = unit(u)
            at = (slice(b * L, (b + 1) * L), slice(j * 128, (j + 1) * 128))
            DP[b * L : (b + 1) * L, 2 * C + j * 128 : 2 * C + (j + 1) * 128] = (
                DV[at] + conv(TR.at[l], GX, u)
            ).astype(BF16)
        value_copies = right_copies(l, 7, DP, val_ranges)
        start_all(value_copies)
        for j in range(NP):
            for h in range(2):
                found = jnp.zeros((128, 256), F32)
                for b in range(B):
                    g = nn(flip, g_tile(b * NP + j))
                    g = jnp.where(low_lane, g, 0.0) if h == 0 else jnp.where(low_lane, 0.0, g)
                    found = found + nt(g.astype(BF16), VX[l, b, :, j * 128 : (j + 1) * 128])
                found = pltpu.roll(found, 129, 1, stride=1, stride_axis=0)
                row = base + 54 + 2 * j + h
                SM[row : row + 1, :] = jnp.sum(found[:, 0:128], axis=0, keepdims=True)
        wait_all(left_hand_on(l, 6, LTA))
        wait_all(right_copies(l, 1, CTX.at[l], out_ranges))
        out0 = items["outval"][0]
        weight_grad(0, LTA, lambda o: CTX[l, :, pl.ds(o, 128)], out0, 128, 128)
        weight_grad(1, LTA, lambda o: CTX[l, :, pl.ds(128 + o, 256)], out0, C - 128, 256)
        advance(l, "inner", 0)
        wait_all(value_copies)
        wait_all(left_hand_on(l, 0, LTH.at[l]))
        weight_grad(0, LTH.at[l], lambda o: DP[:, pl.ds(2 * C + o, 256)], out0 + 128, C - 128, 256)
        weight_grad(1, LTH.at[l], lambda o: DP[:, pl.ds(3 * C - 128 + o, 128)], out0 + C - 128, 128, 128)
        rs_start(l, "outval", 0)
        spread(lambda t: SB.at[t], SR, qsem_s.at[l], qsem_r.at[l], False)
        marks = SR[0].astype(F32)
        for i in range(1, n):
            marks = marks + SR[i].astype(F32)
        marks = marks * (1.0 / z.segment)
        for b in range(B):
            for r in range(S):
                at = slice(b * L + r * z.segment, b * L + (r + 1) * z.segment)
                i = b * S + r
                DP[at, 0:C] = ((DQ[at] + marks[i : i + 1]) * scale).astype(BF16)
                DP[at, C : 2 * C] = ((DK[at] + marks[8 + i : 9 + i]) * scale).astype(BF16)
        key_copies = right_copies(l, 8, DP, key_ranges)
        start_all(key_copies)

        def onto(o):
            x = nt(DP[0:R, 0:C], WP[l, 0, o, :]) + nt(DP[0:R, C : 2 * C], WP[l, 1, o, :])
            return x + nt(DP[0:R, 2 * C : 3 * C], WP[l, 2, o, :])

        swap_start(e + 1, onto)
        bias = jnp.sum(DP[0:R].astype(F32), axis=0, keepdims=True)
        put_small(base + 48, bias[:, 0:C])
        put_small(base + 51, bias[:, 2 * C : 3 * C])
        if l == 0:
            spread(lambda t: SM.at[pl.ds(pl.multiple_of(t * 8, 8), 8)], SMR, ssem_s, ssem_r, True)
            SMR[me] = SM[pl.ds(pl.multiple_of(me * 8, 8), 8), :]
        advance(l, "outer", 1)
        wait_all(key_copies)
        for g in range(2):
            weight_grad(g, LTH.at[l], lambda o: DP[:, pl.ds(g * C + o, 128)], items["keyed"][0], C, 128)
        rs_start(l, "keyed", 0)
        swap_wait(e + 1)
        UP[...] = DT[...] + both(e + 1)

    for l in range(z.layers):
        forward(l)
    results = [out_copy(b, HID.at[pl.ds(b * L, L)], result.at[b]) for b in range(B)]
    start_all(results)
    for b in range(B):
        shown = to_col(mask[b : b + 1, :].astype(F32))
        UP[b * L : (b + 1) * L, :] = cot[b].astype(F32) * shown
    wait_all(results)
    backward(1, {})
    backward(
        0,
        {
            "fed": [("outer", 2)],
            "widened": [("inner", 1), ("outval", 0)],
            "narrowed": [("keyed", 0)],
            "asked": [("outval", 1), ("inner", 2)],
            "regrown": [("keyed", 1)],
            "outer": [("outval", 2)],
            "pinv": [("keyed", 2)],
        },
    )

    def finish(*steps):
        for step in steps:
            advance(0, *step)

    tokens_out = [out_copy(B + b, UP.at[pl.ds(b * L, L)], gtok.at[b]) for b in range(B)]
    start_all(tokens_out)
    spread(lambda t: SM.at[pl.ds(pl.multiple_of(t * 8, 8), 8)], SMR, ssem_s, ssem_r, False)
    total = SMR[0]
    for i in range(1, n):
        total = total + SMR[i]
    SMT[me] = total
    spread(lambda t: SMT.at[me], SMT, tsem_s, tsem_r, True)
    finish(("inner", 1), ("outval", 0), ("outer", 2))
    finish(("keyed", 0), ("inner", 2), ("outval", 1))
    ffn_out = [out_copy(2 * B, OU, gouter), out_copy(2 * B + 1, OI, ginner)]
    start_all(ffn_out)
    spread(lambda t: SMT.at[me], SMT, tsem_s, tsem_r, False)

    def little(at):
        return SMT[at // 8, at % 8 : at % 8 + 1, :]

    for l in range(z.layers):
        base = 60 * l
        for i in range(D // 128):
            lanes = slice(i * 128, (i + 1) * 128)
            for side in range(2):
                for what in range(3):
                    OS[what, l, side : side + 1, lanes] = little(base + 12 * what + 6 * side + i)
        for i in range(F // 128):
            OT[l : l + 1, i * 128 : (i + 1) * 128] = little(base + 36 + i)
        for i in range(C // 128):
            OB1[l, 0:1, i * 128 : (i + 1) * 128] = little(base + 48 + i)
            OB1[l, 1:2, i * 128 : (i + 1) * 128] = little(base + 51 + i)
        for h in range(z.local_heads):
            OT1[l, h : h + 1, :] = little(base + 54 + h)[:, 0:K]
    small_out = [
        out_copy(2 * B + 2 + i, src, dst)
        for i, (src, dst) in enumerate(
            [(OS.at[0], ggain), (OS.at[1], gshift), (OS.at[2], gobias), (OT, gibias), (OB1, gbias), (OT1, gtaps)]
        )
    ]
    start_all(small_out)
    finish(("keyed", 1), ("outval", 2), ("keyed", 2))
    rest_out = [out_copy(2 * B + 8, OP, gproj), out_copy(2 * B + 9, OO, gout)]
    start_all(rest_out)
    wait_all(tokens_out + ffn_out + small_out + rest_out)


def hand_over(count, *refs):
    sems = refs[-1]
    copies = [
        pltpu.make_async_copy(refs[i], refs[count + i], sems.at[i]) for i in range(count)
    ]
    for c in copies:
        c.start()
    for c in copies:
        c.wait()


def fused(z, tokens, cotangent, masked, projections, projection_bias, conv_taps, output_weight,
          output_bias, norm_gain, norm_shift, inner_weight, inner_bias, outer_weight):
    n, B, L, R, D, C, F = z.n, z.batch, z.length, z.rows, z.width, z.cols, z.hidden
    U, H, NL_, NB, CH = z.units, z.local_heads, z.layers, z.bits, z.width // z.n
    V = pltpu.VMEM
    DMA = pltpu.SemaphoreType.DMA
    cols = F + 2 * C
    staged = lambda: V((2,) * NB + (CH, R), BF16)
    gathered = lambda *lead: V(lead + (2,) * NB + (CH, 2 * R), BF16)
    scratch = dict(
        WP=V((NL_, 3, D, C), BF16), WO=V((NL_, C, D), BF16), WI=V((NL_, D, F), BF16), WF=V((NL_, F, D), BF16),
        QS=V((NL_, R, C), BF16), KS=V((NL_, R, C), BF16),
        VX=V((NL_, B, 256, C), BF16), RW=V((NL_, U, 128, 128), F32),
        CTX=V((NL_, 2 * R, C), BF16), T1=V((NL_, R, D), F32), T2=V((NL_, R, D), F32),
        GP=V((NL_, 2 * R, F), BF16), ACT=V((NL_, 2 * R, F), BF16),
        QM=V((NL_, U, 64, 128), F32), KM=V((NL_, U, 64, 128), F32), CR=V((NL_, U, 80, 128), BF16),
        MX=V((NL_, 64, 128), F32), PA=V((NL_, 128, 128), F32), PV=V((NL_, PINV_ITERS, 5, 128, 128), F32),
        PZ=V((NL_, 128, 128), F32), PC=V((64, 128), F32), LTH=gathered(NL_), LTN=gathered(NL_),
        HID=V((R, D), F32), UP=V((R, D), F32), LOW=V((R, D), BF16), PN=V((2, R, D), BF16), PF=V((2, R, D), BF16),
        DPRE=V((2 * R, F), BF16), GXS=V((NL_, B, 256, C), BF16), DQ=V((R, C), F32), DK=V((R, C), F32), DV=V((R, C), F32),
        DP=V((2 * R, 3 * C), BF16), DQM=V((U, 64, 128), F32), DKM=V((U, 64, 128), F32), DR=V((U, 80, 128), BF16),
        SM=V((n * 8, 128), F32), TB=V((2, 8, 256), F32),
        TT=V((NL_, H, 128, 256), BF16), TR=V((NL_, H, 128, 256), BF16), LTF=gathered(), LTA=gathered(),
        LSH=staged(), OP=V((NL_, 3, CH, C), F32), OO=V((NL_, CH, C), F32), OI=V((NL_, CH, F), F32),
        OU=V((NL_, CH, F), F32), OS=V((3, NL_, 2, D), F32), OT=V((NL_, F), F32),
        OB1=V((NL_, 2, C), F32), OT1=V((NL_, H, z.kernel), F32),
        tok=V((B, L, D), BF16), cot=V((B, L, D), BF16), mask=V((B, L), jnp.int32), pbias=V((NL_, 2, C), BF16),
        taps=V((NL_, H, z.kernel), BF16), obias=V((NL_, 2, D), BF16), ngain=V((NL_, 2, D), BF16),
        nshift=V((NL_, 2, D), BF16), ibias=V((NL_, F), BF16),
        MS=V((16, C), BF16), MB=V((n, 16, C), BF16), MD=V((U, 16, 128), BF16), MO=V((n, 16, 128), BF16), XM=V((U, 80, 128), BF16), OB=V((n, 80, 128), BF16),
        SB=V((n, 16, C), BF16), SR=V((n, 16, C), BF16), HS=V((2, R, D), BF16), HR=V((2, R, D), BF16),
        SMR=V((n, 8, 128), F32), SMT=V((n, 8, 128), F32),
        G=V((2,) * NB + (CH, cols), BF16),
        RV=[V((NL_, 2) + (2,) * (NB - 2 - s) + (CH, cols), BF16) for s in range(NB - 1)],
        wsem=DMA((NL_, 4)),
        hsem_s=DMA((4 * NL_, D // 256)), hsem_r=DMA((4 * NL_, D // 256)),
        msem_s=DMA((NL_, n)), msem_r=DMA((NL_, n)), dsem_s=DMA((NL_, U)), dsem_r=DMA((NL_, n)), xsem_s=DMA((2 * NL_, U)), xsem_r=DMA((2 * NL_, n)),
        csem_s=DMA((2 * NL_, n)), csem_r=DMA((2 * NL_, U)), vsem_s=DMA((2 * NL_, 2)), vsem_r=DMA((2 * NL_, 2)),
        osem=DMA((2 * B + 10,)), isem=DMA((9,)),
        asem_s=DMA((NL_, 9, 2)), asem_r=DMA((NL_, 9, 2)), bsem_s=DMA((NL_, 9, 2)), bsem_r=DMA((NL_, 9, 2)),
        gsem_s=DMA((NL_, 4, 2, NB - 1)), gsem_r=DMA((NL_, 4, 2, NB - 1)), qsem_s=DMA((NL_, n)), qsem_r=DMA((NL_, n)),
        ssem_s=DMA((n,)), ssem_r=DMA((n,)), tsem_s=DMA((n,)), tsem_r=DMA((n,)),
    )
    in_vmem = pl.BlockSpec(memory_space=pltpu.VMEM)
    in_hbm = pl.BlockSpec(memory_space=pl.ANY)
    out = lambda *s: jax.ShapeDtypeStruct(s, F32)
    shapes = (
        out(B, L, D), out(B, L, D), out(NL_, 3, CH, C), out(NL_, 2, C), out(NL_, H, z.kernel), out(NL_, CH, C),
        out(NL_, 2, D), out(NL_, 2, D), out(NL_, 2, D), out(NL_, CH, F), out(NL_, F), out(NL_, CH, F),
    )
    outs = pl.pallas_call(
        partial(fused_kernel, z),
        out_shape=shapes,
        in_specs=[in_hbm] * 13,
        out_specs=(in_hbm,) * len(shapes),
        scratch_shapes=scratch,
        compiler_params=pltpu.CompilerParams(
            collective_id=1, has_side_effects=True, vmem_limit_bytes=VMEM_LIMIT
        ),
    )(tokens, cotangent, masked, projection_bias, conv_taps, output_bias, norm_gain, norm_shift, inner_bias,
      projections, output_weight, inner_weight, outer_weight)
    outs = list(
        pl.pallas_call(
            partial(hand_over, len(shapes)),
            out_shape=shapes,
            in_specs=[in_vmem] * len(shapes),
            out_specs=(in_hbm,) * len(shapes),
            scratch_shapes=[DMA((len(shapes),))],
        )(*outs)
    )
    for i in (5, 11):
        outs[i] = jnp.swapaxes(outs[i], 1, 2)
    return tuple(outs)


def solution(mesh):
    in_specs = (
        P(None, "seq", None),
        P(None, "seq", None),
        P(None, "seq"),
        P(None, None, None, "head"),
        P(None, None, "head"),
        P(None, "head", None),
        P(None, "head", None),
        P(),
        P(),
        P(),
        P(None, None, "head"),
        P(None, "head"),
        P(None, "head", None),
    )
    out_specs = (
        P(None, "seq", None),
        P(None, "seq", None),
        P(None, None, "seq", "head"),
        P(None, None, "head"),
        P(None, "head", None),
        P(None, "head", "seq"),
        P(),
        P(),
        P(),
        P(None, "seq", "head"),
        P(None, "head"),
        P(None, "head", "seq"),
    )

    def whole(*args):
        z = Fast(mesh.shape, args[0], args[5], args[10])
        body = partial(fused, z) if z.fits() else on_device
        return jax.shard_map(
            body, mesh=mesh, in_specs=in_specs, out_specs=out_specs, check_vma=False
        )(*args)

    return whole
```
